32 devices in a mesh: grp: 2 (over core), ep: 16 (over z, y, x).
Axes of the slice: x: 2, y: 2, z: 4, core: 2. Of those that a mesh axis runs over, the one named last changes fastest.
Arguments:
- layer_input: bfloat16 [4096, 2048], P(('grp', 'ep')), may hold values from -6 to 6
- attention_gain: bfloat16 [2048], P('ep'), may hold values from 0.099609375 to 1.8984375
- query_weight: bfloat16 [2048, 3072], P('ep'), may hold values from -0.125 to 0.125
- latent_weight: bfloat16 [2048, 576], P('ep'), may hold values from -0.125 to 0.125
- latent_gain: bfloat16 [512], P('ep'), may hold values from 0.099609375 to 1.8984375
- expand_weight: bfloat16 [512, 4096], P('ep'), may hold values from -0.25 to 0.25
- output_weight: bfloat16 [2048, 2048], P('ep'), may hold values from -4 to 4
- feedforward_gain: bfloat16 [2048], P('ep'), may hold values from 0.099609375 to 1.8984375
- router_weight: bfloat16 [2048, 16], P('ep'), may hold values from -0.0625 to 0.0625
- shared_gate: bfloat16 [2048, 2816], P('ep'), may hold values from -0.125 to 0.125
- shared_up: bfloat16 [2048, 2816], P('ep'), may hold values from -0.125 to 0.125
- shared_down: bfloat16 [2816, 2048], P('ep'), may hold values from -0.109375 to 0.109375
- expert_gate: bfloat16 [16, 2048, 1408], P('ep'), may hold values from -0.125 to 0.125
- expert_up: bfloat16 [16, 2048, 1408], P('ep'), may hold values from -0.125 to 0.125
- expert_down: bfloat16 [16, 1408, 2048], P('ep'), may hold values from -0.625 to 0.625
- expert_routes: int32 [4096, 6], P(('grp', 'ep')), may hold values from 0 to 15, all different within a row
- prefix_length: int32 [2], P('grp'), may hold values from 128 to 1024
- output_grad: bfloat16 [4096, 2048], P(('grp', 'ep')), may hold values from -6 to 6
Outputs:
- layer_output: bfloat16 [4096, 2048], P(('grp', 'ep'))
- input_grad: bfloat16 [4096, 2048], P(('grp', 'ep'))
- attention_gain_grad: float32 [2048], P(('grp', 'ep'))
- query_weight_grad: float32 [2048, 3072], P(('grp', 'ep'))
- latent_weight_grad: float32 [2048, 576], P(('grp', 'ep'))
- latent_gain_grad: float32 [512], P(('grp', 'ep'))
- expand_weight_grad: float32 [512, 4096], P(('grp', 'ep'))
- output_weight_grad: float32 [2048, 2048], P(('grp', 'ep'))
- feedforward_gain_grad: float32 [2048], P(('grp', 'ep'))
- router_weight_grad: float32 [2048, 16], P(('grp', 'ep'))
- shared_gate_grad: float32 [2048, 2816], P(('grp', 'ep'))
- shared_up_grad: float32 [2048, 2816], P(('grp', 'ep'))
- shared_down_grad: float32 [2816, 2048], P(('grp', 'ep'))
- expert_gate_grad: float32 [16, 2048, 1408], P('ep', 'grp')
- expert_up_grad: float32 [16, 2048, 1408], P('ep', 'grp')
- expert_down_grad: float32 [16, 1408, 2048], P('ep', 'grp')
The draws below stay inside these ranges and needn't reach their ends.
Inputs may be any that keep to these rules, and one draw needn't show every extreme that they name: `expert_routes`: each row names 6 different experts.
All inputs are finite; a program needn't handle non-finite values.
Results may differ from the reference program's by a relative error of at most 0.02.
Values may be sent and summed in bfloat16 or wider, within the bound.
A program may use at most 384 MiB of HBM per device.

```python
import math
from functools import partial
import jax
import jax.numpy as jnp
from jax import lax

D = 2048
HEADS = 16
NOPE = 128
ROPE = 64
VH = 128
LATENT = 512
FF = 1408
SFF = 2816
TOPK = 6
TOK_DEV = 128
EXPERTS = 16
CAP = 64
SEQLEN = 2048
TOKENS = 4096
N_GRP = 2
N_EP = 16


def steps_of(stream_key, dims, shards, low, largest):
    def one(dim, parts):
        heights = jax.random.uniform(jax.random.fold_in(jax.random.fold_in(stream_key, 6), dim), (parts,), jnp.float32, low / len(shards), largest / len(shards))
        return jnp.repeat(jnp.exp(heights), dims[dim] // parts).reshape((-1,) + (1,) * (len(dims) - dim - 1))

    factor_of = one(*shards[0])
    for cut in shards[1:]:
        factor_of = factor_of * one(*cut)
    return factor_of


def different_ones(key, rows, amount, top, lift):
    ranking = jax.random.permutation(jax.random.fold_in(key, 1), amount)
    pull = ranking
    for power in range(3):
        pull = pull * pull // amount
    pull = pull * lift // amount
    chance = jax.random.randint(jax.random.fold_in(key, 2), (rows, amount), 0, 4096) + pull
    sure = jax.random.permutation(jax.random.fold_in(key, 3), rows)[jnp.arange(amount) % rows]
    chance = jnp.where(jnp.arange(rows)[:, None] == sure[None, :], 1 << 14, chance)
    priority = chance * amount + jnp.arange(amount)
    return lax.top_k(priority.astype(jnp.int32), top)[1].astype(jnp.int32)


def normal_values(stream_key, extent, deviation, reach, split=(), kind=jnp.bfloat16):
    values = jax.random.normal(stream_key, extent, jnp.float32) * deviation
    if len(split) > 0:
        values = steps_of(stream_key, extent, split, -0.22, 0.18) * values
    return jnp.clip(values, min=-reach, max=reach).astype(kind)


def setup_inputs(seed: int = 0) -> dict:
    keys = jax.random.split(jax.random.key(seed), 19)
    return {
        "layer_input": normal_values(keys[0], (TOKENS, D), 1.0, 6.0, ((0, 32),)),
        "attention_gain": jnp.clip(1.0 + 0.18 * jax.random.normal(keys[1], (D,), jnp.float32), 0.099609375, 1.8984375).astype(jnp.bfloat16),
        "query_weight": normal_values(keys[2], (D, HEADS * (NOPE + ROPE)), D ** -0.5, 0.125, ((0, 16),)),
        "latent_weight": normal_values(keys[3], (D, LATENT + ROPE), D ** -0.5, 0.125, ((0, 16),)),
        "latent_gain": jnp.clip(1.0 + 0.18 * jax.random.normal(keys[4], (LATENT,), jnp.float32), 0.099609375, 1.8984375).astype(jnp.bfloat16),
        "expand_weight": normal_values(keys[5], (LATENT, HEADS * (NOPE + VH)), LATENT ** -0.5, 0.25, ((0, 16),)),
        "output_weight": normal_values(keys[6], (HEADS * VH, D), (HEADS * VH * 2 // SEQLEN) ** -0.5, 4.0, ((0, 16),)),
        "feedforward_gain": jnp.clip(1.0 + 0.18 * jax.random.normal(keys[7], (D,), jnp.float32), 0.099609375, 1.8984375).astype(jnp.bfloat16),
        "router_weight": normal_values(keys[8], (D, EXPERTS), (4 * D) ** -0.5, 0.0625, ((0, 16),)),
        "shared_gate": normal_values(keys[9], (D, SFF), D ** -0.5, 0.125, ((0, 16),)),
        "shared_up": normal_values(keys[10], (D, SFF), D ** -0.5, 0.125, ((0, 16),)),
        "shared_down": normal_values(keys[11], (SFF, D), SFF ** -0.5, 0.109375, ((0, 16),)),
        "expert_gate": normal_values(keys[12], (EXPERTS, D, FF), D ** -0.5, 0.125, ((0, 16),)),
        "expert_up": normal_values(keys[13], (EXPERTS, D, FF), D ** -0.5, 0.125, ((0, 16),)),
        "expert_down": normal_values(keys[14], (EXPERTS, FF, D), (FF // 16) ** -0.5, 0.625, ((0, 16),)),
        "expert_routes": different_ones(keys[15], TOKENS, EXPERTS, TOPK, 3072),
        "prefix_length": jax.random.randint(keys[16], (N_GRP,), TOK_DEV, SEQLEN // 2 + 1).astype(jnp.int32),
        "output_grad": normal_values(keys[17], (TOKENS, D), 1.0, 6.0, ((0, 32),)),
    }


EPSILON = 1e-06
MASKED = -1e+30
HIGHEST = lax.Precision.HIGHEST

@jax.custom_vjp
def low(v):
    return lax.optimization_barrier(v.astype(jnp.bfloat16)).astype(jnp.float32)

@jax.custom_vjp
def low_back(v):
    return v

def low_keep(v):
    return (low(v), None)

def low_pass(kept, grad):
    return (grad,)

def back_keep(v):
    return (v, None)

def back_low(kept, grad):
    return (low(grad),)
low.defvjp(low_keep, low_pass)
low_back.defvjp(back_keep, back_low)

def rms_scale(values):
    return lax.rsqrt(lax.optimization_barrier(jnp.mean(values * values, axis=-1, keepdims=True)) + EPSILON)

def rotary_tables(positions):
    halfway = ROPE // 2
    inverse = 10000.0 ** (-(jnp.arange(halfway, dtype=jnp.float32) * 2.0 / ROPE))
    angles = positions[:, None] * inverse[None, :]
    return (jnp.cos(angles), jnp.sin(angles))

def rotate(values, cos_table, sin_table):
    halfway = values.shape[-1] // 2
    first = values[..., :halfway]
    second = values[..., halfway:]
    return jnp.concatenate([first * cos_table - second * sin_table, second * cos_table + first * sin_table], axis=-1)

def matmul(left, right):
    return jnp.dot(left, right, precision=HIGHEST)

def attend_sequence(inputs):
    queries, key_nope, key_rope, values, prefix = inputs
    scale = 1.0 / math.sqrt(NOPE + ROPE)
    scores = jnp.einsum('qhd,khd->hqk', queries[..., :NOPE], key_nope, precision=HIGHEST)
    scores = scores + jnp.einsum('qhd,kd->hqk', queries[..., NOPE:], key_rope, precision=HIGHEST)
    scores = low_back(scores * scale)
    places = jnp.arange(SEQLEN, dtype=jnp.int32)
    visible = (places[None, :] <= places[:, None]) | (places[None, :] < prefix)
    scores = jnp.where(visible[None], scores, MASKED)
    weights = low(jax.nn.softmax(scores, axis=-1))
    attended = jnp.einsum('hqk,khd->qhd', weights, values, precision=HIGHEST)
    return low_back(low(attended))

def expert_group(expert_rows, gate_stack, up_stack, down_stack):
    gate_value = low_back(jnp.einsum('erd,edf->erf', expert_rows, gate_stack, precision=HIGHEST))
    up_value = low_back(jnp.einsum('erd,edf->erf', expert_rows, up_stack, precision=HIGHEST))
    hidden = low(jax.nn.silu(gate_value) * up_value)
    return low_back(low(jnp.einsum('erf,efd->erd', hidden, down_stack, precision=HIGHEST)))

def slot_tables(expert_routes, gates):
    devices = TOKENS // TOK_DEV
    flat_routes = expert_routes.reshape(devices, TOK_DEV * TOPK)
    expert_hot = (flat_routes[..., None] == jnp.arange(EXPERTS, dtype=jnp.int32)).astype(jnp.int32)
    place = lax.optimization_barrier(jnp.sum((jnp.cumsum(expert_hot, axis=1) - 1) * expert_hot, axis=-1))
    kept_mask = place < CAP
    slot_index = flat_routes * CAP + place
    slot_match = (slot_index[..., None] == jnp.arange(EXPERTS * CAP, dtype=jnp.int32)) & kept_mask[..., None]
    ones = slot_match.astype(jnp.float32).reshape(devices, TOK_DEV, TOPK, EXPERTS * CAP)
    dispatch = lax.optimization_barrier(jnp.sum(ones, axis=2))
    weighted = lax.optimization_barrier(jnp.sum(ones * gates.reshape(devices, TOK_DEV, TOPK, 1), axis=2))
    return (dispatch, weighted)

def forward(layer_input, attention_gain, query_weight, latent_weight, latent_gain, expand_weight, output_weight, feedforward_gain, router_weight, shared_gate, shared_up, shared_down, expert_gate, expert_up, expert_down, expert_routes, prefix_length):
    devices = TOKENS // TOK_DEV
    normed = low(layer_input * rms_scale(layer_input) * attention_gain)
    positions = jnp.tile(jnp.arange(SEQLEN, dtype=jnp.float32), N_GRP)
    cos_table, sin_table = rotary_tables(positions)
    query_raw = low_back(matmul(normed, query_weight)).reshape(TOKENS, HEADS, NOPE + ROPE)
    query = low(jnp.concatenate([query_raw[..., :NOPE], rotate(query_raw[..., NOPE:], cos_table[:, None, :], sin_table[:, None, :])], axis=-1))
    compressed = low_back(matmul(normed, latent_weight))
    latent_raw = compressed[:, :LATENT]
    latent = low(latent_raw * rms_scale(latent_raw) * latent_gain)
    key_rope = low(rotate(compressed[:, LATENT:], cos_table, sin_table))
    expanded = low(matmul(latent, expand_weight)).reshape(TOKENS, HEADS, NOPE + VH)
    attended = lax.map(jax.checkpoint(attend_sequence), (query.reshape(N_GRP, SEQLEN, HEADS, NOPE + ROPE), expanded[..., :NOPE].reshape(N_GRP, SEQLEN, HEADS, NOPE), key_rope.reshape(N_GRP, SEQLEN, ROPE), expanded[..., NOPE:].reshape(N_GRP, SEQLEN, HEADS, VH), prefix_length))
    attended = attended.reshape(TOKENS, HEADS * VH)
    residual_mid = layer_input + low_back(matmul(attended, output_weight))
    ffn_in = low(residual_mid * rms_scale(residual_mid) * feedforward_gain)
    logits = low_back(matmul(ffn_in, router_weight))
    router = jax.nn.softmax(logits, axis=-1)
    gates = jnp.take_along_axis(router, expert_routes, axis=1)
    shared_g = low_back(matmul(ffn_in, shared_gate))
    shared_u = low_back(matmul(ffn_in, shared_up))
    shared_hidden = low(jax.nn.silu(shared_g) * shared_u)
    shared_out = matmul(shared_hidden, shared_down)
    dispatch, weighted = slot_tables(expert_routes, gates)
    sent = low_back(jnp.einsum('nts,ntd->nsd', dispatch, ffn_in.reshape(devices, TOK_DEV, D), precision=HIGHEST))
    grouped = sent.reshape(N_GRP, N_EP, EXPERTS, CAP, D).transpose(0, 2, 1, 3, 4).reshape(N_GRP, EXPERTS, N_EP * CAP, D)
    expert_fn = jax.checkpoint(partial(expert_group, gate_stack=expert_gate, up_stack=expert_up, down_stack=expert_down))
    outputs = lax.map(expert_fn, grouped)
    returned = outputs.reshape(N_GRP, EXPERTS, N_EP, CAP, D).transpose(0, 2, 1, 3, 4).reshape(devices, EXPERTS * CAP, D)
    mixture = jnp.einsum('nts,nsd->ntd', weighted, returned, precision=HIGHEST).reshape(TOKENS, D)
    return residual_mid + low_back(shared_out + mixture)

def reference(layer_input, attention_gain, query_weight, latent_weight, latent_gain, expand_weight, output_weight, feedforward_gain, router_weight, shared_gate, shared_up, shared_down, expert_gate, expert_up, expert_down, expert_routes, prefix_length, output_grad):
    floats = tuple((item.astype(jnp.float32) for item in (layer_input, attention_gain, query_weight, latent_weight, latent_gain, expand_weight, output_weight, feedforward_gain, router_weight, shared_gate, shared_up, shared_down, expert_gate, expert_up, expert_down)))

    def wrapped(*values):
        return forward(*values, expert_routes, prefix_length)
    result, pullback = jax.vjp(wrapped, *floats)
    grads = pullback(output_grad.astype(jnp.float32))
    return (result.astype(jnp.bfloat16), grads[0].astype(jnp.bfloat16), grads[1].astype(jnp.float32), grads[2].astype(jnp.float32), grads[3].astype(jnp.float32), grads[4].astype(jnp.float32), grads[5].astype(jnp.float32), grads[6].astype(jnp.float32), grads[7].astype(jnp.float32), grads[8].astype(jnp.float32), grads[9].astype(jnp.float32), grads[10].astype(jnp.float32), grads[11].astype(jnp.float32), grads[12].astype(jnp.float32), grads[13].astype(jnp.float32), grads[14].astype(jnp.float32))
```

```python
import functools
import math

import jax
import jax.numpy as jnp
from jax import lax
from jax.experimental import pallas as pl
from jax.experimental.pallas import tpu as pltpu
from jax.sharding import PartitionSpec as P

D = 2048
HEADS = 16
NOPE = 128
ROPE = 64
VH = 128
LATENT = 512
TOPK = 6

EPSILON = 1e-06
MASKED = -1e30

MESH = pl.DeviceIdType.MESH
ANY = pl.BlockSpec(memory_space=pl.ANY)
DMA = pltpu.SemaphoreType.DMA
F32 = jnp.float32
BF16 = jnp.bfloat16


def remote(src, dst, send, recv, peer):
    return pltpu.make_async_remote_copy(
        src_ref=src,
        dst_ref=dst,
        send_sem=send,
        recv_sem=recv,
        device_id={"ep": peer},
        device_id_type=MESH,
    )


def greet(peers):
    barrier = pltpu.get_barrier_semaphore()
    for peer in peers:
        pl.semaphore_signal(barrier, inc=1, device_id={"ep": peer}, device_id_type=MESH)
    pl.semaphore_wait(barrier, len(peers))


def around(n):
    me = lax.axis_index("ep")
    x, y = me % 2, (me // 2) % 2
    return me, me // 4, y, x, me + 1 - 2 * x, me + 2 - 4 * y


def gather_kernel(n, x_ref, o_ref, own, zs, zr, xs, xr, ys, yr):
    me, z, y, x, px, py = around(n)
    nz = n // 4
    low = me % 4
    half = x_ref.shape[0] // 2
    top, bottom = pl.ds(0, half), pl.ds(half, half)
    at = [((z + k) % nz) * 4 + low for k in range(nz)]
    back = [((z + nz - k) % nz) * 4 + low for k in range(nz)]
    greet([px, py] + at[1:])
    local = pltpu.make_async_copy(x_ref, o_ref.at[me], own)
    local.start()
    sends = []

    def send(copy):
        copy.start()
        sends.append(copy)

    def over_x(src, b, part, i):
        return remote(src.at[part], o_ref.at[b, part], xs.at[i], xr.at[i], px)

    def over_y(src, b, part, i):
        return remote(src.at[part], o_ref.at[b, part], ys.at[i], yr.at[i], py)

    for k in range(1, nz):
        send(remote(x_ref, o_ref.at[me], zs.at[k], zr.at[k], at[k]))
    for k in range(nz):
        b = back[k]
        if k:
            remote(x_ref, o_ref.at[b], zs.at[k], zr.at[k], at[k]).wait_recv()
        src = o_ref.at[b] if k else x_ref
        send(over_x(src, b, top, k))
        send(over_y(src, b, bottom, k))
        send(over_y(src, b, top, nz + k))
        send(over_x(src, b, bottom, nz + k))
    for k in range(nz):
        bx = back[k] + px - me
        by = back[k] + py - me
        over_x(o_ref.at[bx], bx, top, k).wait_recv()
        send(over_y(o_ref.at[bx], bx, top, 2 * nz + k))
        over_y(o_ref.at[by], by, bottom, k).wait_recv()
        send(over_x(o_ref.at[by], by, bottom, 2 * nz + k))
    for k in range(nz):
        bx = back[k] + px - me
        by = back[k] + py - me
        bxy = bx + py - me
        over_y(o_ref.at[by], by, top, nz + k).wait_recv()
        over_x(o_ref.at[bx], bx, bottom, nz + k).wait_recv()
        over_y(o_ref.at[bxy], bxy, top, 2 * nz + k).wait_recv()
        over_x(o_ref.at[bxy], bxy, bottom, 2 * nz + k).wait_recv()
    for copy in sends:
        copy.wait_send()
    local.wait()


def gather(x, cid):
    n = lax.axis_size("ep")
    nz = n // 4
    return pl.pallas_call(
        functools.partial(gather_kernel, n),
        out_shape=jax.ShapeDtypeStruct((n,) + x.shape, x.dtype),
        in_specs=[ANY],
        out_specs=ANY,
        scratch_shapes=[DMA, DMA((nz,)), DMA((nz,))] + [DMA((3 * nz,))] * 4,
        compiler_params=pltpu.CompilerParams(collective_id=cid, has_side_effects=True),
        name="gather",
    )(x)


def add_rows(dst, left, right, rows):
    step = 16

    def body(i, carry):
        r = pl.ds(pl.multiple_of(i * step, step), step)
        dst[r] = (left[r].astype(F32) + right[r].astype(F32)).astype(dst.dtype)
        return carry

    lax.fori_loop(0, rows // step, body, 0)


def scatter_kernel(
    n, p_ref, o_ref, la, lb, a1, b1, a2, b2, zb, lsa, lsb, xs, xr, ys, yr, zs, zr
):
    me, z, y, x, px, py = around(n)
    nz = n // 4
    low = me % 4
    half = p_ref.shape[3] // 2
    top, bottom = pl.ds(0, half), pl.ds(half, half)
    to = [(z + k) % nz for k in range(nz)]
    at = [t * 4 + low for t in to]
    greet([px, py] + at[1:])
    order = list(range(1, nz)) + [0]
    first, second, third = {}, {}, {}
    sends = []
    for k in order:
        t = to[k]
        c = remote(p_ref.at[t, 1 - y, :, top], a1.at[k], ys.at[k], yr.at[k], py)
        d = remote(p_ref.at[t, :, 1 - x, bottom], b1.at[k], xs.at[k], xr.at[k], px)
        c.start()
        d.start()
        e = pltpu.make_async_copy(p_ref.at[t, y, :, top], la.at[k], lsa.at[k])
        f = pltpu.make_async_copy(p_ref.at[t, :, x, bottom], lb.at[k], lsb.at[k])
        e.start()
        f.start()
        first[k] = (c, d, e, f)
        sends += [c, d]
    for k in order:
        c, d, e, f = first[k]
        e.wait()
        c.wait_recv()
        for i in range(2):
            add_rows(la.at[k, i], la.at[k, i], a1.at[k, i], half)
        g = remote(la.at[k, 1 - x], a2.at[k], xs.at[nz + k], xr.at[nz + k], px)
        g.start()
        f.wait()
        d.wait_recv()
        for i in range(2):
            add_rows(lb.at[k, i], lb.at[k, i], b1.at[k, i], half)
        h = remote(lb.at[k, 1 - y], b2.at[k], ys.at[nz + k], yr.at[nz + k], py)
        h.start()
        second[k] = (g, h)
        sends += [g, h]
    for k in order:
        g, h = second[k]
        g.wait_recv()
        add_rows(a2.at[k], la.at[k, x], a2.at[k], half)
        if k:
            c = remote(a2.at[k], zb.at[k, top], zs.at[k], zr.at[k], at[k])
            c.start()
        h.wait_recv()
        add_rows(b2.at[k], lb.at[k, y], b2.at[k], half)
        if k:
            d = remote(b2.at[k], zb.at[k, bottom], zs.at[nz + k], zr.at[nz + k], at[k])
            d.start()
            third[k] = (c, d)
            sends += [c, d]
    for k in range(1, nz):
        c, d = third[k]
        c.wait_recv()
        d.wait_recv()
    for part, offset in ((a2, 0), (b2, half)):

        def body(i, carry, part=part, offset=offset):
            r = pl.ds(pl.multiple_of(i * 16, 16), 16)
            q = pl.ds(pl.multiple_of(i * 16 + offset, 16), 16)
            total = part[0, r].astype(F32)
            for k in range(1, nz):
                total = total + zb[k, q].astype(F32)
            o_ref[q] = total.astype(o_ref.dtype)
            return carry

        lax.fori_loop(0, half // 16, body, 0)
    for copy in sends:
        copy.wait_send()


def scatter(p, cid):
    n = lax.axis_size("ep")
    nz = n // 4
    rows, cols = p.shape[1:]
    half = rows // 2
    p = p.reshape(nz, 2, 2, rows, cols)

    def room(*shape):
        return pltpu.VMEM(shape, p.dtype)

    return pl.pallas_call(
        functools.partial(scatter_kernel, n),
        out_shape=jax.ShapeDtypeStruct((rows, cols), F32),
        in_specs=[ANY],
        out_specs=pl.BlockSpec(memory_space=pltpu.VMEM),
        scratch_shapes=[room(nz, 2, half, cols)] * 4
        + [room(nz, half, cols)] * 2
        + [room(nz, rows, cols)]
        + [DMA((nz,))] * 2
        + [DMA((2 * nz,))] * 6,
        compiler_params=pltpu.CompilerParams(
            collective_id=cid, has_side_effects=True, vmem_limit_bytes=40 << 20
        ),
        name="scatter",
    )(p)


def swap_kernel(n, m, *refs):
    ins, outs, (own, ss, rs) = refs[:m], refs[m : 2 * m], refs[2 * m :]
    me = lax.axis_index("ep")
    to = [(me + k) % n for k in range(n)]
    back = [(me + n - k) % n for k in range(n)]
    greet(to[1:])
    copies = []
    for j in range(m):
        local = pltpu.make_async_copy(ins[j].at[me], outs[j].at[me], own.at[j])
        local.start()
        copies.append(local)
    sends = []
    for k in range(1, n):
        for j in range(m):
            c = remote(ins[j].at[to[k]], outs[j].at[me], ss.at[j, k], rs.at[j, k], to[k])
            c.start()
            sends.append(c)
    for k in range(1, n):
        for j in range(m):
            remote(
                ins[j].at[back[k]], outs[j].at[back[k]], ss.at[j, k], rs.at[j, k], to[k]
            ).wait_recv()
    for c in sends:
        c.wait_send()
    for c in copies:
        c.wait()


def swap(cid, *arrays):
    n = lax.axis_size("ep")
    m = len(arrays)
    return pl.pallas_call(
        functools.partial(swap_kernel, n, m),
        out_shape=[jax.ShapeDtypeStruct(a.shape, a.dtype) for a in arrays],
        in_specs=[ANY] * m,
        out_specs=[ANY] * m,
        scratch_shapes=[DMA((m,)), DMA((m, n)), DMA((m, n))],
        compiler_params=pltpu.CompilerParams(collective_id=cid, has_side_effects=True),
        name="swap",
    )(*arrays)


def over_groups(p):
    groups = lax.axis_size("grp")
    if groups == 2:
        g = lax.axis_index("grp")
        mine = lax.dynamic_index_in_dim(p, g, 0, keepdims=False)
        theirs = lax.dynamic_index_in_dim(p, 1 - g, 0, keepdims=False).astype(BF16)
        return mine.astype(F32) + lax.ppermute(theirs, "grp", [(0, 1), (1, 0)]).astype(F32)
    return lax.psum_scatter(p.astype(BF16), "grp", scatter_dimension=0, tiled=False).astype(F32)


def to_row_owner(block):
    groups, n = lax.axis_size("grp"), lax.axis_size("ep")
    pairs = [(h * n + e, e * groups + h) for h in range(groups) for e in range(n)]
    return lax.ppermute(block.astype(BF16), ("grp", "ep"), pairs).astype(F32)


def product(form, left, right):
    return jnp.einsum(form, left, right, preferred_element_type=F32)


def rms_scale(values):
    return lax.rsqrt(jnp.mean(values * values, axis=-1, keepdims=True) + EPSILON)


def rotary_tables(positions):
    halfway = ROPE // 2
    inverse = 10000.0 ** (-(jnp.arange(halfway, dtype=F32) * 2.0 / ROPE))
    angles = positions[:, None] * inverse[None, :]
    return (jnp.cos(angles), jnp.sin(angles))


def rotate(values, cos_table, sin_table):
    halfway = values.shape[-1] // 2
    first = values[..., :halfway]
    second = values[..., halfway:]
    return jnp.concatenate(
        [first * cos_table - second * sin_table, second * cos_table + first * sin_table], axis=-1
    )


def unrotate(grads, cos_table, sin_table):
    halfway = grads.shape[-1] // 2
    first = grads[..., :halfway]
    second = grads[..., halfway:]
    return jnp.concatenate(
        [first * cos_table + second * sin_table, second * cos_table - first * sin_table], axis=-1
    )


def norm_back(grad_unit, unit_values, scale_values):
    return scale_values * (
        grad_unit - unit_values * jnp.mean(grad_unit * unit_values, axis=-1, keepdims=True)
    )


def silu_back(grad_hidden, gate_value, up_value):
    sigmoid = jax.nn.sigmoid(gate_value)
    grad_gate = grad_hidden * up_value * sigmoid * (1.0 + gate_value * (1.0 - sigmoid))
    grad_up = grad_hidden * gate_value * sigmoid
    return (grad_gate.astype(BF16), grad_up.astype(BF16))


def columns_out(weight, n):
    return weight.T.reshape(n, weight.shape[1] // n, weight.shape[0])


def columns_in(blocks):
    n, width, rows = blocks.shape
    return blocks.transpose(1, 0, 2).reshape(width, n * rows)


def per_device(
    layer_input,
    attention_gain,
    query_weight,
    latent_weight,
    latent_gain,
    expand_weight,
    output_weight,
    feedforward_gain,
    router_weight,
    shared_gate,
    shared_up,
    shared_down,
    expert_gate,
    expert_up,
    expert_down,
    expert_routes,
    prefix_length,
    output_grad,
):
    n = lax.axis_size("ep")
    groups = lax.axis_size("grp")
    e = lax.axis_index("ep")
    tokens = layer_input.shape[0]
    length = tokens * n
    capacity = tokens * TOPK * 4 // (3 * n)
    scale = 1.0 / math.sqrt(NOPE + ROPE)
    rows_dev = attention_gain.shape[0]
    latent_rows = latent_gain.shape[0]

    pad = jnp.zeros((rows_dev - latent_rows,), BF16)
    first_block = jnp.concatenate(
        [
            layer_input,
            latent_weight,
            router_weight,
            attention_gain[:, None],
            feedforward_gain[:, None],
            jnp.concatenate([latent_gain, pad])[:, None],
            expert_routes.astype(BF16),
        ],
        axis=1,
    )
    width = first_block.shape[1]
    first_block = jnp.pad(first_block, ((0, 0), (0, -width % 128)))
    first_all = gather(first_block, 0)
    c0 = D
    c1 = c0 + LATENT + ROPE
    c2 = c1 + n
    all_input = first_all[:, :, :c0].reshape(length, D)
    latent_w = first_all[:, :, c0:c1].reshape(D, LATENT + ROPE)
    router_w = first_all[:, :, c1:c2].reshape(D, n)
    attn_gain = first_all[:, :, c2].reshape(D).astype(F32)
    ffn_gain = first_all[:, :, c2 + 1].reshape(D).astype(F32)
    lat_gain = first_all[:, :latent_rows, c2 + 2].reshape(LATENT).astype(F32)
    routes = first_all[:, :, c2 + 3 : c2 + 3 + TOPK].astype(jnp.int32)

    q_blocks, x_blocks, g_blocks, u_blocks = swap(
        1,
        columns_out(query_weight, n),
        columns_out(expand_weight, n),
        columns_out(shared_gate, n),
        columns_out(shared_up, n),
    )
    query_t = columns_in(q_blocks)
    expand_t = columns_in(x_blocks)
    gate_t = columns_in(g_blocks)
    up_t = columns_in(u_blocks)

    output_w = lax.all_gather(output_weight, "ep", axis=0, tiled=True)
    all_out_grad = lax.all_gather(output_grad, "ep", axis=0, tiled=True)

    def own(values):
        return lax.dynamic_slice_in_dim(values, e * tokens, tokens, 0)

    residual_all = all_input.astype(F32)
    unit_all = residual_all * rms_scale(residual_all)
    normed = (unit_all * attn_gain).astype(BF16)
    places = jnp.arange(length, dtype=jnp.int32)
    cos_table, sin_table = rotary_tables(places.astype(F32))
    query_raw = product("td,cd->tc", normed, query_t)
    query_n = query_raw[:, :NOPE].astype(BF16)
    query_r = rotate(query_raw[:, NOPE:], cos_table, sin_table).astype(BF16)
    compressed = product("td,dc->tc", normed, latent_w)
    latent_raw = compressed[:, :LATENT]
    latent = (latent_raw * rms_scale(latent_raw) * lat_gain).astype(BF16)
    key_rope = rotate(compressed[:, LATENT:], cos_table, sin_table).astype(BF16)
    expanded = product("tl,cl->tc", latent, expand_t).astype(BF16)
    key_nope = expanded[:, :NOPE]
    values = expanded[:, NOPE:]
    visible = (places[None, :] <= places[:, None]) | (places[None, :] < prefix_length[0])

    def attention_scores():
        scores = product("qd,kd->qk", query_n, key_nope)
        scores = scores + product("qd,kd->qk", query_r, key_rope)
        return jnp.where(visible, scores * scale, MASKED)

    scores = attention_scores()
    row_max = jnp.max(scores, axis=-1, keepdims=True)
    log_total = row_max + jnp.log(jnp.sum(jnp.exp(scores - row_max), axis=-1, keepdims=True))
    weights = jnp.exp(scores - log_total).astype(BF16)
    attended_head = product("qk,kd->qd", weights, values).astype(BF16)
    (attended_blocks,) = swap(2, attended_head.reshape(n, tokens, VH))
    attended = attended_blocks.transpose(1, 0, 2).reshape(tokens, HEADS * VH)

    residual_in = layer_input.astype(F32)
    input_scale = rms_scale(residual_in)
    input_unit = residual_in * input_scale
    residual_mid = residual_in + product("ta,ad->td", attended, output_w)
    mid_scale = rms_scale(residual_mid)
    mid_unit = residual_mid * mid_scale
    own_ffn_in = (mid_unit * ffn_gain).astype(BF16)
    ffn_blocks = gather(own_ffn_in, 3)
    ffn_in = ffn_blocks.reshape(length, D)

    out_blocks = all_out_grad.reshape(n, tokens, D)
    router_all = jax.nn.softmax(product("td,de->te", ffn_in, router_w), axis=-1)
    gate_values = jnp.sum(
        jnp.where(jnp.arange(n, dtype=jnp.int32) == e, router_all, 0.0), axis=-1
    ).reshape(n, tokens)
    chosen = jnp.any(routes == e, axis=-1)
    chosen_int = chosen.astype(jnp.int32)
    place = jnp.cumsum(chosen_int, axis=1) - chosen_int
    kept = chosen & (place < capacity)
    dispatch = (
        (place[:, None, :] == jnp.arange(capacity, dtype=jnp.int32)[None, :, None])
        & kept[:, None, :]
    )
    slot_gate = jnp.sum(jnp.where(dispatch, gate_values[:, None, :], 0.0), axis=-1)
    dispatch = dispatch.astype(BF16)
    kept_gate = jnp.where(kept, gate_values, 0.0)

    def to_slots(blocks):
        return product("bst,btd->bsd", dispatch, blocks)

    def to_tokens(slots):
        return product("bst,bsd->btd", dispatch, slots.reshape(n, capacity, D))

    incoming = to_slots(ffn_blocks).astype(BF16).reshape(n * capacity, D)
    out_slots = to_slots(out_blocks)
    slot_grad = (out_slots * slot_gate[:, :, None]).astype(BF16).reshape(n * capacity, D)
    gate_m, up_m, down_m = expert_gate[0], expert_up[0], expert_down[0]
    expert_g = product("rd,df->rf", incoming, gate_m)
    expert_u = product("rd,df->rf", incoming, up_m)
    expert_hidden = (jax.nn.silu(expert_g) * expert_u).astype(BF16)
    expert_out = product("rf,fd->rd", expert_hidden, down_m).astype(BF16)
    slot_dot = jnp.sum(
        out_slots * expert_out.astype(F32).reshape(n, capacity, D), axis=-1
    )
    token_dot = jnp.sum(dispatch.astype(F32) * slot_dot[:, :, None], axis=1)
    shared_g = product("td,fd->tf", ffn_in, gate_t)
    shared_u = product("td,fd->tf", ffn_in, up_t)
    shared_hidden = (jax.nn.silu(shared_g) * shared_u).astype(BF16)
    out_partial = product("tf,fd->td", shared_hidden, shared_down).reshape(n, tokens, D)
    out_partial = (out_partial + to_tokens(expert_out) * kept_gate[:, :, None]).astype(BF16)
    out_sum = lax.psum_scatter(out_partial, "ep", scatter_dimension=0)
    layer_output = (residual_mid + out_sum.astype(F32)).astype(BF16)

    grad_shared_hidden = product("td,fd->tf", all_out_grad, shared_down)
    grad_shared_g, grad_shared_u = silu_back(grad_shared_hidden, shared_g, shared_u)
    grad_expert_hidden = product("rd,fd->rf", slot_grad, down_m)
    grad_expert_g, grad_expert_u = silu_back(grad_expert_hidden, expert_g, expert_u)
    row_grad = (
        product("rf,df->rd", grad_expert_g, gate_m) + product("rf,df->rd", grad_expert_u, up_m)
    ).astype(BF16)
    ffn_partial = product("tf,fd->td", grad_shared_g, gate_t) + product(
        "tf,fd->td", grad_shared_u, up_t
    )
    ffn_partial = (ffn_partial.reshape(n, tokens, D) + to_tokens(row_grad)).astype(BF16)
    own_column = (jnp.arange(128, dtype=jnp.int32) == e).astype(F32)
    dot_partial = (token_dot[:, :, None] * own_column).astype(BF16)
    ffn_sum = scatter(jnp.concatenate([ffn_partial, dot_partial], axis=2), 4)

    grad_down_matrix = product("rf,rd->fd", expert_hidden, slot_grad)
    grad_gate_matrix = product("rd,rf->df", incoming, grad_expert_g)
    grad_up_matrix = product("rd,rf->df", incoming, grad_expert_u)
    expert_gate_grad = over_groups(grad_gate_matrix.reshape(groups, D // groups, -1))[None]
    expert_up_grad = over_groups(grad_up_matrix.reshape(groups, D // groups, -1))[None]
    expert_down_grad = over_groups(
        grad_down_matrix.reshape(groups, grad_down_matrix.shape[0] // groups, D)
    )[None]
    grad_shared_down = product("tf,td->fd", shared_hidden, all_out_grad)
    shared_down_grad = to_row_owner(
        over_groups(grad_shared_down.reshape(groups, grad_shared_down.shape[0] // groups, D))
    )
    grad_shared_gate = product("td,tf->df", ffn_in, grad_shared_g)
    grad_shared_up = product("td,tf->df", ffn_in, grad_shared_u)

    router_own = own(router_all)
    grad_probs = ffn_sum[:, D : D + n]
    grad_logits = (
        router_own * (grad_probs - jnp.sum(router_own * grad_probs, axis=-1, keepdims=True))
    ).astype(BF16)
    grad_ffn_in = ffn_sum[:, :D] + product("te,de->td", grad_logits, router_w)
    grad_ffn_gain = jnp.sum(grad_ffn_in * mid_unit, axis=0)
    grad_mid = output_grad.astype(F32) + norm_back(grad_ffn_in * ffn_gain, mid_unit, mid_scale)
    grad_mid_b = grad_mid.astype(BF16)
    grad_attended = product("td,ad->ta", grad_mid_b, output_w).astype(BF16)
    (grad_att_blocks,) = swap(
        5, grad_attended.reshape(tokens, HEADS, VH).transpose(1, 0, 2)
    )
    grad_att = grad_att_blocks.reshape(length, VH)
    mid_all = lax.all_gather(
        jnp.concatenate([grad_mid_b, jnp.pad(grad_logits, ((0, 0), (0, 128 - n)))], axis=1),
        "ep", axis=0, tiled=True,
    )

    probs = jnp.exp(attention_scores() - log_total)
    grad_weights = product("qd,kd->qk", grad_att, values)
    delta = jnp.sum(probs * grad_weights, axis=-1, keepdims=True)
    grad_scores = (probs * (grad_weights - delta)).astype(BF16)
    grad_query_n = product("qk,kd->qd", grad_scores, key_nope) * scale
    grad_query_r = product("qk,kd->qd", grad_scores, key_rope) * scale
    grad_key_n = product("qk,qd->kd", grad_scores, query_n) * scale
    grad_key_r = product("qk,qd->kd", grad_scores, query_r) * scale
    grad_values = product("qk,qd->kd", probs.astype(BF16), grad_att)
    grad_expanded = jnp.concatenate([grad_key_n, grad_values], axis=1).astype(BF16)
    latent_partial = product("tc,cl->tl", grad_expanded, expand_t)
    latent_partial = jnp.concatenate([latent_partial, grad_key_r], axis=1).astype(BF16)
    latent_sum = scatter(latent_partial.reshape(n, tokens, LATENT + ROPE), 6)
    grad_expand = product("tl,tc->lc", latent, grad_expanded)
    grad_query = jnp.concatenate(
        [grad_query_n, unrotate(grad_query_r, cos_table, sin_table)], axis=1
    ).astype(BF16)
    normed_partial = product("tc,cd->td", grad_query, query_t).astype(BF16)
    normed_sum = scatter(normed_partial.reshape(n, tokens, D), 7)
    grad_query_matrix = product("td,tc->dc", normed, grad_query)

    own_compressed = own(compressed)
    latent_scale = rms_scale(own_compressed[:, :LATENT])
    latent_unit = own_compressed[:, :LATENT] * latent_scale
    grad_latent = latent_sum[:, :LATENT]
    grad_latent_gain = jnp.sum(grad_latent * latent_unit, axis=0)
    grad_compressed = jnp.concatenate(
        [
            norm_back(grad_latent * lat_gain, latent_unit, latent_scale),
            unrotate(latent_sum[:, LATENT:], own(cos_table), own(sin_table)),
        ],
        axis=-1,
    ).astype(BF16)
    compressed_all = gather(grad_compressed, 8).reshape(length, LATENT + ROPE)
    grad_normed = normed_sum + product("tc,dc->td", grad_compressed, latent_w)
    grad_attn_gain = jnp.sum(grad_normed * input_unit, axis=0)
    input_grad = (
        grad_mid + norm_back(grad_normed * attn_gain, input_unit, input_scale)
    ).astype(BF16)

    rows_out = D // (groups * n)

    def own_rows(values):
        blocks = values.reshape(length, groups, n, rows_out)
        return lax.dynamic_index_in_dim(blocks, e, 2, keepdims=False).reshape(
            length, groups * rows_out
        )

    latent_weight_grad = over_groups(
        product("tr,tc->rc", own_rows(normed), compressed_all).reshape(
            groups, rows_out, LATENT + ROPE
        )
    )
    router_weight_grad = over_groups(
        product("tr,te->re", own_rows(ffn_in), mid_all[:, D : D + n]).reshape(groups, rows_out, n)
    )
    grad_output = product("ta,td->ad", attended_head, mid_all[:, :D])
    output_weight_grad = to_row_owner(
        over_groups(grad_output.reshape(groups, grad_output.shape[0] // groups, D))
    )
    side = jnp.concatenate([grad_query_matrix, grad_shared_gate, grad_shared_up], axis=1)
    side = over_groups(side.reshape(groups, D // groups, -1)).astype(BF16)
    expand_rows = LATENT // (groups * n)
    grad_expand = over_groups(grad_expand.reshape(groups, LATENT // groups, -1)).astype(BF16)
    gains = jnp.concatenate(
        [
            grad_attn_gain.reshape(groups, n, rows_out),
            grad_ffn_gain.reshape(groups, n, rows_out),
            grad_latent_gain.reshape(groups, n, expand_rows),
        ],
        axis=2,
    ).transpose(1, 0, 2)
    side_all, expand_all, gain_all = swap(
        9,
        side.reshape(n, rows_out, -1),
        grad_expand.reshape(n, expand_rows, -1),
        gains,
    )
    side_all = side_all.transpose(1, 0, 2).astype(F32)
    query_width = query_t.shape[0]
    shared_width = gate_t.shape[0]
    query_weight_grad = side_all[:, :, :query_width].reshape(rows_out, -1)
    shared_gate_grad = side_all[:, :, query_width : query_width + shared_width].reshape(
        rows_out, -1
    )
    shared_up_grad = side_all[:, :, query_width + shared_width :].reshape(rows_out, -1)
    expand_weight_grad = expand_all.transpose(1, 0, 2).reshape(expand_rows, -1).astype(F32)
    gain_sum = jnp.sum(gain_all, axis=0)
    gain_sum = lax.psum_scatter(gain_sum, "grp", scatter_dimension=0) if groups != 2 else (
        lax.dynamic_index_in_dim(gain_sum, lax.axis_index("grp"), 0, keepdims=False)
        + lax.ppermute(
            lax.dynamic_index_in_dim(gain_sum, 1 - lax.axis_index("grp"), 0, keepdims=False),
            "grp", [(0, 1), (1, 0)],
        )
    )
    attention_gain_grad = gain_sum[:rows_out]
    feedforward_gain_grad = gain_sum[rows_out : 2 * rows_out]
    latent_gain_grad = gain_sum[2 * rows_out :]
    return (
        layer_output,
        input_grad,
        attention_gain_grad,
        query_weight_grad,
        latent_weight_grad,
        latent_gain_grad,
        expand_weight_grad,
        output_weight_grad,
        feedforward_gain_grad,
        router_weight_grad,
        shared_gate_grad,
        shared_up_grad,
        shared_down_grad,
        expert_gate_grad,
        expert_up_grad,
        expert_down_grad,
    )


def solution(mesh):
    return jax.shard_map(
        per_device,
        mesh=mesh,
        in_specs=(
            P(("grp", "ep"), None),
            P("ep"),
            P("ep", None),
            P("ep", None),
            P("ep"),
            P("ep", None),
            P("ep", None),
            P("ep"),
            P("ep", None),
            P("ep", None),
            P("ep", None),
            P("ep", None),
            P("ep", None, None),
            P("ep", None, None),
            P("ep", None, None),
            P(("grp", "ep"), None),
            P("grp"),
            P(("grp", "ep"), None),
        ),
        out_specs=(
            P(("grp", "ep"), None),
            P(("grp", "ep"), None),
            P(("grp", "ep")),
            P(("grp", "ep"), None),
            P(("grp", "ep"), None),
            P(("grp", "ep")),
            P(("grp", "ep"), None),
            P(("grp", "ep"), None),
            P(("grp", "ep")),
            P(("grp", "ep"), None),
            P(("grp", "ep"), None),
            P(("grp", "ep"), None),
            P(("grp", "ep"), None),
            P("ep", "grp", None),
            P("ep", "grp", None),
            P("ep", "grp", None),
        ),
        check_vma=False,
    )
```

```python
import functools
import math

import jax
import jax.numpy as jnp
from jax import lax
from jax.experimental import pallas as pl
from jax.experimental.pallas import tpu as pltpu
from jax.sharding import PartitionSpec as P

D = 2048
HEADS = 16
NOPE = 128
ROPE = 64
VH = 128
LATENT = 512
TOPK = 6

EPSILON = 1e-06
MASKED = -1e30

MESH = pl.DeviceIdType.MESH
ANY = pl.BlockSpec(memory_space=pl.ANY)
DMA = pltpu.SemaphoreType.DMA
F32 = jnp.float32
BF16 = jnp.bfloat16


def remote(src, dst, send, recv, peer):
    return pltpu.make_async_remote_copy(
        src_ref=src,
        dst_ref=dst,
        send_sem=send,
        recv_sem=recv,
        device_id={"ep": peer},
        device_id_type=MESH,
    )


def greet(peers):
    barrier = pltpu.get_barrier_semaphore()
    for peer in peers:
        pl.semaphore_signal(barrier, inc=1, device_id={"ep": peer}, device_id_type=MESH)
    pl.semaphore_wait(barrier, len(peers))


def around(n):
    me = lax.axis_index("ep")
    x, y = me % 2, (me // 2) % 2
    return me, me // 4, y, x, me + 1 - 2 * x, me + 2 - 4 * y


def near(z, nz, below, above):
    for s in range(nz - 1):
        pl.when(z - 1 - s >= 0)(functools.partial(below, s, z - 1 - s))
        pl.when(z + 1 + s < nz)(functools.partial(above, s, z + 1 + s))


def gather_kernel(n, x_ref, o_ref, own, us, ur, ds, dr, xs, xr, ys, yr):
    me, z, y, x, px, py = around(n)
    nz = n // 4
    low = me % 4
    half = x_ref.shape[0] // 2
    top, bottom = pl.ds(0, half), pl.ds(half, half)
    up, down = (me + 4) % n, (me + n - 4) % n
    barrier = pltpu.get_barrier_semaphore()
    greeted = [(px, None), (py, None), (up, z + 1 < nz), (down, z > 0)]
    for peer, there in greeted:

        def hello(peer=peer):
            pl.semaphore_signal(barrier, inc=1, device_id={"ep": peer}, device_id_type=MESH)

        hello() if there is None else pl.when(there)(hello)
    on_line = (z + 1 < nz).astype(jnp.int32) + (z > 0).astype(jnp.int32)
    pl.semaphore_wait(barrier, 2 + on_line)
    local = pltpu.make_async_copy(x_ref, o_ref.at[me], own)
    local.start()

    def over_x(src, b, part, i):
        return remote(src.at[part], o_ref.at[b, part], xs.at[i], xr.at[i], px)

    def over_y(src, b, part, i):
        return remote(src.at[part], o_ref.at[b, part], ys.at[i], yr.at[i], py)

    def upward(src, b, s):
        return remote(src, o_ref.at[b], us.at[s], ur.at[s], up)

    def downward(src, b, s):
        return remote(src, o_ref.at[b], ds.at[s], dr.at[s], down)

    def spread(src, t):
        b = t * 4 + low
        over_x(src, b, top, t).start()
        over_y(src, b, bottom, t).start()
        over_y(src, b, top, nz + t).start()
        over_x(src, b, bottom, nz + t).start()

    pl.when(z + 1 < nz)(lambda: upward(x_ref, me, 0).start())
    pl.when(z > 0)(lambda: downward(x_ref, me, 0).start())
    spread(x_ref, z)

    def from_below(s, t):
        b = t * 4 + low
        upward(o_ref.at[b], b, s).wait_recv()
        pl.when(z + 1 < nz)(lambda: upward(o_ref.at[b], b, s + 1).start())
        spread(o_ref.at[b], t)

    def from_above(s, t):
        b = t * 4 + low
        downward(o_ref.at[b], b, s).wait_recv()
        pl.when(z > 0)(lambda: downward(o_ref.at[b], b, s + 1).start())
        spread(o_ref.at[b], t)

    def turn(s, t):
        bx = t * 4 + low + px - me
        by = t * 4 + low + py - me
        over_x(o_ref.at[bx], bx, top, t).wait_recv()
        over_y(o_ref.at[bx], bx, top, 2 * nz + t).start()
        over_y(o_ref.at[by], by, bottom, t).wait_recv()
        over_x(o_ref.at[by], by, bottom, 2 * nz + t).start()

    for s in range(nz - 1):
        pl.when(z - 1 - s >= 0)(functools.partial(from_below, s, z - 1 - s))
        pl.when(z + 1 + s < nz)(functools.partial(from_above, s, z + 1 + s))
        if s == 0:
            turn(0, z)
        else:
            pl.when(z - s >= 0)(functools.partial(turn, s, z - s))
            pl.when(z + s < nz)(functools.partial(turn, s, z + s))
    pl.when(z - (nz - 1) >= 0)(functools.partial(turn, 0, z - (nz - 1)))
    pl.when(z + (nz - 1) < nz)(functools.partial(turn, 0, z + (nz - 1)))

    def finish(s, t):
        bx = t * 4 + low + px - me
        by = t * 4 + low + py - me
        bxy = bx + py - me
        over_y(o_ref.at[by], by, top, nz + t).wait_recv()
        over_x(o_ref.at[bx], bx, bottom, nz + t).wait_recv()
        over_y(o_ref.at[bxy], bxy, top, 2 * nz + t).wait_recv()
        over_x(o_ref.at[bxy], bxy, bottom, 2 * nz + t).wait_recv()
        for i in range(3):
            over_x(x_ref, me, top, i * nz + t).wait_send()
            over_y(x_ref, me, top, i * nz + t).wait_send()

    finish(0, z)
    near(z, nz, finish, finish)

    def sent_up(s, t):
        upward(x_ref, me, s).wait_send()

    def sent_down(s, t):
        downward(x_ref, me, s).wait_send()

    for s in range(nz - 1):
        pl.when((z + 1 < nz) & (z - s >= 0))(functools.partial(sent_up, s, z))
        pl.when((z > 0) & (z + s < nz))(functools.partial(sent_down, s, z))
    local.wait()


def gather(x, cid):
    n = lax.axis_size("ep")
    nz = n // 4
    return pl.pallas_call(
        functools.partial(gather_kernel, n),
        out_shape=jax.ShapeDtypeStruct((n,) + x.shape, x.dtype),
        in_specs=[ANY],
        out_specs=ANY,
        scratch_shapes=[DMA] + [DMA((nz,))] * 4 + [DMA((3 * nz,))] * 4,
        compiler_params=pltpu.CompilerParams(collective_id=cid, has_side_effects=True),
        name="gather",
    )(x)


def add_rows(dst, left, right, rows):
    step = 16

    def body(i, carry):
        r = pl.ds(pl.multiple_of(i * step, step), step)
        dst[r] = (left[r].astype(F32) + right[r].astype(F32)).astype(dst.dtype)
        return carry

    lax.fori_loop(0, rows // step, body, 0)


def exchange_kernel(n, m, w, *refs):
    refs = list(refs)

    def take(count):
        out = refs[:count]
        del refs[:count]
        return out

    sums_in, swaps_in = take(m), take(w)
    sums_out, swaps_out = take(m), take(w)
    room = [take(7) for _ in range(m)]
    sems = [take(8) for _ in range(m)]
    swap_sems = take(3) if w else None
    me, z, y, x, px, py = around(n)
    nz = n // 4
    low = me % 4
    to = [(z + k) % nz for k in range(nz)]
    at = [t * 4 + low for t in to]
    everyone = [(me + k) % n for k in range(n)]
    back = [(me + n - k) % n for k in range(n)]
    if w:
        greet(everyone[1:])
    else:
        greet([px, py] + at[1:])
    order = [2, 1, 3, 0] if nz == 4 else list(range(1, nz)) + [0]
    sends, copies = [], []

    def halves(j):
        half = sums_in[j].shape[3] // 2
        return half, pl.ds(0, half), pl.ds(half, half)

    first, second, third = {}, {}, {}

    def stage_one(j, k):
        p = sums_in[j]
        half, top, bottom = halves(j)
        la, lb, a1, b1, a2, b2, zb = room[j]
        lsa, lsb, xs, xr, ys, yr, zs, zr = sems[j]
        t = to[k]
        c = remote(p.at[t, 1 - y, :, top], a1.at[k], ys.at[k], yr.at[k], py)
        d = remote(p.at[t, :, 1 - x, bottom], b1.at[k], xs.at[k], xr.at[k], px)
        c.start()
        d.start()
        e = pltpu.make_async_copy(p.at[t, y, :, top], la.at[k], lsa.at[k])
        f = pltpu.make_async_copy(p.at[t, :, x, bottom], lb.at[k], lsb.at[k])
        e.start()
        f.start()
        first[j, k] = (c, d, e, f)
        sends.extend([c, d])

    def stage_two(j, k):
        half, top, bottom = halves(j)
        la, lb, a1, b1, a2, b2, zb = room[j]
        lsa, lsb, xs, xr, ys, yr, zs, zr = sems[j]
        c, d, e, f = first[j, k]
        e.wait()
        c.wait_recv()
        for i in range(2):
            add_rows(la.at[k, i], la.at[k, i], a1.at[k, i], half)
        g = remote(la.at[k, 1 - x], a2.at[k], xs.at[nz + k], xr.at[nz + k], px)
        g.start()
        f.wait()
        d.wait_recv()
        for i in range(2):
            add_rows(lb.at[k, i], lb.at[k, i], b1.at[k, i], half)
        h = remote(lb.at[k, 1 - y], b2.at[k], ys.at[nz + k], yr.at[nz + k], py)
        h.start()
        second[j, k] = (g, h)
        sends.extend([g, h])

    def stage_three(j, k):
        half, top, bottom = halves(j)
        la, lb, a1, b1, a2, b2, zb = room[j]
        lsa, lsb, xs, xr, ys, yr, zs, zr = sems[j]
        g, h = second[j, k]
        g.wait_recv()
        add_rows(a2.at[k], la.at[k, x], a2.at[k], half)
        if k:
            c = remote(a2.at[k], zb.at[k, top], zs.at[k], zr.at[k], at[k])
            c.start()
        h.wait_recv()
        add_rows(b2.at[k], lb.at[k, y], b2.at[k], half)
        if k:
            d = remote(b2.at[k], zb.at[k, bottom], zs.at[nz + k], zr.at[nz + k], at[k])
            d.start()
            third[j, k] = (c, d)
            sends.extend([c, d])

    def start_swaps():
        own, ss, rs = swap_sems
        for j in range(w):
            local = pltpu.make_async_copy(swaps_in[j].at[me], swaps_out[j].at[me], own.at[j])
            local.start()
            copies.append(local)
        for k in range(1, n):
            for j in range(w):
                c = remote(
                    swaps_in[j].at[everyone[k]],
                    swaps_out[j].at[me],
                    ss.at[j, k],
                    rs.at[j, k],
                    everyone[k],
                )
                c.start()
                sends.append(c)

    steps = [(j, k) for j in range(m) for k in order]
    for i in range(min(2, len(steps))):
        stage_one(*steps[i])
    if w:
        start_swaps()
    for i, step in enumerate(steps):
        stage_two(*step)
        if i + 2 < len(steps):
            stage_one(*steps[i + 2])
        if i:
            stage_three(*steps[i - 1])
    if steps:
        stage_three(*steps[-1])
    for j in range(m):
        half, top, bottom = halves(j)
        la, lb, a1, b1, a2, b2, zb = room[j]
        o_ref = sums_out[j]
        for k in range(1, nz):
            c, d = third[j, k]
            c.wait_recv()
            d.wait_recv()
        for part, offset in ((a2, 0), (b2, half)):

            def body(i, carry, part=part, offset=offset, zb=zb, o_ref=o_ref):
                r = pl.ds(pl.multiple_of(i * 16, 16), 16)
                q = pl.ds(pl.multiple_of(i * 16 + offset, 16), 16)
                total = part[0, r].astype(F32)
                for k in range(1, nz):
                    total = total + zb[k, q].astype(F32)
                o_ref[q] = total.astype(o_ref.dtype)
                return carry

            lax.fori_loop(0, half // 16, body, 0)
    if w:
        own, ss, rs = swap_sems
        for k in range(1, n):
            for j in range(w):
                remote(
                    swaps_in[j].at[back[k]],
                    swaps_out[j].at[back[k]],
                    ss.at[j, k],
                    rs.at[j, k],
                    everyone[k],
                ).wait_recv()
    for copy in sends:
        copy.wait_send()
    for copy in copies:
        copy.wait()


def exchange(cid, sums=(), swaps=()):
    n = lax.axis_size("ep")
    nz = n // 4
    m, w = len(sums), len(swaps)
    kept_rows = [p.shape[1] for p in sums]
    sums = [jnp.pad(p, ((0, 0), (0, -p.shape[1] % 32), (0, 0))) for p in sums]
    views = [p.reshape((nz, 2, 2) + p.shape[1:]) for p in sums]
    scratch = []
    for p in sums:
        rows, cols = p.shape[1:]
        half = rows // 2
        scratch += [pltpu.VMEM((nz, 2, half, cols), p.dtype)] * 4
        scratch += [pltpu.VMEM((nz, half, cols), p.dtype)] * 2
        scratch += [pltpu.VMEM((nz, rows, cols), p.dtype)]
    for p in sums:
        scratch += [DMA((nz,))] * 2 + [DMA((2 * nz,))] * 6
    if w:
        scratch += [DMA((w,)), DMA((w, n)), DMA((w, n))]
    out = pl.pallas_call(
        functools.partial(exchange_kernel, n, m, w),
        out_shape=[jax.ShapeDtypeStruct(p.shape[1:], F32) for p in sums]
        + [jax.ShapeDtypeStruct(a.shape, a.dtype) for a in swaps],
        in_specs=[ANY] * (m + w),
        out_specs=[pl.BlockSpec(memory_space=pltpu.VMEM)] * m + [ANY] * w,
        scratch_shapes=scratch,
        compiler_params=pltpu.CompilerParams(
            collective_id=cid, has_side_effects=True, vmem_limit_bytes=(40 << 20) if m else None
        ),
        name="exchange",
    )(*views, *swaps)
    return [a[:rows] for a, rows in zip(out, kept_rows)] + list(out[m:])


def both(p):
    g = lax.axis_index("grp")
    mine = lax.dynamic_index_in_dim(p, g, 0, keepdims=False)
    theirs = lax.dynamic_index_in_dim(p, 1 - g, 0, keepdims=False)
    return mine, lax.ppermute(theirs.astype(BF16), "grp", [(0, 1), (1, 0)])


def over_groups(p):
    if lax.axis_size("grp") == 2:
        mine, other = both(p)
        return mine.astype(F32) + other.astype(F32)
    return lax.psum_scatter(p.astype(BF16), "grp", scatter_dimension=0, tiled=False).astype(F32)


def product_over_groups(left, right):
    groups = lax.axis_size("grp")
    rows = left.shape[1] // groups
    if groups != 2:
        whole = product("km,kn->mn", left, right)
        return over_groups(whole.reshape(groups, rows, -1))
    g = lax.axis_index("grp")
    mine = lax.dynamic_slice_in_dim(left, g * rows, rows, 1)
    theirs = lax.dynamic_slice_in_dim(left, (1 - g) * rows, rows, 1)
    sent = product("km,kn->mn", theirs, right).astype(BF16)
    other = lax.ppermute(sent, "grp", [(0, 1), (1, 0)])
    return product("km,kn->mn", mine, right) + other.astype(F32)


def from_partner(values):
    groups = lax.axis_size("grp")
    return lax.ppermute(values, "grp", [(g, g + 1 - 2 * (g % 2)) for g in range(groups)])


def to_row_owner(block):
    groups, n = lax.axis_size("grp"), lax.axis_size("ep")
    pairs = [(h * n + e, e * groups + h) for h in range(groups) for e in range(n)]
    return lax.ppermute(block.astype(BF16), ("grp", "ep"), pairs).astype(F32)


def product(form, left, right):
    return jnp.einsum(form, left, right, preferred_element_type=F32)


def rms_scale(values):
    return lax.rsqrt(jnp.mean(values * values, axis=-1, keepdims=True) + EPSILON)


def rotary_tables(positions):
    halfway = ROPE // 2
    inverse = 10000.0 ** (-(jnp.arange(halfway, dtype=F32) * 2.0 / ROPE))
    angles = positions[:, None] * inverse[None, :]
    return (jnp.cos(angles), jnp.sin(angles))


def rotate(values, cos_table, sin_table):
    halfway = values.shape[-1] // 2
    first = values[..., :halfway]
    second = values[..., halfway:]
    return jnp.concatenate(
        [first * cos_table - second * sin_table, second * cos_table + first * sin_table], axis=-1
    )


def unrotate(grads, cos_table, sin_table):
    halfway = grads.shape[-1] // 2
    first = grads[..., :halfway]
    second = grads[..., halfway:]
    return jnp.concatenate(
        [first * cos_table + second * sin_table, second * cos_table - first * sin_table], axis=-1
    )


def norm_back(grad_unit, unit_values, scale_values):
    return scale_values * (
        grad_unit - unit_values * jnp.mean(grad_unit * unit_values, axis=-1, keepdims=True)
    )


def silu_back(grad_hidden, gate_value, up_value):
    sigmoid = jax.nn.sigmoid(gate_value)
    grad_gate = grad_hidden * up_value * sigmoid * (1.0 + gate_value * (1.0 - sigmoid))
    grad_up = grad_hidden * gate_value * sigmoid
    return (grad_gate.astype(BF16), grad_up.astype(BF16))


def column_halves(weight, n, half):
    rows, width = weight.shape[0], weight.shape[1] // n
    parts = weight.T.reshape(n, 2, width // 2, rows)
    return lax.dynamic_index_in_dim(parts, half, 1, keepdims=False)


def columns_in(blocks):
    n, width, rows = blocks.shape
    return blocks.transpose(1, 0, 2).reshape(width, n * rows)


def both_halves(mine, other, even):
    return jnp.concatenate([jnp.where(even, mine, other), jnp.where(even, other, mine)], axis=0)


def per_device(
    layer_input,
    attention_gain,
    query_weight,
    latent_weight,
    latent_gain,
    expand_weight,
    output_weight,
    feedforward_gain,
    router_weight,
    shared_gate,
    shared_up,
    shared_down,
    expert_gate,
    expert_up,
    expert_down,
    expert_routes,
    prefix_length,
    output_grad,
):
    n = lax.axis_size("ep")
    groups = lax.axis_size("grp")
    e = lax.axis_index("ep")
    half = lax.axis_index("grp") % 2
    even = half == 0
    tokens = layer_input.shape[0]
    length = tokens * n
    capacity = tokens * TOPK * 4 // (3 * n)
    scale = 1.0 / math.sqrt(NOPE + ROPE)
    rows_dev = attention_gain.shape[0]
    latent_rows = latent_gain.shape[0]
    rows_out = D // (groups * n)
    expand_rows = LATENT // (groups * n)

    pad = jnp.zeros((rows_dev - latent_rows,), BF16)
    first_block = jnp.concatenate(
        [
            layer_input,
            latent_weight,
            router_weight,
            attention_gain[:, None],
            feedforward_gain[:, None],
            jnp.concatenate([latent_gain, pad])[:, None],
            expert_routes.astype(BF16),
        ],
        axis=1,
    )
    width = first_block.shape[1]
    first_block = jnp.pad(first_block, ((0, 0), (0, -width % 128)))
    first_all = gather(first_block, 0)
    c0 = D
    c1 = c0 + LATENT + ROPE
    c2 = c1 + n
    all_input = first_all[:, :, :c0].reshape(length, D)
    latent_w = first_all[:, :, c0:c1].reshape(D, LATENT + ROPE)
    router_w = first_all[:, :, c1:c2].reshape(D, n)
    attn_gain = first_all[:, :, c2].reshape(D).astype(F32)
    ffn_gain = first_all[:, :, c2 + 1].reshape(D).astype(F32)
    lat_gain = first_all[:, :latent_rows, c2 + 2].reshape(LATENT).astype(F32)
    routes = first_all[:, :, c2 + 3 : c2 + 3 + TOPK].astype(jnp.int32)

    q_half, x_half = (
        column_halves(query_weight, n, half),
        column_halves(expand_weight, n, half),
    )
    q_half, x_half, first_all = lax.optimization_barrier((q_half, x_half, first_all))
    q_blocks, x_blocks = exchange(1, swaps=(q_half, x_half))
    q_mine, x_mine = columns_in(q_blocks), columns_in(x_blocks)
    query_t = both_halves(q_mine, from_partner(q_mine), even)
    expand_t = both_halves(x_mine, from_partner(x_mine), even)
    shared_half = jnp.where(even, shared_gate, shared_up)
    shared_half = shared_half.T.reshape(n, shared_half.shape[1] // n, rows_dev)

    out_w_half = lax.dynamic_slice_in_dim(output_weight, half * (D // 2), D // 2, 1)
    out_w_half, later_grad, q_blocks = lax.optimization_barrier(
        (out_w_half, output_grad, q_blocks)
    )
    out_w_mine = lax.all_gather(out_w_half, "ep", axis=0, tiled=True)
    out_w_other = from_partner(out_w_mine)
    all_out_grad = lax.all_gather(later_grad, "ep", axis=0, tiled=True)

    def own(values):
        return lax.dynamic_slice_in_dim(values, e * tokens, tokens, 0)

    residual_all = all_input.astype(F32)
    unit_all = residual_all * rms_scale(residual_all)
    normed = (unit_all * attn_gain).astype(BF16)
    places = jnp.arange(length, dtype=jnp.int32)
    cos_table, sin_table = rotary_tables(places.astype(F32))
    query_raw = product("td,cd->tc", normed, query_t)
    query_n = query_raw[:, :NOPE].astype(BF16)
    query_r = rotate(query_raw[:, NOPE:], cos_table, sin_table).astype(BF16)
    compressed = product("td,dc->tc", normed, latent_w)
    latent_raw = compressed[:, :LATENT]
    latent = (latent_raw * rms_scale(latent_raw) * lat_gain).astype(BF16)
    key_rope = rotate(compressed[:, LATENT:], cos_table, sin_table).astype(BF16)
    expanded = product("tl,cl->tc", latent, expand_t).astype(BF16)
    key_nope = expanded[:, :NOPE]
    values = expanded[:, NOPE:]
    visible = (places[None, :] <= places[:, None]) | (places[None, :] < prefix_length[0])

    def attention_scores():
        scores = product("qd,kd->qk", query_n, key_nope)
        scores = scores + product("qd,kd->qk", query_r, key_rope)
        return jnp.where(visible, scores * scale, MASKED)

    scores = attention_scores()
    row_max = jnp.max(scores, axis=-1, keepdims=True)
    log_total = row_max + jnp.log(jnp.sum(jnp.exp(scores - row_max), axis=-1, keepdims=True))
    weights = jnp.exp(scores - log_total).astype(BF16)
    attended_head = product("qk,kd->qd", weights, values).astype(BF16)
    attended_blocks, shared_blocks = exchange(
        2, swaps=(attended_head.reshape(n, tokens, VH), shared_half)
    )
    attended = attended_blocks.transpose(1, 0, 2).reshape(tokens, HEADS * VH)
    shared_mine = columns_in(shared_blocks)
    shared_other = from_partner(shared_mine)
    gate_t = jnp.where(even, shared_mine, shared_other)
    up_t = jnp.where(even, shared_other, shared_mine)

    residual_in = layer_input.astype(F32)
    input_scale = rms_scale(residual_in)
    input_unit = residual_in * input_scale
    out_mine = product("ta,ad->td", attended, out_w_mine)
    out_other = product("ta,ad->td", attended, out_w_other)
    residual_mid = residual_in + jnp.concatenate(
        [jnp.where(even, out_mine, out_other), jnp.where(even, out_other, out_mine)], axis=1
    )
    mid_scale = rms_scale(residual_mid)
    mid_unit = residual_mid * mid_scale
    own_ffn_in = (mid_unit * ffn_gain).astype(BF16)
    ffn_blocks = gather(own_ffn_in, 3)
    ffn_in = ffn_blocks.reshape(length, D)

    out_blocks = all_out_grad.reshape(n, tokens, D)
    router_all = jax.nn.softmax(product("td,de->te", ffn_in, router_w), axis=-1)
    gate_values = jnp.sum(
        jnp.where(jnp.arange(n, dtype=jnp.int32) == e, router_all, 0.0), axis=-1
    ).reshape(n, tokens)
    chosen = jnp.any(routes == e, axis=-1)
    chosen_int = chosen.astype(jnp.int32)
    place = jnp.cumsum(chosen_int, axis=1) - chosen_int
    kept = chosen & (place < capacity)
    dispatch = (
        (place[:, None, :] == jnp.arange(capacity, dtype=jnp.int32)[None, :, None])
        & kept[:, None, :]
    )
    slot_gate = jnp.sum(jnp.where(dispatch, gate_values[:, None, :], 0.0), axis=-1)
    dispatch = dispatch.astype(BF16)
    kept_gate = jnp.where(kept, gate_values, 0.0)

    def to_slots(blocks):
        return product("bst,btd->bsd", dispatch, blocks)

    def to_tokens(slots):
        return product("bst,bsd->btd", dispatch, slots.reshape(n, capacity, D))

    incoming = to_slots(ffn_blocks).astype(BF16).reshape(n * capacity, D)
    out_slots = to_slots(out_blocks)
    slot_grad = (out_slots * slot_gate[:, :, None]).astype(BF16).reshape(n * capacity, D)
    gate_m, up_m, down_m = expert_gate[0], expert_up[0], expert_down[0]
    expert_g = product("rd,df->rf", incoming, gate_m)
    expert_u = product("rd,df->rf", incoming, up_m)
    expert_hidden = (jax.nn.silu(expert_g) * expert_u).astype(BF16)
    expert_out = product("rf,fd->rd", expert_hidden, down_m).astype(BF16)
    slot_dot = jnp.sum(
        out_slots * expert_out.astype(F32).reshape(n, capacity, D), axis=-1
    )
    token_dot = jnp.sum(dispatch.astype(F32) * slot_dot[:, :, None], axis=1)
    shared_g = product("td,fd->tf", ffn_in, gate_t)
    shared_u = product("td,fd->tf", ffn_in, up_t)
    shared_hidden = (jax.nn.silu(shared_g) * shared_u).astype(BF16)
    out_partial = product("tf,fd->td", shared_hidden, shared_down).reshape(n, tokens, D)
    out_partial = (out_partial + to_tokens(expert_out) * kept_gate[:, :, None]).astype(BF16)
    out_partial, slot_grad, all_out_grad = lax.optimization_barrier(
        (out_partial, slot_grad, all_out_grad)
    )
    out_sum = lax.psum_scatter(out_partial, "ep", scatter_dimension=0)
    layer_output = (residual_mid + out_sum.astype(F32)).astype(BF16)

    grad_shared_hidden = product("td,fd->tf", all_out_grad, shared_down)
    grad_shared_g, grad_shared_u = silu_back(grad_shared_hidden, shared_g, shared_u)
    grad_expert_hidden = product("rd,fd->rf", slot_grad, down_m)
    grad_expert_g, grad_expert_u = silu_back(grad_expert_hidden, expert_g, expert_u)
    row_grad = (
        product("rf,df->rd", grad_expert_g, gate_m) + product("rf,df->rd", grad_expert_u, up_m)
    ).astype(BF16)
    ffn_partial = product("tf,fd->td", grad_shared_g, gate_t) + product(
        "tf,fd->td", grad_shared_u, up_t
    )
    ffn_partial = (ffn_partial.reshape(n, tokens, D) + to_tokens(row_grad)).astype(BF16)
    own_column = (jnp.arange(128, dtype=jnp.int32) == e).astype(F32)
    dot_partial = (token_dot[:, :, None] * own_column).astype(BF16)
    ffn_sum, dot_sum = exchange(4, sums=(ffn_partial, dot_partial))

    expert_down_grad = product_over_groups(expert_hidden, slot_grad)[None]
    expert_gate_grad = product_over_groups(incoming, grad_expert_g)[None]
    expert_up_grad = product_over_groups(incoming, grad_expert_u)[None]
    shared_down_grad = to_row_owner(product_over_groups(shared_hidden, all_out_grad))
    side_shared = product_over_groups(
        ffn_in, jnp.concatenate([grad_shared_g, grad_shared_u], axis=1)
    ).astype(BF16)

    router_own = own(router_all)
    grad_probs = dot_sum[:, :n]
    grad_logits = (
        router_own * (grad_probs - jnp.sum(router_own * grad_probs, axis=-1, keepdims=True))
    ).astype(BF16)
    grad_ffn_in = ffn_sum + product("te,de->td", grad_logits, router_w)
    grad_ffn_gain = jnp.sum(grad_ffn_in * mid_unit, axis=0)
    grad_mid = output_grad.astype(F32) + norm_back(grad_ffn_in * ffn_gain, mid_unit, mid_scale)
    grad_mid_b = grad_mid.astype(BF16)
    mid_left, mid_right = grad_mid_b[:, : D // 2], grad_mid_b[:, D // 2 :]
    grad_attended = (
        product("td,ad->ta", jnp.where(even, mid_left, mid_right), out_w_mine)
        + product("td,ad->ta", jnp.where(even, mid_right, mid_left), out_w_other)
    ).astype(BF16)
    output_w_partial = product_over_groups(attended, grad_mid_b).astype(BF16)
    output_w_partial, grad_attended = lax.optimization_barrier((output_w_partial, grad_attended))
    (grad_att_blocks,) = exchange(
        5, swaps=(grad_attended.reshape(tokens, HEADS, VH).transpose(1, 0, 2),)
    )
    output_w_partial, grad_att_blocks = lax.optimization_barrier(
        (output_w_partial, grad_att_blocks)
    )
    grad_att = grad_att_blocks.reshape(length, VH)
    output_weight_grad = lax.psum_scatter(
        output_w_partial.reshape(n, rows_out, D), "ep", scatter_dimension=0
    ).astype(F32)
    grad_router = product("te,td->ed", grad_logits, own_ffn_in)

    probs = jnp.exp(attention_scores() - log_total)
    grad_weights = product("qd,kd->qk", grad_att, values)
    delta = jnp.sum(probs * grad_weights, axis=-1, keepdims=True)
    grad_scores = (probs * (grad_weights - delta)).astype(BF16)
    grad_query_n = product("qk,kd->qd", grad_scores, key_nope) * scale
    grad_query_r = product("qk,kd->qd", grad_scores, key_rope) * scale
    grad_key_n = product("qk,qd->kd", grad_scores, query_n) * scale
    grad_key_r = product("qk,qd->kd", grad_scores, query_r) * scale
    grad_values = product("qk,qd->kd", probs.astype(BF16), grad_att)
    grad_expanded = jnp.concatenate([grad_key_n, grad_values], axis=1).astype(BF16)
    latent_partial = product("tc,cl->tl", grad_expanded, expand_t).astype(BF16)
    grad_key_r = jnp.pad(grad_key_r, ((0, 0), (0, 128 - ROPE))).astype(BF16)
    latent_sum, rope_sum = exchange(
        6, sums=(latent_partial.reshape(n, tokens, LATENT), grad_key_r.reshape(n, tokens, 128))
    )
    grad_query = jnp.concatenate(
        [grad_query_n, unrotate(grad_query_r, cos_table, sin_table)], axis=1
    ).astype(BF16)
    normed_partial = product("tc,cd->td", grad_query, query_t)
    gain_partial = jnp.sum(normed_partial * unit_all, axis=0)
    normed_partial = normed_partial.astype(BF16).reshape(n, tokens, D)
    side_query = product_over_groups(normed, grad_query).astype(BF16)
    grad_expand = product_over_groups(latent, grad_expanded).astype(BF16)

    own_compressed = own(compressed)
    latent_scale = rms_scale(own_compressed[:, :LATENT])
    latent_unit = own_compressed[:, :LATENT] * latent_scale
    grad_latent_gain = jnp.sum(latent_sum * latent_unit, axis=0)
    grad_compressed = jnp.concatenate(
        [
            norm_back(latent_sum * lat_gain, latent_unit, latent_scale),
            unrotate(rope_sum[:, :ROPE], own(cos_table), own(sin_table)),
        ],
        axis=-1,
    ).astype(BF16)
    own_normed = (input_unit * attn_gain).astype(BF16)
    latent_w_partial = product_over_groups(
        own_normed, jnp.pad(grad_compressed, ((0, 0), (0, 640 - LATENT - ROPE)))
    ).astype(BF16)
    own_part = product("tc,dc->td", grad_compressed, latent_w)
    grad_attn_gain = gain_partial + jnp.sum(own_part * input_unit, axis=0)

    def by_owner(values, rows):
        blocks = values.reshape(-1, groups, n, rows).transpose(2, 1, 0, 3)
        return blocks.reshape(n, groups, -1)

    small = jnp.concatenate(
        [
            by_owner(grad_attn_gain, rows_out),
            by_owner(grad_ffn_gain, rows_out),
            by_owner(grad_router, rows_out),
            by_owner(grad_latent_gain, expand_rows),
        ],
        axis=2,
    )
    normed_sum, latent_weight_sum, query_all, shared_all, expand_all, small_all = exchange(
        7,
        sums=(normed_partial, latent_w_partial.reshape(n, rows_out, -1)),
        swaps=(
            side_query.reshape(n, rows_out, -1),
            side_shared.reshape(n, rows_out, -1),
            grad_expand.reshape(n, expand_rows, -1),
            small,
        ),
    )
    grad_normed = normed_sum + own_part
    input_grad = (
        grad_mid + norm_back(grad_normed * attn_gain, input_unit, input_scale)
    ).astype(BF16)
    latent_weight_grad = latent_weight_sum[:, : LATENT + ROPE]
    query_weight_grad = query_all.transpose(1, 0, 2).reshape(rows_out, -1).astype(F32)
    shared_width = gate_t.shape[0]
    shared_all = shared_all.transpose(1, 0, 2)
    shared_gate_grad = shared_all[:, :, :shared_width].reshape(rows_out, -1).astype(F32)
    shared_up_grad = shared_all[:, :, shared_width:].reshape(rows_out, -1).astype(F32)
    expand_weight_grad = expand_all.transpose(1, 0, 2).reshape(expand_rows, -1).astype(F32)
    small_sum = jnp.sum(small_all, axis=0)
    if groups == 2:
        g = lax.axis_index("grp")
        mine = lax.dynamic_index_in_dim(small_sum, g, 0, keepdims=False)
        theirs = lax.dynamic_index_in_dim(small_sum, 1 - g, 0, keepdims=False)
        small_sum = mine + lax.ppermute(theirs, "grp", [(0, 1), (1, 0)])
    else:
        small_sum = lax.psum_scatter(small_sum, "grp", scatter_dimension=0)
    attention_gain_grad = small_sum[:rows_out]
    feedforward_gain_grad = small_sum[rows_out : 2 * rows_out]
    router_weight_grad = small_sum[2 * rows_out : (2 + n) * rows_out].reshape(n, rows_out).T
    latent_gain_grad = small_sum[(2 + n) * rows_out :]
    return (
        layer_output,
        input_grad,
        attention_gain_grad,
        query_weight_grad,
        latent_weight_grad,
        latent_gain_grad,
        expand_weight_grad,
        output_weight_grad,
        feedforward_gain_grad,
        router_weight_grad,
        shared_gate_grad,
        shared_up_grad,
        shared_down_grad,
        expert_gate_grad,
        expert_up_grad,
        expert_down_grad,
    )


def solution(mesh):
    return jax.shard_map(
        per_device,
        mesh=mesh,
        in_specs=(
            P(("grp", "ep"), None),
            P("ep"),
            P("ep", None),
            P("ep", None),
            P("ep"),
            P("ep", None),
            P("ep", None),
            P("ep"),
            P("ep", None),
            P("ep", None),
            P("ep", None),
            P("ep", None),
            P("ep", None, None),
            P("ep", None, None),
            P("ep", None, None),
            P(("grp", "ep"), None),
            P("grp"),
            P(("grp", "ep"), None),
        ),
        out_specs=(
            P(("grp", "ep"), None),
            P(("grp", "ep"), None),
            P(("grp", "ep")),
            P(("grp", "ep"), None),
            P(("grp", "ep"), None),
            P(("grp", "ep")),
            P(("grp", "ep"), None),
            P(("grp", "ep"), None),
            P(("grp", "ep")),
            P(("grp", "ep"), None),
            P(("grp", "ep"), None),
            P(("grp", "ep"), None),
            P(("grp", "ep"), None),
            P("ep", "grp", None),
            P("ep", "grp", None),
            P("ep", "grp", None),
        ),
        check_vma=False,
    )
```

```python
import functools
import math

import jax
import jax.numpy as jnp
from jax import lax
from jax.experimental import pallas as pl
from jax.experimental.pallas import tpu as pltpu
from jax.sharding import PartitionSpec as P

D = 2048
HEADS = 16
NOPE = 128
ROPE = 64
VH = 128
LATENT = 512
TOPK = 6

EPSILON = 1e-06
MASKED = -1e30

MESH = pl.DeviceIdType.MESH
ANY = pl.BlockSpec(memory_space=pl.ANY)
DMA = pltpu.SemaphoreType.DMA
F32 = jnp.float32
BF16 = jnp.bfloat16


def remote(src, dst, send, recv, peer):
    return pltpu.make_async_remote_copy(
        src_ref=src,
        dst_ref=dst,
        send_sem=send,
        recv_sem=recv,
        device_id={"ep": peer},
        device_id_type=MESH,
    )


def greet(peers):
    barrier = pltpu.get_barrier_semaphore()
    for peer in peers:
        pl.semaphore_signal(barrier, inc=1, device_id={"ep": peer}, device_id_type=MESH)
    pl.semaphore_wait(barrier, len(peers))


def around(n):
    me = lax.axis_index("ep")
    x, y = me % 2, (me // 2) % 2
    return me, me // 4, y, x, me + 1 - 2 * x, me + 2 - 4 * y


def near(z, nz, below, above):
    for s in range(nz - 1):
        pl.when(z - 1 - s >= 0)(functools.partial(below, s, z - 1 - s))
        pl.when(z + 1 + s < nz)(functools.partial(above, s, z + 1 + s))


def gather_kernel(n, x_ref, o_ref, own, us, ur, ds, dr, xs, xr, ys, yr):
    me, z, y, x, px, py = around(n)
    nz = n // 4
    low = me % 4
    half = x_ref.shape[0] // 2
    top, bottom = pl.ds(0, half), pl.ds(half, half)
    up, down = (me + 4) % n, (me + n - 4) % n
    barrier = pltpu.get_barrier_semaphore()
    greeted = [(px, None), (py, None), (up, z + 1 < nz), (down, z > 0)]
    for peer, there in greeted:

        def hello(peer=peer):
            pl.semaphore_signal(barrier, inc=1, device_id={"ep": peer}, device_id_type=MESH)

        hello() if there is None else pl.when(there)(hello)
    on_line = (z + 1 < nz).astype(jnp.int32) + (z > 0).astype(jnp.int32)
    pl.semaphore_wait(barrier, 2 + on_line)
    local = pltpu.make_async_copy(x_ref, o_ref.at[me], own)
    local.start()

    def over_x(src, b, part, i):
        return remote(src.at[part], o_ref.at[b, part], xs.at[i], xr.at[i], px)

    def over_y(src, b, part, i):
        return remote(src.at[part], o_ref.at[b, part], ys.at[i], yr.at[i], py)

    def upward(src, b, s):
        return remote(src, o_ref.at[b], us.at[s], ur.at[s], up)

    def downward(src, b, s):
        return remote(src, o_ref.at[b], ds.at[s], dr.at[s], down)

    def spread(src, t):
        b = t * 4 + low
        over_x(src, b, top, t).start()
        over_y(src, b, bottom, t).start()
        over_y(src, b, top, nz + t).start()
        over_x(src, b, bottom, nz + t).start()

    pl.when(z + 1 < nz)(lambda: upward(x_ref, me, 0).start())
    pl.when(z > 0)(lambda: downward(x_ref, me, 0).start())
    spread(x_ref, z)

    def from_below(s, t):
        b = t * 4 + low
        upward(o_ref.at[b], b, s).wait_recv()
        pl.when(z + 1 < nz)(lambda: upward(o_ref.at[b], b, s + 1).start())
        spread(o_ref.at[b], t)

    def from_above(s, t):
        b = t * 4 + low
        downward(o_ref.at[b], b, s).wait_recv()
        pl.when(z > 0)(lambda: downward(o_ref.at[b], b, s + 1).start())
        spread(o_ref.at[b], t)

    def turn(s, t):
        bx = t * 4 + low + px - me
        by = t * 4 + low + py - me
        over_x(o_ref.at[bx], bx, top, t).wait_recv()
        over_y(o_ref.at[bx], bx, top, 2 * nz + t).start()
        over_y(o_ref.at[by], by, bottom, t).wait_recv()
        over_x(o_ref.at[by], by, bottom, 2 * nz + t).start()

    for s in range(nz - 1):
        pl.when(z - 1 - s >= 0)(functools.partial(from_below, s, z - 1 - s))
        pl.when(z + 1 + s < nz)(functools.partial(from_above, s, z + 1 + s))
        if s == 0:
            turn(0, z)
        else:
            pl.when(z - s >= 0)(functools.partial(turn, s, z - s))
            pl.when(z + s < nz)(functools.partial(turn, s, z + s))
    pl.when(z - (nz - 1) >= 0)(functools.partial(turn, 0, z - (nz - 1)))
    pl.when(z + (nz - 1) < nz)(functools.partial(turn, 0, z + (nz - 1)))

    def finish(s, t):
        bx = t * 4 + low + px - me
        by = t * 4 + low + py - me
        bxy = bx + py - me
        over_y(o_ref.at[by], by, top, nz + t).wait_recv()
        over_x(o_ref.at[bx], bx, bottom, nz + t).wait_recv()
        over_y(o_ref.at[bxy], bxy, top, 2 * nz + t).wait_recv()
        over_x(o_ref.at[bxy], bxy, bottom, 2 * nz + t).wait_recv()
        for i in range(3):
            over_x(x_ref, me, top, i * nz + t).wait_send()
            over_y(x_ref, me, top, i * nz + t).wait_send()

    finish(0, z)
    near(z, nz, finish, finish)

    def sent_up(s, t):
        upward(x_ref, me, s).wait_send()

    def sent_down(s, t):
        downward(x_ref, me, s).wait_send()

    for s in range(nz - 1):
        pl.when((z + 1 < nz) & (z - s >= 0))(functools.partial(sent_up, s, z))
        pl.when((z > 0) & (z + s < nz))(functools.partial(sent_down, s, z))
    local.wait()


def gather(x, cid):
    n = lax.axis_size("ep")
    nz = n // 4
    return pl.pallas_call(
        functools.partial(gather_kernel, n),
        out_shape=jax.ShapeDtypeStruct((n,) + x.shape, x.dtype),
        in_specs=[ANY],
        out_specs=ANY,
        scratch_shapes=[DMA] + [DMA((nz,))] * 4 + [DMA((3 * nz,))] * 4,
        compiler_params=pltpu.CompilerParams(collective_id=cid, has_side_effects=True),
        name="gather",
    )(x)


def add_rows(dst, left, right, rows):
    step = 16

    def body(i, carry):
        r = pl.ds(pl.multiple_of(i * step, step), step)
        dst[r] = (left[r].astype(F32) + right[r].astype(F32)).astype(dst.dtype)
        return carry

    lax.fori_loop(0, rows // step, body, 0)


def exchange_kernel(n, m, w, *refs):
    refs = list(refs)

    def take(count):
        out = refs[:count]
        del refs[:count]
        return out

    sums_in, swaps_in = take(m), take(w)
    sums_out, swaps_out = take(m), take(w)
    room = [take(7) for _ in range(m)]
    sems = [take(8) for _ in range(m)]
    swap_sems = take(3) if w else None
    me, z, y, x, px, py = around(n)
    nz = n // 4
    low = me % 4
    to = [(z + k) % nz for k in range(nz)]
    at = [t * 4 + low for t in to]
    everyone = [(me + k) % n for k in range(n)]
    back = [(me + n - k) % n for k in range(n)]
    if w:
        greet(everyone[1:])
    else:
        greet([px, py] + at[1:])
    order = [2, 1, 3, 0] if nz == 4 else list(range(1, nz)) + [0]
    sends, copies = [], []

    def halves(j):
        half = sums_in[j].shape[3] // 2
        return half, pl.ds(0, half), pl.ds(half, half)

    first, second, third = {}, {}, {}

    def stage_one(j, k):
        p = sums_in[j]
        half, top, bottom = halves(j)
        la, lb, a1, b1, a2, b2, zb = room[j]
        lsa, lsb, xs, xr, ys, yr, zs, zr = sems[j]
        t = to[k]
        c = remote(p.at[t, 1 - y, :, top], a1.at[k], ys.at[k], yr.at[k], py)
        d = remote(p.at[t, :, 1 - x, bottom], b1.at[k], xs.at[k], xr.at[k], px)
        c.start()
        d.start()
        e = pltpu.make_async_copy(p.at[t, y, :, top], la.at[k], lsa.at[k])
        f = pltpu.make_async_copy(p.at[t, :, x, bottom], lb.at[k], lsb.at[k])
        e.start()
        f.start()
        first[j, k] = (c, d, e, f)
        sends.extend([c, d])

    def stage_two(j, k):
        half, top, bottom = halves(j)
        la, lb, a1, b1, a2, b2, zb = room[j]
        lsa, lsb, xs, xr, ys, yr, zs, zr = sems[j]
        c, d, e, f = first[j, k]
        e.wait()
        c.wait_recv()
        for i in range(2):
            add_rows(la.at[k, i], la.at[k, i], a1.at[k, i], half)
        g = remote(la.at[k, 1 - x], a2.at[k], xs.at[nz + k], xr.at[nz + k], px)
        g.start()
        f.wait()
        d.wait_recv()
        for i in range(2):
            add_rows(lb.at[k, i], lb.at[k, i], b1.at[k, i], half)
        h = remote(lb.at[k, 1 - y], b2.at[k], ys.at[nz + k], yr.at[nz + k], py)
        h.start()
        second[j, k] = (g, h)
        sends.extend([g, h])

    def stage_three(j, k):
        half, top, bottom = halves(j)
        la, lb, a1, b1, a2, b2, zb = room[j]
        lsa, lsb, xs, xr, ys, yr, zs, zr = sems[j]
        g, h = second[j, k]
        g.wait_recv()
        add_rows(a2.at[k], la.at[k, x], a2.at[k], half)
        if k:
            c = remote(a2.at[k], zb.at[k, top], zs.at[k], zr.at[k], at[k])
            c.start()
        h.wait_recv()
        add_rows(b2.at[k], lb.at[k, y], b2.at[k], half)
        if k:
            d = remote(b2.at[k], zb.at[k, bottom], zs.at[nz + k], zr.at[nz + k], at[k])
            d.start()
            third[j, k] = (c, d)
            sends.extend([c, d])

    def start_swaps():
        own, ss, rs = swap_sems
        for j in range(w):
            local = pltpu.make_async_copy(swaps_in[j].at[me], swaps_out[j].at[me], own.at[j])
            local.start()
            copies.append(local)
        for k in range(1, n):
            for j in range(w):
                c = remote(
                    swaps_in[j].at[everyone[k]],
                    swaps_out[j].at[me],
                    ss.at[j, k],
                    rs.at[j, k],
                    everyone[k],
                )
                c.start()
                sends.append(c)

    steps = [(j, k) for j in range(m) for k in order]
    for i in range(min(2, len(steps))):
        stage_one(*steps[i])
    if w:
        start_swaps()
    for i, step in enumerate(steps):
        stage_two(*step)
        if i + 2 < len(steps):
            stage_one(*steps[i + 2])
        if i:
            stage_three(*steps[i - 1])
    if steps:
        stage_three(*steps[-1])
    for j in range(m):
        half, top, bottom = halves(j)
        la, lb, a1, b1, a2, b2, zb = room[j]
        o_ref = sums_out[j]
        for k in range(1, nz):
            c, d = third[j, k]
            c.wait_recv()
            d.wait_recv()
        for part, offset in ((a2, 0), (b2, half)):

            def body(i, carry, part=part, offset=offset, zb=zb, o_ref=o_ref):
                r = pl.ds(pl.multiple_of(i * 16, 16), 16)
                q = pl.ds(pl.multiple_of(i * 16 + offset, 16), 16)
                total = part[0, r].astype(F32)
                for k in range(1, nz):
                    total = total + zb[k, q].astype(F32)
                o_ref[q] = total.astype(o_ref.dtype)
                return carry

            lax.fori_loop(0, half // 16, body, 0)
    if w:
        own, ss, rs = swap_sems
        for k in range(1, n):
            for j in range(w):
                remote(
                    swaps_in[j].at[back[k]],
                    swaps_out[j].at[back[k]],
                    ss.at[j, k],
                    rs.at[j, k],
                    everyone[k],
                ).wait_recv()
    for copy in sends:
        copy.wait_send()
    for copy in copies:
        copy.wait()


def exchange(cid, sums=(), swaps=()):
    n = lax.axis_size("ep")
    nz = n // 4
    m, w = len(sums), len(swaps)
    kept_rows = [p.shape[1] for p in sums]
    sums = [jnp.pad(p, ((0, 0), (0, -p.shape[1] % 32), (0, 0))) for p in sums]
    views = [p.reshape((nz, 2, 2) + p.shape[1:]) for p in sums]
    scratch = []
    for p in sums:
        rows, cols = p.shape[1:]
        half = rows // 2
        scratch += [pltpu.VMEM((nz, 2, half, cols), p.dtype)] * 4
        scratch += [pltpu.VMEM((nz, half, cols), p.dtype)] * 2
        scratch += [pltpu.VMEM((nz, rows, cols), p.dtype)]
    for p in sums:
        scratch += [DMA((nz,))] * 2 + [DMA((2 * nz,))] * 6
    if w:
        scratch += [DMA((w,)), DMA((w, n)), DMA((w, n))]
    out = pl.pallas_call(
        functools.partial(exchange_kernel, n, m, w),
        out_shape=[jax.ShapeDtypeStruct(p.shape[1:], F32) for p in sums]
        + [jax.ShapeDtypeStruct(a.shape, a.dtype) for a in swaps],
        in_specs=[ANY] * (m + w),
        out_specs=[pl.BlockSpec(memory_space=pltpu.VMEM)] * m + [ANY] * w,
        scratch_shapes=scratch,
        compiler_params=pltpu.CompilerParams(
            collective_id=cid, has_side_effects=True, vmem_limit_bytes=(40 << 20) if m else None
        ),
        name="exchange",
    )(*views, *swaps)
    return [a[:rows] for a, rows in zip(out, kept_rows)] + list(out[m:])


def both(p):
    g = lax.axis_index("grp")
    mine = lax.dynamic_index_in_dim(p, g, 0, keepdims=False)
    theirs = lax.dynamic_index_in_dim(p, 1 - g, 0, keepdims=False)
    return mine, lax.ppermute(theirs.astype(BF16), "grp", [(0, 1), (1, 0)])


def over_groups(p):
    if lax.axis_size("grp") == 2:
        mine, other = both(p)
        return mine.astype(F32) + other.astype(F32)
    return lax.psum_scatter(p.astype(BF16), "grp", scatter_dimension=0, tiled=False).astype(F32)


def product_over_groups(left, right):
    groups = lax.axis_size("grp")
    rows = left.shape[1] // groups
    if groups != 2:
        whole = product("km,kn->mn", left, right)
        return over_groups(whole.reshape(groups, rows, -1))
    g = lax.axis_index("grp")
    mine = lax.dynamic_slice_in_dim(left, g * rows, rows, 1)
    theirs = lax.dynamic_slice_in_dim(left, (1 - g) * rows, rows, 1)
    sent = product("km,kn->mn", theirs, right).astype(BF16)
    other = lax.ppermute(sent, "grp", [(0, 1), (1, 0)])
    return product("km,kn->mn", mine, right) + other.astype(F32)


def from_partner(values):
    groups = lax.axis_size("grp")
    return lax.ppermute(values, "grp", [(g, g + 1 - 2 * (g % 2)) for g in range(groups)])


def to_row_owner(block):
    groups, n = lax.axis_size("grp"), lax.axis_size("ep")
    pairs = [(h * n + e, e * groups + h) for h in range(groups) for e in range(n)]
    return lax.ppermute(block.astype(BF16), ("grp", "ep"), pairs).astype(F32)


def sum_async(p):
    n = lax.axis_size("ep")
    nz = n // 4
    e = lax.axis_index("ep")
    z, y, x = e // 4, (e // 2) % 2, e % 2
    rows, cols = p.shape[1:]
    p = p.reshape(nz, 2, 2, rows, cols)
    top, bottom = p[:, :, :, : rows // 2], p[:, :, :, rows // 2 :]

    def fold(part, place, axis, bit):
        kept = lax.dynamic_index_in_dim(part, place, axis, keepdims=False)
        sent = lax.dynamic_index_in_dim(part, 1 - place, axis, keepdims=False)
        got = lax.ppermute(sent, "ep", [(i, i ^ bit) for i in range(n)])
        return (kept.astype(F32) + got.astype(F32)).astype(p.dtype)

    top = fold(fold(top, y, 1, 2), x, 1, 1)
    bottom = fold(fold(bottom, x, 2, 1), y, 1, 2)
    line = jnp.concatenate([top, bottom], axis=1)
    total = lax.dynamic_index_in_dim(line, z, 0, keepdims=False).astype(F32)
    for k in range(1, nz):
        sent = lax.dynamic_index_in_dim(line, (z + k) % nz, 0, keepdims=False)
        total = total + lax.ppermute(sent, "ep", [(i, (i + 4 * k) % n) for i in range(n)]).astype(F32)
    return total


def dot(left, right):
    return jnp.dot(left, right, preferred_element_type=F32)


def dot_nt(left, right):
    return lax.dot_general(left, right, (((1,), (1,)), ((), ())), preferred_element_type=F32)


KEYS = 512


def scores_of(scale, prefix, k, q, first_key, first_query):
    scores = dot_nt(k, q) * scale
    key = first_key + lax.broadcasted_iota(jnp.int32, scores.shape, 0)
    query = first_query + lax.broadcasted_iota(jnp.int32, scores.shape, 1)
    return jnp.where((key <= query) | (key < prefix), scores, MASKED)


def key_blocks(prefix, last_query):
    return (jnp.maximum(last_query, prefix) + KEYS - 1) // KEYS


def attend_kernel(scale, prefix_ref, q_ref, k_ref, v_ref, attended_ref, exact_ref, lse_ref):
    q = q_ref[...]
    rows = q.shape[0]
    start = pl.program_id(0) * rows
    prefix = prefix_ref[0]

    def step(j, carry):
        top, total, out = carry
        s = scores_of(scale, prefix, k_ref[j], q, j * KEYS, start)
        new_top = jnp.maximum(top, jnp.max(s, axis=0, keepdims=True))
        p = jnp.exp(s - new_top)
        shrink = jnp.exp(top - new_top)
        total = total * shrink + jnp.sum(p, axis=0, keepdims=True)
        return new_top, total, out * shrink + dot(v_ref[j], p.astype(BF16))

    top, total, out = lax.fori_loop(
        0,
        key_blocks(prefix, start + rows),
        step,
        (
            jnp.full((1, rows), MASKED, F32),
            jnp.zeros((1, rows), F32),
            jnp.zeros((v_ref.shape[1], rows), F32),
        ),
    )
    lse_ref[...] = top + jnp.log(total)
    exact = (out / total).T
    exact_ref[...] = exact
    attended_ref[...] = exact.astype(BF16)


def attend(prefix, q, k, v):
    length, depth = q.shape
    values = v.shape[1]
    rows = 256
    v = v.reshape(length // KEYS, KEYS, values).transpose(0, 2, 1)
    k = k.reshape(length // KEYS, KEYS, depth)
    return pl.pallas_call(
        functools.partial(attend_kernel, 1.0 / math.sqrt(NOPE + ROPE)),
        grid=(length // rows,),
        in_specs=[
            pl.BlockSpec(memory_space=pltpu.SMEM),
            pl.BlockSpec((rows, depth), lambda i: (i, 0)),
            pl.BlockSpec(k.shape, lambda i: (0, 0, 0)),
            pl.BlockSpec(v.shape, lambda i: (0, 0, 0)),
        ],
        out_specs=[
            pl.BlockSpec((rows, values), lambda i: (i, 0)),
            pl.BlockSpec((rows, values), lambda i: (i, 0)),
            pl.BlockSpec((1, rows), lambda i: (0, i)),
        ],
        out_shape=[
            jax.ShapeDtypeStruct((length, values), BF16),
            jax.ShapeDtypeStruct((length, values), F32),
            jax.ShapeDtypeStruct((1, length), F32),
        ],
        compiler_params=pltpu.CompilerParams(vmem_limit_bytes=32 << 20),
        name="attend",
    )(prefix, q, k, v)


def attend_back_kernel(
    scale, prefix_ref, q_ref, g_ref, lse_ref, delta_ref, k_ref, v_ref, dq_ref, dk_ref, dv_ref
):
    q, g = q_ref[...], g_ref[...]
    rows = q.shape[0]
    start = pl.program_id(0) * rows
    prefix = prefix_ref[0]

    @pl.when(pl.program_id(0) == 0)
    def _():
        dk_ref[...] = jnp.zeros_like(dk_ref)
        dv_ref[...] = jnp.zeros_like(dv_ref)

    def step(j, dq):
        k = k_ref[j]
        p = jnp.exp(scores_of(scale, prefix, k, q, j * KEYS, start) - lse_ref[...])
        ds = (p * (dot_nt(v_ref[j], g) - delta_ref[...]) * scale).astype(BF16)
        dv_ref[j] += dot(p.astype(BF16), g)
        dk_ref[j] += dot(ds, q)
        return dq + lax.dot_general(
            ds, k, (((0,), (0,)), ((), ())), preferred_element_type=F32
        )

    dq_ref[...] = lax.fori_loop(
        0, key_blocks(prefix, start + rows), step, jnp.zeros(dq_ref.shape, F32)
    )


def attend_back(prefix, q, g, lse, delta, k, v):
    length, depth = q.shape
    values = v.shape[1]
    rows = 256
    k = k.reshape(length // KEYS, KEYS, depth)
    v = v.reshape(length // KEYS, KEYS, values)
    dq, dk, dv = pl.pallas_call(
        functools.partial(attend_back_kernel, 1.0 / math.sqrt(NOPE + ROPE)),
        grid=(length // rows,),
        in_specs=[
            pl.BlockSpec(memory_space=pltpu.SMEM),
            pl.BlockSpec((rows, depth), lambda i: (i, 0)),
            pl.BlockSpec((rows, values), lambda i: (i, 0)),
            pl.BlockSpec((1, rows), lambda i: (0, i)),
            pl.BlockSpec((1, rows), lambda i: (0, i)),
            pl.BlockSpec(k.shape, lambda i: (0, 0, 0)),
            pl.BlockSpec(v.shape, lambda i: (0, 0, 0)),
        ],
        out_specs=[
            pl.BlockSpec((rows, depth), lambda i: (i, 0)),
            pl.BlockSpec(k.shape, lambda i: (0, 0, 0)),
            pl.BlockSpec(v.shape, lambda i: (0, 0, 0)),
        ],
        out_shape=[
            jax.ShapeDtypeStruct((length, depth), F32),
            jax.ShapeDtypeStruct(k.shape, F32),
            jax.ShapeDtypeStruct(v.shape, F32),
        ],
        compiler_params=pltpu.CompilerParams(vmem_limit_bytes=40 << 20),
        name="attend_back",
    )(prefix, q, g, lse, delta, k, v)
    return dq, dk.reshape(length, depth), dv.reshape(length, values)


def ffn_kernel(
    n,
    x_ref,
    y_ref,
    slots_ref,
    tokens_ref,
    own_ref,
    router_ref,
    sg_ref,
    su_ref,
    sd_ref,
    eg_ref,
    eu_ref,
    ed_ref,
    out_ref,
    ffn_ref,
    dot_ref,
    probs_ref,
    rows_ref,
    hidden_ref,
    slot_grad_ref,
    grad_g_ref,
    grad_u_ref,
    shared_h_ref,
    shared_dg_ref,
    shared_du_ref,
    expert_out,
    row_grad,
):
    blocks, tokens = x_ref.shape[:2]
    capacity = slots_ref.shape[1]
    own = own_ref[...]
    lanes = lax.broadcasted_iota(jnp.int32, (tokens, own.shape[1]), 1)
    gates = []
    for b in range(blocks):
        x, y = x_ref[b], y_ref[b]
        logits = jnp.where(lanes < n, dot(x, router_ref[...]), MASKED)
        raised = jnp.exp(logits - jnp.max(logits, axis=-1, keepdims=True))
        probs = raised / jnp.sum(raised, axis=-1, keepdims=True)
        probs_ref[b] = probs
        gate = jnp.sum(probs * own, axis=-1, keepdims=True)
        gates.append(gate)
        part = pl.ds(b * capacity, capacity)
        rows_ref[part] = dot(slots_ref[b], x).astype(BF16)
        weighted = (gate * y.astype(F32)).astype(BF16)
        slot_grad_ref[part] = dot(slots_ref[b], weighted).astype(BF16)
    rows = rows_ref[...]
    slot_grad = slot_grad_ref[...]
    g = dot(rows, eg_ref[...])
    u = dot(rows, eu_ref[...])
    sigmoid = 1.0 / (1.0 + jnp.exp(-g))
    silu = g * sigmoid
    hidden = (silu * u).astype(BF16)
    hidden_ref[...] = hidden
    expert_out[...] = dot(hidden, ed_ref[...]).astype(BF16)
    grad_hidden = dot_nt(slot_grad, ed_ref[...])
    grad_g = (grad_hidden * u * sigmoid * (1.0 + g * (1.0 - sigmoid))).astype(BF16)
    grad_u = (grad_hidden * silu).astype(BF16)
    grad_g_ref[...] = grad_g
    grad_u_ref[...] = grad_u
    row_grad[...] = (dot_nt(grad_g, eg_ref[...]) + dot_nt(grad_u, eu_ref[...])).astype(BF16)
    x = x_ref[...].reshape(blocks * tokens, -1)
    y = y_ref[...].reshape(blocks * tokens, -1)
    g = dot_nt(x, sg_ref[...])
    u = dot_nt(x, su_ref[...])
    grad_hidden = dot_nt(y, sd_ref[...])
    sigmoid = 1.0 / (1.0 + jnp.exp(-g))
    silu = g * sigmoid
    hidden = (silu * u).astype(BF16)
    grad_g = (grad_hidden * u * sigmoid * (1.0 + g * (1.0 - sigmoid))).astype(BF16)
    grad_u = (grad_hidden * silu).astype(BF16)
    for ref, value in ((shared_h_ref, hidden), (shared_dg_ref, grad_g), (shared_du_ref, grad_u)):
        ref[...] = value.reshape(blocks, tokens, -1)
    width = x.shape[1]
    chunk = width // 4
    met = [0.0] * blocks
    for c in range(width // chunk):
        cols = pl.ds(c * chunk, chunk)
        shared_out = dot(hidden, sd_ref[:, cols])
        shared_ffn = dot(grad_g, sg_ref[:, cols]) + dot(grad_u, su_ref[:, cols])
        for b in range(blocks):
            part = pl.ds(b * capacity, capacity)
            here = slice(b * tokens, (b + 1) * tokens)
            picked = dot(tokens_ref[b], expert_out[part, cols])
            met[b] += jnp.sum(picked * y_ref[b, :, cols].astype(F32), axis=-1, keepdims=True)
            out_ref[b, :, cols] = (shared_out[here] + picked * gates[b]).astype(BF16)
            back = dot(tokens_ref[b], row_grad[part, cols])
            ffn_ref[b, :, cols] = (shared_ffn[here] + back).astype(BF16)
    for b in range(blocks):
        dot_ref[b] = (met[b] * own).astype(BF16)


def ffn(x, y, slots, own_lane, router_w, gate_t, up_t, down, gate_m, up_m, down_m):
    n, tokens, width = x.shape
    capacity = slots.shape[1]
    hidden = gate_m.shape[1]
    shared = gate_t.shape[0]
    group = 4

    def whole(a):
        return pl.BlockSpec(a.shape, lambda i: (0,) * a.ndim, pipeline_mode=pl.Buffered(1))

    def block(*shape):
        return pl.BlockSpec((group,) + shape, lambda i: (i, 0, 0))

    def slot_rows(cols):
        return pl.BlockSpec((group * capacity, cols), lambda i: (i, 0))

    def tokens_of(cols, kind=BF16):
        return jax.ShapeDtypeStruct((n, tokens, cols), kind)

    def slots_of(cols):
        return jax.ShapeDtypeStruct((n * capacity, cols), BF16)

    weights = (own_lane, router_w, gate_t, up_t, down, gate_m, up_m, down_m)
    return pl.pallas_call(
        functools.partial(ffn_kernel, n),
        grid=(n // group,),
        in_specs=[
            block(tokens, width),
            block(tokens, width),
            block(capacity, tokens),
            block(tokens, capacity),
        ]
        + [whole(a) for a in weights],
        out_specs=[
            block(tokens, width),
            block(tokens, width),
            block(tokens, 128),
            block(tokens, 128),
            slot_rows(width),
            slot_rows(hidden),
            slot_rows(width),
            slot_rows(hidden),
            slot_rows(hidden),
            block(tokens, shared),
            block(tokens, shared),
            block(tokens, shared),
        ],
        out_shape=[
            tokens_of(width),
            tokens_of(width),
            tokens_of(128),
            tokens_of(128, F32),
            slots_of(width),
            slots_of(hidden),
            slots_of(width),
            slots_of(hidden),
            slots_of(hidden),
            tokens_of(shared),
            tokens_of(shared),
            tokens_of(shared),
        ],
        scratch_shapes=[
            pltpu.VMEM((group * capacity, width), BF16),
            pltpu.VMEM((group * capacity, width), BF16),
        ],
        compiler_params=pltpu.CompilerParams(vmem_limit_bytes=60 << 20),
        name="ffn",
    )(x, y, slots, slots.transpose(0, 2, 1), *weights)


def product(form, left, right):
    return jnp.einsum(form, left, right, preferred_element_type=F32)


def rms_scale(values):
    return lax.rsqrt(jnp.mean(values * values, axis=-1, keepdims=True) + EPSILON)


def rotary_tables(tokens, n):
    halfway = ROPE // 2
    inverse = 10000.0 ** (-(jnp.arange(halfway, dtype=F32) * 2.0 / ROPE))
    inverse = jnp.concatenate([inverse, inverse])
    sign = jnp.where(jnp.arange(ROPE) < halfway, -1.0, 1.0)
    base = (jnp.arange(n, dtype=F32) * tokens)[:, None] * inverse
    step = jnp.arange(tokens, dtype=F32)[:, None] * inverse
    base_cos, base_sin = jnp.cos(base)[:, None], jnp.sin(base)[:, None]
    step_cos, step_sin = jnp.cos(step)[None], jnp.sin(step)[None]
    cos_table = base_cos * step_cos - base_sin * step_sin
    sin_table = (base_sin * step_cos + base_cos * step_sin) * sign
    return cos_table.reshape(n * tokens, ROPE), sin_table.reshape(n * tokens, ROPE)


def unrotate(grads, cos_table, sin_table):
    halfway = grads.shape[-1] // 2
    first = grads[..., :halfway]
    second = grads[..., halfway:]
    return jnp.concatenate(
        [first * cos_table + second * sin_table, second * cos_table - first * sin_table], axis=-1
    )


def norm_back(grad_unit, unit_values, scale_values):
    return scale_values * (
        grad_unit - unit_values * jnp.mean(grad_unit * unit_values, axis=-1, keepdims=True)
    )


def column_halves(weight, n, half):
    rows, width = weight.shape[0], weight.shape[1] // n
    parts = weight.T.reshape(n, 2, width // 2, rows)
    return lax.dynamic_index_in_dim(parts, half, 1, keepdims=False)


def columns_in(blocks):
    n, width, rows = blocks.shape
    return blocks.transpose(1, 0, 2).reshape(width, n * rows)


def both_halves(mine, other, even):
    return jnp.concatenate([jnp.where(even, mine, other), jnp.where(even, other, mine)], axis=0)


def per_device(
    layer_input,
    attention_gain,
    query_weight,
    latent_weight,
    latent_gain,
    expand_weight,
    output_weight,
    feedforward_gain,
    router_weight,
    shared_gate,
    shared_up,
    shared_down,
    expert_gate,
    expert_up,
    expert_down,
    expert_routes,
    prefix_length,
    output_grad,
):
    n = lax.axis_size("ep")
    groups = lax.axis_size("grp")
    e = lax.axis_index("ep")
    half = lax.axis_index("grp") % 2
    even = half == 0
    tokens = layer_input.shape[0]
    length = tokens * n
    capacity = tokens * TOPK * 4 // (3 * n)
    rows_dev = attention_gain.shape[0]
    latent_rows = latent_gain.shape[0]
    rows_out = D // (groups * n)
    expand_rows = LATENT // (groups * n)

    pad = jnp.zeros((rows_dev - latent_rows,), BF16)
    first_block = jnp.concatenate(
        [
            layer_input,
            latent_weight,
            router_weight,
            attention_gain[:, None],
            feedforward_gain[:, None],
            jnp.concatenate([latent_gain, pad])[:, None],
            expert_routes.astype(BF16),
        ],
        axis=1,
    )
    width = first_block.shape[1]
    first_block = jnp.pad(first_block, ((0, 0), (0, -width % 128)))
    first_all = gather(first_block, 0)
    c0 = D
    c1 = c0 + LATENT + ROPE
    c2 = c1 + n
    all_input = first_all[:, :, :c0].reshape(length, D)
    latent_w = first_all[:, :, c0:c1].reshape(D, LATENT + ROPE)
    router_w = first_all[:, :, c1:c2].reshape(D, n)
    attn_gain = first_all[:, :, c2].reshape(D).astype(F32)
    ffn_gain = first_all[:, :, c2 + 1].reshape(D).astype(F32)
    lat_gain = first_all[:, :latent_rows, c2 + 2].reshape(LATENT).astype(F32)
    routes = first_all[:, :, c2 + 3 : c2 + 3 + TOPK].astype(jnp.int32)

    q_half, x_half = (
        column_halves(query_weight, n, half),
        column_halves(expand_weight, n, half),
    )
    q_half, x_half, first_all = lax.optimization_barrier((q_half, x_half, first_all))
    q_blocks, x_blocks = exchange(1, swaps=(q_half, x_half))
    q_mine, x_mine = columns_in(q_blocks), columns_in(x_blocks)
    query_t = both_halves(q_mine, from_partner(q_mine), even)
    expand_t = both_halves(x_mine, from_partner(x_mine), even)
    shared_half = jnp.where(even, shared_gate, shared_up)
    shared_half = shared_half.T.reshape(n, shared_half.shape[1] // n, rows_dev)

    out_w_half = lax.dynamic_slice_in_dim(output_weight, half * (D // 2), D // 2, 1)
    later_grad, q_blocks = lax.optimization_barrier((output_grad, q_blocks))
    out_w_mine = lax.all_gather(out_w_half, "ep", axis=0, tiled=True)
    out_w_other = from_partner(out_w_mine)
    all_out_grad = lax.all_gather(later_grad, "ep", axis=0, tiled=True)

    def own(values):
        return lax.dynamic_slice_in_dim(values, e * tokens, tokens, 0)

    residual_all = all_input.astype(F32)
    unit_all = residual_all * rms_scale(residual_all)
    normed = (unit_all * attn_gain).astype(BF16)
    cos_table, sin_table = rotary_tables(tokens, n)
    turned = jnp.concatenate(
        [query_t, query_t[NOPE + ROPE // 2 :], query_t[NOPE : NOPE + ROPE // 2]], axis=0
    )
    query_raw = product("td,cd->tc", normed, turned)
    query_r = query_raw[:, NOPE : NOPE + ROPE] * cos_table + query_raw[:, NOPE + ROPE :] * sin_table
    query = jnp.concatenate(
        [query_raw[:, :NOPE], query_r, jnp.zeros((length, ROPE), F32)], axis=1
    ).astype(BF16)
    latent_turned = jnp.concatenate(
        [latent_w, latent_w[:, LATENT + ROPE // 2 :], latent_w[:, LATENT : LATENT + ROPE // 2]],
        axis=1,
    )
    compressed = product("td,dc->tc", normed, latent_turned)
    latent_raw = compressed[:, :LATENT]
    latent = (latent_raw * rms_scale(latent_raw) * lat_gain).astype(BF16)
    rope_raw, rope_swapped = compressed[:, LATENT : LATENT + ROPE], compressed[:, LATENT + ROPE :]
    expanded = product("tl,cl->tc", latent, expand_t).astype(BF16)
    keys = jnp.concatenate(
        [
            expanded[:, :NOPE],
            (rope_raw * cos_table + rope_swapped * sin_table).astype(BF16),
            (rope_swapped * cos_table - rope_raw * sin_table).astype(BF16),
        ],
        axis=1,
    )
    values = expanded[:, NOPE:]
    attended_head, attended_exact, lse = attend(prefix_length, query, keys, values)
    attended_blocks, shared_blocks = exchange(
        2, swaps=(attended_head.reshape(n, tokens, VH), shared_half)
    )
    attended = attended_blocks.transpose(1, 0, 2).reshape(tokens, HEADS * VH)
    shared_mine = columns_in(shared_blocks)
    shared_other = from_partner(shared_mine)
    gate_t = jnp.where(even, shared_mine, shared_other)
    up_t = jnp.where(even, shared_other, shared_mine)

    residual_in = layer_input.astype(F32)
    input_scale = rms_scale(residual_in)
    input_unit = residual_in * input_scale
    out_mine = product("ta,ad->td", attended, out_w_mine)
    out_other = product("ta,ad->td", attended, out_w_other)
    residual_mid = residual_in + jnp.concatenate(
        [jnp.where(even, out_mine, out_other), jnp.where(even, out_other, out_mine)], axis=1
    )
    mid_scale = rms_scale(residual_mid)
    mid_unit = residual_mid * mid_scale
    own_ffn_in = (mid_unit * ffn_gain).astype(BF16)
    ffn_blocks = gather(own_ffn_in, 3)
    ffn_in = ffn_blocks.reshape(length, D)

    own_lane = (jnp.arange(128, dtype=jnp.int32) == e).astype(F32)[None]
    chosen = jnp.any(routes == e, axis=-1)
    chosen_int = chosen.astype(jnp.int32)
    place = jnp.cumsum(chosen_int, axis=1) - chosen_int
    kept = chosen & (place < capacity)
    dispatch = (
        (place[:, None, :] == jnp.arange(capacity, dtype=jnp.int32)[None, :, None])
        & kept[:, None, :]
    ).astype(BF16)
    shared_width = gate_t.shape[0]
    fill = ((0, -shared_width % 128), (0, 0))
    (
        out_partial,
        ffn_partial,
        dot_partial,
        router_all,
        incoming,
        expert_hidden,
        slot_grad,
        grad_expert_g,
        grad_expert_u,
        shared_hidden,
        grad_shared_g,
        grad_shared_u,
    ) = ffn(
        ffn_blocks,
        all_out_grad.reshape(n, tokens, D),
        dispatch,
        own_lane,
        jnp.pad(router_w, ((0, 0), (0, 128 - n))),
        jnp.pad(gate_t, fill),
        jnp.pad(up_t, fill),
        jnp.pad(shared_down, fill),
        expert_gate[0],
        expert_up[0],
        expert_down[0],
    )
    out_sum = lax.psum_scatter(out_partial, "ep", scatter_dimension=0)
    layer_output = (residual_mid + out_sum.astype(F32)).astype(BF16)
    ffn_sum, dot_sum = exchange(4, sums=(ffn_partial, dot_partial))

    def shared_columns(values):
        return values.reshape(length, -1)[:, :shared_width]

    expert_down_grad = product_over_groups(expert_hidden, slot_grad)[None]
    expert_gate_grad = product_over_groups(incoming, grad_expert_g)[None]
    expert_up_grad = product_over_groups(incoming, grad_expert_u)[None]
    shared_down_grad = to_row_owner(product_over_groups(shared_columns(shared_hidden), all_out_grad))
    side_shared = product_over_groups(
        ffn_in,
        jnp.concatenate([shared_columns(grad_shared_g), shared_columns(grad_shared_u)], axis=1),
    ).astype(BF16)

    router_own = lax.dynamic_index_in_dim(router_all, e, 0, keepdims=False)[:, :n]
    grad_probs = dot_sum[:, :n]
    grad_logits = (
        router_own * (grad_probs - jnp.sum(router_own * grad_probs, axis=-1, keepdims=True))
    ).astype(BF16)
    grad_ffn_in = ffn_sum + product("te,de->td", grad_logits, router_w)
    grad_ffn_gain = jnp.sum(grad_ffn_in * mid_unit, axis=0)
    grad_mid = output_grad.astype(F32) + norm_back(grad_ffn_in * ffn_gain, mid_unit, mid_scale)
    grad_mid_b = grad_mid.astype(BF16)
    mid_left, mid_right = grad_mid_b[:, : D // 2], grad_mid_b[:, D // 2 :]
    grad_attended = (
        product("td,ad->ta", jnp.where(even, mid_left, mid_right), out_w_mine)
        + product("td,ad->ta", jnp.where(even, mid_right, mid_left), out_w_other)
    ).astype(BF16)
    output_w_partial = product_over_groups(attended, grad_mid_b).astype(BF16)
    output_w_partial, grad_attended = lax.optimization_barrier((output_w_partial, grad_attended))
    (grad_att_blocks,) = exchange(
        5, swaps=(grad_attended.reshape(tokens, HEADS, VH).transpose(1, 0, 2),)
    )
    output_w_partial, grad_att_blocks = lax.optimization_barrier(
        (output_w_partial, grad_att_blocks)
    )
    grad_att = grad_att_blocks.reshape(length, VH)
    output_weight_grad = sum_async(output_w_partial.reshape(n, rows_out, D))
    grad_router = product("te,td->ed", grad_logits, own_ffn_in)

    delta = jnp.sum(grad_att.astype(F32) * attended_exact, axis=-1)[None]
    grad_query_raw, grad_keys, grad_values = attend_back(
        prefix_length, query, grad_att, lse, delta, keys, values
    )
    grad_key_n = grad_keys[:, :NOPE]
    grad_expanded = jnp.concatenate([grad_key_n, grad_values], axis=1).astype(BF16)
    latent_partial = product("tc,cl->tl", grad_expanded, expand_t).astype(BF16)
    grad_key_r = grad_keys[:, NOPE:].astype(BF16)
    latent_sum, rope_sum = exchange(
        6, sums=(latent_partial.reshape(n, tokens, LATENT), grad_key_r.reshape(n, tokens, 128))
    )
    grad_query = jnp.concatenate(
        [
            grad_query_raw[:, :NOPE],
            grad_query_raw[:, NOPE : NOPE + ROPE] * cos_table
            - grad_query_raw[:, NOPE + ROPE :] * sin_table,
        ],
        axis=1,
    ).astype(BF16)
    normed_partial = product("tc,cd->td", grad_query, query_t)
    gain_partial = jnp.sum(normed_partial * unit_all, axis=0)
    normed_partial = normed_partial.astype(BF16).reshape(n, tokens, D)
    side_query = product_over_groups(normed, grad_query).astype(BF16)
    grad_expand = product_over_groups(latent, grad_expanded).astype(BF16)

    own_compressed = own(compressed)
    latent_scale = rms_scale(own_compressed[:, :LATENT])
    latent_unit = own_compressed[:, :LATENT] * latent_scale
    grad_latent_gain = jnp.sum(latent_sum * latent_unit, axis=0)
    grad_compressed = jnp.concatenate(
        [
            norm_back(latent_sum * lat_gain, latent_unit, latent_scale),
            unrotate(
                rope_sum[:, :ROPE],
                own(cos_table)[:, : ROPE // 2],
                own(sin_table)[:, ROPE // 2 :],
            ),
        ],
        axis=-1,
    ).astype(BF16)
    own_normed = (input_unit * attn_gain).astype(BF16)
    latent_w_partial = product_over_groups(
        own_normed, jnp.pad(grad_compressed, ((0, 0), (0, 640 - LATENT - ROPE)))
    ).astype(BF16)
    own_part = product("tc,dc->td", grad_compressed, latent_w)
    grad_attn_gain = gain_partial + jnp.sum(own_part * input_unit, axis=0)

    def by_owner(values, rows):
        blocks = values.reshape(-1, groups, n, rows).transpose(2, 1, 0, 3)
        return blocks.reshape(n, groups, -1)

    small = jnp.concatenate(
        [
            by_owner(grad_attn_gain, rows_out),
            by_owner(grad_ffn_gain, rows_out),
            by_owner(grad_router, rows_out),
            by_owner(grad_latent_gain, expand_rows),
        ],
        axis=2,
    )
    normed_sum, latent_weight_sum, query_all, shared_all, expand_all, small_all = exchange(
        7,
        sums=(normed_partial, latent_w_partial.reshape(n, rows_out, -1)),
        swaps=(
            side_query.reshape(n, rows_out, -1),
            side_shared.reshape(n, rows_out, -1),
            grad_expand.reshape(n, expand_rows, -1),
            small,
        ),
    )
    grad_normed = normed_sum + own_part
    input_grad = (
        grad_mid + norm_back(grad_normed * attn_gain, input_unit, input_scale)
    ).astype(BF16)
    latent_weight_grad = latent_weight_sum[:, : LATENT + ROPE]
    query_weight_grad = query_all.transpose(1, 0, 2).reshape(rows_out, -1).astype(F32)
    shared_all = shared_all.transpose(1, 0, 2)
    shared_gate_grad = shared_all[:, :, :shared_width].reshape(rows_out, -1).astype(F32)
    shared_up_grad = shared_all[:, :, shared_width:].reshape(rows_out, -1).astype(F32)
    expand_weight_grad = expand_all.transpose(1, 0, 2).reshape(expand_rows, -1).astype(F32)
    small_sum = jnp.sum(small_all, axis=0)
    if groups == 2:
        g = lax.axis_index("grp")
        mine = lax.dynamic_index_in_dim(small_sum, g, 0, keepdims=False)
        theirs = lax.dynamic_index_in_dim(small_sum, 1 - g, 0, keepdims=False)
        small_sum = mine + lax.ppermute(theirs, "grp", [(0, 1), (1, 0)])
    else:
        small_sum = lax.psum_scatter(small_sum, "grp", scatter_dimension=0)
    attention_gain_grad = small_sum[:rows_out]
    feedforward_gain_grad = small_sum[rows_out : 2 * rows_out]
    router_weight_grad = small_sum[2 * rows_out : (2 + n) * rows_out].reshape(n, rows_out).T
    latent_gain_grad = small_sum[(2 + n) * rows_out :]
    return (
        layer_output,
        input_grad,
        attention_gain_grad,
        query_weight_grad,
        latent_weight_grad,
        latent_gain_grad,
        expand_weight_grad,
        output_weight_grad,
        feedforward_gain_grad,
        router_weight_grad,
        shared_gate_grad,
        shared_up_grad,
        shared_down_grad,
        expert_gate_grad,
        expert_up_grad,
        expert_down_grad,
    )


def solution(mesh):
    return jax.shard_map(
        per_device,
        mesh=mesh,
        in_specs=(
            P(("grp", "ep"), None),
            P("ep"),
            P("ep", None),
            P("ep", None),
            P("ep"),
            P("ep", None),
            P("ep", None),
            P("ep"),
            P("ep", None),
            P("ep", None),
            P("ep", None),
            P("ep", None),
            P("ep", None, None),
            P("ep", None, None),
            P("ep", None, None),
            P(("grp", "ep"), None),
            P("grp"),
            P(("grp", "ep"), None),
        ),
        out_specs=(
            P(("grp", "ep"), None),
            P(("grp", "ep"), None),
            P(("grp", "ep")),
            P(("grp", "ep"), None),
            P(("grp", "ep"), None),
            P(("grp", "ep")),
            P(("grp", "ep"), None),
            P(("grp", "ep"), None),
            P(("grp", "ep")),
            P(("grp", "ep"), None),
            P(("grp", "ep"), None),
            P(("grp", "ep"), None),
            P(("grp", "ep"), None),
            P("ep", "grp", None),
            P("ep", "grp", None),
            P("ep", "grp", None),
        ),
        check_vma=False,
    )
```

```python
import functools
import math

import jax
import jax.numpy as jnp
from jax import lax
from jax.experimental import pallas as pl
from jax.experimental.pallas import tpu as pltpu
from jax.sharding import PartitionSpec as P

D = 2048
HEADS = 16
NOPE = 128
ROPE = 64
VH = 128
LATENT = 512
TOPK = 6

EPSILON = 1e-06
MASKED = -1e30

MESH = pl.DeviceIdType.MESH
ANY = pl.BlockSpec(memory_space=pl.ANY)
DMA = pltpu.SemaphoreType.DMA
F32 = jnp.float32
BF16 = jnp.bfloat16


def remote(src, dst, send, recv, peer):
    return pltpu.make_async_remote_copy(
        src_ref=src,
        dst_ref=dst,
        send_sem=send,
        recv_sem=recv,
        device_id={"ep": peer},
        device_id_type=MESH,
    )


def greet(peers):
    barrier = pltpu.get_barrier_semaphore()
    for peer in peers:
        pl.semaphore_signal(barrier, inc=1, device_id={"ep": peer}, device_id_type=MESH)
    pl.semaphore_wait(barrier, len(peers))


def around(n):
    me = lax.axis_index("ep")
    x, y = me % 2, (me // 2) % 2
    return me, me // 4, y, x, me + 1 - 2 * x, me + 2 - 4 * y


def near(z, nz, below, above):
    for s in range(nz - 1):
        pl.when(z - 1 - s >= 0)(functools.partial(below, s, z - 1 - s))
        pl.when(z + 1 + s < nz)(functools.partial(above, s, z + 1 + s))


def gather_kernel(n, x_ref, o_ref, own, us, ur, ds, dr, xs, xr, ys, yr):
    me, z, y, x, px, py = around(n)
    nz = n // 4
    low = me % 4
    half = x_ref.shape[0] // 2
    top, bottom = pl.ds(0, half), pl.ds(half, half)
    up, down = (me + 4) % n, (me + n - 4) % n
    barrier = pltpu.get_barrier_semaphore()
    greeted = [(px, None), (py, None), (up, z + 1 < nz), (down, z > 0)]
    for peer, there in greeted:

        def hello(peer=peer):
            pl.semaphore_signal(barrier, inc=1, device_id={"ep": peer}, device_id_type=MESH)

        hello() if there is None else pl.when(there)(hello)
    on_line = (z + 1 < nz).astype(jnp.int32) + (z > 0).astype(jnp.int32)
    pl.semaphore_wait(barrier, 2 + on_line)
    local = pltpu.make_async_copy(x_ref, o_ref.at[me], own)
    local.start()

    def over_x(src, b, part, i):
        return remote(src.at[part], o_ref.at[b, part], xs.at[i], xr.at[i], px)

    def over_y(src, b, part, i):
        return remote(src.at[part], o_ref.at[b, part], ys.at[i], yr.at[i], py)

    def upward(src, b, s):
        return remote(src, o_ref.at[b], us.at[s], ur.at[s], up)

    def downward(src, b, s):
        return remote(src, o_ref.at[b], ds.at[s], dr.at[s], down)

    def spread(src, t):
        b = t * 4 + low
        over_x(src, b, top, t).start()
        over_y(src, b, bottom, t).start()
        over_y(src, b, top, nz + t).start()
        over_x(src, b, bottom, nz + t).start()

    pl.when(z + 1 < nz)(lambda: upward(x_ref, me, 0).start())
    pl.when(z > 0)(lambda: downward(x_ref, me, 0).start())
    spread(x_ref, z)

    def from_below(s, t):
        b = t * 4 + low
        upward(o_ref.at[b], b, s).wait_recv()
        pl.when(z + 1 < nz)(lambda: upward(o_ref.at[b], b, s + 1).start())
        spread(o_ref.at[b], t)

    def from_above(s, t):
        b = t * 4 + low
        downward(o_ref.at[b], b, s).wait_recv()
        pl.when(z > 0)(lambda: downward(o_ref.at[b], b, s + 1).start())
        spread(o_ref.at[b], t)

    def turn(s, t):
        bx = t * 4 + low + px - me
        by = t * 4 + low + py - me
        over_x(o_ref.at[bx], bx, top, t).wait_recv()
        over_y(o_ref.at[bx], bx, top, 2 * nz + t).start()
        over_y(o_ref.at[by], by, bottom, t).wait_recv()
        over_x(o_ref.at[by], by, bottom, 2 * nz + t).start()

    for s in range(nz - 1):
        pl.when(z - 1 - s >= 0)(functools.partial(from_below, s, z - 1 - s))
        pl.when(z + 1 + s < nz)(functools.partial(from_above, s, z + 1 + s))
        if s == 0:
            turn(0, z)
        else:
            pl.when(z - s >= 0)(functools.partial(turn, s, z - s))
            pl.when(z + s < nz)(functools.partial(turn, s, z + s))
    pl.when(z - (nz - 1) >= 0)(functools.partial(turn, 0, z - (nz - 1)))
    pl.when(z + (nz - 1) < nz)(functools.partial(turn, 0, z + (nz - 1)))

    def finish(s, t):
        bx = t * 4 + low + px - me
        by = t * 4 + low + py - me
        bxy = bx + py - me
        over_y(o_ref.at[by], by, top, nz + t).wait_recv()
        over_x(o_ref.at[bx], bx, bottom, nz + t).wait_recv()
        over_y(o_ref.at[bxy], bxy, top, 2 * nz + t).wait_recv()
        over_x(o_ref.at[bxy], bxy, bottom, 2 * nz + t).wait_recv()
        for i in range(3):
            over_x(x_ref, me, top, i * nz + t).wait_send()
            over_y(x_ref, me, top, i * nz + t).wait_send()

    finish(0, z)
    near(z, nz, finish, finish)

    def sent_up(s, t):
        upward(x_ref, me, s).wait_send()

    def sent_down(s, t):
        downward(x_ref, me, s).wait_send()

    for s in range(nz - 1):
        pl.when((z + 1 < nz) & (z - s >= 0))(functools.partial(sent_up, s, z))
        pl.when((z > 0) & (z + s < nz))(functools.partial(sent_down, s, z))
    local.wait()


def gather(x, cid):
    n = lax.axis_size("ep")
    nz = n // 4
    return pl.pallas_call(
        functools.partial(gather_kernel, n),
        out_shape=jax.ShapeDtypeStruct((n,) + x.shape, x.dtype),
        in_specs=[ANY],
        out_specs=ANY,
        scratch_shapes=[DMA] + [DMA((nz,))] * 4 + [DMA((3 * nz,))] * 4,
        compiler_params=pltpu.CompilerParams(collective_id=cid, has_side_effects=True),
        name="gather",
    )(x)


def add_rows(dst, left, right, rows):
    step = 16

    def body(i, carry):
        r = pl.ds(pl.multiple_of(i * step, step), step)
        dst[r] = (left[r].astype(F32) + right[r].astype(F32)).astype(dst.dtype)
        return carry

    lax.fori_loop(0, rows // step, body, 0)


def exchange_kernel(n, m, w, laid, *refs):
    refs = list(refs)

    def take(count):
        out = refs[:count]
        del refs[:count]
        return out

    sums_in, swaps_in = take(m), take(w)
    sums_out, swaps_out = take(m), take(w)
    room = [take(7) for _ in range(m)]
    sems = [take(8) for _ in range(m)]
    swap_sems = take(3) if w else None
    side_by_side = swaps_out[w - laid :]
    swaps_out = swaps_out[: w - laid] + take(laid)
    me, z, y, x, px, py = around(n)
    nz = n // 4
    low = me % 4
    to = [(z + k) % nz for k in range(nz)]
    at = [t * 4 + low for t in to]
    everyone = [(me + k) % n for k in range(n)]
    back = [(me + n - k) % n for k in range(n)]
    if w:
        greet(everyone[1:])
    else:
        greet([px, py] + at[1:])
    order = [2, 1, 3, 0] if nz == 4 else list(range(1, nz)) + [0]
    sends, copies = [], []

    def halves(j):
        half = sums_in[j].shape[3] // 2
        return half, pl.ds(0, half), pl.ds(half, half)

    first, second, third = {}, {}, {}

    def stage_one(j, k):
        p = sums_in[j]
        half, top, bottom = halves(j)
        la, lb, a1, b1, a2, b2, zb = room[j]
        lsa, lsb, xs, xr, ys, yr, zs, zr = sems[j]
        t = to[k]
        c = remote(p.at[t, 1 - y, :, top], a1.at[k], ys.at[k], yr.at[k], py)
        d = remote(p.at[t, :, 1 - x, bottom], b1.at[k], xs.at[k], xr.at[k], px)
        c.start()
        d.start()
        e = pltpu.make_async_copy(p.at[t, y, :, top], la.at[k], lsa.at[k])
        f = pltpu.make_async_copy(p.at[t, :, x, bottom], lb.at[k], lsb.at[k])
        e.start()
        f.start()
        first[j, k] = (c, d, e, f)
        sends.extend([c, d])

    def stage_two(j, k):
        half, top, bottom = halves(j)
        la, lb, a1, b1, a2, b2, zb = room[j]
        lsa, lsb, xs, xr, ys, yr, zs, zr = sems[j]
        c, d, e, f = first[j, k]
        e.wait()
        c.wait_recv()
        for i in range(2):
            add_rows(la.at[k, i], la.at[k, i], a1.at[k, i], half)
        g = remote(la.at[k, 1 - x], a2.at[k], xs.at[nz + k], xr.at[nz + k], px)
        g.start()
        f.wait()
        d.wait_recv()
        for i in range(2):
            add_rows(lb.at[k, i], lb.at[k, i], b1.at[k, i], half)
        h = remote(lb.at[k, 1 - y], b2.at[k], ys.at[nz + k], yr.at[nz + k], py)
        h.start()
        second[j, k] = (g, h)
        sends.extend([g, h])

    def stage_three(j, k):
        half, top, bottom = halves(j)
        la, lb, a1, b1, a2, b2, zb = room[j]
        lsa, lsb, xs, xr, ys, yr, zs, zr = sems[j]
        g, h = second[j, k]
        g.wait_recv()
        add_rows(a2.at[k], la.at[k, x], a2.at[k], half)
        if k:
            c = remote(a2.at[k], zb.at[k, top], zs.at[k], zr.at[k], at[k])
            c.start()
        h.wait_recv()
        add_rows(b2.at[k], lb.at[k, y], b2.at[k], half)
        if k:
            d = remote(b2.at[k], zb.at[k, bottom], zs.at[nz + k], zr.at[nz + k], at[k])
            d.start()
            third[j, k] = (c, d)
            sends.extend([c, d])

    def start_swaps():
        own, ss, rs = swap_sems
        for j in range(w):
            local = pltpu.make_async_copy(swaps_in[j].at[me], swaps_out[j].at[me], own.at[j])
            local.start()
            copies.append(local)
        for k in range(1, n):
            for j in range(w):
                c = remote(
                    swaps_in[j].at[everyone[k]],
                    swaps_out[j].at[me],
                    ss.at[j, k],
                    rs.at[j, k],
                    everyone[k],
                )
                c.start()
                sends.append(c)

    steps = [(j, k) for j in range(m) for k in order]
    for i in range(min(2, len(steps))):
        stage_one(*steps[i])
    if w:
        start_swaps()
    for i, step in enumerate(steps):
        stage_two(*step)
        if i + 2 < len(steps):
            stage_one(*steps[i + 2])
        if i:
            stage_three(*steps[i - 1])
    if steps:
        stage_three(*steps[-1])
    if w:
        own, ss, rs = swap_sems
        for k in range(1, n):
            for j in range(w):
                remote(
                    swaps_in[j].at[back[k]],
                    swaps_out[j].at[back[k]],
                    ss.at[j, k],
                    rs.at[j, k],
                    everyone[k],
                ).wait_recv()
        for copy in copies:
            copy.wait()
        for wide, got in zip(side_by_side, swaps_out[w - laid :]):
            width = got.shape[2]
            for k in range(n):
                wide[:, k * width : (k + 1) * width] = got[k].astype(F32)
    for j in range(m):
        half, top, bottom = halves(j)
        la, lb, a1, b1, a2, b2, zb = room[j]
        o_ref = sums_out[j]
        for k in range(1, nz):
            c, d = third[j, k]
            c.wait_recv()
            d.wait_recv()
        for part, offset in ((a2, 0), (b2, half)):

            def body(i, carry, part=part, offset=offset, zb=zb, o_ref=o_ref):
                r = pl.ds(pl.multiple_of(i * 16, 16), 16)
                q = pl.ds(pl.multiple_of(i * 16 + offset, 16), 16)
                total = part[0, r].astype(F32)
                for k in range(1, nz):
                    total = total + zb[k, q].astype(F32)
                o_ref[q] = total.astype(o_ref.dtype)
                return carry

            lax.fori_loop(0, half // 16, body, 0)
    for copy in sends:
        copy.wait_send()


def exchange(cid, sums=(), swaps=(), laid=0):
    n = lax.axis_size("ep")
    nz = n // 4
    m, w = len(sums), len(swaps)
    kept_rows = [p.shape[1] for p in sums]
    sums = [jnp.pad(p, ((0, 0), (0, -p.shape[1] % 32), (0, 0))) for p in sums]
    views = [p.reshape((nz, 2, 2) + p.shape[1:]) for p in sums]
    scratch = []
    for p in sums:
        rows, cols = p.shape[1:]
        half = rows // 2
        scratch += [pltpu.VMEM((nz, 2, half, cols), p.dtype)] * 4
        scratch += [pltpu.VMEM((nz, half, cols), p.dtype)] * 2
        scratch += [pltpu.VMEM((nz, rows, cols), p.dtype)]
    for p in sums:
        scratch += [DMA((nz,))] * 2 + [DMA((2 * nz,))] * 6
    if w:
        scratch += [DMA((w,)), DMA((w, n)), DMA((w, n))]
    plain, wide = swaps[: w - laid], swaps[w - laid :]
    scratch += [pltpu.VMEM(a.shape, a.dtype) for a in wide]
    out = pl.pallas_call(
        functools.partial(exchange_kernel, n, m, w, laid),
        out_shape=[jax.ShapeDtypeStruct(p.shape[1:], F32) for p in sums]
        + [jax.ShapeDtypeStruct(a.shape, a.dtype) for a in plain]
        + [jax.ShapeDtypeStruct((a.shape[1], n * a.shape[2]), F32) for a in wide],
        in_specs=[ANY] * (m + w),
        out_specs=[pl.BlockSpec(memory_space=pltpu.VMEM)] * m
        + [ANY] * (w - laid)
        + [pl.BlockSpec(memory_space=pltpu.VMEM)] * laid,
        scratch_shapes=scratch,
        compiler_params=pltpu.CompilerParams(
            collective_id=cid, has_side_effects=True, vmem_limit_bytes=(40 << 20) if m else None
        ),
        name="exchange",
    )(*views, *swaps)
    return [a[:rows] for a, rows in zip(out, kept_rows)] + list(out[m:])


def both(p):
    g = lax.axis_index("grp")
    mine = lax.dynamic_index_in_dim(p, g, 0, keepdims=False)
    theirs = lax.dynamic_index_in_dim(p, 1 - g, 0, keepdims=False)
    return mine, lax.ppermute(theirs.astype(BF16), "grp", [(0, 1), (1, 0)])


def over_groups(p):
    if lax.axis_size("grp") == 2:
        mine, other = both(p)
        return mine.astype(F32) + other.astype(F32)
    return lax.psum_scatter(p.astype(BF16), "grp", scatter_dimension=0, tiled=False).astype(F32)


def product_over_groups(left, right):
    groups = lax.axis_size("grp")
    rows = left.shape[1] // groups
    if groups != 2:
        whole = product("km,kn->mn", left, right)
        return over_groups(whole.reshape(groups, rows, -1))
    g = lax.axis_index("grp")
    mine = lax.dynamic_slice_in_dim(left, g * rows, rows, 1)
    theirs = lax.dynamic_slice_in_dim(left, (1 - g) * rows, rows, 1)
    sent = product("km,kn->mn", theirs, right).astype(BF16)
    other = lax.ppermute(sent, "grp", [(0, 1), (1, 0)])
    return product("km,kn->mn", mine, right) + other.astype(F32)


def from_partner(values):
    groups = lax.axis_size("grp")
    return lax.ppermute(values, "grp", [(g, g + 1 - 2 * (g % 2)) for g in range(groups)])


def to_row_owner(block):
    groups, n = lax.axis_size("grp"), lax.axis_size("ep")
    pairs = [(h * n + e, e * groups + h) for h in range(groups) for e in range(n)]
    return lax.ppermute(block.astype(BF16), ("grp", "ep"), pairs).astype(F32)


def sum_async(p):
    n = lax.axis_size("ep")
    nz = n // 4
    e = lax.axis_index("ep")
    z, y, x = e // 4, (e // 2) % 2, e % 2
    rows, cols = p.shape[1:]
    p = p.reshape(nz, 2, 2, rows, cols)
    top, bottom = p[:, :, :, : rows // 2], p[:, :, :, rows // 2 :]

    def fold(part, place, axis, bit):
        kept = lax.dynamic_index_in_dim(part, place, axis, keepdims=False)
        sent = lax.dynamic_index_in_dim(part, 1 - place, axis, keepdims=False)
        got = lax.ppermute(sent, "ep", [(i, i ^ bit) for i in range(n)])
        return (kept.astype(F32) + got.astype(F32)).astype(p.dtype)

    top = fold(fold(top, y, 1, 2), x, 1, 1)
    bottom = fold(fold(bottom, x, 2, 1), y, 1, 2)
    line = jnp.concatenate([top, bottom], axis=1)
    total = lax.dynamic_index_in_dim(line, z, 0, keepdims=False).astype(F32)
    for k in range(1, nz):
        sent = lax.dynamic_index_in_dim(line, (z + k) % nz, 0, keepdims=False)
        total = total + lax.ppermute(sent, "ep", [(i, (i + 4 * k) % n) for i in range(n)]).astype(F32)
    return total


def dot(left, right):
    return jnp.dot(left, right, preferred_element_type=F32)


def dot_nt(left, right):
    return lax.dot_general(left, right, (((1,), (1,)), ((), ())), preferred_element_type=F32)


def front_kernel(
    x_ref, cos_ref, sin_ref, gain_ref, lat_gain_ref, wq_ref, wl_ref, we_ref,
    normed_ref, query_ref, keys_ref, values_ref, latent_ref,
):
    blocks, tokens = x_ref.shape[:2]
    rows = blocks * tokens
    width = gain_ref.shape[1]
    x = x_ref[:, :, :width].reshape(rows, width).astype(F32)
    normed = (x * rms_scale(x) * gain_ref[...]).astype(BF16)
    normed_ref[...] = normed
    cos, sin = cos_ref[...], sin_ref[...]
    own_half = lax.broadcasted_iota(jnp.int32, cos.shape, 1) < ROPE

    def turn(pair):
        return pair * cos + pltpu.roll(pair, ROPE, 1) * sin

    query = dot_nt(normed, wq_ref[...])
    query_ref[:, :NOPE] = query[:, :NOPE].astype(BF16)
    query_ref[:, NOPE:] = jnp.where(own_half, turn(query[:, NOPE:]), 0.0).astype(BF16)
    compressed = dot(normed, wl_ref[...])
    raw = compressed[:, :LATENT]
    latent = (raw * rms_scale(raw) * lat_gain_ref[...]).astype(BF16)
    latent_ref[...] = latent
    expanded = dot_nt(latent, we_ref[...])
    keys_ref[:, :NOPE] = expanded[:, :NOPE].astype(BF16)
    keys_ref[:, NOPE:] = turn(compressed[:, LATENT:]).astype(BF16)
    values_ref[...] = expanded[:, NOPE:].astype(BF16)


def front(x, cos, sin, gain, lat_gain, wq, wl, we):
    n, tokens, width = x.shape
    length = n * tokens
    blocks = 2
    rows = blocks * tokens

    def whole(a):
        return pl.BlockSpec(a.shape, lambda i: (0,) * a.ndim, pipeline_mode=pl.Buffered(1))

    def rows_of(cols):
        return pl.BlockSpec((rows, cols), lambda i: (i, 0))

    def out(cols):
        return jax.ShapeDtypeStruct((length, cols), BF16)

    cols = (gain.shape[1], wq.shape[0], NOPE + 2 * ROPE, VH, LATENT)
    return pl.pallas_call(
        front_kernel,
        grid=(n // blocks,),
        in_specs=[
            pl.BlockSpec((blocks, tokens, width), lambda i: (i, 0, 0)),
            rows_of(2 * ROPE),
            rows_of(2 * ROPE),
        ]
        + [whole(a) for a in (gain, lat_gain, wq, wl, we)],
        out_specs=[rows_of(c) for c in cols],
        out_shape=[out(c) for c in cols],
        compiler_params=pltpu.CompilerParams(vmem_limit_bytes=48 << 20),
        name="front",
    )(x, cos, sin, gain, lat_gain, wq, wl, we)


def back_kernel(
    x_ref, cos_ref, sin_ref, dq_ref, dk_ref, dv_ref, wq_ref, we_ref,
    query_ref, expanded_ref, latent_ref, rope_ref, normed_ref, gain_ref,
):
    blocks, tokens = x_ref.shape[:2]
    rows = blocks * tokens
    width = gain_ref.shape[1]
    own_half = lax.broadcasted_iota(jnp.int32, cos_ref.shape, 1) < ROPE
    pair = dq_ref[:, NOPE:] * jnp.where(own_half, cos_ref[...], sin_ref[...])
    pair = jnp.where(own_half, pair + pltpu.roll(pair, ROPE, 1), 0.0)
    query_ref[:, :NOPE] = dq_ref[:, :NOPE].astype(BF16)
    query_ref[:, NOPE:] = pair.astype(BF16)
    part = dot(query_ref[...], wq_ref[...])
    normed_ref[...] = part.astype(BF16)
    x = x_ref[:, :, :width].reshape(rows, width).astype(F32)
    gain = jnp.sum(part * (x * rms_scale(x)), axis=0, keepdims=True)

    @pl.when(pl.program_id(0) == 0)
    def _():
        gain_ref[...] = gain

    @pl.when(pl.program_id(0) > 0)
    def _():
        gain_ref[...] += gain

    expanded_ref[:, :NOPE] = dk_ref[:, :NOPE].astype(BF16)
    expanded_ref[:, NOPE:] = dv_ref[...].astype(BF16)
    latent_ref[...] = dot(expanded_ref[...], we_ref[...]).astype(BF16)
    rope_ref[...] = dk_ref[:, NOPE:].astype(BF16)


def back(x, cos, sin, dq, dk, dv, wq, we):
    n, tokens, width = x.shape
    length = n * tokens
    blocks = 2
    rows = blocks * tokens
    model = wq.shape[1]

    def whole(a):
        return pl.BlockSpec(a.shape, lambda i: (0,) * a.ndim, pipeline_mode=pl.Buffered(1))

    def rows_of(cols):
        return pl.BlockSpec((rows, cols), lambda i: (i, 0))

    def out(cols):
        return jax.ShapeDtypeStruct((length, cols), BF16)

    cols = (NOPE + 2 * ROPE, NOPE + VH, LATENT, 2 * ROPE, model)
    return pl.pallas_call(
        back_kernel,
        grid=(n // blocks,),
        in_specs=[
            pl.BlockSpec((blocks, tokens, width), lambda i: (i, 0, 0)),
            rows_of(2 * ROPE),
            rows_of(2 * ROPE),
            rows_of(dq.shape[1]),
            rows_of(dk.shape[1]),
            rows_of(dv.shape[1]),
            whole(wq),
            whole(we),
        ],
        out_specs=[rows_of(c) for c in cols] + [pl.BlockSpec((1, model), lambda i: (0, 0))],
        out_shape=[out(c) for c in cols] + [jax.ShapeDtypeStruct((1, model), F32)],
        compiler_params=pltpu.CompilerParams(vmem_limit_bytes=48 << 20),
        name="back",
    )(x, cos, sin, dq, dk, dv, wq, we)


KEYS = 512


def scores_of(scale, prefix, k, q, first_key, first_query):
    scores = dot_nt(k, q) * scale
    key = first_key + lax.broadcasted_iota(jnp.int32, scores.shape, 0)
    query = first_query + lax.broadcasted_iota(jnp.int32, scores.shape, 1)
    return jnp.where((key <= query) | (key < prefix), scores, MASKED)


def key_blocks(prefix, last_query):
    return (jnp.maximum(last_query, prefix) + KEYS - 1) // KEYS


def attend_kernel(scale, prefix_ref, q_ref, k_ref, v_ref, attended_ref, exact_ref, lse_ref):
    q = q_ref[...]
    rows = q.shape[0]
    start = pl.program_id(0) * rows
    prefix = prefix_ref[0]

    def step(j, carry):
        top, total, out = carry
        s = scores_of(scale, prefix, k_ref[j], q, j * KEYS, start)
        new_top = jnp.maximum(top, jnp.max(s, axis=0, keepdims=True))
        p = jnp.exp(s - new_top)
        shrink = jnp.exp(top - new_top)
        total = total * shrink + jnp.sum(p, axis=0, keepdims=True)
        return new_top, total, out * shrink + dot(v_ref[j], p.astype(BF16))

    top, total, out = lax.fori_loop(
        0,
        key_blocks(prefix, start + rows),
        step,
        (
            jnp.full((1, rows), MASKED, F32),
            jnp.zeros((1, rows), F32),
            jnp.zeros((v_ref.shape[1], rows), F32),
        ),
    )
    lse_ref[...] = top + jnp.log(total)
    exact = (out / total).T
    exact_ref[...] = exact
    attended_ref[...] = exact.astype(BF16)


def attend(prefix, q, k, v):
    length, depth = q.shape
    values = v.shape[1]
    rows = 256
    v = v.reshape(length // KEYS, KEYS, values).transpose(0, 2, 1)
    k = k.reshape(length // KEYS, KEYS, depth)
    return pl.pallas_call(
        functools.partial(attend_kernel, 1.0 / math.sqrt(NOPE + ROPE)),
        grid=(length // rows,),
        in_specs=[
            pl.BlockSpec(memory_space=pltpu.SMEM),
            pl.BlockSpec((rows, depth), lambda i: (i, 0)),
            pl.BlockSpec(k.shape, lambda i: (0, 0, 0)),
            pl.BlockSpec(v.shape, lambda i: (0, 0, 0)),
        ],
        out_specs=[
            pl.BlockSpec((rows, values), lambda i: (i, 0)),
            pl.BlockSpec((rows, values), lambda i: (i, 0)),
            pl.BlockSpec((1, rows), lambda i: (0, i)),
        ],
        out_shape=[
            jax.ShapeDtypeStruct((length, values), BF16),
            jax.ShapeDtypeStruct((length, values), F32),
            jax.ShapeDtypeStruct((1, length), F32),
        ],
        compiler_params=pltpu.CompilerParams(vmem_limit_bytes=32 << 20),
        name="attend",
    )(prefix, q, k, v)


def attend_back_kernel(
    scale, prefix_ref, q_ref, g_ref, lse_ref, delta_ref, k_ref, v_ref, dq_ref, dk_ref, dv_ref
):
    q, g = q_ref[...], g_ref[...]
    rows = q.shape[0]
    start = pl.program_id(0) * rows
    prefix = prefix_ref[0]

    @pl.when(pl.program_id(0) == 0)
    def _():
        dk_ref[...] = jnp.zeros_like(dk_ref)
        dv_ref[...] = jnp.zeros_like(dv_ref)

    def step(j, dq):
        k = k_ref[j]
        p = jnp.exp(scores_of(scale, prefix, k, q, j * KEYS, start) - lse_ref[...])
        ds = (p * (dot_nt(v_ref[j], g) - delta_ref[...]) * scale).astype(BF16)
        dv_ref[j] += dot(p.astype(BF16), g)
        dk_ref[j] += dot(ds, q)
        return dq + lax.dot_general(
            ds, k, (((0,), (0,)), ((), ())), preferred_element_type=F32
        )

    dq_ref[...] = lax.fori_loop(
        0, key_blocks(prefix, start + rows), step, jnp.zeros(dq_ref.shape, F32)
    )


def attend_back(prefix, q, g, lse, delta, k, v):
    length, depth = q.shape
    values = v.shape[1]
    rows = 256
    k = k.reshape(length // KEYS, KEYS, depth)
    v = v.reshape(length // KEYS, KEYS, values)
    dq, dk, dv = pl.pallas_call(
        functools.partial(attend_back_kernel, 1.0 / math.sqrt(NOPE + ROPE)),
        grid=(length // rows,),
        in_specs=[
            pl.BlockSpec(memory_space=pltpu.SMEM),
            pl.BlockSpec((rows, depth), lambda i: (i, 0)),
            pl.BlockSpec((rows, values), lambda i: (i, 0)),
            pl.BlockSpec((1, rows), lambda i: (0, i)),
            pl.BlockSpec((1, rows), lambda i: (0, i)),
            pl.BlockSpec(k.shape, lambda i: (0, 0, 0)),
            pl.BlockSpec(v.shape, lambda i: (0, 0, 0)),
        ],
        out_specs=[
            pl.BlockSpec((rows, depth), lambda i: (i, 0)),
            pl.BlockSpec(k.shape, lambda i: (0, 0, 0)),
            pl.BlockSpec(v.shape, lambda i: (0, 0, 0)),
        ],
        out_shape=[
            jax.ShapeDtypeStruct((length, depth), F32),
            jax.ShapeDtypeStruct(k.shape, F32),
            jax.ShapeDtypeStruct(v.shape, F32),
        ],
        compiler_params=pltpu.CompilerParams(vmem_limit_bytes=40 << 20),
        name="attend_back",
    )(prefix, q, g, lse, delta, k, v)
    return dq, dk.reshape(length, depth), dv.reshape(length, values)


def ffn_kernel(
    n,
    x_ref,
    y_ref,
    slots_ref,
    tokens_ref,
    own_ref,
    router_ref,
    sg_ref,
    su_ref,
    sd_ref,
    eg_ref,
    eu_ref,
    ed_ref,
    out_ref,
    ffn_ref,
    dot_ref,
    probs_ref,
    rows_ref,
    hidden_ref,
    slot_grad_ref,
    grad_g_ref,
    grad_u_ref,
    shared_h_ref,
    shared_dg_ref,
    shared_du_ref,
    expert_out,
    row_grad,
):
    blocks, tokens = x_ref.shape[:2]
    capacity = slots_ref.shape[1]
    own = own_ref[...]
    lanes = lax.broadcasted_iota(jnp.int32, (tokens, own.shape[1]), 1)
    gates = []
    for b in range(blocks):
        x, y = x_ref[b], y_ref[b]
        logits = jnp.where(lanes < n, dot(x, router_ref[...]), MASKED)
        raised = jnp.exp(logits - jnp.max(logits, axis=-1, keepdims=True))
        probs = raised / jnp.sum(raised, axis=-1, keepdims=True)
        probs_ref[b] = probs
        gate = jnp.sum(probs * own, axis=-1, keepdims=True)
        gates.append(gate)
        part = pl.ds(b * capacity, capacity)
        rows_ref[part] = dot(slots_ref[b], x).astype(BF16)
        weighted = (gate * y.astype(F32)).astype(BF16)
        slot_grad_ref[part] = dot(slots_ref[b], weighted).astype(BF16)
    rows = rows_ref[...]
    slot_grad = slot_grad_ref[...]
    g = dot(rows, eg_ref[...])
    u = dot(rows, eu_ref[...])
    sigmoid = 1.0 / (1.0 + jnp.exp(-g))
    silu = g * sigmoid
    hidden = (silu * u).astype(BF16)
    hidden_ref[...] = hidden
    expert_out[...] = dot(hidden, ed_ref[...]).astype(BF16)
    grad_hidden = dot_nt(slot_grad, ed_ref[...])
    grad_g = (grad_hidden * u * sigmoid * (1.0 + g * (1.0 - sigmoid))).astype(BF16)
    grad_u = (grad_hidden * silu).astype(BF16)
    grad_g_ref[...] = grad_g
    grad_u_ref[...] = grad_u
    row_grad[...] = (dot_nt(grad_g, eg_ref[...]) + dot_nt(grad_u, eu_ref[...])).astype(BF16)
    x = x_ref[...].reshape(blocks * tokens, -1)
    y = y_ref[...].reshape(blocks * tokens, -1)
    g = dot_nt(x, sg_ref[...])
    u = dot_nt(x, su_ref[...])
    grad_hidden = dot_nt(y, sd_ref[...])
    sigmoid = 1.0 / (1.0 + jnp.exp(-g))
    silu = g * sigmoid
    hidden = (silu * u).astype(BF16)
    grad_g = (grad_hidden * u * sigmoid * (1.0 + g * (1.0 - sigmoid))).astype(BF16)
    grad_u = (grad_hidden * silu).astype(BF16)
    for ref, value in ((shared_h_ref, hidden), (shared_dg_ref, grad_g), (shared_du_ref, grad_u)):
        ref[...] = value.reshape(blocks, tokens, -1)
    width = x.shape[1]
    chunk = width // 4
    met = [0.0] * blocks
    for c in range(width // chunk):
        cols = pl.ds(c * chunk, chunk)
        shared_out = dot(hidden, sd_ref[:, cols])
        shared_ffn = dot(grad_g, sg_ref[:, cols]) + dot(grad_u, su_ref[:, cols])
        for b in range(blocks):
            part = pl.ds(b * capacity, capacity)
            here = slice(b * tokens, (b + 1) * tokens)
            picked = dot(tokens_ref[b], expert_out[part, cols])
            met[b] += jnp.sum(picked * y_ref[b, :, cols].astype(F32), axis=-1, keepdims=True)
            out_ref[b, :, cols] = (shared_out[here] + picked * gates[b]).astype(BF16)
            back = dot(tokens_ref[b], row_grad[part, cols])
            ffn_ref[b, :, cols] = (shared_ffn[here] + back).astype(BF16)
    for b in range(blocks):
        dot_ref[b] = (met[b] * own).astype(BF16)


def ffn(x, y, slots, own_lane, router_w, gate_t, up_t, down, gate_m, up_m, down_m):
    n, tokens, width = x.shape
    capacity = slots.shape[1]
    hidden = gate_m.shape[1]
    shared = gate_t.shape[0]
    group = 4

    def whole(a):
        return pl.BlockSpec(a.shape, lambda i: (0,) * a.ndim, pipeline_mode=pl.Buffered(1))

    def block(*shape):
        return pl.BlockSpec((group,) + shape, lambda i: (i, 0, 0))

    def slot_rows(cols):
        return pl.BlockSpec((group * capacity, cols), lambda i: (i, 0))

    def tokens_of(cols, kind=BF16):
        return jax.ShapeDtypeStruct((n, tokens, cols), kind)

    def slots_of(cols):
        return jax.ShapeDtypeStruct((n * capacity, cols), BF16)

    weights = (own_lane, router_w, gate_t, up_t, down, gate_m, up_m, down_m)
    return pl.pallas_call(
        functools.partial(ffn_kernel, n),
        grid=(n // group,),
        in_specs=[
            block(tokens, width),
            block(tokens, width),
            block(capacity, tokens),
            block(tokens, capacity),
        ]
        + [whole(a) for a in weights],
        out_specs=[
            block(tokens, width),
            block(tokens, width),
            block(tokens, 128),
            block(tokens, 128),
            slot_rows(width),
            slot_rows(hidden),
            slot_rows(width),
            slot_rows(hidden),
            slot_rows(hidden),
            block(tokens, shared),
            block(tokens, shared),
            block(tokens, shared),
        ],
        out_shape=[
            tokens_of(width),
            tokens_of(width),
            tokens_of(128),
            tokens_of(128, F32),
            slots_of(width),
            slots_of(hidden),
            slots_of(width),
            slots_of(hidden),
            slots_of(hidden),
            tokens_of(shared),
            tokens_of(shared),
            tokens_of(shared),
        ],
        scratch_shapes=[
            pltpu.VMEM((group * capacity, width), BF16),
            pltpu.VMEM((group * capacity, width), BF16),
        ],
        compiler_params=pltpu.CompilerParams(vmem_limit_bytes=60 << 20),
        name="ffn",
    )(x, y, slots, slots.transpose(0, 2, 1), *weights)


def product(form, left, right):
    return jnp.einsum(form, left, right, preferred_element_type=F32)


def rms_scale(values):
    return lax.rsqrt(jnp.mean(values * values, axis=-1, keepdims=True) + EPSILON)


def rotary_tables(tokens, n):
    halfway = ROPE // 2
    inverse = 10000.0 ** (-(jnp.arange(halfway, dtype=F32) * 2.0 / ROPE))
    inverse = jnp.concatenate([inverse] * 4)
    lane = jnp.arange(2 * ROPE)
    sign = jnp.where((lane < halfway) | (lane >= 3 * halfway), -1.0, 1.0)
    base = (jnp.arange(n, dtype=F32) * tokens)[:, None] * inverse
    step = jnp.arange(tokens, dtype=F32)[:, None] * inverse
    base_cos, base_sin = jnp.cos(base)[:, None], jnp.sin(base)[:, None]
    step_cos, step_sin = jnp.cos(step)[None], jnp.sin(step)[None]
    cos_table = base_cos * step_cos - base_sin * step_sin
    sin_table = (base_sin * step_cos + base_cos * step_sin) * sign
    return cos_table.reshape(n * tokens, -1), sin_table.reshape(n * tokens, -1)


def unrotate(grads, cos_table, sin_table):
    halfway = grads.shape[-1] // 2
    first = grads[..., :halfway]
    second = grads[..., halfway:]
    return jnp.concatenate(
        [first * cos_table + second * sin_table, second * cos_table - first * sin_table], axis=-1
    )


def norm_back(grad_unit, unit_values, scale_values):
    return scale_values * (
        grad_unit - unit_values * jnp.mean(grad_unit * unit_values, axis=-1, keepdims=True)
    )


def column_halves(weight, n, half):
    rows, width = weight.shape[0], weight.shape[1] // n
    parts = weight.T.reshape(n, 2, width // 2, rows)
    return lax.dynamic_index_in_dim(parts, half, 1, keepdims=False)


def columns_in(blocks):
    n, width, rows = blocks.shape
    return blocks.transpose(1, 0, 2).reshape(width, n * rows)


def both_halves(mine, other, even):
    return jnp.concatenate([jnp.where(even, mine, other), jnp.where(even, other, mine)], axis=0)


def per_device(
    layer_input,
    attention_gain,
    query_weight,
    latent_weight,
    latent_gain,
    expand_weight,
    output_weight,
    feedforward_gain,
    router_weight,
    shared_gate,
    shared_up,
    shared_down,
    expert_gate,
    expert_up,
    expert_down,
    expert_routes,
    prefix_length,
    output_grad,
):
    n = lax.axis_size("ep")
    groups = lax.axis_size("grp")
    e = lax.axis_index("ep")
    half = lax.axis_index("grp") % 2
    even = half == 0
    tokens = layer_input.shape[0]
    length = tokens * n
    capacity = tokens * TOPK * 4 // (3 * n)
    rows_dev = attention_gain.shape[0]
    latent_rows = latent_gain.shape[0]
    rows_out = D // (groups * n)
    expand_rows = LATENT // (groups * n)

    pad = jnp.zeros((rows_dev - latent_rows,), BF16)
    first_block = jnp.concatenate(
        [
            layer_input,
            latent_weight,
            router_weight,
            attention_gain[:, None],
            feedforward_gain[:, None],
            jnp.concatenate([latent_gain, pad])[:, None],
            expert_routes.astype(BF16),
        ],
        axis=1,
    )
    width = first_block.shape[1]
    first_block = jnp.pad(first_block, ((0, 0), (0, -width % 128)))
    first_all = gather(first_block, 0)
    c0 = D
    c1 = c0 + LATENT + ROPE
    c2 = c1 + n
    latent_w = first_all[:, :, c0:c1].reshape(D, LATENT + ROPE)
    router_w = first_all[:, :, c1:c2].reshape(D, n)
    attn_gain = first_all[:, :, c2].reshape(D).astype(F32)
    ffn_gain = first_all[:, :, c2 + 1].reshape(D).astype(F32)
    lat_gain = first_all[:, :latent_rows, c2 + 2].reshape(LATENT).astype(F32)
    routes = first_all[:, :, c2 + 3 : c2 + 3 + TOPK].astype(jnp.int32)

    q_half, x_half = (
        column_halves(query_weight, n, half),
        column_halves(expand_weight, n, half),
    )
    q_half, x_half, first_all = lax.optimization_barrier((q_half, x_half, first_all))
    q_blocks, x_blocks = exchange(1, swaps=(q_half, x_half))
    q_mine, x_mine = columns_in(q_blocks), columns_in(x_blocks)
    query_t = both_halves(q_mine, from_partner(q_mine), even)
    expand_t = both_halves(x_mine, from_partner(x_mine), even)
    shared_half = jnp.where(even, shared_gate, shared_up)
    shared_half = shared_half.T.reshape(n, shared_half.shape[1] // n, rows_dev)

    out_w_half = lax.dynamic_slice_in_dim(output_weight, half * (D // 2), D // 2, 1)
    later_grad, q_blocks = lax.optimization_barrier((output_grad, q_blocks))
    out_w_mine = lax.all_gather(out_w_half, "ep", axis=0, tiled=True)
    out_w_other = from_partner(out_w_mine)
    all_out_grad = lax.all_gather(later_grad, "ep", axis=0, tiled=True)

    def own(values):
        return lax.dynamic_slice_in_dim(values, e * tokens, tokens, 0)

    cos_table, sin_table = rotary_tables(tokens, n)
    turned = jnp.concatenate(
        [query_t, query_t[NOPE + ROPE // 2 :], query_t[NOPE : NOPE + ROPE // 2]], axis=0
    )
    latent_turned = jnp.concatenate(
        [latent_w, latent_w[:, LATENT + ROPE // 2 :], latent_w[:, LATENT : LATENT + ROPE // 2]],
        axis=1,
    )
    normed, query, keys, values, latent = front(
        first_all, cos_table, sin_table, attn_gain[None], lat_gain[None], turned, latent_turned, expand_t
    )
    attended_head, attended_exact, lse = attend(prefix_length, query, keys, values)
    attended_blocks, shared_blocks = exchange(
        2, swaps=(attended_head.reshape(n, tokens, VH), shared_half)
    )
    attended = attended_blocks.transpose(1, 0, 2).reshape(tokens, HEADS * VH)
    shared_mine = columns_in(shared_blocks)
    shared_other = from_partner(shared_mine)
    gate_t = jnp.where(even, shared_mine, shared_other)
    up_t = jnp.where(even, shared_other, shared_mine)

    residual_in = layer_input.astype(F32)
    input_scale = rms_scale(residual_in)
    input_unit = residual_in * input_scale
    out_mine = product("ta,ad->td", attended, out_w_mine)
    out_other = product("ta,ad->td", attended, out_w_other)
    residual_mid = residual_in + jnp.concatenate(
        [jnp.where(even, out_mine, out_other), jnp.where(even, out_other, out_mine)], axis=1
    )
    mid_scale = rms_scale(residual_mid)
    mid_unit = residual_mid * mid_scale
    own_ffn_in = (mid_unit * ffn_gain).astype(BF16)
    ffn_blocks = gather(own_ffn_in, 3)
    ffn_in = ffn_blocks.reshape(length, D)

    own_lane = (jnp.arange(128, dtype=jnp.int32) == e).astype(F32)[None]
    chosen = jnp.any(routes == e, axis=-1)
    chosen_int = chosen.astype(jnp.int32)
    place = jnp.cumsum(chosen_int, axis=1) - chosen_int
    kept = chosen & (place < capacity)
    dispatch = (
        (place[:, None, :] == jnp.arange(capacity, dtype=jnp.int32)[None, :, None])
        & kept[:, None, :]
    ).astype(BF16)
    shared_width = gate_t.shape[0]
    fill = ((0, -shared_width % 128), (0, 0))
    (
        out_partial,
        ffn_partial,
        dot_partial,
        router_all,
        incoming,
        expert_hidden,
        slot_grad,
        grad_expert_g,
        grad_expert_u,
        shared_hidden,
        grad_shared_g,
        grad_shared_u,
    ) = ffn(
        ffn_blocks,
        all_out_grad.reshape(n, tokens, D),
        dispatch,
        own_lane,
        jnp.pad(router_w, ((0, 0), (0, 128 - n))),
        jnp.pad(gate_t, fill),
        jnp.pad(up_t, fill),
        jnp.pad(shared_down, fill),
        expert_gate[0],
        expert_up[0],
        expert_down[0],
    )
    ffn_sum, dot_sum = exchange(4, sums=(ffn_partial, dot_partial))
    out_partial, ffn_sum = lax.optimization_barrier((out_partial, ffn_sum))
    out_sum = lax.psum_scatter(out_partial, "ep", scatter_dimension=0)
    layer_output = (residual_mid + out_sum.astype(F32)).astype(BF16)

    def shared_columns(values):
        return values.reshape(length, -1)[:, :shared_width]

    expert_down_grad = product_over_groups(expert_hidden, slot_grad)[None]
    expert_gate_grad = product_over_groups(incoming, grad_expert_g)[None]
    expert_up_grad = product_over_groups(incoming, grad_expert_u)[None]
    shared_down_grad = to_row_owner(product_over_groups(shared_columns(shared_hidden), all_out_grad))
    side_shared = product_over_groups(
        ffn_in,
        jnp.concatenate([shared_columns(grad_shared_g), shared_columns(grad_shared_u)], axis=1),
    ).astype(BF16)

    router_own = lax.dynamic_index_in_dim(router_all, e, 0, keepdims=False)[:, :n]
    grad_probs = dot_sum[:, :n]
    grad_logits = (
        router_own * (grad_probs - jnp.sum(router_own * grad_probs, axis=-1, keepdims=True))
    ).astype(BF16)
    grad_ffn_in = ffn_sum + product("te,de->td", grad_logits, router_w)
    grad_ffn_gain = jnp.sum(grad_ffn_in * mid_unit, axis=0)
    grad_mid = output_grad.astype(F32) + norm_back(grad_ffn_in * ffn_gain, mid_unit, mid_scale)
    grad_mid_b = grad_mid.astype(BF16)
    mid_left, mid_right = grad_mid_b[:, : D // 2], grad_mid_b[:, D // 2 :]
    grad_attended = (
        product("td,ad->ta", jnp.where(even, mid_left, mid_right), out_w_mine)
        + product("td,ad->ta", jnp.where(even, mid_right, mid_left), out_w_other)
    ).astype(BF16)
    output_w_partial = product_over_groups(attended, grad_mid_b).astype(BF16)
    output_w_partial, grad_attended = lax.optimization_barrier((output_w_partial, grad_attended))
    (grad_att_blocks,) = exchange(
        5, swaps=(grad_attended.reshape(tokens, HEADS, VH).transpose(1, 0, 2),)
    )
    output_w_partial, grad_att_blocks = lax.optimization_barrier(
        (output_w_partial, grad_att_blocks)
    )
    grad_att = grad_att_blocks.reshape(length, VH)
    output_weight_grad = sum_async(output_w_partial.reshape(n, rows_out, D))
    grad_router = product("te,td->ed", grad_logits, own_ffn_in)

    delta = jnp.sum(grad_att.astype(F32) * attended_exact, axis=-1)[None]
    grad_query_raw, grad_keys, grad_values = attend_back(
        prefix_length, query, grad_att, lse, delta, keys, values
    )
    (
        grad_query,
        grad_expanded,
        latent_partial,
        rope_partial,
        normed_partial,
        gain_partial,
    ) = back(
        first_all, cos_table, sin_table, grad_query_raw, grad_keys, grad_values, turned, expand_t
    )
    latent_sum, rope_sum = exchange(
        6,
        sums=(
            latent_partial.reshape(n, tokens, LATENT),
            rope_partial.reshape(n, tokens, 2 * ROPE),
        ),
    )
    side_query = product_over_groups(normed, grad_query)[:, : query_t.shape[0]].astype(BF16)
    grad_expand = product_over_groups(latent, grad_expanded).astype(BF16)

    own_normed = (input_unit * attn_gain).astype(BF16)
    own_raw = product("td,dc->tc", own_normed, latent_w[:, :LATENT])
    latent_scale = rms_scale(own_raw)
    latent_unit = own_raw * latent_scale
    grad_latent_gain = jnp.sum(latent_sum * latent_unit, axis=0)
    grad_compressed = jnp.concatenate(
        [
            norm_back(latent_sum * lat_gain, latent_unit, latent_scale),
            unrotate(
                rope_sum[:, :ROPE],
                own(cos_table)[:, : ROPE // 2],
                own(sin_table)[:, ROPE // 2 : ROPE],
            ),
        ],
        axis=-1,
    ).astype(BF16)
    latent_w_partial = product_over_groups(
        own_normed, jnp.pad(grad_compressed, ((0, 0), (0, 640 - LATENT - ROPE)))
    ).astype(BF16)
    own_part = product("tc,dc->td", grad_compressed, latent_w)
    grad_attn_gain = gain_partial[0] + jnp.sum(own_part * input_unit, axis=0)

    def by_owner(values, rows):
        blocks = values.reshape(-1, groups, n, rows).transpose(2, 1, 0, 3)
        return blocks.reshape(n, groups, -1)

    small = jnp.concatenate(
        [
            by_owner(grad_attn_gain, rows_out),
            by_owner(grad_ffn_gain, rows_out),
            by_owner(grad_router, rows_out),
            by_owner(grad_latent_gain, expand_rows),
        ],
        axis=2,
    )
    small = small.transpose(1, 0, 2)
    if groups == 2:
        g = lax.axis_index("grp")
        mine = lax.dynamic_index_in_dim(small, g, 0, keepdims=False)
        theirs = lax.dynamic_index_in_dim(small, 1 - g, 0, keepdims=False)
        small = mine + lax.ppermute(theirs, "grp", [(0, 1), (1, 0)])
    else:
        small = lax.psum_scatter(small, "grp", scatter_dimension=0)
    (
        normed_sum,
        latent_weight_sum,
        small_all,
        query_weight_grad,
        shared_gate_grad,
        shared_up_grad,
        expand_weight_grad,
    ) = exchange(
        7,
        sums=(normed_partial.reshape(n, tokens, D), latent_w_partial.reshape(n, rows_out, -1)),
        swaps=(
            small[:, None],
            side_query.reshape(n, rows_out, -1),
            side_shared[:, :shared_width].reshape(n, rows_out, -1),
            side_shared[:, shared_width:].reshape(n, rows_out, -1),
            grad_expand.reshape(n, expand_rows, -1),
        ),
        laid=4,
    )
    grad_normed = normed_sum + own_part
    input_grad = (
        grad_mid + norm_back(grad_normed * attn_gain, input_unit, input_scale)
    ).astype(BF16)
    latent_weight_grad = latent_weight_sum[:, : LATENT + ROPE]
    small_sum = jnp.sum(small_all[:, 0], axis=0)
    attention_gain_grad = small_sum[:rows_out]
    feedforward_gain_grad = small_sum[rows_out : 2 * rows_out]
    router_weight_grad = small_sum[2 * rows_out : (2 + n) * rows_out].reshape(n, rows_out).T
    latent_gain_grad = small_sum[(2 + n) * rows_out :]
    return (
        layer_output,
        input_grad,
        attention_gain_grad,
        query_weight_grad,
        latent_weight_grad,
        latent_gain_grad,
        expand_weight_grad,
        output_weight_grad,
        feedforward_gain_grad,
        router_weight_grad,
        shared_gate_grad,
        shared_up_grad,
        shared_down_grad,
        expert_gate_grad,
        expert_up_grad,
        expert_down_grad,
    )


def solution(mesh):
    return jax.shard_map(
        per_device,
        mesh=mesh,
        in_specs=(
            P(("grp", "ep"), None),
            P("ep"),
            P("ep", None),
            P("ep", None),
            P("ep"),
            P("ep", None),
            P("ep", None),
            P("ep"),
            P("ep", None),
            P("ep", None),
            P("ep", None),
            P("ep", None),
            P("ep", None, None),
            P("ep", None, None),
            P("ep", None, None),
            P(("grp", "ep"), None),
            P("grp"),
            P(("grp", "ep"), None),
        ),
        out_specs=(
            P(("grp", "ep"), None),
            P(("grp", "ep"), None),
            P(("grp", "ep")),
            P(("grp", "ep"), None),
            P(("grp", "ep"), None),
            P(("grp", "ep")),
            P(("grp", "ep"), None),
            P(("grp", "ep"), None),
            P(("grp", "ep")),
            P(("grp", "ep"), None),
            P(("grp", "ep"), None),
            P(("grp", "ep"), None),
            P(("grp", "ep"), None),
            P("ep", "grp", None),
            P("ep", "grp", None),
            P("ep", "grp", None),
        ),
        check_vma=False,
    )
```

```python
import functools
import math

import jax
import jax.numpy as jnp
from jax import lax
from jax.experimental import pallas as pl
from jax.experimental.pallas import tpu as pltpu
from jax.sharding import PartitionSpec as P

D = 2048
HEADS = 16
NOPE = 128
ROPE = 64
VH = 128
LATENT = 512
TOPK = 6

EPSILON = 1e-06
MASKED = -1e30

MESH = pl.DeviceIdType.MESH
ANY = pl.BlockSpec(memory_space=pl.ANY)
DMA = pltpu.SemaphoreType.DMA
F32 = jnp.float32
BF16 = jnp.bfloat16


def remote(src, dst, send, recv, peer):
    return pltpu.make_async_remote_copy(
        src_ref=src,
        dst_ref=dst,
        send_sem=send,
        recv_sem=recv,
        device_id={"ep": peer},
        device_id_type=MESH,
    )


def greet(peers):
    barrier = pltpu.get_barrier_semaphore()
    for peer in peers:
        pl.semaphore_signal(barrier, inc=1, device_id={"ep": peer}, device_id_type=MESH)
    pl.semaphore_wait(barrier, len(peers))


def around(n):
    me = lax.axis_index("ep")
    x, y = me % 2, (me // 2) % 2
    return me, me // 4, y, x, me + 1 - 2 * x, me + 2 - 4 * y


def near(z, nz, below, above):
    for s in range(nz - 1):
        pl.when(z - 1 - s >= 0)(functools.partial(below, s, z - 1 - s))
        pl.when(z + 1 + s < nz)(functools.partial(above, s, z + 1 + s))


def greet_near(px, py, up, down, z, nz):
    barrier = pltpu.get_barrier_semaphore()
    for peer, there in ((px, None), (py, None), (up, z + 1 < nz), (down, z > 0)):

        def hello(peer=peer):
            pl.semaphore_signal(barrier, inc=1, device_id={"ep": peer}, device_id_type=MESH)

        hello() if there is None else pl.when(there)(hello)
    on_line = (z + 1 < nz).astype(jnp.int32) + (z > 0).astype(jnp.int32)
    pl.semaphore_wait(barrier, 2 + on_line)


def start_swaps(n, ins, outs, sems):
    own, ss, rs = sems
    me = lax.axis_index("ep")
    sends, copies = [], []
    for j in range(len(ins)):
        local = pltpu.make_async_copy(ins[j].at[me], outs[j].at[me], own.at[j])
        local.start()
        copies.append(local)
    for k in range(1, n):
        to = (me + k) % n
        for j in range(len(ins)):
            c = remote(ins[j].at[to], outs[j].at[me], ss.at[j, k], rs.at[j, k], to)
            c.start()
            sends.append(c)
    return sends, copies


def end_swaps(n, ins, outs, sems, started):
    own, ss, rs = sems
    me = lax.axis_index("ep")
    sends, copies = started
    for k in range(1, n):
        to, back = (me + k) % n, (me + n - k) % n
        for j in range(len(ins)):
            remote(ins[j].at[back], outs[j].at[back], ss.at[j, k], rs.at[j, k], to).wait_recv()
    for copy in sends:
        copy.wait_send()
    for copy in copies:
        copy.wait()


def gather_kernel(n, w, x_ref, *refs):
    swaps_in, o_ref, swaps_out = refs[:w], refs[w], refs[w + 1 : 2 * w + 1]
    own, us, ur, ds, dr, xs, xr, ys, yr, *swap_sems = refs[2 * w + 1 :]
    me, z, y, x, px, py = around(n)
    nz = n // 4
    low = me % 4
    half = x_ref.shape[0] // 2
    top, bottom = pl.ds(0, half), pl.ds(half, half)
    up, down = (me + 4) % n, (me + n - 4) % n
    everyone = [(me + k) % n for k in range(n)]
    if w:
        greet(everyone[1:])
    else:
        greet_near(px, py, up, down, z, nz)
    local = pltpu.make_async_copy(x_ref, o_ref.at[me], own)
    local.start()

    def over_x(src, b, part, i):
        return remote(src.at[part], o_ref.at[b, part], xs.at[i], xr.at[i], px)

    def over_y(src, b, part, i):
        return remote(src.at[part], o_ref.at[b, part], ys.at[i], yr.at[i], py)

    def upward(src, b, s):
        return remote(src, o_ref.at[b], us.at[s], ur.at[s], up)

    def downward(src, b, s):
        return remote(src, o_ref.at[b], ds.at[s], dr.at[s], down)

    def spread(src, t):
        b = t * 4 + low
        over_x(src, b, top, t).start()
        over_y(src, b, bottom, t).start()
        over_y(src, b, top, nz + t).start()
        over_x(src, b, bottom, nz + t).start()

    pl.when(z + 1 < nz)(lambda: upward(x_ref, me, 0).start())
    pl.when(z > 0)(lambda: downward(x_ref, me, 0).start())
    spread(x_ref, z)
    swapping = start_swaps(n, swaps_in, swaps_out, swap_sems) if w else None

    def from_below(s, t):
        b = t * 4 + low
        upward(o_ref.at[b], b, s).wait_recv()
        pl.when(z + 1 < nz)(lambda: upward(o_ref.at[b], b, s + 1).start())
        spread(o_ref.at[b], t)

    def from_above(s, t):
        b = t * 4 + low
        downward(o_ref.at[b], b, s).wait_recv()
        pl.when(z > 0)(lambda: downward(o_ref.at[b], b, s + 1).start())
        spread(o_ref.at[b], t)

    def turn(s, t):
        bx = t * 4 + low + px - me
        by = t * 4 + low + py - me
        over_x(o_ref.at[bx], bx, top, t).wait_recv()
        over_y(o_ref.at[bx], bx, top, 2 * nz + t).start()
        over_y(o_ref.at[by], by, bottom, t).wait_recv()
        over_x(o_ref.at[by], by, bottom, 2 * nz + t).start()

    for s in range(nz - 1):
        pl.when(z - 1 - s >= 0)(functools.partial(from_below, s, z - 1 - s))
        pl.when(z + 1 + s < nz)(functools.partial(from_above, s, z + 1 + s))
        if s == 0:
            turn(0, z)
        else:
            pl.when(z - s >= 0)(functools.partial(turn, s, z - s))
            pl.when(z + s < nz)(functools.partial(turn, s, z + s))
    pl.when(z - (nz - 1) >= 0)(functools.partial(turn, 0, z - (nz - 1)))
    pl.when(z + (nz - 1) < nz)(functools.partial(turn, 0, z + (nz - 1)))

    def finish(s, t):
        bx = t * 4 + low + px - me
        by = t * 4 + low + py - me
        bxy = bx + py - me
        over_y(o_ref.at[by], by, top, nz + t).wait_recv()
        over_x(o_ref.at[bx], bx, bottom, nz + t).wait_recv()
        over_y(o_ref.at[bxy], bxy, top, 2 * nz + t).wait_recv()
        over_x(o_ref.at[bxy], bxy, bottom, 2 * nz + t).wait_recv()
        for i in range(3):
            over_x(x_ref, me, top, i * nz + t).wait_send()
            over_y(x_ref, me, top, i * nz + t).wait_send()

    finish(0, z)
    near(z, nz, finish, finish)

    def sent_up(s, t):
        upward(x_ref, me, s).wait_send()

    def sent_down(s, t):
        downward(x_ref, me, s).wait_send()

    for s in range(nz - 1):
        pl.when((z + 1 < nz) & (z - s >= 0))(functools.partial(sent_up, s, z))
        pl.when((z > 0) & (z + s < nz))(functools.partial(sent_down, s, z))
    local.wait()
    if w:
        end_swaps(n, swaps_in, swaps_out, swap_sems, swapping)


def gather(x, cid, swaps=()):
    n = lax.axis_size("ep")
    w = len(swaps)
    nz = n // 4
    return pl.pallas_call(
        functools.partial(gather_kernel, n, w),
        out_shape=[jax.ShapeDtypeStruct((n,) + x.shape, x.dtype)]
        + [jax.ShapeDtypeStruct(a.shape, a.dtype) for a in swaps],
        in_specs=[ANY] * (1 + w),
        out_specs=[ANY] * (1 + w),
        scratch_shapes=[DMA]
        + [DMA((nz,))] * 4
        + [DMA((3 * nz,))] * 4
        + ([DMA((w,)), DMA((w, n)), DMA((w, n))] if w else []),
        compiler_params=pltpu.CompilerParams(collective_id=cid, has_side_effects=True),
        name="gather",
    )(x, *swaps)


def add_rows(dst, left, right, rows):
    step = 16

    def body(i, carry):
        r = pl.ds(pl.multiple_of(i * step, step), step)
        dst[r] = (left[r].astype(F32) + right[r].astype(F32)).astype(dst.dtype)
        return carry

    lax.fori_loop(0, rows // step, body, 0)


TILE = 128


def exchange_kernel(n, m, w, laid, jobs, *refs):
    refs = list(refs)

    def take(count):
        out = refs[:count]
        del refs[:count]
        return out

    sums_in, swaps_in = take(m), take(w)
    jobs_in = [take(2) for _ in range(jobs)]
    sums_out, swaps_out, jobs_out = take(m), take(w), take(jobs)
    room = [take(7) for _ in range(m)]
    sems = [take(8) for _ in range(m)]
    swap_sems = take(3) if w else None
    side_by_side = swaps_out[w - laid :]
    swaps_out = swaps_out[: w - laid] + take(laid)
    desks = [take(5) for _ in range(jobs)]
    me, z, y, x, px, py = around(n)
    nz = n // 4
    low = me % 4
    to = [(z + k) % nz for k in range(nz)]
    at = [t * 4 + low for t in to]
    if w:
        greet([(me + k) % n for k in range(1, n)])
    else:
        greet([px, py] + at[1:])
    order = [2, 1, 3, 0] if nz == 4 else list(range(1, nz)) + [0]
    sends = []

    def halves(j):
        half = sums_in[j].shape[3] // 2
        return half, pl.ds(0, half), pl.ds(half, half)

    first, second, third = {}, {}, {}

    def stage_one(j, k):
        p = sums_in[j]
        half, top, bottom = halves(j)
        la, lb, a1, b1, a2, b2, zb = room[j]
        lsa, lsb, xs, xr, ys, yr, zs, zr = sems[j]
        t = to[k]
        c = remote(p.at[t, 1 - y, :, top], a1.at[k], ys.at[k], yr.at[k], py)
        d = remote(p.at[t, :, 1 - x, bottom], b1.at[k], xs.at[k], xr.at[k], px)
        c.start()
        d.start()
        e = pltpu.make_async_copy(p.at[t, y, :, top], la.at[k], lsa.at[k])
        f = pltpu.make_async_copy(p.at[t, :, x, bottom], lb.at[k], lsb.at[k])
        e.start()
        f.start()
        first[j, k] = (c, d, e, f)
        sends.extend([c, d])

    def stage_two(j, k):
        half, top, bottom = halves(j)
        la, lb, a1, b1, a2, b2, zb = room[j]
        lsa, lsb, xs, xr, ys, yr, zs, zr = sems[j]
        c, d, e, f = first[j, k]
        e.wait()
        c.wait_recv()
        for i in range(2):
            add_rows(la.at[k, i], la.at[k, i], a1.at[k, i], half)
        g = remote(la.at[k, 1 - x], a2.at[k], xs.at[nz + k], xr.at[nz + k], px)
        g.start()
        f.wait()
        d.wait_recv()
        for i in range(2):
            add_rows(lb.at[k, i], lb.at[k, i], b1.at[k, i], half)
        h = remote(lb.at[k, 1 - y], b2.at[k], ys.at[nz + k], yr.at[nz + k], py)
        h.start()
        second[j, k] = (g, h)
        sends.extend([g, h])

    def stage_three(j, k):
        half, top, bottom = halves(j)
        la, lb, a1, b1, a2, b2, zb = room[j]
        lsa, lsb, xs, xr, ys, yr, zs, zr = sems[j]
        g, h = second[j, k]
        g.wait_recv()
        add_rows(a2.at[k], la.at[k, x], a2.at[k], half)
        if k:
            c = remote(a2.at[k], zb.at[k, top], zs.at[k], zr.at[k], at[k])
            c.start()
        h.wait_recv()
        add_rows(b2.at[k], lb.at[k, y], b2.at[k], half)
        if k:
            d = remote(b2.at[k], zb.at[k, bottom], zs.at[nz + k], zr.at[nz + k], at[k])
            d.start()
            third[j, k] = (c, d)
            sends.extend([c, d])

    loads = []
    for (left, right), (left_v, right_v, page, in_sem, out_sem) in zip(jobs_in, desks):
        for i, (src, dst) in enumerate(((left, left_v), (right, right_v))):
            loads.append(pltpu.make_async_copy(src, dst, in_sem.at[i]))

    def tile(j, i):
        left_v, right_v, page, in_sem, out_sem = desks[j]
        slot = i % 2
        write = pltpu.make_async_copy(
            page.at[slot],
            jobs_out[j].at[pl.ds(pl.multiple_of(i * TILE, TILE), TILE)],
            out_sem.at[slot],
        )
        value = lax.dot_general(
            left_v[:, pl.ds(pl.multiple_of(i * TILE, TILE), TILE)],
            right_v[...],
            (((0,), (0,)), ((), ())),
            preferred_element_type=F32,
        )
        pl.when(i >= 2)(write.wait)
        page[slot] = value.astype(page.dtype)
        write.start()

    tiles = [desk[0].shape[1] // TILE for desk in desks]
    loaded = []

    def work(step, of):
        first, last = sum(tiles) * step // of, sum(tiles) * (step + 1) // of
        for j in range(jobs):
            start = sum(tiles[:j])
            low, high = max(first - start, 0), min(last - start, tiles[j])
            if low >= high:
                continue
            if j not in loaded:
                loaded.append(j)
                loads[2 * j].wait()
                loads[2 * j + 1].wait()
            lax.fori_loop(low, high, lambda i, c, j=j: (tile(j, i), c)[1], 0)

    steps = [(j, k) for j in range(m) for k in order]
    ahead = 3 if jobs else 2
    for i in range(min(ahead, len(steps))):
        stage_one(*steps[i])
    for copy in loads:
        copy.start()
    if w:
        swapping = start_swaps(n, swaps_in, swaps_out, swap_sems)
    for i, step in enumerate(steps):
        stage_two(*step)
        if i + ahead < len(steps):
            stage_one(*steps[i + ahead])
        if i:
            stage_three(*steps[i - 1])
        work(i, len(steps))
    if steps:
        stage_three(*steps[-1])
    if w:
        end_swaps(n, swaps_in, swaps_out, swap_sems, swapping)
        for wide, got in zip(side_by_side, swaps_out[w - laid :]):
            width = got.shape[2]
            for k in range(n):
                wide[:, k * width : (k + 1) * width] = got[k].astype(F32)
    for j in range(m):
        half, top, bottom = halves(j)
        la, lb, a1, b1, a2, b2, zb = room[j]
        o_ref = sums_out[j]
        for k in range(1, nz):
            c, d = third[j, k]
            c.wait_recv()
            d.wait_recv()
        for part, offset in ((a2, 0), (b2, half)):

            def body(i, carry, part=part, offset=offset, zb=zb, o_ref=o_ref):
                r = pl.ds(pl.multiple_of(i * 16, 16), 16)
                q = pl.ds(pl.multiple_of(i * 16 + offset, 16), 16)
                total = part[0, r].astype(F32)
                for k in range(1, nz):
                    total = total + zb[k, q].astype(F32)
                o_ref[q] = total.astype(o_ref.dtype)
                return carry

            lax.fori_loop(0, half // 16, body, 0)
    for copy in sends:
        copy.wait_send()
    for j in range(jobs):
        left_v, right_v, page, in_sem, out_sem = desks[j]
        for slot in range(2):
            rows = jobs_out[j].at[pl.ds(0, TILE)]
            pltpu.make_async_copy(page.at[slot], rows, out_sem.at[slot]).wait()


def exchange(cid, sums=(), swaps=(), laid=0, jobs=()):
    n = lax.axis_size("ep")
    nz = n // 4
    m, w = len(sums), len(swaps)
    kept_rows = [p.shape[1] for p in sums]
    sums = [jnp.pad(p, ((0, 0), (0, -p.shape[1] % 32), (0, 0))) for p in sums]
    views = [p.reshape((nz, 2, 2) + p.shape[1:]) for p in sums]
    scratch = []
    for p in sums:
        rows, cols = p.shape[1:]
        half = rows // 2
        scratch += [pltpu.VMEM((nz, 2, half, cols), p.dtype)] * 4
        scratch += [pltpu.VMEM((nz, half, cols), p.dtype)] * 2
        scratch += [pltpu.VMEM((nz, rows, cols), p.dtype)]
    for p in sums:
        scratch += [DMA((nz,))] * 2 + [DMA((2 * nz,))] * 6
    if w:
        scratch += [DMA((w,)), DMA((w, n)), DMA((w, n))]
    plain, wide = swaps[: w - laid], swaps[w - laid :]
    scratch += [pltpu.VMEM(a.shape, a.dtype) for a in wide]
    for left, right in jobs:
        scratch += [pltpu.VMEM(left.shape, left.dtype), pltpu.VMEM(right.shape, right.dtype)]
        scratch += [pltpu.VMEM((2, TILE, right.shape[1]), BF16), DMA((2,)), DMA((2,))]
    out = pl.pallas_call(
        functools.partial(exchange_kernel, n, m, w, laid, len(jobs)),
        out_shape=[jax.ShapeDtypeStruct(p.shape[1:], F32) for p in sums]
        + [jax.ShapeDtypeStruct(a.shape, a.dtype) for a in plain]
        + [jax.ShapeDtypeStruct((a.shape[1], n * a.shape[2]), F32) for a in wide]
        + [jax.ShapeDtypeStruct((a.shape[1], b.shape[1]), BF16) for a, b in jobs],
        in_specs=[ANY] * (m + w + 2 * len(jobs)),
        out_specs=[pl.BlockSpec(memory_space=pltpu.VMEM)] * m
        + [ANY] * (w - laid)
        + [pl.BlockSpec(memory_space=pltpu.VMEM)] * laid
        + [ANY] * len(jobs),
        scratch_shapes=scratch,
        compiler_params=pltpu.CompilerParams(
            collective_id=cid, has_side_effects=True, vmem_limit_bytes=(60 if jobs else 40) << 20 if m else None
        ),
        name="exchange",
    )(*views, *swaps, *(a for job in jobs for a in job))
    return [a[:rows] for a, rows in zip(out, kept_rows)] + list(out[m:])


def both(p):
    g = lax.axis_index("grp")
    mine = lax.dynamic_index_in_dim(p, g, 0, keepdims=False)
    theirs = lax.dynamic_index_in_dim(p, 1 - g, 0, keepdims=False)
    return mine, lax.ppermute(theirs.astype(BF16), "grp", [(0, 1), (1, 0)])


def over_groups(p):
    if lax.axis_size("grp") == 2:
        mine, other = both(p)
        return mine.astype(F32) + other.astype(F32)
    return lax.psum_scatter(p.astype(BF16), "grp", scatter_dimension=0, tiled=False).astype(F32)


def product_over_groups(left, right):
    groups = lax.axis_size("grp")
    rows = left.shape[1] // groups
    if groups != 2:
        whole = product("km,kn->mn", left, right)
        return over_groups(whole.reshape(groups, rows, -1))
    g = lax.axis_index("grp")
    mine = lax.dynamic_slice_in_dim(left, g * rows, rows, 1)
    theirs = lax.dynamic_slice_in_dim(left, (1 - g) * rows, rows, 1)
    sent = product("km,kn->mn", theirs, right).astype(BF16)
    other = lax.ppermute(sent, "grp", [(0, 1), (1, 0)])
    return product("km,kn->mn", mine, right) + other.astype(F32)


def from_partner(values):
    groups = lax.axis_size("grp")
    return lax.ppermute(values, "grp", [(g, g + 1 - 2 * (g % 2)) for g in range(groups)])


def to_row_owner(block):
    groups, n = lax.axis_size("grp"), lax.axis_size("ep")
    pairs = [(h * n + e, e * groups + h) for h in range(groups) for e in range(n)]
    return lax.ppermute(block.astype(BF16), ("grp", "ep"), pairs).astype(F32)


def dot(left, right):
    return jnp.dot(left, right, preferred_element_type=F32)


def dot_nt(left, right):
    return lax.dot_general(left, right, (((1,), (1,)), ((), ())), preferred_element_type=F32)


def front_kernel(
    x_ref, cos_ref, sin_ref, gain_ref, lat_gain_ref, wq_ref, wl_ref, we_ref,
    normed_ref, query_ref, keys_ref, values_ref, latent_ref,
):
    blocks, tokens = x_ref.shape[:2]
    rows = blocks * tokens
    width = gain_ref.shape[1]
    x = x_ref[:, :, :width].reshape(rows, width).astype(F32)
    normed = (x * rms_scale(x) * gain_ref[...]).astype(BF16)
    normed_ref[...] = normed
    cos, sin = cos_ref[...], sin_ref[...]
    own_half = lax.broadcasted_iota(jnp.int32, cos.shape, 1) < ROPE

    def turn(pair):
        return pair * cos + pltpu.roll(pair, ROPE, 1) * sin

    query = dot_nt(normed, wq_ref[...])
    query_ref[:, :NOPE] = query[:, :NOPE].astype(BF16)
    query_ref[:, NOPE:] = jnp.where(own_half, turn(query[:, NOPE:]), 0.0).astype(BF16)
    compressed = dot(normed, wl_ref[...])
    raw = compressed[:, :LATENT]
    latent = (raw * rms_scale(raw) * lat_gain_ref[...]).astype(BF16)
    latent_ref[...] = latent
    expanded = dot_nt(latent, we_ref[...])
    keys_ref[:, :NOPE] = expanded[:, :NOPE].astype(BF16)
    keys_ref[:, NOPE:] = turn(compressed[:, LATENT:]).astype(BF16)
    values_ref[...] = expanded[:, NOPE:].astype(BF16)


def front(x, cos, sin, gain, lat_gain, wq, wl, we):
    n, tokens, width = x.shape
    length = n * tokens
    blocks = 2
    rows = blocks * tokens

    def whole(a):
        return pl.BlockSpec(a.shape, lambda i: (0,) * a.ndim, pipeline_mode=pl.Buffered(1))

    def rows_of(cols):
        return pl.BlockSpec((rows, cols), lambda i: (i, 0))

    def out(cols):
        return jax.ShapeDtypeStruct((length, cols), BF16)

    cols = (gain.shape[1], wq.shape[0], NOPE + 2 * ROPE, VH, LATENT)
    return pl.pallas_call(
        front_kernel,
        grid=(n // blocks,),
        in_specs=[
            pl.BlockSpec((blocks, tokens, width), lambda i: (i, 0, 0)),
            rows_of(2 * ROPE),
            rows_of(2 * ROPE),
        ]
        + [whole(a) for a in (gain, lat_gain, wq, wl, we)],
        out_specs=[rows_of(c) for c in cols],
        out_shape=[out(c) for c in cols],
        compiler_params=pltpu.CompilerParams(vmem_limit_bytes=48 << 20),
        name="front",
    )(x, cos, sin, gain, lat_gain, wq, wl, we)


def back_kernel(
    x_ref, cos_ref, sin_ref, dq_ref, dk_ref, dv_ref, wq_ref, we_ref,
    query_ref, expanded_ref, latent_ref, rope_ref, normed_ref, gain_ref,
):
    blocks, tokens = x_ref.shape[:2]
    rows = blocks * tokens
    width = gain_ref.shape[1]
    own_half = lax.broadcasted_iota(jnp.int32, cos_ref.shape, 1) < ROPE
    pair = dq_ref[:, NOPE:] * jnp.where(own_half, cos_ref[...], sin_ref[...])
    pair = jnp.where(own_half, pair + pltpu.roll(pair, ROPE, 1), 0.0)
    query_ref[:, :NOPE] = dq_ref[:, :NOPE].astype(BF16)
    query_ref[:, NOPE:] = pair.astype(BF16)
    part = dot(query_ref[...], wq_ref[...])
    normed_ref[...] = part.astype(BF16)
    x = x_ref[:, :, :width].reshape(rows, width).astype(F32)
    gain = jnp.sum(part * (x * rms_scale(x)), axis=0, keepdims=True)

    @pl.when(pl.program_id(0) == 0)
    def _():
        gain_ref[...] = gain

    @pl.when(pl.program_id(0) > 0)
    def _():
        gain_ref[...] += gain

    expanded_ref[:, :NOPE] = dk_ref[:, :NOPE].astype(BF16)
    expanded_ref[:, NOPE:] = dv_ref[...].astype(BF16)
    latent_ref[...] = dot(expanded_ref[...], we_ref[...]).astype(BF16)
    rope_ref[...] = dk_ref[:, NOPE:].astype(BF16)


def back(x, cos, sin, dq, dk, dv, wq, we):
    n, tokens, width = x.shape
    length = n * tokens
    blocks = 2
    rows = blocks * tokens
    model = wq.shape[1]

    def whole(a):
        return pl.BlockSpec(a.shape, lambda i: (0,) * a.ndim, pipeline_mode=pl.Buffered(1))

    def rows_of(cols):
        return pl.BlockSpec((rows, cols), lambda i: (i, 0))

    def out(cols):
        return jax.ShapeDtypeStruct((length, cols), BF16)

    cols = (NOPE + 2 * ROPE, NOPE + VH, LATENT, 2 * ROPE, model)
    return pl.pallas_call(
        back_kernel,
        grid=(n // blocks,),
        in_specs=[
            pl.BlockSpec((blocks, tokens, width), lambda i: (i, 0, 0)),
            rows_of(2 * ROPE),
            rows_of(2 * ROPE),
            rows_of(dq.shape[1]),
            rows_of(dk.shape[1]),
            rows_of(dv.shape[1]),
            whole(wq),
            whole(we),
        ],
        out_specs=[rows_of(c) for c in cols] + [pl.BlockSpec((1, model), lambda i: (0, 0))],
        out_shape=[out(c) for c in cols] + [jax.ShapeDtypeStruct((1, model), F32)],
        compiler_params=pltpu.CompilerParams(vmem_limit_bytes=48 << 20),
        name="back",
    )(x, cos, sin, dq, dk, dv, wq, we)


KEYS = 512


def scores_of(scale, prefix, k, q, first_key, first_query):
    scores = dot_nt(k, q) * scale
    key = first_key + lax.broadcasted_iota(jnp.int32, scores.shape, 0)
    query = first_query + lax.broadcasted_iota(jnp.int32, scores.shape, 1)
    return jnp.where((key <= query) | (key < prefix), scores, MASKED)


def key_blocks(prefix, last_query):
    return (jnp.maximum(last_query, prefix) + KEYS - 1) // KEYS


def attend_kernel(scale, prefix_ref, q_ref, k_ref, v_ref, attended_ref, exact_ref, lse_ref):
    q = q_ref[...]
    rows = q.shape[0]
    start = pl.program_id(0) * rows
    prefix = prefix_ref[0]

    def step(j, carry):
        top, total, out = carry
        s = scores_of(scale, prefix, k_ref[j], q, j * KEYS, start)
        new_top = jnp.maximum(top, jnp.max(s, axis=0, keepdims=True))
        p = jnp.exp(s - new_top)
        shrink = jnp.exp(top - new_top)
        total = total * shrink + jnp.sum(p, axis=0, keepdims=True)
        return new_top, total, out * shrink + dot(v_ref[j], p.astype(BF16))

    top, total, out = lax.fori_loop(
        0,
        key_blocks(prefix, start + rows),
        step,
        (
            jnp.full((1, rows), MASKED, F32),
            jnp.zeros((1, rows), F32),
            jnp.zeros((v_ref.shape[1], rows), F32),
        ),
    )
    lse_ref[...] = top + jnp.log(total)
    exact = (out / total).T
    exact_ref[...] = exact
    attended_ref[...] = exact.astype(BF16)


def attend(prefix, q, k, v):
    length, depth = q.shape
    values = v.shape[1]
    rows = 256
    v = v.reshape(length // KEYS, KEYS, values).transpose(0, 2, 1)
    k = k.reshape(length // KEYS, KEYS, depth)
    return pl.pallas_call(
        functools.partial(attend_kernel, 1.0 / math.sqrt(NOPE + ROPE)),
        grid=(length // rows,),
        in_specs=[
            pl.BlockSpec(memory_space=pltpu.SMEM),
            pl.BlockSpec((rows, depth), lambda i: (i, 0)),
            pl.BlockSpec(k.shape, lambda i: (0, 0, 0)),
            pl.BlockSpec(v.shape, lambda i: (0, 0, 0)),
        ],
        out_specs=[
            pl.BlockSpec((rows, values), lambda i: (i, 0)),
            pl.BlockSpec((rows, values), lambda i: (i, 0)),
            pl.BlockSpec((1, rows), lambda i: (0, i)),
        ],
        out_shape=[
            jax.ShapeDtypeStruct((length, values), BF16),
            jax.ShapeDtypeStruct((length, values), F32),
            jax.ShapeDtypeStruct((1, length), F32),
        ],
        compiler_params=pltpu.CompilerParams(vmem_limit_bytes=32 << 20),
        name="attend",
    )(prefix, q, k, v)


def attend_back_kernel(
    scale, prefix_ref, q_ref, g_ref, lse_ref, delta_ref, k_ref, v_ref, dq_ref, dk_ref, dv_ref
):
    q, g = q_ref[...], g_ref[...]
    rows = q.shape[0]
    start = pl.program_id(0) * rows
    prefix = prefix_ref[0]

    @pl.when(pl.program_id(0) == 0)
    def _():
        dk_ref[...] = jnp.zeros_like(dk_ref)
        dv_ref[...] = jnp.zeros_like(dv_ref)

    def step(j, dq):
        k = k_ref[j]
        p = jnp.exp(scores_of(scale, prefix, k, q, j * KEYS, start) - lse_ref[...])
        ds = (p * (dot_nt(v_ref[j], g) - delta_ref[...]) * scale).astype(BF16)
        dv_ref[j] += dot(p.astype(BF16), g)
        dk_ref[j] += dot(ds, q)
        return dq + lax.dot_general(
            ds, k, (((0,), (0,)), ((), ())), preferred_element_type=F32
        )

    dq_ref[...] = lax.fori_loop(
        0, key_blocks(prefix, start + rows), step, jnp.zeros(dq_ref.shape, F32)
    )


def attend_back(prefix, q, g, lse, delta, k, v):
    length, depth = q.shape
    values = v.shape[1]
    rows = 256
    k = k.reshape(length // KEYS, KEYS, depth)
    v = v.reshape(length // KEYS, KEYS, values)
    dq, dk, dv = pl.pallas_call(
        functools.partial(attend_back_kernel, 1.0 / math.sqrt(NOPE + ROPE)),
        grid=(length // rows,),
        in_specs=[
            pl.BlockSpec(memory_space=pltpu.SMEM),
            pl.BlockSpec((rows, depth), lambda i: (i, 0)),
            pl.BlockSpec((rows, values), lambda i: (i, 0)),
            pl.BlockSpec((1, rows), lambda i: (0, i)),
            pl.BlockSpec((1, rows), lambda i: (0, i)),
            pl.BlockSpec(k.shape, lambda i: (0, 0, 0)),
            pl.BlockSpec(v.shape, lambda i: (0, 0, 0)),
        ],
        out_specs=[
            pl.BlockSpec((rows, depth), lambda i: (i, 0)),
            pl.BlockSpec(k.shape, lambda i: (0, 0, 0)),
            pl.BlockSpec(v.shape, lambda i: (0, 0, 0)),
        ],
        out_shape=[
            jax.ShapeDtypeStruct((length, depth), F32),
            jax.ShapeDtypeStruct(k.shape, F32),
            jax.ShapeDtypeStruct(v.shape, F32),
        ],
        compiler_params=pltpu.CompilerParams(vmem_limit_bytes=40 << 20),
        name="attend_back",
    )(prefix, q, g, lse, delta, k, v)
    return dq, dk.reshape(length, depth), dv.reshape(length, values)


def ffn_kernel(
    n,
    x_ref,
    y_ref,
    slots_ref,
    tokens_ref,
    own_ref,
    router_ref,
    sg_ref,
    su_ref,
    sd_ref,
    eg_ref,
    eu_ref,
    ed_ref,
    out_ref,
    ffn_ref,
    dot_ref,
    probs_ref,
    rows_ref,
    hidden_ref,
    slot_grad_ref,
    grad_gu_ref,
    shared_h_ref,
    shared_dg_ref,
    shared_du_ref,
    expert_out,
    row_grad,
):
    blocks, tokens = x_ref.shape[:2]
    capacity = slots_ref.shape[1]
    own = own_ref[...]
    lanes = lax.broadcasted_iota(jnp.int32, (tokens, own.shape[1]), 1)
    gates = []
    for b in range(blocks):
        x, y = x_ref[b], y_ref[b]
        logits = jnp.where(lanes < n, dot(x, router_ref[...]), MASKED)
        raised = jnp.exp(logits - jnp.max(logits, axis=-1, keepdims=True))
        probs = raised / jnp.sum(raised, axis=-1, keepdims=True)
        probs_ref[b] = probs
        gate = jnp.sum(probs * own, axis=-1, keepdims=True)
        gates.append(gate)
        part = pl.ds(b * capacity, capacity)
        rows_ref[part] = dot(slots_ref[b], x).astype(BF16)
        weighted = (gate * y.astype(F32)).astype(BF16)
        slot_grad_ref[part] = dot(slots_ref[b], weighted).astype(BF16)
    rows = rows_ref[...]
    slot_grad = slot_grad_ref[...]
    g = dot(rows, eg_ref[...])
    u = dot(rows, eu_ref[...])
    sigmoid = 1.0 / (1.0 + jnp.exp(-g))
    silu = g * sigmoid
    hidden = (silu * u).astype(BF16)
    hidden_ref[...] = hidden
    expert_out[...] = dot(hidden, ed_ref[...]).astype(BF16)
    grad_hidden = dot_nt(slot_grad, ed_ref[...])
    grad_g = (grad_hidden * u * sigmoid * (1.0 + g * (1.0 - sigmoid))).astype(BF16)
    grad_u = (grad_hidden * silu).astype(BF16)
    grad_gu_ref[:, : grad_g.shape[1]] = grad_g
    grad_gu_ref[:, grad_g.shape[1] :] = grad_u
    row_grad[...] = (dot_nt(grad_g, eg_ref[...]) + dot_nt(grad_u, eu_ref[...])).astype(BF16)
    x = x_ref[...].reshape(blocks * tokens, -1)
    y = y_ref[...].reshape(blocks * tokens, -1)
    g = dot_nt(x, sg_ref[...])
    u = dot_nt(x, su_ref[...])
    grad_hidden = dot_nt(y, sd_ref[...])
    sigmoid = 1.0 / (1.0 + jnp.exp(-g))
    silu = g * sigmoid
    hidden = (silu * u).astype(BF16)
    grad_g = (grad_hidden * u * sigmoid * (1.0 + g * (1.0 - sigmoid))).astype(BF16)
    grad_u = (grad_hidden * silu).astype(BF16)
    for ref, value in ((shared_h_ref, hidden), (shared_dg_ref, grad_g), (shared_du_ref, grad_u)):
        ref[...] = value.reshape(blocks, tokens, -1)
    width = x.shape[1]
    chunk = width // 4
    met = [0.0] * blocks
    for c in range(width // chunk):
        cols = pl.ds(c * chunk, chunk)
        shared_out = dot(hidden, sd_ref[:, cols])
        shared_ffn = dot(grad_g, sg_ref[:, cols]) + dot(grad_u, su_ref[:, cols])
        for b in range(blocks):
            part = pl.ds(b * capacity, capacity)
            here = slice(b * tokens, (b + 1) * tokens)
            picked = dot(tokens_ref[b], expert_out[part, cols])
            met[b] += jnp.sum(picked * y_ref[b, :, cols].astype(F32), axis=-1, keepdims=True)
            out_ref[b, :, cols] = (shared_out[here] + picked * gates[b]).astype(BF16)
            back = dot(tokens_ref[b], row_grad[part, cols])
            ffn_ref[b, :, cols] = (shared_ffn[here] + back).astype(BF16)
    for b in range(blocks):
        dot_ref[b] = (met[b] * own).astype(BF16)


def ffn(x, y, slots, own_lane, router_w, gate_t, up_t, down, gate_m, up_m, down_m):
    n, tokens, width = x.shape
    capacity = slots.shape[1]
    hidden = gate_m.shape[1]
    shared = gate_t.shape[0]
    group = 4

    def whole(a):
        return pl.BlockSpec(a.shape, lambda i: (0,) * a.ndim, pipeline_mode=pl.Buffered(1))

    def block(*shape):
        return pl.BlockSpec((group,) + shape, lambda i: (i, 0, 0))

    def slot_rows(cols):
        return pl.BlockSpec((group * capacity, cols), lambda i: (i, 0))

    def tokens_of(cols, kind=BF16):
        return jax.ShapeDtypeStruct((n, tokens, cols), kind)

    def slots_of(cols):
        return jax.ShapeDtypeStruct((n * capacity, cols), BF16)

    weights = (own_lane, router_w, gate_t, up_t, down, gate_m, up_m, down_m)
    return pl.pallas_call(
        functools.partial(ffn_kernel, n),
        grid=(n // group,),
        in_specs=[
            block(tokens, width),
            block(tokens, width),
            block(capacity, tokens),
            block(tokens, capacity),
        ]
        + [whole(a) for a in weights],
        out_specs=[
            block(tokens, width),
            block(tokens, width),
            block(tokens, 128),
            block(tokens, 128),
            slot_rows(width),
            slot_rows(hidden),
            slot_rows(width),
            slot_rows(2 * hidden),
            block(tokens, shared),
            block(tokens, shared),
            block(tokens, shared),
        ],
        out_shape=[
            tokens_of(width),
            tokens_of(width),
            tokens_of(128),
            tokens_of(128, F32),
            slots_of(width),
            slots_of(hidden),
            slots_of(width),
            slots_of(2 * hidden),
            tokens_of(shared),
            tokens_of(shared),
            tokens_of(shared),
        ],
        scratch_shapes=[
            pltpu.VMEM((group * capacity, width), BF16),
            pltpu.VMEM((group * capacity, width), BF16),
        ],
        compiler_params=pltpu.CompilerParams(vmem_limit_bytes=60 << 20),
        name="ffn",
    )(x, y, slots, slots.transpose(0, 2, 1), *weights)


def product(form, left, right):
    return jnp.einsum(form, left, right, preferred_element_type=F32)


def rms_scale(values):
    return lax.rsqrt(jnp.mean(values * values, axis=-1, keepdims=True) + EPSILON)


def rotary_tables(tokens, n):
    halfway = ROPE // 2
    inverse = 10000.0 ** (-(jnp.arange(halfway, dtype=F32) * 2.0 / ROPE))
    inverse = jnp.concatenate([inverse] * 4)
    lane = jnp.arange(2 * ROPE)
    sign = jnp.where((lane < halfway) | (lane >= 3 * halfway), -1.0, 1.0)
    base = (jnp.arange(n, dtype=F32) * tokens)[:, None] * inverse
    step = jnp.arange(tokens, dtype=F32)[:, None] * inverse
    base_cos, base_sin = jnp.cos(base)[:, None], jnp.sin(base)[:, None]
    step_cos, step_sin = jnp.cos(step)[None], jnp.sin(step)[None]
    cos_table = base_cos * step_cos - base_sin * step_sin
    sin_table = (base_sin * step_cos + base_cos * step_sin) * sign
    return cos_table.reshape(n * tokens, -1), sin_table.reshape(n * tokens, -1)


def unrotate(grads, cos_table, sin_table):
    halfway = grads.shape[-1] // 2
    first = grads[..., :halfway]
    second = grads[..., halfway:]
    return jnp.concatenate(
        [first * cos_table + second * sin_table, second * cos_table - first * sin_table], axis=-1
    )


def norm_back(grad_unit, unit_values, scale_values):
    return scale_values * (
        grad_unit - unit_values * jnp.mean(grad_unit * unit_values, axis=-1, keepdims=True)
    )


def column_halves(weight, n, half):
    rows, width = weight.shape[0], weight.shape[1] // n
    parts = weight.T.reshape(n, 2, width // 2, rows)
    return lax.dynamic_index_in_dim(parts, half, 1, keepdims=False)


def columns_in(blocks):
    n, width, rows = blocks.shape
    return blocks.transpose(1, 0, 2).reshape(width, n * rows)


def both_halves(mine, other, even):
    return jnp.concatenate([jnp.where(even, mine, other), jnp.where(even, other, mine)], axis=0)


def per_device(
    layer_input,
    attention_gain,
    query_weight,
    latent_weight,
    latent_gain,
    expand_weight,
    output_weight,
    feedforward_gain,
    router_weight,
    shared_gate,
    shared_up,
    shared_down,
    expert_gate,
    expert_up,
    expert_down,
    expert_routes,
    prefix_length,
    output_grad,
):
    n = lax.axis_size("ep")
    groups = lax.axis_size("grp")
    e = lax.axis_index("ep")
    half = lax.axis_index("grp") % 2
    even = half == 0
    tokens = layer_input.shape[0]
    length = tokens * n
    capacity = tokens * TOPK * 4 // (3 * n)
    rows_dev = attention_gain.shape[0]
    latent_rows = latent_gain.shape[0]
    rows_out = D // (groups * n)
    expand_rows = LATENT // (groups * n)

    pad = jnp.zeros((rows_dev - latent_rows,), BF16)
    first_block = jnp.concatenate(
        [
            layer_input,
            latent_weight,
            router_weight,
            attention_gain[:, None],
            feedforward_gain[:, None],
            jnp.concatenate([latent_gain, pad])[:, None],
            expert_routes.astype(BF16),
        ],
        axis=1,
    )
    width = first_block.shape[1]
    first_block = jnp.pad(first_block, ((0, 0), (0, -width % 128)))
    shared_half = jnp.where(even, shared_gate, shared_up)
    first_all, q_blocks, x_blocks, shared_blocks = gather(
        first_block,
        0,
        swaps=(
            column_halves(query_weight, n, half),
            column_halves(expand_weight, n, half),
            shared_half.T.reshape(n, shared_half.shape[1] // n, rows_dev),
        ),
    )
    c0 = D
    c1 = c0 + LATENT + ROPE
    c2 = c1 + n
    latent_w = first_all[:, :, c0:c1].reshape(D, LATENT + ROPE)
    router_w = first_all[:, :, c1:c2].reshape(D, n)
    attn_gain = first_all[:, :, c2].reshape(D).astype(F32)
    ffn_gain = first_all[:, :, c2 + 1].reshape(D).astype(F32)
    lat_gain = first_all[:, :latent_rows, c2 + 2].reshape(LATENT).astype(F32)
    routes = first_all[:, :, c2 + 3 : c2 + 3 + TOPK].astype(jnp.int32)

    out_w_half = lax.dynamic_slice_in_dim(output_weight, half * (D // 2), D // 2, 1)
    all_out_grad = lax.all_gather(output_grad, "ep", axis=0, tiled=True)
    out_w_half, q_blocks = lax.optimization_barrier((out_w_half, q_blocks))
    out_w_mine = lax.all_gather(out_w_half, "ep", axis=0, tiled=True)
    out_w_other = from_partner(out_w_mine)

    q_mine, x_mine = columns_in(q_blocks), columns_in(x_blocks)
    query_t = both_halves(q_mine, from_partner(q_mine), even)
    expand_t = both_halves(x_mine, from_partner(x_mine), even)
    shared_mine = columns_in(shared_blocks)
    shared_other = from_partner(shared_mine)
    gate_t = jnp.where(even, shared_mine, shared_other)
    up_t = jnp.where(even, shared_other, shared_mine)

    def own(values):
        return lax.dynamic_slice_in_dim(values, e * tokens, tokens, 0)

    cos_table, sin_table = rotary_tables(tokens, n)
    turned = jnp.concatenate(
        [query_t, query_t[NOPE + ROPE // 2 :], query_t[NOPE : NOPE + ROPE // 2]], axis=0
    )
    latent_turned = jnp.concatenate(
        [latent_w, latent_w[:, LATENT + ROPE // 2 :], latent_w[:, LATENT : LATENT + ROPE // 2]],
        axis=1,
    )
    normed, query, keys, values, latent = front(
        first_all, cos_table, sin_table, attn_gain[None], lat_gain[None], turned, latent_turned, expand_t
    )
    attended_head, attended_exact, lse = attend(prefix_length, query, keys, values)
    (attended_blocks,) = exchange(2, swaps=(attended_head.reshape(n, tokens, VH),))
    attended = attended_blocks.transpose(1, 0, 2).reshape(tokens, HEADS * VH)

    residual_in = layer_input.astype(F32)
    input_scale = rms_scale(residual_in)
    input_unit = residual_in * input_scale
    out_mine = product("ta,ad->td", attended, out_w_mine)
    out_other = product("ta,ad->td", attended, out_w_other)
    residual_mid = residual_in + jnp.concatenate(
        [jnp.where(even, out_mine, out_other), jnp.where(even, out_other, out_mine)], axis=1
    )
    mid_scale = rms_scale(residual_mid)
    mid_unit = residual_mid * mid_scale
    own_ffn_in = (mid_unit * ffn_gain).astype(BF16)
    (ffn_blocks,) = gather(own_ffn_in, 3)
    ffn_in = ffn_blocks.reshape(length, D)

    own_lane = (jnp.arange(128, dtype=jnp.int32) == e).astype(F32)[None]
    chosen = jnp.any(routes == e, axis=-1)
    chosen_int = chosen.astype(jnp.int32)
    place = jnp.cumsum(chosen_int, axis=1) - chosen_int
    kept = chosen & (place < capacity)
    dispatch = (
        (place[:, None, :] == jnp.arange(capacity, dtype=jnp.int32)[None, :, None])
        & kept[:, None, :]
    ).astype(BF16)
    shared_width = gate_t.shape[0]
    fill = ((0, -shared_width % 128), (0, 0))
    (
        out_partial,
        ffn_partial,
        dot_partial,
        router_all,
        incoming,
        expert_hidden,
        slot_grad,
        grad_expert_gu,
        shared_hidden,
        grad_shared_g,
        grad_shared_u,
    ) = ffn(
        ffn_blocks,
        all_out_grad.reshape(n, tokens, D),
        dispatch,
        own_lane,
        jnp.pad(router_w, ((0, 0), (0, 128 - n))),
        jnp.pad(gate_t, fill),
        jnp.pad(up_t, fill),
        jnp.pad(shared_down, fill),
        expert_gate[0],
        expert_up[0],
        expert_down[0],
    )
    ffn_sum, dot_sum, out_sum, grad_down_m, grad_gate_up_m = exchange(
        4,
        sums=(ffn_partial, dot_partial, out_partial),
        jobs=((expert_hidden, slot_grad), (incoming, grad_expert_gu)),
    )
    layer_output = (residual_mid + out_sum).astype(BF16)

    def shared_columns(values):
        return values.reshape(length, -1)[:, :shared_width]

    hidden = expert_down.shape[1]

    def by_group(values):
        return over_groups(values.reshape(groups, values.shape[0] // groups, -1))[None]

    expert_down_grad = by_group(grad_down_m)
    expert_gate_grad = by_group(grad_gate_up_m[:, :hidden])
    expert_up_grad = by_group(grad_gate_up_m[:, hidden:])
    shared_down_grad = to_row_owner(product_over_groups(shared_columns(shared_hidden), all_out_grad))
    side_shared = product_over_groups(
        ffn_in,
        jnp.concatenate([shared_columns(grad_shared_g), shared_columns(grad_shared_u)], axis=1),
    ).astype(BF16)

    router_own = lax.dynamic_index_in_dim(router_all, e, 0, keepdims=False)[:, :n]
    grad_probs = dot_sum[:, :n]
    grad_logits = (
        router_own * (grad_probs - jnp.sum(router_own * grad_probs, axis=-1, keepdims=True))
    ).astype(BF16)
    grad_ffn_in = ffn_sum + product("te,de->td", grad_logits, router_w)
    grad_ffn_gain = jnp.sum(grad_ffn_in * mid_unit, axis=0)
    grad_mid = output_grad.astype(F32) + norm_back(grad_ffn_in * ffn_gain, mid_unit, mid_scale)
    grad_mid_b = grad_mid.astype(BF16)
    mid_left, mid_right = grad_mid_b[:, : D // 2], grad_mid_b[:, D // 2 :]
    grad_attended = (
        product("td,ad->ta", jnp.where(even, mid_left, mid_right), out_w_mine)
        + product("td,ad->ta", jnp.where(even, mid_right, mid_left), out_w_other)
    ).astype(BF16)
    output_w_partial = product_over_groups(attended, grad_mid_b).astype(BF16)
    output_w_partial, grad_attended = lax.optimization_barrier((output_w_partial, grad_attended))
    (grad_att_blocks,) = exchange(
        5, swaps=(grad_attended.reshape(tokens, HEADS, VH).transpose(1, 0, 2),)
    )
    output_w_partial, grad_att_blocks = lax.optimization_barrier(
        (output_w_partial, grad_att_blocks)
    )
    grad_att = grad_att_blocks.reshape(length, VH)
    output_weight_grad = lax.psum_scatter(
        output_w_partial.reshape(n, rows_out, D), "ep", scatter_dimension=0
    ).astype(F32)
    grad_router = product("te,td->ed", grad_logits, own_ffn_in)

    delta = jnp.sum(grad_att.astype(F32) * attended_exact, axis=-1)[None]
    grad_query_raw, grad_keys, grad_values = attend_back(
        prefix_length, query, grad_att, lse, delta, keys, values
    )
    (
        grad_query,
        grad_expanded,
        latent_partial,
        rope_partial,
        normed_partial,
        gain_partial,
    ) = back(
        first_all, cos_table, sin_table, grad_query_raw, grad_keys, grad_values, turned, expand_t
    )
    latent_sum, rope_sum = exchange(
        6,
        sums=(
            latent_partial.reshape(n, tokens, LATENT),
            rope_partial.reshape(n, tokens, 2 * ROPE),
        ),
    )
    side_query = product_over_groups(normed, grad_query)[:, : query_t.shape[0]].astype(BF16)
    grad_expand = product_over_groups(latent, grad_expanded).astype(BF16)

    own_normed = (input_unit * attn_gain).astype(BF16)
    own_raw = product("td,dc->tc", own_normed, latent_w[:, :LATENT])
    latent_scale = rms_scale(own_raw)
    latent_unit = own_raw * latent_scale
    grad_latent_gain = jnp.sum(latent_sum * latent_unit, axis=0)
    grad_compressed = jnp.concatenate(
        [
            norm_back(latent_sum * lat_gain, latent_unit, latent_scale),
            unrotate(
                rope_sum[:, :ROPE],
                own(cos_table)[:, : ROPE // 2],
                own(sin_table)[:, ROPE // 2 : ROPE],
            ),
        ],
        axis=-1,
    ).astype(BF16)
    latent_w_partial = product_over_groups(
        own_normed, jnp.pad(grad_compressed, ((0, 0), (0, 640 - LATENT - ROPE)))
    ).astype(BF16)
    own_part = product("tc,dc->td", grad_compressed, latent_w)
    grad_attn_gain = gain_partial[0] + jnp.sum(own_part * input_unit, axis=0)

    def by_owner(values, rows):
        blocks = values.reshape(-1, groups, n, rows).transpose(2, 1, 0, 3)
        return blocks.reshape(n, groups, -1)

    small = jnp.concatenate(
        [
            by_owner(grad_attn_gain, rows_out),
            by_owner(grad_ffn_gain, rows_out),
            by_owner(grad_router, rows_out),
            by_owner(grad_latent_gain, expand_rows),
        ],
        axis=2,
    )
    small = small.transpose(1, 0, 2)
    if groups == 2:
        g = lax.axis_index("grp")
        mine = lax.dynamic_index_in_dim(small, g, 0, keepdims=False)
        theirs = lax.dynamic_index_in_dim(small, 1 - g, 0, keepdims=False)
        small = mine + lax.ppermute(theirs, "grp", [(0, 1), (1, 0)])
    else:
        small = lax.psum_scatter(small, "grp", scatter_dimension=0)
    (
        normed_sum,
        latent_weight_sum,
        small_all,
        query_weight_grad,
        shared_gate_grad,
        shared_up_grad,
        expand_weight_grad,
    ) = exchange(
        7,
        sums=(normed_partial.reshape(n, tokens, D), latent_w_partial.reshape(n, rows_out, -1)),
        swaps=(
            small[:, None],
            side_query.reshape(n, rows_out, -1),
            side_shared[:, :shared_width].reshape(n, rows_out, -1),
            side_shared[:, shared_width:].reshape(n, rows_out, -1),
            grad_expand.reshape(n, expand_rows, -1),
        ),
        laid=4,
    )
    grad_normed = normed_sum + own_part
    input_grad = (
        grad_mid + norm_back(grad_normed * attn_gain, input_unit, input_scale)
    ).astype(BF16)
    latent_weight_grad = latent_weight_sum[:, : LATENT + ROPE]
    small_sum = jnp.sum(small_all[:, 0], axis=0)
    attention_gain_grad = small_sum[:rows_out]
    feedforward_gain_grad = small_sum[rows_out : 2 * rows_out]
    router_weight_grad = small_sum[2 * rows_out : (2 + n) * rows_out].reshape(n, rows_out).T
    latent_gain_grad = small_sum[(2 + n) * rows_out :]
    return (
        layer_output,
        input_grad,
        attention_gain_grad,
        query_weight_grad,
        latent_weight_grad,
        latent_gain_grad,
        expand_weight_grad,
        output_weight_grad,
        feedforward_gain_grad,
        router_weight_grad,
        shared_gate_grad,
        shared_up_grad,
        shared_down_grad,
        expert_gate_grad,
        expert_up_grad,
        expert_down_grad,
    )


def solution(mesh):
    return jax.shard_map(
        per_device,
        mesh=mesh,
        in_specs=(
            P(("grp", "ep"), None),
            P("ep"),
            P("ep", None),
            P("ep", None),
            P("ep"),
            P("ep", None),
            P("ep", None),
            P("ep"),
            P("ep", None),
            P("ep", None),
            P("ep", None),
            P("ep", None),
            P("ep", None, None),
            P("ep", None, None),
            P("ep", None, None),
            P(("grp", "ep"), None),
            P("grp"),
            P(("grp", "ep"), None),
        ),
        out_specs=(
            P(("grp", "ep"), None),
            P(("grp", "ep"), None),
            P(("grp", "ep")),
            P(("grp", "ep"), None),
            P(("grp", "ep"), None),
            P(("grp", "ep")),
            P(("grp", "ep"), None),
            P(("grp", "ep"), None),
            P(("grp", "ep")),
            P(("grp", "ep"), None),
            P(("grp", "ep"), None),
            P(("grp", "ep"), None),
            P(("grp", "ep"), None),
            P("ep", "grp", None),
            P("ep", "grp", None),
            P("ep", "grp", None),
        ),
        check_vma=False,
    )
```

```python
import functools
import math

import jax
import jax.numpy as jnp
from jax import lax
from jax.experimental import pallas as pl
from jax.experimental.pallas import tpu as pltpu
from jax.sharding import PartitionSpec as P

D = 2048
HEADS = 16
NOPE = 128
ROPE = 64
VH = 128
LATENT = 512
TOPK = 6

EPSILON = 1e-06
MASKED = -1e30

MESH = pl.DeviceIdType.MESH
ANY = pl.BlockSpec(memory_space=pl.ANY)
DMA = pltpu.SemaphoreType.DMA
F32 = jnp.float32
BF16 = jnp.bfloat16


def remote(src, dst, send, recv, peer):
    return pltpu.make_async_remote_copy(
        src_ref=src,
        dst_ref=dst,
        send_sem=send,
        recv_sem=recv,
        device_id={"ep": peer},
        device_id_type=MESH,
    )


def greet(peers):
    barrier = pltpu.get_barrier_semaphore()
    for peer in peers:
        pl.semaphore_signal(barrier, inc=1, device_id={"ep": peer}, device_id_type=MESH)
    pl.semaphore_wait(barrier, len(peers))


def around(n):
    me = lax.axis_index("ep")
    x, y = me % 2, (me // 2) % 2
    return me, me // 4, y, x, me + 1 - 2 * x, me + 2 - 4 * y


def near(z, nz, below, above):
    for s in range(nz - 1):
        pl.when(z - 1 - s >= 0)(functools.partial(below, s, z - 1 - s))
        pl.when(z + 1 + s < nz)(functools.partial(above, s, z + 1 + s))


def greet_near(px, py, up, down, z, nz):
    barrier = pltpu.get_barrier_semaphore()
    for peer, there in ((px, None), (py, None), (up, z + 1 < nz), (down, z > 0)):

        def hello(peer=peer):
            pl.semaphore_signal(barrier, inc=1, device_id={"ep": peer}, device_id_type=MESH)

        hello() if there is None else pl.when(there)(hello)
    on_line = (z + 1 < nz).astype(jnp.int32) + (z > 0).astype(jnp.int32)
    pl.semaphore_wait(barrier, 2 + on_line)


def start_swaps(n, ins, outs, sems):
    own, ss, rs = sems
    me = lax.axis_index("ep")
    sends, copies = [], []
    for j in range(len(ins)):
        local = pltpu.make_async_copy(ins[j].at[me], outs[j].at[me], own.at[j])
        local.start()
        copies.append(local)
    for k in range(1, n):
        to = (me + k) % n
        for j in range(len(ins)):
            c = remote(ins[j].at[to], outs[j].at[me], ss.at[j, k], rs.at[j, k], to)
            c.start()
            sends.append(c)
    return sends, copies


def end_swaps(n, ins, outs, sems, started):
    own, ss, rs = sems
    me = lax.axis_index("ep")
    sends, copies = started
    for k in range(1, n):
        to, back = (me + k) % n, (me + n - k) % n
        for j in range(len(ins)):
            remote(ins[j].at[back], outs[j].at[back], ss.at[j, k], rs.at[j, k], to).wait_recv()
    for copy in sends:
        copy.wait_send()
    for copy in copies:
        copy.wait()


def gather_kernel(n, w, x_ref, *refs):
    swaps_in, o_ref, swaps_out = refs[:w], refs[w], refs[w + 1 : 2 * w + 1]
    own, us, ur, ds, dr, xs, xr, ys, yr, *swap_sems = refs[2 * w + 1 :]
    me, z, y, x, px, py = around(n)
    nz = n // 4
    low = me % 4
    half = x_ref.shape[0] // 2
    top, bottom = pl.ds(0, half), pl.ds(half, half)
    up, down = (me + 4) % n, (me + n - 4) % n
    everyone = [(me + k) % n for k in range(n)]
    if w:
        greet(everyone[1:])
    else:
        greet_near(px, py, up, down, z, nz)
    local = pltpu.make_async_copy(x_ref, o_ref.at[me], own)
    local.start()

    def over_x(src, b, part, i):
        return remote(src.at[part], o_ref.at[b, part], xs.at[i], xr.at[i], px)

    def over_y(src, b, part, i):
        return remote(src.at[part], o_ref.at[b, part], ys.at[i], yr.at[i], py)

    def upward(src, b, s):
        return remote(src, o_ref.at[b], us.at[s], ur.at[s], up)

    def downward(src, b, s):
        return remote(src, o_ref.at[b], ds.at[s], dr.at[s], down)

    def spread(src, t):
        b = t * 4 + low
        over_x(src, b, top, t).start()
        over_y(src, b, bottom, t).start()
        over_y(src, b, top, nz + t).start()
        over_x(src, b, bottom, nz + t).start()

    pl.when(z + 1 < nz)(lambda: upward(x_ref, me, 0).start())
    pl.when(z > 0)(lambda: downward(x_ref, me, 0).start())
    spread(x_ref, z)
    swapping = start_swaps(n, swaps_in, swaps_out, swap_sems) if w else None

    def from_below(s, t):
        b = t * 4 + low
        upward(o_ref.at[b], b, s).wait_recv()
        pl.when(z + 1 < nz)(lambda: upward(o_ref.at[b], b, s + 1).start())
        spread(o_ref.at[b], t)

    def from_above(s, t):
        b = t * 4 + low
        downward(o_ref.at[b], b, s).wait_recv()
        pl.when(z > 0)(lambda: downward(o_ref.at[b], b, s + 1).start())
        spread(o_ref.at[b], t)

    def turn(s, t):
        bx = t * 4 + low + px - me
        by = t * 4 + low + py - me
        over_x(o_ref.at[bx], bx, top, t).wait_recv()
        over_y(o_ref.at[bx], bx, top, 2 * nz + t).start()
        over_y(o_ref.at[by], by, bottom, t).wait_recv()
        over_x(o_ref.at[by], by, bottom, 2 * nz + t).start()

    for s in range(nz - 1):
        pl.when(z - 1 - s >= 0)(functools.partial(from_below, s, z - 1 - s))
        pl.when(z + 1 + s < nz)(functools.partial(from_above, s, z + 1 + s))
        if s == 0:
            turn(0, z)
        else:
            pl.when(z - s >= 0)(functools.partial(turn, s, z - s))
            pl.when(z + s < nz)(functools.partial(turn, s, z + s))
    pl.when(z - (nz - 1) >= 0)(functools.partial(turn, 0, z - (nz - 1)))
    pl.when(z + (nz - 1) < nz)(functools.partial(turn, 0, z + (nz - 1)))

    def finish(s, t):
        bx = t * 4 + low + px - me
        by = t * 4 + low + py - me
        bxy = bx + py - me
        over_y(o_ref.at[by], by, top, nz + t).wait_recv()
        over_x(o_ref.at[bx], bx, bottom, nz + t).wait_recv()
        over_y(o_ref.at[bxy], bxy, top, 2 * nz + t).wait_recv()
        over_x(o_ref.at[bxy], bxy, bottom, 2 * nz + t).wait_recv()
        for i in range(3):
            over_x(x_ref, me, top, i * nz + t).wait_send()
            over_y(x_ref, me, top, i * nz + t).wait_send()

    finish(0, z)
    near(z, nz, finish, finish)

    def sent_up(s, t):
        upward(x_ref, me, s).wait_send()

    def sent_down(s, t):
        downward(x_ref, me, s).wait_send()

    for s in range(nz - 1):
        pl.when((z + 1 < nz) & (z - s >= 0))(functools.partial(sent_up, s, z))
        pl.when((z > 0) & (z + s < nz))(functools.partial(sent_down, s, z))
    local.wait()
    if w:
        end_swaps(n, swaps_in, swaps_out, swap_sems, swapping)


def gather(x, cid, swaps=()):
    n = lax.axis_size("ep")
    w = len(swaps)
    nz = n // 4
    return pl.pallas_call(
        functools.partial(gather_kernel, n, w),
        out_shape=[jax.ShapeDtypeStruct((n,) + x.shape, x.dtype)]
        + [jax.ShapeDtypeStruct(a.shape, a.dtype) for a in swaps],
        in_specs=[ANY] * (1 + w),
        out_specs=[ANY] * (1 + w),
        scratch_shapes=[DMA]
        + [DMA((nz,))] * 4
        + [DMA((3 * nz,))] * 4
        + ([DMA((w,)), DMA((w, n)), DMA((w, n))] if w else []),
        compiler_params=pltpu.CompilerParams(collective_id=cid, has_side_effects=True),
        name="gather",
    )(x, *swaps)


def add_rows(dst, left, right, rows):
    step = 16

    def body(i, carry):
        r = pl.ds(pl.multiple_of(i * step, step), step)
        dst[r] = (left[r].astype(F32) + right[r].astype(F32)).astype(dst.dtype)
        return carry

    lax.fori_loop(0, rows // step, body, 0)


TILE = 128


def exchange_kernel(n, m, w, laid, jobs, *refs):
    refs = list(refs)

    def take(count):
        out = refs[:count]
        del refs[:count]
        return out

    sums_in, swaps_in = take(m), take(w)
    jobs_in = [take(2) for _ in jobs]
    sums_out, swaps_out, jobs_out = take(m), take(w), [take(parts) for parts in jobs]
    room = [take(7) for _ in range(m)]
    sems = [take(8) for _ in range(m)]
    swap_sems = take(3) if w else None
    side_by_side = swaps_out[w - laid :]
    swaps_out = swaps_out[: w - laid] + take(laid)
    desks = [take(5) for _ in jobs]
    me, z, y, x, px, py = around(n)
    nz = n // 4
    low = me % 4
    to = [(z + k) % nz for k in range(nz)]
    at = [t * 4 + low for t in to]
    if w:
        greet([(me + k) % n for k in range(1, n)])
    else:
        greet([px, py] + at[1:])
    order = [2, 1, 3, 0] if nz == 4 else list(range(1, nz)) + [0]
    sends = []

    def halves(j):
        half = sums_in[j].shape[3] // 2
        return half, pl.ds(0, half), pl.ds(half, half)

    first, second, third = {}, {}, {}

    def stage_one(j, k):
        p = sums_in[j]
        half, top, bottom = halves(j)
        la, lb, a1, b1, a2, b2, zb = room[j]
        lsa, lsb, xs, xr, ys, yr, zs, zr = sems[j]
        t = to[k]
        c = remote(p.at[t, 1 - y, :, top], a1.at[k], ys.at[k], yr.at[k], py)
        d = remote(p.at[t, :, 1 - x, bottom], b1.at[k], xs.at[k], xr.at[k], px)
        c.start()
        d.start()
        e = pltpu.make_async_copy(p.at[t, y, :, top], la.at[k], lsa.at[k])
        f = pltpu.make_async_copy(p.at[t, :, x, bottom], lb.at[k], lsb.at[k])
        e.start()
        f.start()
        first[j, k] = (c, d, e, f)
        sends.extend([c, d])

    def stage_two(j, k):
        half, top, bottom = halves(j)
        la, lb, a1, b1, a2, b2, zb = room[j]
        lsa, lsb, xs, xr, ys, yr, zs, zr = sems[j]
        c, d, e, f = first[j, k]
        e.wait()
        c.wait_recv()
        for i in range(2):
            add_rows(la.at[k, i], la.at[k, i], a1.at[k, i], half)
        g = remote(la.at[k, 1 - x], a2.at[k], xs.at[nz + k], xr.at[nz + k], px)
        g.start()
        f.wait()
        d.wait_recv()
        for i in range(2):
            add_rows(lb.at[k, i], lb.at[k, i], b1.at[k, i], half)
        h = remote(lb.at[k, 1 - y], b2.at[k], ys.at[nz + k], yr.at[nz + k], py)
        h.start()
        second[j, k] = (g, h)
        sends.extend([g, h])

    def stage_three(j, k):
        half, top, bottom = halves(j)
        la, lb, a1, b1, a2, b2, zb = room[j]
        lsa, lsb, xs, xr, ys, yr, zs, zr = sems[j]
        g, h = second[j, k]
        g.wait_recv()
        add_rows(a2.at[k], la.at[k, x], a2.at[k], half)
        if k:
            c = remote(a2.at[k], zb.at[k, top], zs.at[k], zr.at[k], at[k])
            c.start()
        h.wait_recv()
        add_rows(b2.at[k], lb.at[k, y], b2.at[k], half)
        if k:
            d = remote(b2.at[k], zb.at[k, bottom], zs.at[nz + k], zr.at[nz + k], at[k])
            d.start()
            third[j, k] = (c, d)
            sends.extend([c, d])

    loads = []
    for (left, right), (left_v, right_v, page, in_sem, out_sem) in zip(jobs_in, desks):
        for i, (src, dst) in enumerate(((left, left_v), (right, right_v))):
            loads.append(pltpu.make_async_copy(src, dst, in_sem.at[i]))

    def writes(j, i):
        left_v, right_v, page, in_sem, out_sem = desks[j]
        slot = i % 2
        rows = pl.ds(pl.multiple_of(i * TILE, TILE), TILE)
        return [
            pltpu.make_async_copy(page.at[slot, part], out.at[rows], out_sem.at[slot, part])
            for part, out in enumerate(jobs_out[j])
        ]

    def tile(j, i):
        left_v, right_v, page, in_sem, out_sem = desks[j]
        value = lax.dot_general(
            left_v[:, pl.ds(pl.multiple_of(i * TILE, TILE), TILE)],
            right_v[...],
            (((0,), (0,)), ((), ())),
            preferred_element_type=F32,
        ).astype(page.dtype)
        width = page.shape[3]
        for part, write in enumerate(writes(j, i)):
            pl.when(i >= 2)(write.wait)
            page[i % 2, part] = value[:, part * width : (part + 1) * width]
            write.start()

    tiles = [desk[0].shape[1] // TILE for desk in desks]
    loaded = []

    def work(step, of):
        first, last = sum(tiles) * step // of, sum(tiles) * (step + 1) // of
        for j in range(len(jobs)):
            start = sum(tiles[:j])
            low, high = max(first - start, 0), min(last - start, tiles[j])
            if low >= high:
                continue
            if j not in loaded:
                loaded.append(j)
                loads[2 * j].wait()
                loads[2 * j + 1].wait()
            lax.fori_loop(low, high, lambda i, c, j=j: (tile(j, i), c)[1], 0)

    steps = [(j, k) for j in range(m) for k in order]
    ahead = 3 if jobs else 2
    for i in range(min(ahead, len(steps))):
        stage_one(*steps[i])
    for copy in loads:
        copy.start()
    if w:
        swapping = start_swaps(n, swaps_in, swaps_out, swap_sems)
    for i, step in enumerate(steps):
        stage_two(*step)
        if i + ahead < len(steps):
            stage_one(*steps[i + ahead])
        if i:
            stage_three(*steps[i - 1])
        work(i, len(steps))
    if steps:
        stage_three(*steps[-1])
    if w:
        end_swaps(n, swaps_in, swaps_out, swap_sems, swapping)
        for wide, got in zip(side_by_side, swaps_out[w - laid :]):
            width = got.shape[2]
            for k in range(n):
                wide[:, k * width : (k + 1) * width] = got[k].astype(F32)
    for j in range(m):
        half, top, bottom = halves(j)
        la, lb, a1, b1, a2, b2, zb = room[j]
        o_ref = sums_out[j]
        for k in range(1, nz):
            c, d = third[j, k]
            c.wait_recv()
            d.wait_recv()
        for part, offset in ((a2, 0), (b2, half)):

            def body(i, carry, part=part, offset=offset, zb=zb, o_ref=o_ref):
                r = pl.ds(pl.multiple_of(i * 16, 16), 16)
                q = pl.ds(pl.multiple_of(i * 16 + offset, 16), 16)
                total = part[0, r].astype(F32)
                for k in range(1, nz):
                    total = total + zb[k, q].astype(F32)
                o_ref[q] = total.astype(o_ref.dtype)
                return carry

            lax.fori_loop(0, half // 16, body, 0)
    for copy in sends:
        copy.wait_send()
    for j in range(len(jobs)):
        for i in range(min(2, tiles[j])):
            for write in writes(j, i):
                write.wait()


def exchange(cid, sums=(), swaps=(), laid=0, jobs=()):
    n = lax.axis_size("ep")
    nz = n // 4
    m, w = len(sums), len(swaps)
    kept_rows = [p.shape[1] for p in sums]
    sums = [jnp.pad(p, ((0, 0), (0, -p.shape[1] % 32), (0, 0))) for p in sums]
    views = [p.reshape((nz, 2, 2) + p.shape[1:]) for p in sums]
    scratch = []
    for p in sums:
        rows, cols = p.shape[1:]
        half = rows // 2
        scratch += [pltpu.VMEM((nz, 2, half, cols), p.dtype)] * 4
        scratch += [pltpu.VMEM((nz, half, cols), p.dtype)] * 2
        scratch += [pltpu.VMEM((nz, rows, cols), p.dtype)]
    for p in sums:
        scratch += [DMA((nz,))] * 2 + [DMA((2 * nz,))] * 6
    if w:
        scratch += [DMA((w,)), DMA((w, n)), DMA((w, n))]
    plain, wide = swaps[: w - laid], swaps[w - laid :]
    scratch += [pltpu.VMEM(a.shape, a.dtype) for a in wide]
    for left, right, parts in jobs:
        scratch += [pltpu.VMEM(left.shape, left.dtype), pltpu.VMEM(right.shape, right.dtype)]
        scratch += [pltpu.VMEM((2, parts, TILE, right.shape[1] // parts), BF16)]
        scratch += [DMA((2,)), DMA((2, parts))]
    out = pl.pallas_call(
        functools.partial(exchange_kernel, n, m, w, laid, [parts for _, _, parts in jobs]),
        out_shape=[jax.ShapeDtypeStruct(p.shape[1:], F32) for p in sums]
        + [jax.ShapeDtypeStruct(a.shape, a.dtype) for a in plain]
        + [jax.ShapeDtypeStruct((a.shape[1], n * a.shape[2]), F32) for a in wide]
        + [
            jax.ShapeDtypeStruct((a.shape[1], b.shape[1] // parts), BF16)
            for a, b, parts in jobs
            for _ in range(parts)
        ],
        in_specs=[ANY] * (m + w + 2 * len(jobs)),
        out_specs=[pl.BlockSpec(memory_space=pltpu.VMEM)] * m
        + [ANY] * (w - laid)
        + [pl.BlockSpec(memory_space=pltpu.VMEM)] * laid
        + [ANY] * sum(parts for _, _, parts in jobs),
        scratch_shapes=scratch,
        compiler_params=pltpu.CompilerParams(
            collective_id=cid, has_side_effects=True, vmem_limit_bytes=(60 if jobs else 40) << 20 if m else None
        ),
        name="exchange",
    )(*views, *swaps, *(a for job in jobs for a in job[:2]))
    return [a[:rows] for a, rows in zip(out, kept_rows)] + list(out[m:])


def both(p):
    g = lax.axis_index("grp")
    mine = lax.dynamic_index_in_dim(p, g, 0, keepdims=False)
    theirs = lax.dynamic_index_in_dim(p, 1 - g, 0, keepdims=False)
    return mine, lax.ppermute(theirs.astype(BF16), "grp", [(0, 1), (1, 0)])


def over_groups(p):
    if lax.axis_size("grp") == 2:
        mine, other = both(p)
        return mine.astype(F32) + other.astype(F32)
    return lax.psum_scatter(p.astype(BF16), "grp", scatter_dimension=0, tiled=False).astype(F32)


def product_over_groups(left, right):
    groups = lax.axis_size("grp")
    rows = left.shape[1] // groups
    if groups != 2:
        whole = product("km,kn->mn", left, right)
        return over_groups(whole.reshape(groups, rows, -1))
    g = lax.axis_index("grp")
    mine = lax.dynamic_slice_in_dim(left, g * rows, rows, 1)
    theirs = lax.dynamic_slice_in_dim(left, (1 - g) * rows, rows, 1)
    sent = product("km,kn->mn", theirs, right).astype(BF16)
    other = lax.ppermute(sent, "grp", [(0, 1), (1, 0)])
    return product("km,kn->mn", mine, right) + other.astype(F32)


def from_partner(values):
    groups = lax.axis_size("grp")
    return lax.ppermute(values, "grp", [(g, g + 1 - 2 * (g % 2)) for g in range(groups)])


def to_row_owner(block):
    groups, n = lax.axis_size("grp"), lax.axis_size("ep")
    pairs = [(h * n + e, e * groups + h) for h in range(groups) for e in range(n)]
    return lax.ppermute(block.astype(BF16), ("grp", "ep"), pairs).astype(F32)


def dot(left, right):
    return jnp.dot(left, right, preferred_element_type=F32)


def dot_nt(left, right):
    return lax.dot_general(left, right, (((1,), (1,)), ((), ())), preferred_element_type=F32)


def front_kernel(
    x_ref, cos_ref, sin_ref, gain_ref, lat_gain_ref, wq_ref, wl_ref, we_ref,
    normed_ref, query_ref, keys_ref, values_ref, latent_ref,
):
    blocks, tokens = x_ref.shape[:2]
    rows = blocks * tokens
    x = x_ref[...].reshape(rows, gain_ref.shape[1]).astype(F32)
    normed = (x * rms_scale(x) * gain_ref[...]).astype(BF16)
    normed_ref[...] = normed
    cos, sin = cos_ref[...], sin_ref[...]
    own_half = lax.broadcasted_iota(jnp.int32, cos.shape, 1) < ROPE

    def turn(pair):
        return pair * cos + pltpu.roll(pair, ROPE, 1) * sin

    query = dot_nt(normed, wq_ref[...])
    query_ref[:, :NOPE] = query[:, :NOPE].astype(BF16)
    query_ref[:, NOPE:] = jnp.where(own_half, turn(query[:, NOPE:]), 0.0).astype(BF16)
    compressed = dot(normed, wl_ref[...])
    raw = compressed[:, :LATENT]
    latent = (raw * rms_scale(raw) * lat_gain_ref[...]).astype(BF16)
    latent_ref[...] = latent
    expanded = dot_nt(latent, we_ref[...])
    keys_ref[:, :NOPE] = expanded[:, :NOPE].astype(BF16)
    keys_ref[:, NOPE:] = turn(compressed[:, LATENT:]).astype(BF16)
    values_ref[...] = expanded[:, NOPE:].astype(BF16)


def front(x, cos, sin, gain, lat_gain, wq, wl, we):
    n, tokens = x.shape[:2]
    model = gain.shape[1]
    length = n * tokens
    blocks = 2
    rows = blocks * tokens

    def whole(a):
        return pl.BlockSpec(a.shape, lambda i: (0,) * a.ndim, pipeline_mode=pl.Buffered(1))

    def rows_of(cols):
        return pl.BlockSpec((rows, cols), lambda i: (i, 0))

    def out(cols):
        return jax.ShapeDtypeStruct((length, cols), BF16)

    cols = (model, wq.shape[0], NOPE + 2 * ROPE, VH, LATENT)
    return pl.pallas_call(
        front_kernel,
        grid=(n // blocks,),
        in_specs=[
            pl.BlockSpec((blocks, tokens, model), lambda i: (i, 0, 0)),
            rows_of(2 * ROPE),
            rows_of(2 * ROPE),
        ]
        + [whole(a) for a in (gain, lat_gain, wq, wl, we)],
        out_specs=[rows_of(c) for c in cols],
        out_shape=[out(c) for c in cols],
        compiler_params=pltpu.CompilerParams(vmem_limit_bytes=48 << 20),
        name="front",
    )(x, cos, sin, gain, lat_gain, wq, wl, we)


def back_kernel(
    x_ref, cos_ref, sin_ref, dq_ref, dk_ref, dv_ref, wq_ref, we_ref,
    query_ref, expanded_ref, latent_ref, rope_ref, normed_ref, gain_ref,
):
    blocks, tokens = x_ref.shape[:2]
    rows = blocks * tokens
    own_half = lax.broadcasted_iota(jnp.int32, cos_ref.shape, 1) < ROPE
    pair = dq_ref[:, NOPE:] * jnp.where(own_half, cos_ref[...], sin_ref[...])
    pair = jnp.where(own_half, pair + pltpu.roll(pair, ROPE, 1), 0.0)
    query_ref[:, :NOPE] = dq_ref[:, :NOPE].astype(BF16)
    query_ref[:, NOPE:] = pair.astype(BF16)
    part = dot(query_ref[...], wq_ref[...])
    normed_ref[...] = part.astype(BF16)
    x = x_ref[...].reshape(rows, gain_ref.shape[1]).astype(F32)
    gain = jnp.sum(part * (x * rms_scale(x)), axis=0, keepdims=True)

    @pl.when(pl.program_id(0) == 0)
    def _():
        gain_ref[...] = gain

    @pl.when(pl.program_id(0) > 0)
    def _():
        gain_ref[...] += gain

    expanded_ref[:, :NOPE] = dk_ref[:, :NOPE].astype(BF16)
    expanded_ref[:, NOPE:] = dv_ref[...].astype(BF16)
    latent_ref[...] = dot(expanded_ref[...], we_ref[...]).astype(BF16)
    rope_ref[...] = dk_ref[:, NOPE:].astype(BF16)


def back(x, cos, sin, dq, dk, dv, wq, we):
    n, tokens = x.shape[:2]
    length = n * tokens
    blocks = 2
    rows = blocks * tokens
    model = wq.shape[1]

    def whole(a):
        return pl.BlockSpec(a.shape, lambda i: (0,) * a.ndim, pipeline_mode=pl.Buffered(1))

    def rows_of(cols):
        return pl.BlockSpec((rows, cols), lambda i: (i, 0))

    def out(cols):
        return jax.ShapeDtypeStruct((length, cols), BF16)

    cols = (NOPE + 2 * ROPE, NOPE + VH, LATENT, 2 * ROPE, model)
    return pl.pallas_call(
        back_kernel,
        grid=(n // blocks,),
        in_specs=[
            pl.BlockSpec((blocks, tokens, model), lambda i: (i, 0, 0)),
            rows_of(2 * ROPE),
            rows_of(2 * ROPE),
            rows_of(dq.shape[1]),
            rows_of(dk.shape[1]),
            rows_of(dv.shape[1]),
            whole(wq),
            whole(we),
        ],
        out_specs=[rows_of(c) for c in cols] + [pl.BlockSpec((1, model), lambda i: (0, 0))],
        out_shape=[out(c) for c in cols] + [jax.ShapeDtypeStruct((1, model), F32)],
        compiler_params=pltpu.CompilerParams(vmem_limit_bytes=48 << 20),
        name="back",
    )(x, cos, sin, dq, dk, dv, wq, we)


KEYS = 512


def scores_of(scale, prefix, k, q, first_key, first_query):
    scores = dot_nt(k, q) * scale
    key = first_key + lax.broadcasted_iota(jnp.int32, scores.shape, 0)
    query = first_query + lax.broadcasted_iota(jnp.int32, scores.shape, 1)
    return jnp.where((key <= query) | (key < prefix), scores, MASKED)


def key_blocks(prefix, last_query):
    return (jnp.maximum(last_query, prefix) + KEYS - 1) // KEYS


def attend_kernel(scale, prefix_ref, q_ref, k_ref, v_ref, attended_ref, exact_ref, lse_ref):
    q = q_ref[...]
    rows = q.shape[0]
    start = pl.program_id(0) * rows
    prefix = prefix_ref[0]

    def step(j, carry):
        top, total, out = carry
        s = scores_of(scale, prefix, k_ref[j], q, j * KEYS, start)
        new_top = jnp.maximum(top, jnp.max(s, axis=0, keepdims=True))
        p = jnp.exp(s - new_top)
        shrink = jnp.exp(top - new_top)
        total = total * shrink + jnp.sum(p, axis=0, keepdims=True)
        return new_top, total, out * shrink + dot(v_ref[j], p.astype(BF16))

    top, total, out = lax.fori_loop(
        0,
        key_blocks(prefix, start + rows),
        step,
        (
            jnp.full((1, rows), MASKED, F32),
            jnp.zeros((1, rows), F32),
            jnp.zeros((v_ref.shape[1], rows), F32),
        ),
    )
    lse_ref[...] = top + jnp.log(total)
    exact = (out / total).T
    exact_ref[...] = exact
    attended_ref[...] = exact.astype(BF16)


def attend(prefix, q, k, v):
    length, depth = q.shape
    values = v.shape[1]
    rows = 256
    v = v.reshape(length // KEYS, KEYS, values).transpose(0, 2, 1)
    k = k.reshape(length // KEYS, KEYS, depth)
    return pl.pallas_call(
        functools.partial(attend_kernel, 1.0 / math.sqrt(NOPE + ROPE)),
        grid=(length // rows,),
        in_specs=[
            pl.BlockSpec(memory_space=pltpu.SMEM),
            pl.BlockSpec((rows, depth), lambda i: (i, 0)),
            pl.BlockSpec(k.shape, lambda i: (0, 0, 0)),
            pl.BlockSpec(v.shape, lambda i: (0, 0, 0)),
        ],
        out_specs=[
            pl.BlockSpec((rows, values), lambda i: (i, 0)),
            pl.BlockSpec((rows, values), lambda i: (i, 0)),
            pl.BlockSpec((1, rows), lambda i: (0, i)),
        ],
        out_shape=[
            jax.ShapeDtypeStruct((length, values), BF16),
            jax.ShapeDtypeStruct((length, values), F32),
            jax.ShapeDtypeStruct((1, length), F32),
        ],
        compiler_params=pltpu.CompilerParams(vmem_limit_bytes=32 << 20),
        name="attend",
    )(prefix, q, k, v)


def attend_back_kernel(
    scale, prefix_ref, q_ref, g_ref, lse_ref, delta_ref, k_ref, v_ref, dq_ref, dk_ref, dv_ref
):
    q, g = q_ref[...], g_ref[...]
    rows = q.shape[0]
    start = pl.program_id(0) * rows
    prefix = prefix_ref[0]

    @pl.when(pl.program_id(0) == 0)
    def _():
        dk_ref[...] = jnp.zeros_like(dk_ref)
        dv_ref[...] = jnp.zeros_like(dv_ref)

    def step(j, dq):
        k = k_ref[j]
        p = jnp.exp(scores_of(scale, prefix, k, q, j * KEYS, start) - lse_ref[...])
        ds = (p * (dot_nt(v_ref[j], g) - delta_ref[...]) * scale).astype(BF16)
        dv_ref[j] += dot(p.astype(BF16), g)
        dk_ref[j] += dot(ds, q)
        return dq + lax.dot_general(
            ds, k, (((0,), (0,)), ((), ())), preferred_element_type=F32
        )

    dq_ref[...] = lax.fori_loop(
        0, key_blocks(prefix, start + rows), step, jnp.zeros(dq_ref.shape, F32)
    )


def attend_back(prefix, q, g, lse, delta, k, v):
    length, depth = q.shape
    values = v.shape[1]
    rows = 256
    k = k.reshape(length // KEYS, KEYS, depth)
    v = v.reshape(length // KEYS, KEYS, values)
    dq, dk, dv = pl.pallas_call(
        functools.partial(attend_back_kernel, 1.0 / math.sqrt(NOPE + ROPE)),
        grid=(length // rows,),
        in_specs=[
            pl.BlockSpec(memory_space=pltpu.SMEM),
            pl.BlockSpec((rows, depth), lambda i: (i, 0)),
            pl.BlockSpec((rows, values), lambda i: (i, 0)),
            pl.BlockSpec((1, rows), lambda i: (0, i)),
            pl.BlockSpec((1, rows), lambda i: (0, i)),
            pl.BlockSpec(k.shape, lambda i: (0, 0, 0)),
            pl.BlockSpec(v.shape, lambda i: (0, 0, 0)),
        ],
        out_specs=[
            pl.BlockSpec((rows, depth), lambda i: (i, 0)),
            pl.BlockSpec(k.shape, lambda i: (0, 0, 0)),
            pl.BlockSpec(v.shape, lambda i: (0, 0, 0)),
        ],
        out_shape=[
            jax.ShapeDtypeStruct((length, depth), F32),
            jax.ShapeDtypeStruct(k.shape, F32),
            jax.ShapeDtypeStruct(v.shape, F32),
        ],
        compiler_params=pltpu.CompilerParams(vmem_limit_bytes=40 << 20),
        name="attend_back",
    )(prefix, q, g, lse, delta, k, v)
    return dq, dk.reshape(length, depth), dv.reshape(length, values)


def ffn_kernel(
    n,
    x_ref,
    y_ref,
    slots_ref,
    tokens_ref,
    own_ref,
    router_ref,
    sg_ref,
    su_ref,
    sd_ref,
    eg_ref,
    eu_ref,
    ed_ref,
    out_ref,
    ffn_ref,
    dot_ref,
    probs_ref,
    rows_ref,
    hidden_ref,
    slot_grad_ref,
    grad_gu_ref,
    shared_h_ref,
    shared_gu_ref,
    expert_out,
    row_grad,
):
    blocks, tokens = x_ref.shape[:2]
    capacity = slots_ref.shape[1]
    own = own_ref[...]
    lanes = lax.broadcasted_iota(jnp.int32, (tokens, own.shape[1]), 1)
    gates = []
    for b in range(blocks):
        x, y = x_ref[b], y_ref[b]
        logits = jnp.where(lanes < n, dot(x, router_ref[...]), MASKED)
        raised = jnp.exp(logits - jnp.max(logits, axis=-1, keepdims=True))
        probs = raised / jnp.sum(raised, axis=-1, keepdims=True)
        probs_ref[b] = probs
        gate = jnp.sum(probs * own, axis=-1, keepdims=True)
        gates.append(gate)
        part = pl.ds(b * capacity, capacity)
        rows_ref[part] = dot(slots_ref[b], x).astype(BF16)
        weighted = (gate * y.astype(F32)).astype(BF16)
        slot_grad_ref[part] = dot(slots_ref[b], weighted).astype(BF16)
    rows = rows_ref[...]
    slot_grad = slot_grad_ref[...]
    g = dot(rows, eg_ref[...])
    u = dot(rows, eu_ref[...])
    sigmoid = 1.0 / (1.0 + jnp.exp(-g))
    silu = g * sigmoid
    hidden = (silu * u).astype(BF16)
    hidden_ref[...] = hidden
    expert_out[...] = dot(hidden, ed_ref[...]).astype(BF16)
    grad_hidden = dot_nt(slot_grad, ed_ref[...])
    grad_g = (grad_hidden * u * sigmoid * (1.0 + g * (1.0 - sigmoid))).astype(BF16)
    grad_u = (grad_hidden * silu).astype(BF16)
    grad_gu_ref[:, : grad_g.shape[1]] = grad_g
    grad_gu_ref[:, grad_g.shape[1] :] = grad_u
    row_grad[...] = (dot_nt(grad_g, eg_ref[...]) + dot_nt(grad_u, eu_ref[...])).astype(BF16)
    x = x_ref[...].reshape(blocks * tokens, -1)
    y = y_ref[...].reshape(blocks * tokens, -1)
    g = dot_nt(x, sg_ref[...])
    u = dot_nt(x, su_ref[...])
    grad_hidden = dot_nt(y, sd_ref[...])
    sigmoid = 1.0 / (1.0 + jnp.exp(-g))
    silu = g * sigmoid
    hidden = (silu * u).astype(BF16)
    grad_g = (grad_hidden * u * sigmoid * (1.0 + g * (1.0 - sigmoid))).astype(BF16)
    grad_u = (grad_hidden * silu).astype(BF16)
    shared = hidden.shape[1]
    shared_h_ref[...] = hidden.reshape(blocks, tokens, shared)
    shared_gu_ref[:, :, :shared] = grad_g.reshape(blocks, tokens, shared)
    shared_gu_ref[:, :, shared:] = grad_u.reshape(blocks, tokens, shared)
    width = x.shape[1]
    chunk = width // 4
    met = [0.0] * blocks
    for c in range(width // chunk):
        cols = pl.ds(c * chunk, chunk)
        shared_out = dot(hidden, sd_ref[:, cols])
        shared_ffn = dot(grad_g, sg_ref[:, cols]) + dot(grad_u, su_ref[:, cols])
        for b in range(blocks):
            part = pl.ds(b * capacity, capacity)
            here = slice(b * tokens, (b + 1) * tokens)
            picked = dot(tokens_ref[b], expert_out[part, cols])
            met[b] += jnp.sum(picked * y_ref[b, :, cols].astype(F32), axis=-1, keepdims=True)
            out_ref[b, :, cols] = (shared_out[here] + picked * gates[b]).astype(BF16)
            back = dot(tokens_ref[b], row_grad[part, cols])
            ffn_ref[b, :, cols] = (shared_ffn[here] + back).astype(BF16)
    for b in range(blocks):
        dot_ref[b] = (met[b] * own).astype(BF16)


def ffn(x, y, slots, own_lane, router_w, gate_t, up_t, down, gate_m, up_m, down_m):
    n, tokens, width = x.shape
    capacity = slots.shape[1]
    hidden = gate_m.shape[1]
    shared = gate_t.shape[0]
    group = 4

    def whole(a):
        return pl.BlockSpec(a.shape, lambda i: (0,) * a.ndim, pipeline_mode=pl.Buffered(1))

    def block(*shape):
        return pl.BlockSpec((group,) + shape, lambda i: (i, 0, 0))

    def slot_rows(cols):
        return pl.BlockSpec((group * capacity, cols), lambda i: (i, 0))

    def tokens_of(cols, kind=BF16):
        return jax.ShapeDtypeStruct((n, tokens, cols), kind)

    def slots_of(cols):
        return jax.ShapeDtypeStruct((n * capacity, cols), BF16)

    weights = (own_lane, router_w, gate_t, up_t, down, gate_m, up_m, down_m)
    return pl.pallas_call(
        functools.partial(ffn_kernel, n),
        grid=(n // group,),
        in_specs=[
            block(tokens, width),
            block(tokens, width),
            block(capacity, tokens),
            block(tokens, capacity),
        ]
        + [whole(a) for a in weights],
        out_specs=[
            block(tokens, width),
            block(tokens, width),
            block(tokens, 128),
            block(tokens, 128),
            slot_rows(width),
            slot_rows(hidden),
            slot_rows(width),
            slot_rows(2 * hidden),
            block(tokens, shared),
            block(tokens, 2 * shared),
        ],
        out_shape=[
            tokens_of(width),
            tokens_of(width),
            tokens_of(128),
            tokens_of(128, F32),
            slots_of(width),
            slots_of(hidden),
            slots_of(width),
            slots_of(2 * hidden),
            tokens_of(shared),
            tokens_of(2 * shared),
        ],
        scratch_shapes=[
            pltpu.VMEM((group * capacity, width), BF16),
            pltpu.VMEM((group * capacity, width), BF16),
        ],
        compiler_params=pltpu.CompilerParams(vmem_limit_bytes=60 << 20),
        name="ffn",
    )(x, y, slots, slots.transpose(0, 2, 1), *weights)


def product(form, left, right):
    return jnp.einsum(form, left, right, preferred_element_type=F32)


def rms_scale(values):
    return lax.rsqrt(jnp.mean(values * values, axis=-1, keepdims=True) + EPSILON)


def rotary_tables(tokens, n):
    halfway = ROPE // 2
    inverse = 10000.0 ** (-(jnp.arange(halfway, dtype=F32) * 2.0 / ROPE))
    inverse = jnp.concatenate([inverse] * 4)
    lane = jnp.arange(2 * ROPE)
    sign = jnp.where((lane < halfway) | (lane >= 3 * halfway), -1.0, 1.0)
    base = (jnp.arange(n, dtype=F32) * tokens)[:, None] * inverse
    step = jnp.arange(tokens, dtype=F32)[:, None] * inverse
    base_cos, base_sin = jnp.cos(base)[:, None], jnp.sin(base)[:, None]
    step_cos, step_sin = jnp.cos(step)[None], jnp.sin(step)[None]
    cos_table = base_cos * step_cos - base_sin * step_sin
    sin_table = (base_sin * step_cos + base_cos * step_sin) * sign
    return cos_table.reshape(n * tokens, -1), sin_table.reshape(n * tokens, -1)


def unrotate(grads, cos_table, sin_table):
    halfway = grads.shape[-1] // 2
    first = grads[..., :halfway]
    second = grads[..., halfway:]
    return jnp.concatenate(
        [first * cos_table + second * sin_table, second * cos_table - first * sin_table], axis=-1
    )


def norm_back(grad_unit, unit_values, scale_values):
    return scale_values * (
        grad_unit - unit_values * jnp.mean(grad_unit * unit_values, axis=-1, keepdims=True)
    )


def column_halves(weight, n, half):
    rows, width = weight.shape[0], weight.shape[1] // n
    parts = weight.T.reshape(n, 2, width // 2, rows)
    return lax.dynamic_index_in_dim(parts, half, 1, keepdims=False)


def columns_in(blocks):
    n, width, rows = blocks.shape
    return blocks.transpose(1, 0, 2).reshape(width, n * rows)


def both_halves(mine, other, even):
    return jnp.concatenate([jnp.where(even, mine, other), jnp.where(even, other, mine)], axis=0)


def per_device(
    layer_input,
    attention_gain,
    query_weight,
    latent_weight,
    latent_gain,
    expand_weight,
    output_weight,
    feedforward_gain,
    router_weight,
    shared_gate,
    shared_up,
    shared_down,
    expert_gate,
    expert_up,
    expert_down,
    expert_routes,
    prefix_length,
    output_grad,
):
    n = lax.axis_size("ep")
    groups = lax.axis_size("grp")
    e = lax.axis_index("ep")
    half = lax.axis_index("grp") % 2
    even = half == 0
    tokens = layer_input.shape[0]
    length = tokens * n
    capacity = tokens * TOPK * 4 // (3 * n)
    rows_dev = attention_gain.shape[0]
    latent_rows = latent_gain.shape[0]
    rows_out = D // (groups * n)
    expand_rows = LATENT // (groups * n)

    pad = jnp.zeros((rows_dev - latent_rows,), BF16)
    first_block = jnp.concatenate(
        [
            layer_input,
            latent_weight,
            router_weight,
            attention_gain[:, None],
            feedforward_gain[:, None],
            jnp.concatenate([latent_gain, pad])[:, None],
            expert_routes.astype(BF16),
        ],
        axis=1,
    )
    width = first_block.shape[1]
    out_w_half = lax.dynamic_slice_in_dim(output_weight, half * (D // 2), D // 2, 1)
    first_block = jnp.concatenate(
        [first_block, jnp.zeros((tokens, -width % 128), BF16), out_w_half], axis=1
    )
    shared_half = jnp.where(even, shared_gate, shared_up)
    first_all, q_blocks, x_blocks, shared_blocks = gather(
        first_block,
        0,
        swaps=(
            column_halves(query_weight, n, half),
            column_halves(expand_weight, n, half),
            shared_half.T.reshape(n, shared_half.shape[1] // n, rows_dev),
        ),
    )
    c0 = D
    c1 = c0 + LATENT + ROPE
    c2 = c1 + n
    latent_w = first_all[:, :, c0:c1].reshape(D, LATENT + ROPE)
    router_w = first_all[:, :, c1:c2].reshape(D, n)
    attn_gain = first_all[:, :, c2].reshape(D).astype(F32)
    ffn_gain = first_all[:, :, c2 + 1].reshape(D).astype(F32)
    lat_gain = first_all[:, :latent_rows, c2 + 2].reshape(LATENT).astype(F32)
    routes = first_all[:, :, c2 + 3 : c2 + 3 + TOPK].astype(jnp.int32)

    out_w_mine = first_all[:, :, -(D // 2) :].reshape(D, D // 2)
    out_w_other = from_partner(out_w_mine)
    later_grad, q_blocks = lax.optimization_barrier((output_grad, q_blocks))
    all_out_grad = lax.all_gather(later_grad, "ep", axis=0, tiled=True)

    q_mine, x_mine = columns_in(q_blocks), columns_in(x_blocks)
    query_t = both_halves(q_mine, from_partner(q_mine), even)
    expand_t = both_halves(x_mine, from_partner(x_mine), even)
    shared_mine = columns_in(shared_blocks)
    shared_other = from_partner(shared_mine)
    gate_t = jnp.where(even, shared_mine, shared_other)
    up_t = jnp.where(even, shared_other, shared_mine)

    def own(values):
        return lax.dynamic_slice_in_dim(values, e * tokens, tokens, 0)

    cos_table, sin_table = rotary_tables(tokens, n)
    turned = jnp.concatenate(
        [query_t, query_t[NOPE + ROPE // 2 :], query_t[NOPE : NOPE + ROPE // 2]], axis=0
    )
    latent_turned = jnp.concatenate(
        [latent_w, latent_w[:, LATENT + ROPE // 2 :], latent_w[:, LATENT : LATENT + ROPE // 2]],
        axis=1,
    )
    normed, query, keys, values, latent = front(
        first_all, cos_table, sin_table, attn_gain[None], lat_gain[None], turned, latent_turned, expand_t
    )
    attended_head, attended_exact, lse = attend(prefix_length, query, keys, values)
    (attended_blocks,) = exchange(2, swaps=(attended_head.reshape(n, tokens, VH),))
    attended = attended_blocks.transpose(1, 0, 2).reshape(tokens, HEADS * VH)

    residual_in = layer_input.astype(F32)
    input_scale = rms_scale(residual_in)
    input_unit = residual_in * input_scale
    out_mine = product("ta,ad->td", attended, out_w_mine)
    out_other = product("ta,ad->td", attended, out_w_other)
    residual_mid = residual_in + jnp.concatenate(
        [jnp.where(even, out_mine, out_other), jnp.where(even, out_other, out_mine)], axis=1
    )
    mid_scale = rms_scale(residual_mid)
    mid_unit = residual_mid * mid_scale
    own_ffn_in = (mid_unit * ffn_gain).astype(BF16)
    (ffn_blocks,) = gather(own_ffn_in, 3)
    ffn_in = ffn_blocks.reshape(length, D)

    own_lane = (jnp.arange(128, dtype=jnp.int32) == e).astype(F32)[None]
    chosen = jnp.any(routes == e, axis=-1)
    chosen_int = chosen.astype(jnp.int32)
    place = jnp.cumsum(chosen_int, axis=1) - chosen_int
    kept = chosen & (place < capacity)
    dispatch = (
        (place[:, None, :] == jnp.arange(capacity, dtype=jnp.int32)[None, :, None])
        & kept[:, None, :]
    ).astype(BF16)
    shared_width = gate_t.shape[0]
    fill = ((0, -shared_width % 128), (0, 0))
    (
        out_partial,
        ffn_partial,
        dot_partial,
        router_all,
        incoming,
        expert_hidden,
        slot_grad,
        grad_expert_gu,
        shared_hidden,
        grad_shared_gu,
    ) = ffn(
        ffn_blocks,
        all_out_grad.reshape(n, tokens, D),
        dispatch,
        own_lane,
        jnp.pad(router_w, ((0, 0), (0, 128 - n))),
        jnp.pad(gate_t, fill),
        jnp.pad(up_t, fill),
        jnp.pad(shared_down, fill),
        expert_gate[0],
        expert_up[0],
        expert_down[0],
    )
    ffn_sum, dot_sum, out_sum, grad_down_m, grad_gate_m, grad_up_m = exchange(
        4,
        sums=(ffn_partial, dot_partial, out_partial),
        jobs=((expert_hidden, slot_grad, 1), (incoming, grad_expert_gu, 2)),
    )
    layer_output = (residual_mid + out_sum).astype(BF16)

    def by_group(values):
        return over_groups(values.reshape(groups, values.shape[0] // groups, -1))

    expert_down_grad = by_group(grad_down_m)[None]
    expert_gate_grad = by_group(grad_gate_m)[None]
    expert_up_grad = by_group(grad_up_m)[None]

    router_own = lax.dynamic_index_in_dim(router_all, e, 0, keepdims=False)[:, :n]
    grad_probs = dot_sum[:, :n]
    grad_logits = (
        router_own * (grad_probs - jnp.sum(router_own * grad_probs, axis=-1, keepdims=True))
    ).astype(BF16)
    grad_ffn_in = ffn_sum + product("te,de->td", grad_logits, router_w)
    grad_ffn_gain = jnp.sum(grad_ffn_in * mid_unit, axis=0)
    grad_mid = output_grad.astype(F32) + norm_back(grad_ffn_in * ffn_gain, mid_unit, mid_scale)
    grad_mid_b = grad_mid.astype(BF16)
    mid_left, mid_right = grad_mid_b[:, : D // 2], grad_mid_b[:, D // 2 :]
    grad_attended = (
        product("td,ad->ta", jnp.where(even, mid_left, mid_right), out_w_mine)
        + product("td,ad->ta", jnp.where(even, mid_right, mid_left), out_w_other)
    ).astype(BF16)
    output_w_partial = product_over_groups(attended, grad_mid_b).astype(BF16)
    output_w_partial, grad_attended = lax.optimization_barrier((output_w_partial, grad_attended))
    (grad_att_blocks,) = exchange(
        5, swaps=(grad_attended.reshape(tokens, HEADS, VH).transpose(1, 0, 2),)
    )
    output_w_partial, grad_att_blocks = lax.optimization_barrier(
        (output_w_partial, grad_att_blocks)
    )
    grad_att = grad_att_blocks.reshape(length, VH)
    output_weight_grad = lax.psum_scatter(
        output_w_partial.reshape(n, rows_out, D), "ep", scatter_dimension=0
    ).astype(F32)
    grad_router = product("te,td->ed", grad_logits, own_ffn_in)

    delta = jnp.sum(grad_att.astype(F32) * attended_exact, axis=-1)[None]
    grad_query_raw, grad_keys, grad_values = attend_back(
        prefix_length, query, grad_att, lse, delta, keys, values
    )
    (
        grad_query,
        grad_expanded,
        latent_partial,
        rope_partial,
        normed_partial,
        gain_partial,
    ) = back(
        first_all, cos_table, sin_table, grad_query_raw, grad_keys, grad_values, turned, expand_t
    )
    latent_sum, rope_sum, side_gate, side_up, side_down, side_query, side_expand = exchange(
        6,
        sums=(
            latent_partial.reshape(n, tokens, LATENT),
            rope_partial.reshape(n, tokens, 2 * ROPE),
        ),
        jobs=(
            (ffn_in, grad_shared_gu.reshape(length, -1), 2),
            (shared_hidden.reshape(length, -1), all_out_grad, 1),
            (normed, grad_query, 1),
            (latent, grad_expanded, 1),
        ),
    )
    shared_down_grad = to_row_owner(by_group(side_down[:shared_width]))
    side_gate = by_group(side_gate)[:, :shared_width].astype(BF16)
    side_up = by_group(side_up)[:, :shared_width].astype(BF16)
    side_query = by_group(side_query)[:, : query_t.shape[0]].astype(BF16)
    grad_expand = by_group(side_expand).astype(BF16)

    own_normed = (input_unit * attn_gain).astype(BF16)
    own_raw = product("td,dc->tc", own_normed, latent_w[:, :LATENT])
    latent_scale = rms_scale(own_raw)
    latent_unit = own_raw * latent_scale
    grad_latent_gain = jnp.sum(latent_sum * latent_unit, axis=0)
    grad_compressed = jnp.concatenate(
        [
            norm_back(latent_sum * lat_gain, latent_unit, latent_scale),
            unrotate(
                rope_sum[:, :ROPE],
                own(cos_table)[:, : ROPE // 2],
                own(sin_table)[:, ROPE // 2 : ROPE],
            ),
        ],
        axis=-1,
    ).astype(BF16)
    latent_w_partial = product_over_groups(
        own_normed, jnp.pad(grad_compressed, ((0, 0), (0, 640 - LATENT - ROPE)))
    ).astype(BF16)
    own_part = product("tc,dc->td", grad_compressed, latent_w)
    grad_attn_gain = gain_partial[0] + jnp.sum(own_part * input_unit, axis=0)

    def by_owner(values, rows):
        blocks = values.reshape(-1, groups, n, rows).transpose(2, 1, 0, 3)
        return blocks.reshape(n, groups, -1)

    small = jnp.concatenate(
        [
            by_owner(grad_attn_gain, rows_out),
            by_owner(grad_ffn_gain, rows_out),
            by_owner(grad_router, rows_out),
            by_owner(grad_latent_gain, expand_rows),
        ],
        axis=2,
    )
    small = small.transpose(1, 0, 2)
    if groups == 2:
        g = lax.axis_index("grp")
        mine = lax.dynamic_index_in_dim(small, g, 0, keepdims=False)
        theirs = lax.dynamic_index_in_dim(small, 1 - g, 0, keepdims=False)
        small = mine + lax.ppermute(theirs, "grp", [(0, 1), (1, 0)])
    else:
        small = lax.psum_scatter(small, "grp", scatter_dimension=0)
    (
        normed_sum,
        latent_weight_sum,
        small_all,
        query_weight_grad,
        shared_gate_grad,
        shared_up_grad,
        expand_weight_grad,
    ) = exchange(
        7,
        sums=(normed_partial.reshape(n, tokens, D), latent_w_partial.reshape(n, rows_out, -1)),
        swaps=(
            small[:, None],
            side_query.reshape(n, rows_out, -1),
            side_gate.reshape(n, rows_out, -1),
            side_up.reshape(n, rows_out, -1),
            grad_expand.reshape(n, expand_rows, -1),
        ),
        laid=4,
    )
    grad_normed = normed_sum + own_part
    input_grad = (
        grad_mid + norm_back(grad_normed * attn_gain, input_unit, input_scale)
    ).astype(BF16)
    latent_weight_grad = latent_weight_sum[:, : LATENT + ROPE]
    small_sum = jnp.sum(small_all[:, 0], axis=0)
    attention_gain_grad = small_sum[:rows_out]
    feedforward_gain_grad = small_sum[rows_out : 2 * rows_out]
    router_weight_grad = small_sum[2 * rows_out : (2 + n) * rows_out].reshape(n, rows_out).T
    latent_gain_grad = small_sum[(2 + n) * rows_out :]
    return (
        layer_output,
        input_grad,
        attention_gain_grad,
        query_weight_grad,
        latent_weight_grad,
        latent_gain_grad,
        expand_weight_grad,
        output_weight_grad,
        feedforward_gain_grad,
        router_weight_grad,
        shared_gate_grad,
        shared_up_grad,
        shared_down_grad,
        expert_gate_grad,
        expert_up_grad,
        expert_down_grad,
    )


def solution(mesh):
    return jax.shard_map(
        per_device,
        mesh=mesh,
        in_specs=(
            P(("grp", "ep"), None),
            P("ep"),
            P("ep", None),
            P("ep", None),
            P("ep"),
            P("ep", None),
            P("ep", None),
            P("ep"),
            P("ep", None),
            P("ep", None),
            P("ep", None),
            P("ep", None),
            P("ep", None, None),
            P("ep", None, None),
            P("ep", None, None),
            P(("grp", "ep"), None),
            P("grp"),
            P(("grp", "ep"), None),
        ),
        out_specs=(
            P(("grp", "ep"), None),
            P(("grp", "ep"), None),
            P(("grp", "ep")),
            P(("grp", "ep"), None),
            P(("grp", "ep"), None),
            P(("grp", "ep")),
            P(("grp", "ep"), None),
            P(("grp", "ep"), None),
            P(("grp", "ep")),
            P(("grp", "ep"), None),
            P(("grp", "ep"), None),
            P(("grp", "ep"), None),
            P(("grp", "ep"), None),
            P("ep", "grp", None),
            P("ep", "grp", None),
            P("ep", "grp", None),
        ),
        check_vma=False,
    )
```

```python
import functools
import math

import jax
import jax.numpy as jnp
from jax import lax
from jax.experimental import pallas as pl
from jax.experimental.pallas import tpu as pltpu
from jax.sharding import PartitionSpec as P

D = 2048
HEADS = 16
NOPE = 128
ROPE = 64
VH = 128
LATENT = 512
TOPK = 6

EPSILON = 1e-06
MASKED = -1e30

MESH = pl.DeviceIdType.MESH
ANY = pl.BlockSpec(memory_space=pl.ANY)
DMA = pltpu.SemaphoreType.DMA
F32 = jnp.float32
BF16 = jnp.bfloat16


def remote(src, dst, send, recv, peer):
    return pltpu.make_async_remote_copy(
        src_ref=src,
        dst_ref=dst,
        send_sem=send,
        recv_sem=recv,
        device_id={"ep": peer},
        device_id_type=MESH,
    )


def greet(peers):
    barrier = pltpu.get_barrier_semaphore()
    for peer in peers:
        pl.semaphore_signal(barrier, inc=1, device_id={"ep": peer}, device_id_type=MESH)
    pl.semaphore_wait(barrier, len(peers))


def around(n):
    me = lax.axis_index("ep")
    x, y = me % 2, (me // 2) % 2
    return me, me // 4, y, x, me + 1 - 2 * x, me + 2 - 4 * y


def near(z, nz, below, above):
    for s in range(nz - 1):
        pl.when(z - 1 - s >= 0)(functools.partial(below, s, z - 1 - s))
        pl.when(z + 1 + s < nz)(functools.partial(above, s, z + 1 + s))


def greet_near(px, py, up, down, z, nz):
    barrier = pltpu.get_barrier_semaphore()
    for peer, there in ((px, None), (py, None), (up, z + 1 < nz), (down, z > 0)):

        def hello(peer=peer):
            pl.semaphore_signal(barrier, inc=1, device_id={"ep": peer}, device_id_type=MESH)

        hello() if there is None else pl.when(there)(hello)
    on_line = (z + 1 < nz).astype(jnp.int32) + (z > 0).astype(jnp.int32)
    pl.semaphore_wait(barrier, 2 + on_line)


def start_swaps(n, ins, outs, sems):
    own, ss, rs = sems
    me = lax.axis_index("ep")
    sends, copies = [], []
    for j in range(len(ins)):
        local = pltpu.make_async_copy(ins[j].at[me], outs[j].at[me], own.at[j])
        local.start()
        copies.append(local)
    for k in range(1, n):
        to = (me + k) % n
        for j in range(len(ins)):
            c = remote(ins[j].at[to], outs[j].at[me], ss.at[j, k], rs.at[j, k], to)
            c.start()
            sends.append(c)
    return sends, copies


def end_swaps(n, ins, outs, sems, started):
    own, ss, rs = sems
    me = lax.axis_index("ep")
    sends, copies = started
    for k in range(1, n):
        to, back = (me + k) % n, (me + n - k) % n
        for j in range(len(ins)):
            remote(ins[j].at[back], outs[j].at[back], ss.at[j, k], rs.at[j, k], to).wait_recv()
    for copy in sends:
        copy.wait_send()
    for copy in copies:
        copy.wait()


def gather_kernel(n, w, x_ref, *refs):
    swaps_in, o_ref, swaps_out = refs[:w], refs[w], refs[w + 1 : 2 * w + 1]
    own, us, ur, ds, dr, xs, xr, ys, yr, *swap_sems = refs[2 * w + 1 :]
    me, z, y, x, px, py = around(n)
    nz = n // 4
    low = me % 4
    half = x_ref.shape[0] // 2
    top, bottom = pl.ds(0, half), pl.ds(half, half)
    up, down = (me + 4) % n, (me + n - 4) % n
    everyone = [(me + k) % n for k in range(n)]
    if w:
        greet(everyone[1:])
    else:
        greet_near(px, py, up, down, z, nz)
    local = pltpu.make_async_copy(x_ref, o_ref.at[me], own)
    local.start()

    def over_x(src, b, part, i):
        return remote(src.at[part], o_ref.at[b, part], xs.at[i], xr.at[i], px)

    def over_y(src, b, part, i):
        return remote(src.at[part], o_ref.at[b, part], ys.at[i], yr.at[i], py)

    def upward(src, b, s):
        return remote(src, o_ref.at[b], us.at[s], ur.at[s], up)

    def downward(src, b, s):
        return remote(src, o_ref.at[b], ds.at[s], dr.at[s], down)

    def spread(src, t):
        b = t * 4 + low
        over_x(src, b, top, t).start()
        over_y(src, b, bottom, t).start()
        over_y(src, b, top, nz + t).start()
        over_x(src, b, bottom, nz + t).start()

    pl.when(z + 1 < nz)(lambda: upward(x_ref, me, 0).start())
    pl.when(z > 0)(lambda: downward(x_ref, me, 0).start())
    spread(x_ref, z)
    swapping = start_swaps(n, swaps_in, swaps_out, swap_sems) if w else None

    def from_below(s, t):
        b = t * 4 + low
        upward(o_ref.at[b], b, s).wait_recv()
        pl.when(z + 1 < nz)(lambda: upward(o_ref.at[b], b, s + 1).start())
        spread(o_ref.at[b], t)

    def from_above(s, t):
        b = t * 4 + low
        downward(o_ref.at[b], b, s).wait_recv()
        pl.when(z > 0)(lambda: downward(o_ref.at[b], b, s + 1).start())
        spread(o_ref.at[b], t)

    def turn(s, t):
        bx = t * 4 + low + px - me
        by = t * 4 + low + py - me
        over_x(o_ref.at[bx], bx, top, t).wait_recv()
        over_y(o_ref.at[bx], bx, top, 2 * nz + t).start()
        over_y(o_ref.at[by], by, bottom, t).wait_recv()
        over_x(o_ref.at[by], by, bottom, 2 * nz + t).start()

    for s in range(nz - 1):
        pl.when(z - 1 - s >= 0)(functools.partial(from_below, s, z - 1 - s))
        pl.when(z + 1 + s < nz)(functools.partial(from_above, s, z + 1 + s))
        if s == 0:
            turn(0, z)
        else:
            pl.when(z - s >= 0)(functools.partial(turn, s, z - s))
            pl.when(z + s < nz)(functools.partial(turn, s, z + s))
    pl.when(z - (nz - 1) >= 0)(functools.partial(turn, 0, z - (nz - 1)))
    pl.when(z + (nz - 1) < nz)(functools.partial(turn, 0, z + (nz - 1)))

    def finish(s, t):
        bx = t * 4 + low + px - me
        by = t * 4 + low + py - me
        bxy = bx + py - me
        over_y(o_ref.at[by], by, top, nz + t).wait_recv()
        over_x(o_ref.at[bx], bx, bottom, nz + t).wait_recv()
        over_y(o_ref.at[bxy], bxy, top, 2 * nz + t).wait_recv()
        over_x(o_ref.at[bxy], bxy, bottom, 2 * nz + t).wait_recv()
        for i in range(3):
            over_x(x_ref, me, top, i * nz + t).wait_send()
            over_y(x_ref, me, top, i * nz + t).wait_send()

    finish(0, z)
    near(z, nz, finish, finish)

    def sent_up(s, t):
        upward(x_ref, me, s).wait_send()

    def sent_down(s, t):
        downward(x_ref, me, s).wait_send()

    for s in range(nz - 1):
        pl.when((z + 1 < nz) & (z - s >= 0))(functools.partial(sent_up, s, z))
        pl.when((z > 0) & (z + s < nz))(functools.partial(sent_down, s, z))
    local.wait()
    if w:
        end_swaps(n, swaps_in, swaps_out, swap_sems, swapping)


def gather(x, cid, swaps=()):
    n = lax.axis_size("ep")
    w = len(swaps)
    nz = n // 4
    return pl.pallas_call(
        functools.partial(gather_kernel, n, w),
        out_shape=[jax.ShapeDtypeStruct((n,) + x.shape, x.dtype)]
        + [jax.ShapeDtypeStruct(a.shape, a.dtype) for a in swaps],
        in_specs=[ANY] * (1 + w),
        out_specs=[ANY] * (1 + w),
        scratch_shapes=[DMA]
        + [DMA((nz,))] * 4
        + [DMA((3 * nz,))] * 4
        + ([DMA((w,)), DMA((w, n)), DMA((w, n))] if w else []),
        compiler_params=pltpu.CompilerParams(collective_id=cid, has_side_effects=True),
        name="gather",
    )(x, *swaps)


def add_rows(dst, left, right, rows):
    step = 16

    def body(i, carry):
        r = pl.ds(pl.multiple_of(i * step, step), step)
        dst[r] = (left[r].astype(F32) + right[r].astype(F32)).astype(dst.dtype)
        return carry

    lax.fori_loop(0, rows // step, body, 0)


TILE = 128


def exchange_kernel(n, m, w, laid, jobs, *refs):
    refs = list(refs)

    def take(count):
        out = refs[:count]
        del refs[:count]
        return out

    sums_in, swaps_in = take(m), take(w)
    jobs_in = [take(2) for _ in jobs]
    sums_out, swaps_out, jobs_out = take(m), take(w), [take(parts) for parts in jobs]
    room = [take(7) for _ in range(m)]
    sems = [take(8) for _ in range(m)]
    swap_sems = take(3) if w else None
    side_by_side = swaps_out[w - laid :]
    swaps_out = swaps_out[: w - laid] + take(laid)
    desks = [take(5) for _ in jobs]
    me, z, y, x, px, py = around(n)
    nz = n // 4
    low = me % 4
    to = [(z + k) % nz for k in range(nz)]
    at = [t * 4 + low for t in to]
    if w:
        greet([(me + k) % n for k in range(1, n)])
    else:
        greet([px, py] + at[1:])
    order = [2, 1, 3, 0] if nz == 4 else list(range(1, nz)) + [0]
    sends = []

    def halves(j):
        half = sums_in[j].shape[3] // 2
        return half, pl.ds(0, half), pl.ds(half, half)

    first, second, third = {}, {}, {}

    def stage_one(j, k):
        p = sums_in[j]
        half, top, bottom = halves(j)
        la, lb, a1, b1, a2, b2, zb = room[j]
        lsa, lsb, xs, xr, ys, yr, zs, zr = sems[j]
        t = to[k]
        c = remote(p.at[t, 1 - y, :, top], a1.at[k], ys.at[k], yr.at[k], py)
        d = remote(p.at[t, :, 1 - x, bottom], b1.at[k], xs.at[k], xr.at[k], px)
        c.start()
        d.start()
        e = pltpu.make_async_copy(p.at[t, y, :, top], la.at[k], lsa.at[k])
        f = pltpu.make_async_copy(p.at[t, :, x, bottom], lb.at[k], lsb.at[k])
        e.start()
        f.start()
        first[j, k] = (c, d, e, f)
        sends.extend([c, d])

    def stage_two(j, k):
        half, top, bottom = halves(j)
        la, lb, a1, b1, a2, b2, zb = room[j]
        lsa, lsb, xs, xr, ys, yr, zs, zr = sems[j]
        c, d, e, f = first[j, k]
        e.wait()
        c.wait_recv()
        for i in range(2):
            add_rows(la.at[k, i], la.at[k, i], a1.at[k, i], half)
        g = remote(la.at[k, 1 - x], a2.at[k], xs.at[nz + k], xr.at[nz + k], px)
        g.start()
        f.wait()
        d.wait_recv()
        for i in range(2):
            add_rows(lb.at[k, i], lb.at[k, i], b1.at[k, i], half)
        h = remote(lb.at[k, 1 - y], b2.at[k], ys.at[nz + k], yr.at[nz + k], py)
        h.start()
        second[j, k] = (g, h)
        sends.extend([g, h])

    def stage_three(j, k):
        half, top, bottom = halves(j)
        la, lb, a1, b1, a2, b2, zb = room[j]
        lsa, lsb, xs, xr, ys, yr, zs, zr = sems[j]
        g, h = second[j, k]
        g.wait_recv()
        add_rows(a2.at[k], la.at[k, x], a2.at[k], half)
        if k:
            c = remote(a2.at[k], zb.at[k, top], zs.at[k], zr.at[k], at[k])
            c.start()
        h.wait_recv()
        add_rows(b2.at[k], lb.at[k, y], b2.at[k], half)
        if k:
            d = remote(b2.at[k], zb.at[k, bottom], zs.at[nz + k], zr.at[nz + k], at[k])
            d.start()
            third[j, k] = (c, d)
            sends.extend([c, d])

    loads = []
    for (left, right), (left_v, right_v, page, in_sem, out_sem) in zip(jobs_in, desks):
        for i, (src, dst) in enumerate(((left, left_v), (right, right_v))):
            loads.append(pltpu.make_async_copy(src, dst, in_sem.at[i]))

    def writes(j, i):
        left_v, right_v, page, in_sem, out_sem = desks[j]
        slot = i % 2
        rows = pl.ds(pl.multiple_of(i * TILE, TILE), TILE)
        return [
            pltpu.make_async_copy(page.at[slot, part], out.at[rows], out_sem.at[slot, part])
            for part, out in enumerate(jobs_out[j])
        ]

    def tile(j, i):
        left_v, right_v, page, in_sem, out_sem = desks[j]
        value = lax.dot_general(
            left_v[:, pl.ds(pl.multiple_of(i * TILE, TILE), TILE)],
            right_v[...],
            (((0,), (0,)), ((), ())),
            preferred_element_type=F32,
        ).astype(page.dtype)
        width = page.shape[3]
        for part, write in enumerate(writes(j, i)):
            pl.when(i >= 2)(write.wait)
            page[i % 2, part] = value[:, part * width : (part + 1) * width]
            write.start()

    tiles = [desk[0].shape[1] // TILE for desk in desks]
    loaded = []

    def work(step, of):
        first, last = sum(tiles) * step // of, sum(tiles) * (step + 1) // of
        for j in range(len(jobs)):
            start = sum(tiles[:j])
            low, high = max(first - start, 0), min(last - start, tiles[j])
            if low >= high:
                continue
            if j not in loaded:
                loaded.append(j)
                loads[2 * j].wait()
                loads[2 * j + 1].wait()
            lax.fori_loop(low, high, lambda i, c, j=j: (tile(j, i), c)[1], 0)

    steps = [(j, k) for j in range(m) for k in order]
    ahead = 3 if jobs else 2
    for i in range(min(ahead, len(steps))):
        stage_one(*steps[i])
    for copy in loads:
        copy.start()
    if w:
        swapping = start_swaps(n, swaps_in, swaps_out, swap_sems)
    for i, step in enumerate(steps):
        stage_two(*step)
        if i + ahead < len(steps):
            stage_one(*steps[i + ahead])
        if i:
            stage_three(*steps[i - 1])
        work(i, len(steps))
    if steps:
        stage_three(*steps[-1])
    if w:
        end_swaps(n, swaps_in, swaps_out, swap_sems, swapping)
        for wide, got in zip(side_by_side, swaps_out[w - laid :]):
            width = got.shape[2]
            for k in range(n):
                wide[:, k * width : (k + 1) * width] = got[k].astype(F32)
    for j in range(m):
        half, top, bottom = halves(j)
        la, lb, a1, b1, a2, b2, zb = room[j]
        o_ref = sums_out[j]
        for k in range(1, nz):
            c, d = third[j, k]
            c.wait_recv()
            d.wait_recv()
        for part, offset in ((a2, 0), (b2, half)):

            def body(i, carry, part=part, offset=offset, zb=zb, o_ref=o_ref):
                r = pl.ds(pl.multiple_of(i * 16, 16), 16)
                q = pl.ds(pl.multiple_of(i * 16 + offset, 16), 16)
                total = part[0, r].astype(F32)
                for k in range(1, nz):
                    total = total + zb[k, q].astype(F32)
                o_ref[q] = total.astype(o_ref.dtype)
                return carry

            lax.fori_loop(0, half // 16, body, 0)
    for copy in sends:
        copy.wait_send()
    for j in range(len(jobs)):
        for i in range(min(2, tiles[j])):
            for write in writes(j, i):
                write.wait()


def exchange(cid, sums=(), swaps=(), laid=0, jobs=()):
    n = lax.axis_size("ep")
    nz = n // 4
    m, w = len(sums), len(swaps)
    kept_rows = [p.shape[1] for p in sums]
    sums = [jnp.pad(p, ((0, 0), (0, -p.shape[1] % 32), (0, 0))) for p in sums]
    views = [p.reshape((nz, 2, 2) + p.shape[1:]) for p in sums]
    scratch = []
    for p in sums:
        rows, cols = p.shape[1:]
        half = rows // 2
        scratch += [pltpu.VMEM((nz, 2, half, cols), p.dtype)] * 4
        scratch += [pltpu.VMEM((nz, half, cols), p.dtype)] * 2
        scratch += [pltpu.VMEM((nz, rows, cols), p.dtype)]
    for p in sums:
        scratch += [DMA((nz,))] * 2 + [DMA((2 * nz,))] * 6
    if w:
        scratch += [DMA((w,)), DMA((w, n)), DMA((w, n))]
    plain, wide = swaps[: w - laid], swaps[w - laid :]
    scratch += [pltpu.VMEM(a.shape, a.dtype) for a in wide]
    for left, right, parts in jobs:
        scratch += [pltpu.VMEM(left.shape, left.dtype), pltpu.VMEM(right.shape, right.dtype)]
        scratch += [pltpu.VMEM((2, parts, TILE, right.shape[1] // parts), BF16)]
        scratch += [DMA((2,)), DMA((2, parts))]
    out = pl.pallas_call(
        functools.partial(exchange_kernel, n, m, w, laid, [parts for _, _, parts in jobs]),
        out_shape=[jax.ShapeDtypeStruct(p.shape[1:], F32) for p in sums]
        + [jax.ShapeDtypeStruct(a.shape, a.dtype) for a in plain]
        + [jax.ShapeDtypeStruct((a.shape[1], n * a.shape[2]), F32) for a in wide]
        + [
            jax.ShapeDtypeStruct((a.shape[1], b.shape[1] // parts), BF16)
            for a, b, parts in jobs
            for _ in range(parts)
        ],
        in_specs=[ANY] * (m + w + 2 * len(jobs)),
        out_specs=[pl.BlockSpec(memory_space=pltpu.VMEM)] * m
        + [ANY] * (w - laid)
        + [pl.BlockSpec(memory_space=pltpu.VMEM)] * laid
        + [ANY] * sum(parts for _, _, parts in jobs),
        scratch_shapes=scratch,
        compiler_params=pltpu.CompilerParams(
            collective_id=cid, has_side_effects=True, vmem_limit_bytes=(60 if jobs else 40) << 20 if m else None
        ),
        name="exchange",
    )(*views, *swaps, *(a for job in jobs for a in job[:2]))
    return [a[:rows] for a, rows in zip(out, kept_rows)] + list(out[m:])


def both(p):
    g = lax.axis_index("grp")
    mine = lax.dynamic_index_in_dim(p, g, 0, keepdims=False)
    theirs = lax.dynamic_index_in_dim(p, 1 - g, 0, keepdims=False)
    return mine, lax.ppermute(theirs.astype(BF16), "grp", [(0, 1), (1, 0)])


def over_groups(p):
    if lax.axis_size("grp") == 2:
        mine, other = both(p)
        return mine.astype(F32) + other.astype(F32)
    return lax.psum_scatter(p.astype(BF16), "grp", scatter_dimension=0, tiled=False).astype(F32)


def product_over_groups(left, right):
    groups = lax.axis_size("grp")
    rows = left.shape[1] // groups
    if groups != 2:
        whole = product("km,kn->mn", left, right)
        return over_groups(whole.reshape(groups, rows, -1))
    g = lax.axis_index("grp")
    mine = lax.dynamic_slice_in_dim(left, g * rows, rows, 1)
    theirs = lax.dynamic_slice_in_dim(left, (1 - g) * rows, rows, 1)
    sent = product("km,kn->mn", theirs, right).astype(BF16)
    other = lax.ppermute(sent, "grp", [(0, 1), (1, 0)])
    return product("km,kn->mn", mine, right) + other.astype(F32)


def from_partner(values):
    groups = lax.axis_size("grp")
    return lax.ppermute(values, "grp", [(g, g + 1 - 2 * (g % 2)) for g in range(groups)])


def to_row_owner(block):
    groups, n = lax.axis_size("grp"), lax.axis_size("ep")
    pairs = [(h * n + e, e * groups + h) for h in range(groups) for e in range(n)]
    return lax.ppermute(block.astype(BF16), ("grp", "ep"), pairs).astype(F32)


def dot(left, right):
    return jnp.dot(left, right, preferred_element_type=F32)


def dot_nt(left, right):
    return lax.dot_general(left, right, (((1,), (1,)), ((), ())), preferred_element_type=F32)


def front_kernel(
    x_ref, cos_ref, sin_ref, gain_ref, lat_gain_ref, wq_ref, wl_ref, we_ref,
    normed_ref, query_ref, keys_ref, values_ref, latent_ref,
):
    blocks, tokens = x_ref.shape[:2]
    rows = blocks * tokens
    x = x_ref[...].reshape(rows, gain_ref.shape[1]).astype(F32)
    normed = (x * rms_scale(x) * gain_ref[...]).astype(BF16)
    normed_ref[...] = normed
    cos, sin = cos_ref[...], sin_ref[...]
    own_half = lax.broadcasted_iota(jnp.int32, cos.shape, 1) < ROPE

    def turn(pair):
        return pair * cos + pltpu.roll(pair, ROPE, 1) * sin

    query = dot_nt(normed, wq_ref[...])
    query_ref[:, :NOPE] = query[:, :NOPE].astype(BF16)
    query_ref[:, NOPE:] = jnp.where(own_half, turn(query[:, NOPE:]), 0.0).astype(BF16)
    compressed = dot(normed, wl_ref[...])
    raw = compressed[:, :LATENT]
    latent = (raw * rms_scale(raw) * lat_gain_ref[...]).astype(BF16)
    latent_ref[...] = latent
    expanded = dot(latent, we_ref[...])
    keys_ref[:, :NOPE] = expanded[:, :NOPE].astype(BF16)
    keys_ref[:, NOPE:] = turn(compressed[:, LATENT:]).astype(BF16)
    values_ref[...] = expanded[:, NOPE:].astype(BF16)


def front(x, cos, sin, gain, lat_gain, wq, wl, we):
    n, tokens = x.shape[:2]
    model = gain.shape[1]
    length = n * tokens
    blocks = 2
    rows = blocks * tokens

    def whole(a):
        return pl.BlockSpec(a.shape, lambda i: (0,) * a.ndim, pipeline_mode=pl.Buffered(1))

    def rows_of(cols):
        return pl.BlockSpec((rows, cols), lambda i: (i, 0))

    def out(cols):
        return jax.ShapeDtypeStruct((length, cols), BF16)

    cols = (model, wq.shape[0], NOPE + 2 * ROPE, VH, LATENT)
    return pl.pallas_call(
        front_kernel,
        grid=(n // blocks,),
        in_specs=[
            pl.BlockSpec((blocks, tokens, model), lambda i: (i, 0, 0)),
            rows_of(2 * ROPE),
            rows_of(2 * ROPE),
        ]
        + [whole(a) for a in (gain, lat_gain, wq, wl, we)],
        out_specs=[rows_of(c) for c in cols],
        out_shape=[out(c) for c in cols],
        compiler_params=pltpu.CompilerParams(vmem_limit_bytes=48 << 20),
        name="front",
    )(x, cos, sin, gain, lat_gain, wq, wl, we)


def back_kernel(
    cos_ref, sin_ref, dq_ref, dk_ref, dv_ref, we_ref, query_ref, expanded_ref, latent_ref, rope_ref
):
    own_half = lax.broadcasted_iota(jnp.int32, cos_ref.shape, 1) < ROPE
    pair = dq_ref[:, NOPE:] * jnp.where(own_half, cos_ref[...], sin_ref[...])
    pair = jnp.where(own_half, pair + pltpu.roll(pair, ROPE, 1), 0.0)
    query_ref[:, :NOPE] = dq_ref[:, :NOPE].astype(BF16)
    query_ref[:, NOPE:] = pair.astype(BF16)
    expanded_ref[:, :NOPE] = dk_ref[:, :NOPE].astype(BF16)
    expanded_ref[:, NOPE:] = dv_ref[...].astype(BF16)
    latent_ref[...] = dot_nt(expanded_ref[...], we_ref[...]).astype(BF16)
    rope_ref[...] = dk_ref[:, NOPE:].astype(BF16)


def back(cos, sin, dq, dk, dv, we):
    length = dq.shape[0]
    rows = 512

    def rows_of(cols):
        return pl.BlockSpec((rows, cols), lambda i: (i, 0))

    def out(cols):
        return jax.ShapeDtypeStruct((length, cols), BF16)

    cols = (NOPE + 2 * ROPE, NOPE + VH, LATENT, 2 * ROPE)
    return pl.pallas_call(
        back_kernel,
        grid=(length // rows,),
        in_specs=[rows_of(a.shape[1]) for a in (cos, sin, dq, dk, dv)]
        + [pl.BlockSpec(we.shape, lambda i: (0, 0))],
        out_specs=[rows_of(c) for c in cols],
        out_shape=[out(c) for c in cols],
        compiler_params=pltpu.CompilerParams(vmem_limit_bytes=40 << 20),
        name="back",
    )(cos, sin, dq, dk, dv, we)


KEYS = 512


def scores_of(scale, prefix, k, q, first_key, first_query):
    scores = dot_nt(k, q) * scale
    key = first_key + lax.broadcasted_iota(jnp.int32, scores.shape, 0)
    query = first_query + lax.broadcasted_iota(jnp.int32, scores.shape, 1)
    return jnp.where((key <= query) | (key < prefix), scores, MASKED)


def key_blocks(prefix, last_query):
    return (jnp.maximum(last_query, prefix) + KEYS - 1) // KEYS


def attend_kernel(scale, prefix_ref, q_ref, k_ref, v_ref, attended_ref, exact_ref, lse_ref):
    q = q_ref[...]
    rows = q.shape[0]
    start = pl.program_id(0) * rows
    prefix = prefix_ref[0]

    def step(j, carry):
        top, total, out = carry
        s = scores_of(scale, prefix, k_ref[j], q, j * KEYS, start)
        new_top = jnp.maximum(top, jnp.max(s, axis=0, keepdims=True))
        p = jnp.exp(s - new_top)
        shrink = jnp.exp(top - new_top)
        total = total * shrink + jnp.sum(p, axis=0, keepdims=True)
        return new_top, total, out * shrink + dot(v_ref[j], p.astype(BF16))

    top, total, out = lax.fori_loop(
        0,
        key_blocks(prefix, start + rows),
        step,
        (
            jnp.full((1, rows), MASKED, F32),
            jnp.zeros((1, rows), F32),
            jnp.zeros((v_ref.shape[1], rows), F32),
        ),
    )
    lse_ref[...] = top + jnp.log(total)
    exact = (out / total).T
    exact_ref[...] = exact
    attended_ref[...] = exact.astype(BF16)


def attend(prefix, q, k, v):
    length, depth = q.shape
    values = v.shape[1]
    rows = 256
    v = v.reshape(length // KEYS, KEYS, values).transpose(0, 2, 1)
    k = k.reshape(length // KEYS, KEYS, depth)
    return pl.pallas_call(
        functools.partial(attend_kernel, 1.0 / math.sqrt(NOPE + ROPE)),
        grid=(length // rows,),
        in_specs=[
            pl.BlockSpec(memory_space=pltpu.SMEM),
            pl.BlockSpec((rows, depth), lambda i: (i, 0)),
            pl.BlockSpec(k.shape, lambda i: (0, 0, 0)),
            pl.BlockSpec(v.shape, lambda i: (0, 0, 0)),
        ],
        out_specs=[
            pl.BlockSpec((rows, values), lambda i: (i, 0)),
            pl.BlockSpec((rows, values), lambda i: (i, 0)),
            pl.BlockSpec((1, rows), lambda i: (0, i)),
        ],
        out_shape=[
            jax.ShapeDtypeStruct((length, values), BF16),
            jax.ShapeDtypeStruct((length, values), F32),
            jax.ShapeDtypeStruct((1, length), F32),
        ],
        compiler_params=pltpu.CompilerParams(vmem_limit_bytes=32 << 20),
        name="attend",
    )(prefix, q, k, v)


def attend_back_kernel(
    scale, prefix_ref, q_ref, g_ref, lse_ref, delta_ref, k_ref, v_ref, dq_ref, dk_ref, dv_ref
):
    q, g = q_ref[...], g_ref[...]
    rows = q.shape[0]
    start = pl.program_id(0) * rows
    prefix = prefix_ref[0]

    @pl.when(pl.program_id(0) == 0)
    def _():
        dk_ref[...] = jnp.zeros_like(dk_ref)
        dv_ref[...] = jnp.zeros_like(dv_ref)

    def step(j, dq):
        k = k_ref[j]
        p = jnp.exp(scores_of(scale, prefix, k, q, j * KEYS, start) - lse_ref[...])
        ds = (p * (dot_nt(v_ref[j], g) - delta_ref[...]) * scale).astype(BF16)
        dv_ref[j] += dot(p.astype(BF16), g)
        dk_ref[j] += dot(ds, q)
        return dq + lax.dot_general(
            ds, k, (((0,), (0,)), ((), ())), preferred_element_type=F32
        )

    dq_ref[...] = lax.fori_loop(
        0, key_blocks(prefix, start + rows), step, jnp.zeros(dq_ref.shape, F32)
    )


def attend_back(prefix, q, g, lse, delta, k, v):
    length, depth = q.shape
    values = v.shape[1]
    rows = 256
    k = k.reshape(length // KEYS, KEYS, depth)
    v = v.reshape(length // KEYS, KEYS, values)
    dq, dk, dv = pl.pallas_call(
        functools.partial(attend_back_kernel, 1.0 / math.sqrt(NOPE + ROPE)),
        grid=(length // rows,),
        in_specs=[
            pl.BlockSpec(memory_space=pltpu.SMEM),
            pl.BlockSpec((rows, depth), lambda i: (i, 0)),
            pl.BlockSpec((rows, values), lambda i: (i, 0)),
            pl.BlockSpec((1, rows), lambda i: (0, i)),
            pl.BlockSpec((1, rows), lambda i: (0, i)),
            pl.BlockSpec(k.shape, lambda i: (0, 0, 0)),
            pl.BlockSpec(v.shape, lambda i: (0, 0, 0)),
        ],
        out_specs=[
            pl.BlockSpec((rows, depth), lambda i: (i, 0)),
            pl.BlockSpec(k.shape, lambda i: (0, 0, 0)),
            pl.BlockSpec(v.shape, lambda i: (0, 0, 0)),
        ],
        out_shape=[
            jax.ShapeDtypeStruct((length, depth), F32),
            jax.ShapeDtypeStruct(k.shape, F32),
            jax.ShapeDtypeStruct(v.shape, F32),
        ],
        compiler_params=pltpu.CompilerParams(vmem_limit_bytes=40 << 20),
        name="attend_back",
    )(prefix, q, g, lse, delta, k, v)
    return dq, dk.reshape(length, depth), dv.reshape(length, values)


def ffn_kernel(
    n,
    x_ref,
    y_ref,
    slots_ref,
    tokens_ref,
    own_ref,
    router_ref,
    sg_ref,
    su_ref,
    sd_ref,
    eg_ref,
    eu_ref,
    ed_ref,
    out_ref,
    ffn_ref,
    dot_ref,
    probs_ref,
    rows_ref,
    hidden_ref,
    slot_grad_ref,
    grad_gu_ref,
    shared_h_ref,
    shared_gu_ref,
    expert_out,
    row_grad,
):
    blocks, tokens = x_ref.shape[:2]
    capacity = slots_ref.shape[1]
    own = own_ref[...]
    lanes = lax.broadcasted_iota(jnp.int32, (tokens, own.shape[1]), 1)
    gates = []
    for b in range(blocks):
        x, y = x_ref[b], y_ref[b]
        logits = jnp.where(lanes < n, dot(x, router_ref[...]), MASKED)
        raised = jnp.exp(logits - jnp.max(logits, axis=-1, keepdims=True))
        probs = raised / jnp.sum(raised, axis=-1, keepdims=True)
        probs_ref[b] = probs
        gate = jnp.sum(probs * own, axis=-1, keepdims=True)
        gates.append(gate)
        part = pl.ds(b * capacity, capacity)
        rows_ref[part] = dot(slots_ref[b], x).astype(BF16)
        weighted = (gate * y.astype(F32)).astype(BF16)
        slot_grad_ref[part] = dot(slots_ref[b], weighted).astype(BF16)
    rows = rows_ref[...]
    slot_grad = slot_grad_ref[...]
    g = dot(rows, eg_ref[...])
    u = dot(rows, eu_ref[...])
    sigmoid = 1.0 / (1.0 + jnp.exp(-g))
    silu = g * sigmoid
    hidden = (silu * u).astype(BF16)
    hidden_ref[...] = hidden
    expert_out[...] = dot(hidden, ed_ref[...]).astype(BF16)
    grad_hidden = dot_nt(slot_grad, ed_ref[...])
    grad_g = (grad_hidden * u * sigmoid * (1.0 + g * (1.0 - sigmoid))).astype(BF16)
    grad_u = (grad_hidden * silu).astype(BF16)
    grad_gu_ref[:, : grad_g.shape[1]] = grad_g
    grad_gu_ref[:, grad_g.shape[1] :] = grad_u
    row_grad[...] = (dot_nt(grad_g, eg_ref[...]) + dot_nt(grad_u, eu_ref[...])).astype(BF16)
    x = x_ref[...].reshape(blocks * tokens, -1)
    y = y_ref[...].reshape(blocks * tokens, -1)
    g = dot_nt(x, sg_ref[...])
    u = dot_nt(x, su_ref[...])
    grad_hidden = dot_nt(y, sd_ref[...])
    sigmoid = 1.0 / (1.0 + jnp.exp(-g))
    silu = g * sigmoid
    hidden = (silu * u).astype(BF16)
    grad_g = (grad_hidden * u * sigmoid * (1.0 + g * (1.0 - sigmoid))).astype(BF16)
    grad_u = (grad_hidden * silu).astype(BF16)
    shared = hidden.shape[1]
    shared_h_ref[...] = hidden.reshape(blocks, tokens, shared)
    shared_gu_ref[:, :, :shared] = grad_g.reshape(blocks, tokens, shared)
    shared_gu_ref[:, :, shared:] = grad_u.reshape(blocks, tokens, shared)
    width = x.shape[1]
    chunk = width // 4
    met = [0.0] * blocks
    for c in range(width // chunk):
        cols = pl.ds(c * chunk, chunk)
        shared_out = dot(hidden, sd_ref[:, cols])
        shared_ffn = dot(grad_g, sg_ref[:, cols]) + dot(grad_u, su_ref[:, cols])
        for b in range(blocks):
            part = pl.ds(b * capacity, capacity)
            here = slice(b * tokens, (b + 1) * tokens)
            picked = dot(tokens_ref[b], expert_out[part, cols])
            met[b] += jnp.sum(picked * y_ref[b, :, cols].astype(F32), axis=-1, keepdims=True)
            out_ref[b, :, cols] = (shared_out[here] + picked * gates[b]).astype(BF16)
            back = dot(tokens_ref[b], row_grad[part, cols])
            ffn_ref[b, :, cols] = (shared_ffn[here] + back).astype(BF16)
    for b in range(blocks):
        dot_ref[b] = (met[b] * own).astype(BF16)


def ffn(x, y, slots, own_lane, router_w, gate_t, up_t, down, gate_m, up_m, down_m):
    n, tokens, width = x.shape
    capacity = slots.shape[1]
    hidden = gate_m.shape[1]
    shared = gate_t.shape[0]
    group = 4

    def whole(a):
        return pl.BlockSpec(a.shape, lambda i: (0,) * a.ndim, pipeline_mode=pl.Buffered(1))

    def block(*shape):
        return pl.BlockSpec((group,) + shape, lambda i: (i, 0, 0))

    def slot_rows(cols):
        return pl.BlockSpec((group * capacity, cols), lambda i: (i, 0))

    def tokens_of(cols, kind=BF16):
        return jax.ShapeDtypeStruct((n, tokens, cols), kind)

    def slots_of(cols):
        return jax.ShapeDtypeStruct((n * capacity, cols), BF16)

    weights = (own_lane, router_w, gate_t, up_t, down, gate_m, up_m, down_m)
    return pl.pallas_call(
        functools.partial(ffn_kernel, n),
        grid=(n // group,),
        in_specs=[
            block(tokens, width),
            block(tokens, width),
            block(capacity, tokens),
            block(tokens, capacity),
        ]
        + [whole(a) for a in weights],
        out_specs=[
            block(tokens, width),
            block(tokens, width),
            block(tokens, 128),
            block(tokens, 128),
            slot_rows(width),
            slot_rows(hidden),
            slot_rows(width),
            slot_rows(2 * hidden),
            block(tokens, shared),
            block(tokens, 2 * shared),
        ],
        out_shape=[
            tokens_of(width),
            tokens_of(width),
            tokens_of(128),
            tokens_of(128, F32),
            slots_of(width),
            slots_of(hidden),
            slots_of(width),
            slots_of(2 * hidden),
            tokens_of(shared),
            tokens_of(2 * shared),
        ],
        scratch_shapes=[
            pltpu.VMEM((group * capacity, width), BF16),
            pltpu.VMEM((group * capacity, width), BF16),
        ],
        compiler_params=pltpu.CompilerParams(vmem_limit_bytes=60 << 20),
        name="ffn",
    )(x, y, slots, slots.transpose(0, 2, 1), *weights)


def product(form, left, right):
    return jnp.einsum(form, left, right, preferred_element_type=F32)


def rms_scale(values):
    return lax.rsqrt(jnp.mean(values * values, axis=-1, keepdims=True) + EPSILON)


def rotary_tables(tokens, n):
    halfway = ROPE // 2
    inverse = 10000.0 ** (-(jnp.arange(halfway, dtype=F32) * 2.0 / ROPE))
    inverse = jnp.concatenate([inverse] * 4)
    lane = jnp.arange(2 * ROPE)
    sign = jnp.where((lane < halfway) | (lane >= 3 * halfway), -1.0, 1.0)
    base = (jnp.arange(n, dtype=F32) * tokens)[:, None] * inverse
    step = jnp.arange(tokens, dtype=F32)[:, None] * inverse
    base_cos, base_sin = jnp.cos(base)[:, None], jnp.sin(base)[:, None]
    step_cos, step_sin = jnp.cos(step)[None], jnp.sin(step)[None]
    cos_table = base_cos * step_cos - base_sin * step_sin
    sin_table = (base_sin * step_cos + base_cos * step_sin) * sign
    return cos_table.reshape(n * tokens, -1), sin_table.reshape(n * tokens, -1)


def unrotate(grads, cos_table, sin_table):
    halfway = grads.shape[-1] // 2
    first = grads[..., :halfway]
    second = grads[..., halfway:]
    return jnp.concatenate(
        [first * cos_table + second * sin_table, second * cos_table - first * sin_table], axis=-1
    )


def norm_back(grad_unit, unit_values, scale_values):
    return scale_values * (
        grad_unit - unit_values * jnp.mean(grad_unit * unit_values, axis=-1, keepdims=True)
    )


def column_halves(weight, n, half):
    rows, width = weight.shape[0], weight.shape[1] // n
    parts = weight.T.reshape(n, 2, width // 2, rows)
    return lax.dynamic_index_in_dim(parts, half, 1, keepdims=False)


def columns_in(blocks):
    n, width, rows = blocks.shape
    return blocks.transpose(1, 0, 2).reshape(width, n * rows)


def both_halves(mine, other, even, axis=0):
    return jnp.concatenate([jnp.where(even, mine, other), jnp.where(even, other, mine)], axis=axis)


def per_device(
    layer_input,
    attention_gain,
    query_weight,
    latent_weight,
    latent_gain,
    expand_weight,
    output_weight,
    feedforward_gain,
    router_weight,
    shared_gate,
    shared_up,
    shared_down,
    expert_gate,
    expert_up,
    expert_down,
    expert_routes,
    prefix_length,
    output_grad,
):
    n = lax.axis_size("ep")
    groups = lax.axis_size("grp")
    e = lax.axis_index("ep")
    half = lax.axis_index("grp") % 2
    even = half == 0
    tokens = layer_input.shape[0]
    length = tokens * n
    capacity = tokens * TOPK * 4 // (3 * n)
    rows_dev = attention_gain.shape[0]
    latent_rows = latent_gain.shape[0]
    rows_out = D // (groups * n)
    expand_rows = LATENT // (groups * n)

    pad = jnp.zeros((rows_dev - latent_rows,), BF16)
    first_block = jnp.concatenate(
        [
            layer_input,
            latent_weight,
            router_weight,
            attention_gain[:, None],
            feedforward_gain[:, None],
            jnp.concatenate([latent_gain, pad])[:, None],
            expert_routes.astype(BF16),
        ],
        axis=1,
    )
    width = first_block.shape[1]
    out_w_half = lax.dynamic_slice_in_dim(output_weight, half * (D // 2), D // 2, 1)
    first_block = jnp.concatenate(
        [first_block, jnp.zeros((tokens, -width % 128), BF16), out_w_half], axis=1
    )
    shared_half = jnp.where(even, shared_gate, shared_up)
    expand_half = lax.dynamic_index_in_dim(
        expand_weight.reshape(latent_rows, n, 2, -1), half, 2, keepdims=False
    ).transpose(1, 0, 2)
    first_all, q_blocks, x_blocks, shared_blocks = gather(
        first_block,
        0,
        swaps=(
            column_halves(query_weight, n, half),
            expand_half,
            shared_half.T.reshape(n, shared_half.shape[1] // n, rows_dev),
        ),
    )
    c0 = D
    c1 = c0 + LATENT + ROPE
    c2 = c1 + n
    latent_w = first_all[:, :, c0:c1].reshape(D, LATENT + ROPE)
    router_w = first_all[:, :, c1:c2].reshape(D, n)
    attn_gain = first_all[:, :, c2].reshape(D).astype(F32)
    ffn_gain = first_all[:, :, c2 + 1].reshape(D).astype(F32)
    lat_gain = first_all[:, :latent_rows, c2 + 2].reshape(LATENT).astype(F32)
    routes = first_all[:, :, c2 + 3 : c2 + 3 + TOPK].astype(jnp.int32)

    out_w_mine = first_all[:, :, -(D // 2) :].reshape(D, D // 2)
    out_w_other = from_partner(out_w_mine)
    later_grad, q_blocks = lax.optimization_barrier((output_grad, q_blocks))
    all_out_grad = lax.all_gather(later_grad, "ep", axis=0, tiled=True)

    q_mine, x_mine = columns_in(q_blocks), x_blocks.reshape(LATENT, -1)
    query_t = both_halves(q_mine, from_partner(q_mine), even)
    expand_w = both_halves(x_mine, from_partner(x_mine), even, 1)
    shared_mine = columns_in(shared_blocks)
    shared_other = from_partner(shared_mine)
    gate_t = jnp.where(even, shared_mine, shared_other)
    up_t = jnp.where(even, shared_other, shared_mine)

    def own(values):
        return lax.dynamic_slice_in_dim(values, e * tokens, tokens, 0)

    cos_table, sin_table = rotary_tables(tokens, n)
    turned = jnp.concatenate(
        [query_t, query_t[NOPE + ROPE // 2 :], query_t[NOPE : NOPE + ROPE // 2]], axis=0
    )
    latent_turned = jnp.concatenate(
        [latent_w, latent_w[:, LATENT + ROPE // 2 :], latent_w[:, LATENT : LATENT + ROPE // 2]],
        axis=1,
    )
    normed, query, keys, values, latent = front(
        first_all, cos_table, sin_table, attn_gain[None], lat_gain[None], turned, latent_turned, expand_w
    )
    attended_head, attended_exact, lse = attend(prefix_length, query, keys, values)
    (attended_blocks,) = exchange(2, swaps=(attended_head.reshape(n, tokens, VH),))
    attended = attended_blocks.transpose(1, 0, 2).reshape(tokens, HEADS * VH)

    residual_in = layer_input.astype(F32)
    input_scale = rms_scale(residual_in)
    input_unit = residual_in * input_scale
    out_mine = product("ta,ad->td", attended, out_w_mine)
    out_other = product("ta,ad->td", attended, out_w_other)
    residual_mid = residual_in + jnp.concatenate(
        [jnp.where(even, out_mine, out_other), jnp.where(even, out_other, out_mine)], axis=1
    )
    mid_scale = rms_scale(residual_mid)
    mid_unit = residual_mid * mid_scale
    own_ffn_in = (mid_unit * ffn_gain).astype(BF16)
    (ffn_blocks,) = gather(own_ffn_in, 3)
    query_cols = query_weight.shape[1] // 2
    query_w_half = lax.dynamic_slice_in_dim(query_weight, half * query_cols, query_cols, 1)
    query_w_half, ffn_blocks = lax.optimization_barrier((query_w_half, ffn_blocks))
    query_w_mine = lax.all_gather(query_w_half, "ep", axis=0, tiled=True)
    query_w_other = from_partner(query_w_mine)
    ffn_in = ffn_blocks.reshape(length, D)

    own_lane = (jnp.arange(128, dtype=jnp.int32) == e).astype(F32)[None]
    chosen = jnp.any(routes == e, axis=-1)
    chosen_int = chosen.astype(jnp.int32)
    place = jnp.cumsum(chosen_int, axis=1) - chosen_int
    kept = chosen & (place < capacity)
    dispatch = (
        (place[:, None, :] == jnp.arange(capacity, dtype=jnp.int32)[None, :, None])
        & kept[:, None, :]
    ).astype(BF16)
    shared_width = gate_t.shape[0]
    fill = ((0, -shared_width % 128), (0, 0))
    (
        out_partial,
        ffn_partial,
        dot_partial,
        router_all,
        incoming,
        expert_hidden,
        slot_grad,
        grad_expert_gu,
        shared_hidden,
        grad_shared_gu,
    ) = ffn(
        ffn_blocks,
        all_out_grad.reshape(n, tokens, D),
        dispatch,
        own_lane,
        jnp.pad(router_w, ((0, 0), (0, 128 - n))),
        jnp.pad(gate_t, fill),
        jnp.pad(up_t, fill),
        jnp.pad(shared_down, fill),
        expert_gate[0],
        expert_up[0],
        expert_down[0],
    )
    ffn_sum, dot_sum, out_sum, grad_down_m, grad_gate_m, grad_up_m = exchange(
        4,
        sums=(ffn_partial, dot_partial, out_partial),
        jobs=((expert_hidden, slot_grad, 1), (incoming, grad_expert_gu, 2)),
    )
    layer_output = (residual_mid + out_sum).astype(BF16)

    def by_group(values):
        return over_groups(values.reshape(groups, values.shape[0] // groups, -1))

    expert_down_grad = by_group(grad_down_m)[None]
    expert_gate_grad = by_group(grad_gate_m)[None]
    expert_up_grad = by_group(grad_up_m)[None]

    router_own = lax.dynamic_index_in_dim(router_all, e, 0, keepdims=False)[:, :n]
    grad_probs = dot_sum[:, :n]
    grad_logits = (
        router_own * (grad_probs - jnp.sum(router_own * grad_probs, axis=-1, keepdims=True))
    ).astype(BF16)
    grad_ffn_in = ffn_sum + product("te,de->td", grad_logits, router_w)
    grad_ffn_gain = jnp.sum(grad_ffn_in * mid_unit, axis=0)
    grad_mid = output_grad.astype(F32) + norm_back(grad_ffn_in * ffn_gain, mid_unit, mid_scale)
    grad_mid_b = grad_mid.astype(BF16)
    mid_left, mid_right = grad_mid_b[:, : D // 2], grad_mid_b[:, D // 2 :]
    grad_attended = (
        product("td,ad->ta", jnp.where(even, mid_left, mid_right), out_w_mine)
        + product("td,ad->ta", jnp.where(even, mid_right, mid_left), out_w_other)
    ).astype(BF16)
    output_w_partial = product_over_groups(attended, grad_mid_b).astype(BF16)
    output_w_partial, grad_attended = lax.optimization_barrier((output_w_partial, grad_attended))
    (grad_att_blocks,) = exchange(
        5, swaps=(grad_attended.reshape(tokens, HEADS, VH).transpose(1, 0, 2),)
    )
    output_w_partial, grad_att_blocks = lax.optimization_barrier(
        (output_w_partial, grad_att_blocks)
    )
    grad_att = grad_att_blocks.reshape(length, VH)
    output_weight_grad = lax.psum_scatter(
        output_w_partial.reshape(n, rows_out, D), "ep", scatter_dimension=0
    ).astype(F32)
    grad_router = product("te,td->ed", grad_logits, own_ffn_in)

    delta = jnp.sum(grad_att.astype(F32) * attended_exact, axis=-1)[None]
    grad_query_raw, grad_keys, grad_values = attend_back(
        prefix_length, query, grad_att, lse, delta, keys, values
    )
    grad_query, grad_expanded, latent_partial, rope_partial = back(
        cos_table, sin_table, grad_query_raw, grad_keys, grad_values, expand_w
    )
    (
        latent_sum,
        rope_sum,
        query_blocks,
        side_gate,
        side_up,
        side_down,
        side_query,
        side_expand,
    ) = exchange(
        6,
        sums=(
            latent_partial.reshape(n, tokens, LATENT),
            rope_partial.reshape(n, tokens, 2 * ROPE),
        ),
        swaps=(grad_query.reshape(n, tokens, -1),),
        jobs=(
            (ffn_in, grad_shared_gu.reshape(length, -1), 2),
            (shared_hidden.reshape(length, -1), all_out_grad, 1),
            (normed, grad_query, 1),
            (latent, grad_expanded, 1),
        ),
    )
    shared_down_grad = to_row_owner(by_group(side_down[:shared_width]))
    side_gate = by_group(side_gate)[:, :shared_width].astype(BF16)
    side_up = by_group(side_up)[:, :shared_width].astype(BF16)
    side_query = by_group(side_query)[:, : query_t.shape[0]].astype(BF16)
    grad_expand = by_group(side_expand).astype(BF16)

    own_normed = (input_unit * attn_gain).astype(BF16)
    own_raw = product("td,dc->tc", own_normed, latent_w[:, :LATENT])
    latent_scale = rms_scale(own_raw)
    latent_unit = own_raw * latent_scale
    grad_latent_gain = jnp.sum(latent_sum * latent_unit, axis=0)
    grad_compressed = jnp.concatenate(
        [
            norm_back(latent_sum * lat_gain, latent_unit, latent_scale),
            unrotate(
                rope_sum[:, :ROPE],
                own(cos_table)[:, : ROPE // 2],
                own(sin_table)[:, ROPE // 2 : ROPE],
            ),
        ],
        axis=-1,
    ).astype(BF16)
    latent_w_partial = product_over_groups(
        own_normed, jnp.pad(grad_compressed, ((0, 0), (0, 640 - LATENT - ROPE)))
    ).astype(BF16)
    own_part = product("tc,dc->td", grad_compressed, latent_w)

    def of_heads(part):
        heads = lax.dynamic_slice_in_dim(query_blocks, part * (n // 2), n // 2, 0)
        return heads[:, :, : NOPE + ROPE].transpose(1, 0, 2).reshape(tokens, -1)

    grad_normed = (
        product("tc,dc->td", of_heads(half), query_w_mine)
        + product("tc,dc->td", of_heads(1 - half), query_w_other)
        + own_part
    )
    grad_attn_gain = jnp.sum(grad_normed * input_unit, axis=0)

    def by_owner(values, rows):
        blocks = values.reshape(-1, groups, n, rows).transpose(2, 1, 0, 3)
        return blocks.reshape(n, groups, -1)

    small = jnp.concatenate(
        [
            by_owner(grad_attn_gain, rows_out),
            by_owner(grad_ffn_gain, rows_out),
            by_owner(grad_router, rows_out),
            by_owner(grad_latent_gain, expand_rows),
        ],
        axis=2,
    )
    small = small.transpose(1, 0, 2)
    if groups == 2:
        g = lax.axis_index("grp")
        mine = lax.dynamic_index_in_dim(small, g, 0, keepdims=False)
        theirs = lax.dynamic_index_in_dim(small, 1 - g, 0, keepdims=False)
        small = mine + lax.ppermute(theirs, "grp", [(0, 1), (1, 0)])
    else:
        small = lax.psum_scatter(small, "grp", scatter_dimension=0)
    (
        latent_weight_sum,
        small_all,
        query_weight_grad,
        shared_gate_grad,
        shared_up_grad,
        expand_weight_grad,
    ) = exchange(
        7,
        sums=(latent_w_partial.reshape(n, rows_out, -1),),
        swaps=(
            small[:, None],
            side_query.reshape(n, rows_out, -1),
            side_gate.reshape(n, rows_out, -1),
            side_up.reshape(n, rows_out, -1),
            grad_expand.reshape(n, expand_rows, -1),
        ),
        laid=4,
    )
    input_grad = (
        grad_mid + norm_back(grad_normed * attn_gain, input_unit, input_scale)
    ).astype(BF16)
    latent_weight_grad = latent_weight_sum[:, : LATENT + ROPE]
    small_sum = jnp.sum(small_all[:, 0], axis=0)
    attention_gain_grad = small_sum[:rows_out]
    feedforward_gain_grad = small_sum[rows_out : 2 * rows_out]
    router_weight_grad = small_sum[2 * rows_out : (2 + n) * rows_out].reshape(n, rows_out).T
    latent_gain_grad = small_sum[(2 + n) * rows_out :]
    return (
        layer_output,
        input_grad,
        attention_gain_grad,
        query_weight_grad,
        latent_weight_grad,
        latent_gain_grad,
        expand_weight_grad,
        output_weight_grad,
        feedforward_gain_grad,
        router_weight_grad,
        shared_gate_grad,
        shared_up_grad,
        shared_down_grad,
        expert_gate_grad,
        expert_up_grad,
        expert_down_grad,
    )


def solution(mesh):
    return jax.shard_map(
        per_device,
        mesh=mesh,
        in_specs=(
            P(("grp", "ep"), None),
            P("ep"),
            P("ep", None),
            P("ep", None),
            P("ep"),
            P("ep", None),
            P("ep", None),
            P("ep"),
            P("ep", None),
            P("ep", None),
            P("ep", None),
            P("ep", None),
            P("ep", None, None),
            P("ep", None, None),
            P("ep", None, None),
            P(("grp", "ep"), None),
            P("grp"),
            P(("grp", "ep"), None),
        ),
        out_specs=(
            P(("grp", "ep"), None),
            P(("grp", "ep"), None),
            P(("grp", "ep")),
            P(("grp", "ep"), None),
            P(("grp", "ep"), None),
            P(("grp", "ep")),
            P(("grp", "ep"), None),
            P(("grp", "ep"), None),
            P(("grp", "ep")),
            P(("grp", "ep"), None),
            P(("grp", "ep"), None),
            P(("grp", "ep"), None),
            P(("grp", "ep"), None),
            P("ep", "grp", None),
            P("ep", "grp", None),
            P("ep", "grp", None),
        ),
        check_vma=False,
    )
```

```python
import functools
import math

import jax
import jax.numpy as jnp
from jax import lax
from jax.experimental import pallas as pl
from jax.experimental.pallas import tpu as pltpu
from jax.sharding import PartitionSpec as P

D = 2048
HEADS = 16
NOPE = 128
ROPE = 64
VH = 128
LATENT = 512
TOPK = 6

EPSILON = 1e-06
MASKED = -1e30

MESH = pl.DeviceIdType.MESH
ANY = pl.BlockSpec(memory_space=pl.ANY)
DMA = pltpu.SemaphoreType.DMA
F32 = jnp.float32
BF16 = jnp.bfloat16


def remote(src, dst, send, recv, peer):
    return pltpu.make_async_remote_copy(
        src_ref=src,
        dst_ref=dst,
        send_sem=send,
        recv_sem=recv,
        device_id={"ep": peer},
        device_id_type=MESH,
    )


def greet(peers):
    barrier = pltpu.get_barrier_semaphore()
    for peer in peers:
        pl.semaphore_signal(barrier, inc=1, device_id={"ep": peer}, device_id_type=MESH)
    pl.semaphore_wait(barrier, len(peers))


def around(n):
    me = lax.axis_index("ep")
    x, y = me % 2, (me // 2) % 2
    return me, me // 4, y, x, me + 1 - 2 * x, me + 2 - 4 * y


def near(z, nz, below, above):
    for s in range(nz - 1):
        pl.when(z - 1 - s >= 0)(functools.partial(below, s, z - 1 - s))
        pl.when(z + 1 + s < nz)(functools.partial(above, s, z + 1 + s))


def greet_near(px, py, up, down, z, nz):
    barrier = pltpu.get_barrier_semaphore()
    for peer, there in ((px, None), (py, None), (up, z + 1 < nz), (down, z > 0)):

        def hello(peer=peer):
            pl.semaphore_signal(barrier, inc=1, device_id={"ep": peer}, device_id_type=MESH)

        hello() if there is None else pl.when(there)(hello)
    on_line = (z + 1 < nz).astype(jnp.int32) + (z > 0).astype(jnp.int32)
    pl.semaphore_wait(barrier, 2 + on_line)


def start_swaps(n, ins, outs, sems):
    own, ss, rs = sems
    me = lax.axis_index("ep")
    sends, copies = [], []
    for j in range(len(ins)):
        local = pltpu.make_async_copy(ins[j].at[me], outs[j].at[me], own.at[j])
        local.start()
        copies.append(local)
    for k in range(1, n):
        to = (me + k) % n
        for j in range(len(ins)):
            c = remote(ins[j].at[to], outs[j].at[me], ss.at[j, k], rs.at[j, k], to)
            c.start()
            sends.append(c)
    return sends, copies


def end_swaps(n, ins, outs, sems, started):
    own, ss, rs = sems
    me = lax.axis_index("ep")
    sends, copies = started
    for k in range(1, n):
        to, back = (me + k) % n, (me + n - k) % n
        for j in range(len(ins)):
            remote(ins[j].at[back], outs[j].at[back], ss.at[j, k], rs.at[j, k], to).wait_recv()
    for copy in sends:
        copy.wait_send()
    for copy in copies:
        copy.wait()


def gather_kernel(n, w, x_ref, *refs):
    swaps_in, o_ref, swaps_out = refs[:w], refs[w], refs[w + 1 : 2 * w + 1]
    own, us, ur, ds, dr, xs, xr, ys, yr, *swap_sems = refs[2 * w + 1 :]
    me, z, y, x, px, py = around(n)
    nz = n // 4
    low = me % 4
    half = x_ref.shape[0] // 2
    top, bottom = pl.ds(0, half), pl.ds(half, half)
    up, down = (me + 4) % n, (me + n - 4) % n
    everyone = [(me + k) % n for k in range(n)]
    if w:
        greet(everyone[1:])
    else:
        greet_near(px, py, up, down, z, nz)
    local = pltpu.make_async_copy(x_ref, o_ref.at[me], own)
    local.start()

    def over_x(src, b, part, i):
        return remote(src.at[part], o_ref.at[b, part], xs.at[i], xr.at[i], px)

    def over_y(src, b, part, i):
        return remote(src.at[part], o_ref.at[b, part], ys.at[i], yr.at[i], py)

    def upward(src, b, s):
        return remote(src, o_ref.at[b], us.at[s], ur.at[s], up)

    def downward(src, b, s):
        return remote(src, o_ref.at[b], ds.at[s], dr.at[s], down)

    def spread(src, t):
        b = t * 4 + low
        over_x(src, b, top, t).start()
        over_y(src, b, bottom, t).start()
        over_y(src, b, top, nz + t).start()
        over_x(src, b, bottom, nz + t).start()

    pl.when(z + 1 < nz)(lambda: upward(x_ref, me, 0).start())
    pl.when(z > 0)(lambda: downward(x_ref, me, 0).start())
    spread(x_ref, z)
    swapping = start_swaps(n, swaps_in, swaps_out, swap_sems) if w else None

    def from_below(s, t):
        b = t * 4 + low
        upward(o_ref.at[b], b, s).wait_recv()
        pl.when(z + 1 < nz)(lambda: upward(o_ref.at[b], b, s + 1).start())
        spread(o_ref.at[b], t)

    def from_above(s, t):
        b = t * 4 + low
        downward(o_ref.at[b], b, s).wait_recv()
        pl.when(z > 0)(lambda: downward(o_ref.at[b], b, s + 1).start())
        spread(o_ref.at[b], t)

    def turn(s, t):
        bx = t * 4 + low + px - me
        by = t * 4 + low + py - me
        over_x(o_ref.at[bx], bx, top, t).wait_recv()
        over_y(o_ref.at[bx], bx, top, 2 * nz + t).start()
        over_y(o_ref.at[by], by, bottom, t).wait_recv()
        over_x(o_ref.at[by], by, bottom, 2 * nz + t).start()

    for s in range(nz - 1):
        pl.when(z - 1 - s >= 0)(functools.partial(from_below, s, z - 1 - s))
        pl.when(z + 1 + s < nz)(functools.partial(from_above, s, z + 1 + s))
        if s == 0:
            turn(0, z)
        else:
            pl.when(z - s >= 0)(functools.partial(turn, s, z - s))
            pl.when(z + s < nz)(functools.partial(turn, s, z + s))
    pl.when(z - (nz - 1) >= 0)(functools.partial(turn, 0, z - (nz - 1)))
    pl.when(z + (nz - 1) < nz)(functools.partial(turn, 0, z + (nz - 1)))

    def finish(s, t):
        bx = t * 4 + low + px - me
        by = t * 4 + low + py - me
        bxy = bx + py - me
        over_y(o_ref.at[by], by, top, nz + t).wait_recv()
        over_x(o_ref.at[bx], bx, bottom, nz + t).wait_recv()
        over_y(o_ref.at[bxy], bxy, top, 2 * nz + t).wait_recv()
        over_x(o_ref.at[bxy], bxy, bottom, 2 * nz + t).wait_recv()
        for i in range(3):
            over_x(x_ref, me, top, i * nz + t).wait_send()
            over_y(x_ref, me, top, i * nz + t).wait_send()

    finish(0, z)
    near(z, nz, finish, finish)

    def sent_up(s, t):
        upward(x_ref, me, s).wait_send()

    def sent_down(s, t):
        downward(x_ref, me, s).wait_send()

    for s in range(nz - 1):
        pl.when((z + 1 < nz) & (z - s >= 0))(functools.partial(sent_up, s, z))
        pl.when((z > 0) & (z + s < nz))(functools.partial(sent_down, s, z))
    local.wait()
    if w:
        end_swaps(n, swaps_in, swaps_out, swap_sems, swapping)


def gather(x, cid, swaps=()):
    n = lax.axis_size("ep")
    w = len(swaps)
    nz = n // 4
    return pl.pallas_call(
        functools.partial(gather_kernel, n, w),
        out_shape=[jax.ShapeDtypeStruct((n,) + x.shape, x.dtype)]
        + [jax.ShapeDtypeStruct(a.shape, a.dtype) for a in swaps],
        in_specs=[ANY] * (1 + w),
        out_specs=[ANY] * (1 + w),
        scratch_shapes=[DMA]
        + [DMA((nz,))] * 4
        + [DMA((3 * nz,))] * 4
        + ([DMA((w,)), DMA((w, n)), DMA((w, n))] if w else []),
        compiler_params=pltpu.CompilerParams(collective_id=cid, has_side_effects=True),
        name="gather",
    )(x, *swaps)


def add_rows(dst, left, right, rows):
    step = 16

    def body(i, carry):
        r = pl.ds(pl.multiple_of(i * step, step), step)
        dst[r] = (left[r].astype(F32) + right[r].astype(F32)).astype(dst.dtype)
        return carry

    lax.fori_loop(0, rows // step, body, 0)


TILE = 128


def exchange_kernel(n, m, w, laid, groups, jobs, *refs):
    refs = list(refs)

    def take(count):
        out = refs[:count]
        del refs[:count]
        return out

    sums_in, swaps_in = take(m), take(w)
    jobs_in = [take(2) for _ in jobs]
    sums_out, swaps_out, jobs_out = take(m), take(w), [take(parts * blocks) for parts, blocks in jobs]
    room = [take(7) for _ in range(m)]
    sems = [take(8) for _ in range(m)]
    swap_sems = take(3) if w else None
    side_by_side = swaps_out[w - laid :]
    swaps_out = swaps_out[: w - laid] + take(laid)
    desks = [take(5) for _ in jobs]
    me, z, y, x, px, py = around(n)
    nz = n // 4
    low = me % 4
    to = [(z + k) % nz for k in range(nz)]
    at = [t * 4 + low for t in to]
    if w:
        greet([(me + k) % n for k in range(1, n)])
    else:
        greet([px, py] + at[1:])
    order = [2, 1, 3, 0] if nz == 4 else list(range(1, nz)) + [0]
    sends = []

    def halves(j):
        half = sums_in[j].shape[3] // 2
        return half, pl.ds(0, half), pl.ds(half, half)

    first, second, third = {}, {}, {}

    def stage_one(j, k):
        p = sums_in[j]
        half, top, bottom = halves(j)
        la, lb, a1, b1, a2, b2, zb = room[j]
        lsa, lsb, xs, xr, ys, yr, zs, zr = sems[j]
        t = to[k]
        c = remote(p.at[t, 1 - y, :, top], a1.at[k], ys.at[k], yr.at[k], py)
        d = remote(p.at[t, :, 1 - x, bottom], b1.at[k], xs.at[k], xr.at[k], px)
        c.start()
        d.start()
        e = pltpu.make_async_copy(p.at[t, y, :, top], la.at[k], lsa.at[k])
        f = pltpu.make_async_copy(p.at[t, :, x, bottom], lb.at[k], lsb.at[k])
        e.start()
        f.start()
        first[j, k] = (c, d, e, f)
        sends.extend([c, d])

    def stage_two(j, k):
        half, top, bottom = halves(j)
        la, lb, a1, b1, a2, b2, zb = room[j]
        lsa, lsb, xs, xr, ys, yr, zs, zr = sems[j]
        c, d, e, f = first[j, k]
        e.wait()
        c.wait_recv()
        for i in range(2):
            add_rows(la.at[k, i], la.at[k, i], a1.at[k, i], half)
        g = remote(la.at[k, 1 - x], a2.at[k], xs.at[nz + k], xr.at[nz + k], px)
        g.start()
        f.wait()
        d.wait_recv()
        for i in range(2):
            add_rows(lb.at[k, i], lb.at[k, i], b1.at[k, i], half)
        h = remote(lb.at[k, 1 - y], b2.at[k], ys.at[nz + k], yr.at[nz + k], py)
        h.start()
        second[j, k] = (g, h)
        sends.extend([g, h])

    def stage_three(j, k):
        half, top, bottom = halves(j)
        la, lb, a1, b1, a2, b2, zb = room[j]
        lsa, lsb, xs, xr, ys, yr, zs, zr = sems[j]
        g, h = second[j, k]
        g.wait_recv()
        add_rows(a2.at[k], la.at[k, x], a2.at[k], half)
        if k:
            c = remote(a2.at[k], zb.at[k, top], zs.at[k], zr.at[k], at[k])
            c.start()
        h.wait_recv()
        add_rows(b2.at[k], lb.at[k, y], b2.at[k], half)
        if k:
            d = remote(b2.at[k], zb.at[k, bottom], zs.at[nz + k], zr.at[nz + k], at[k])
            d.start()
            third[j, k] = (c, d)
            sends.extend([c, d])

    loads = []
    for (left, right), (left_v, right_v, page, in_sem, out_sem) in zip(jobs_in, desks):
        for i, (src, dst) in enumerate(((left, left_v), (right, right_v))):
            loads.append(pltpu.make_async_copy(src, dst, in_sem.at[i]))

    def pieces(j):
        parts, blocks = jobs[j]
        rows = jobs_out[j][0].shape[0]
        piece = math.gcd(TILE, rows)
        return [(q * piece, piece) for q in range(TILE // piece)]

    def start_write(j, i, part):
        left_v, right_v, page, in_sem, out_sem = desks[j]
        parts, blocks = jobs[j]
        outs = jobs_out[j][part * blocks : (part + 1) * blocks]
        rows = outs[0].shape[0]
        for q, (offset, piece) in enumerate(pieces(j)):
            row = i * TILE + offset
            src = page.at[i % 2, part, pl.ds(offset, piece)]
            owner = (row // rows + blocks - (lax.axis_index("grp") if blocks > 1 else 0)) % blocks
            inside = pl.ds(pl.multiple_of(row % rows, piece), piece)
            for k, out in enumerate(outs):
                copy = pltpu.make_async_copy(src, out.at[inside], out_sem.at[i % 2, part, q])
                if blocks > 1:
                    pl.when(owner == k)(copy.start)
                else:
                    copy.start()

    def wait_write(j, i, part):
        left_v, right_v, page, in_sem, out_sem = desks[j]
        for q, (offset, piece) in enumerate(pieces(j)):
            src = page.at[i % 2, part, pl.ds(offset, piece)]
            out = jobs_out[j][part * jobs[j][1]].at[pl.ds(0, piece)]
            pltpu.make_async_copy(src, out, out_sem.at[i % 2, part, q]).wait()

    def tile(j, i):
        left_v, right_v, page, in_sem, out_sem = desks[j]
        value = lax.dot_general(
            left_v[:, pl.ds(pl.multiple_of(i * TILE, TILE), TILE)],
            right_v[...],
            (((0,), (0,)), ((), ())),
            preferred_element_type=F32,
        ).astype(page.dtype)
        width = page.shape[3]
        for part in range(jobs[j][0]):
            pl.when(i >= 2)(functools.partial(wait_write, j, i, part))
            page[i % 2, part] = value[:, part * width : (part + 1) * width]
            start_write(j, i, part)

    tiles = [desk[0].shape[1] // TILE for desk in desks]
    loaded = []

    def work(step, of):
        first, last = sum(tiles) * step // of, sum(tiles) * (step + 1) // of
        for j in range(len(jobs)):
            start = sum(tiles[:j])
            low, high = max(first - start, 0), min(last - start, tiles[j])
            if low >= high:
                continue
            if j not in loaded:
                loaded.append(j)
                loads[2 * j].wait()
                loads[2 * j + 1].wait()
            lax.fori_loop(low, high, lambda i, c, j=j: (tile(j, i), c)[1], 0)

    steps = [(j, k) for j in range(m) for k in order]
    ahead = 3 if jobs else 2
    for i in range(min(ahead, len(steps))):
        stage_one(*steps[i])
    for copy in loads:
        copy.start()
    if w:
        swapping = start_swaps(n, swaps_in, swaps_out, swap_sems)
    for i, step in enumerate(steps):
        stage_two(*step)
        if i + ahead < len(steps):
            stage_one(*steps[i + ahead])
        if i:
            stage_three(*steps[i - 1])
        work(i, len(steps))
    if steps:
        stage_three(*steps[-1])
    if w:
        end_swaps(n, swaps_in, swaps_out, swap_sems, swapping)
        for wide, got in zip(side_by_side, swaps_out[w - laid :]):
            width = got.shape[2]
            for k in range(n):
                wide[:, k * width : (k + 1) * width] = got[k].astype(F32)
    for j in range(m):
        half, top, bottom = halves(j)
        la, lb, a1, b1, a2, b2, zb = room[j]
        o_ref = sums_out[j]
        for k in range(1, nz):
            c, d = third[j, k]
            c.wait_recv()
            d.wait_recv()
        for part, offset in ((a2, 0), (b2, half)):

            def body(i, carry, part=part, offset=offset, zb=zb, o_ref=o_ref):
                r = pl.ds(pl.multiple_of(i * 16, 16), 16)
                q = pl.ds(pl.multiple_of(i * 16 + offset, 16), 16)
                total = part[0, r].astype(F32)
                for k in range(1, nz):
                    total = total + zb[k, q].astype(F32)
                o_ref[q] = total.astype(o_ref.dtype)
                return carry

            lax.fori_loop(0, half // 16, body, 0)
    for copy in sends:
        copy.wait_send()
    for j in range(len(jobs)):
        for i in range(min(2, tiles[j])):
            for part in range(jobs[j][0]):
                wait_write(j, i, part)


def exchange(cid, sums=(), swaps=(), laid=0, jobs=()):
    n = lax.axis_size("ep")
    nz = n // 4
    groups = lax.axis_size("grp")
    m, w = len(sums), len(swaps)
    kept_rows = [p.shape[1] for p in sums]
    sums = [jnp.pad(p, ((0, 0), (0, -p.shape[1] % 32), (0, 0))) for p in sums]
    views = [p.reshape((nz, 2, 2) + p.shape[1:]) for p in sums]
    scratch = []
    for p in sums:
        rows, cols = p.shape[1:]
        half = rows // 2
        scratch += [pltpu.VMEM((nz, 2, half, cols), p.dtype)] * 4
        scratch += [pltpu.VMEM((nz, half, cols), p.dtype)] * 2
        scratch += [pltpu.VMEM((nz, rows, cols), p.dtype)]
    for p in sums:
        scratch += [DMA((nz,))] * 2 + [DMA((2 * nz,))] * 6
    if w:
        scratch += [DMA((w,)), DMA((w, n)), DMA((w, n))]
    plain, wide = swaps[: w - laid], swaps[w - laid :]
    scratch += [pltpu.VMEM(a.shape, a.dtype) for a in wide]
    jobs_out = []
    for left, right, parts, blocks in jobs:
        rows, cols = left.shape[1] // blocks, right.shape[1] // parts
        jobs_out += [jax.ShapeDtypeStruct((rows, cols), BF16)] * (parts * blocks)
        scratch += [pltpu.VMEM(left.shape, left.dtype), pltpu.VMEM(right.shape, right.dtype)]
        scratch += [pltpu.VMEM((2, parts, TILE, cols), BF16), DMA((2,))]
        scratch += [DMA((2, parts, TILE // math.gcd(TILE, rows)))]
    out = pl.pallas_call(
        functools.partial(exchange_kernel, n, m, w, laid, groups, [job[2:] for job in jobs]),
        out_shape=[jax.ShapeDtypeStruct(p.shape[1:], F32) for p in sums]
        + [jax.ShapeDtypeStruct(a.shape, a.dtype) for a in plain]
        + [jax.ShapeDtypeStruct((a.shape[1], n * a.shape[2]), F32) for a in wide]
        + jobs_out,
        in_specs=[ANY] * (m + w + 2 * len(jobs)),
        out_specs=[pl.BlockSpec(memory_space=pltpu.VMEM)] * m
        + [ANY] * (w - laid)
        + [pl.BlockSpec(memory_space=pltpu.VMEM)] * laid
        + [ANY] * len(jobs_out),
        scratch_shapes=scratch,
        compiler_params=pltpu.CompilerParams(
            collective_id=cid, has_side_effects=True, vmem_limit_bytes=(60 if jobs else 40) << 20 if m else None
        ),
        name="exchange",
    )(*views, *swaps, *(a for job in jobs for a in job[:2]))
    return [a[:rows] for a, rows in zip(out, kept_rows)] + list(out[m:])


def both(p):
    g = lax.axis_index("grp")
    mine = lax.dynamic_index_in_dim(p, g, 0, keepdims=False)
    theirs = lax.dynamic_index_in_dim(p, 1 - g, 0, keepdims=False)
    return mine, lax.ppermute(theirs.astype(BF16), "grp", [(0, 1), (1, 0)])


def over_groups(p):
    if lax.axis_size("grp") == 2:
        mine, other = both(p)
        return mine.astype(F32) + other.astype(F32)
    return lax.psum_scatter(p.astype(BF16), "grp", scatter_dimension=0, tiled=False).astype(F32)


def product_over_groups(left, right):
    groups = lax.axis_size("grp")
    rows = left.shape[1] // groups
    if groups != 2:
        whole = product("km,kn->mn", left, right)
        return over_groups(whole.reshape(groups, rows, -1))
    g = lax.axis_index("grp")
    mine = lax.dynamic_slice_in_dim(left, g * rows, rows, 1)
    theirs = lax.dynamic_slice_in_dim(left, (1 - g) * rows, rows, 1)
    sent = product("km,kn->mn", theirs, right).astype(BF16)
    other = lax.ppermute(sent, "grp", [(0, 1), (1, 0)])
    return product("km,kn->mn", mine, right) + other.astype(F32)


def from_partner(values):
    groups = lax.axis_size("grp")
    return lax.ppermute(values, "grp", [(g, g + 1 - 2 * (g % 2)) for g in range(groups)])


def to_row_owner(block):
    groups, n = lax.axis_size("grp"), lax.axis_size("ep")
    pairs = [(h * n + e, e * groups + h) for h in range(groups) for e in range(n)]
    return lax.ppermute(block.astype(BF16), ("grp", "ep"), pairs).astype(F32)


def dot(left, right):
    return jnp.dot(left, right, preferred_element_type=F32)


def dot_nt(left, right):
    return lax.dot_general(left, right, (((1,), (1,)), ((), ())), preferred_element_type=F32)


def front_kernel(
    x_ref, cos_ref, sin_ref, gain_ref, lat_gain_ref, wq_ref, wl_ref, we_ref,
    normed_ref, query_ref, keys_ref, values_ref, latent_ref,
):
    blocks, tokens = x_ref.shape[:2]
    rows = blocks * tokens
    x = x_ref[...].reshape(rows, gain_ref.shape[1]).astype(F32)
    normed = (x * rms_scale(x) * gain_ref[...]).astype(BF16)
    normed_ref[...] = normed
    cos, sin = cos_ref[...], sin_ref[...]
    own_half = lax.broadcasted_iota(jnp.int32, cos.shape, 1) < ROPE

    def turn(pair):
        return pair * cos + pltpu.roll(pair, ROPE, 1) * sin

    query = dot_nt(normed, wq_ref[...])
    query_ref[:, :NOPE] = query[:, :NOPE].astype(BF16)
    query_ref[:, NOPE:] = jnp.where(own_half, turn(query[:, NOPE:]), 0.0).astype(BF16)
    compressed = dot(normed, wl_ref[...])
    raw = compressed[:, :LATENT]
    latent = (raw * rms_scale(raw) * lat_gain_ref[...]).astype(BF16)
    latent_ref[...] = latent
    expanded = dot(latent, we_ref[...])
    keys_ref[:, :NOPE] = expanded[:, :NOPE].astype(BF16)
    keys_ref[:, NOPE:] = turn(compressed[:, LATENT:]).astype(BF16)
    values_ref[...] = expanded[:, NOPE:].astype(BF16)


def front(x, cos, sin, gain, lat_gain, wq, wl, we):
    n, tokens = x.shape[:2]
    model = gain.shape[1]
    length = n * tokens
    blocks = 2
    rows = blocks * tokens

    def whole(a):
        return pl.BlockSpec(a.shape, lambda i: (0,) * a.ndim, pipeline_mode=pl.Buffered(1))

    def rows_of(cols):
        return pl.BlockSpec((rows, cols), lambda i: (i, 0))

    def out(cols):
        return jax.ShapeDtypeStruct((length, cols), BF16)

    cols = (model, wq.shape[0], NOPE + 2 * ROPE, VH, LATENT)
    return pl.pallas_call(
        front_kernel,
        grid=(n // blocks,),
        in_specs=[
            pl.BlockSpec((blocks, tokens, model), lambda i: (i, 0, 0)),
            rows_of(2 * ROPE),
            rows_of(2 * ROPE),
        ]
        + [whole(a) for a in (gain, lat_gain, wq, wl, we)],
        out_specs=[rows_of(c) for c in cols],
        out_shape=[out(c) for c in cols],
        compiler_params=pltpu.CompilerParams(vmem_limit_bytes=48 << 20),
        name="front",
    )(x, cos, sin, gain, lat_gain, wq, wl, we)


def back_kernel(
    cos_ref, sin_ref, dq_ref, dk_ref, dv_ref, we_ref, query_ref, expanded_ref, latent_ref, rope_ref
):
    own_half = lax.broadcasted_iota(jnp.int32, cos_ref.shape, 1) < ROPE
    pair = dq_ref[:, NOPE:] * jnp.where(own_half, cos_ref[...], sin_ref[...])
    pair = jnp.where(own_half, pair + pltpu.roll(pair, ROPE, 1), 0.0)
    query_ref[:, :NOPE] = dq_ref[:, :NOPE].astype(BF16)
    query_ref[:, NOPE:] = pair.astype(BF16)
    expanded_ref[:, :NOPE] = dk_ref[:, :NOPE].astype(BF16)
    expanded_ref[:, NOPE:] = dv_ref[...].astype(BF16)
    latent_ref[...] = dot_nt(expanded_ref[...], we_ref[...]).astype(BF16)
    rope_ref[...] = dk_ref[:, NOPE:].astype(BF16)


def back(cos, sin, dq, dk, dv, we):
    length = dq.shape[0]
    rows = 512

    def rows_of(cols):
        return pl.BlockSpec((rows, cols), lambda i: (i, 0))

    def out(cols):
        return jax.ShapeDtypeStruct((length, cols), BF16)

    cols = (NOPE + 2 * ROPE, NOPE + VH, LATENT, 2 * ROPE)
    return pl.pallas_call(
        back_kernel,
        grid=(length // rows,),
        in_specs=[rows_of(a.shape[1]) for a in (cos, sin, dq, dk, dv)]
        + [pl.BlockSpec(we.shape, lambda i: (0, 0))],
        out_specs=[rows_of(c) for c in cols],
        out_shape=[out(c) for c in cols],
        compiler_params=pltpu.CompilerParams(vmem_limit_bytes=40 << 20),
        name="back",
    )(cos, sin, dq, dk, dv, we)


KEYS = 512


def scores_of(scale, prefix, k, q, first_key, first_query):
    scores = dot_nt(k, q) * scale
    key = first_key + lax.broadcasted_iota(jnp.int32, scores.shape, 0)
    query = first_query + lax.broadcasted_iota(jnp.int32, scores.shape, 1)
    return jnp.where((key <= query) | (key < prefix), scores, MASKED)


def key_blocks(prefix, last_query):
    return (jnp.maximum(last_query, prefix) + KEYS - 1) // KEYS


def attend_kernel(scale, prefix_ref, q_ref, k_ref, v_ref, attended_ref, exact_ref, lse_ref):
    q = q_ref[...]
    rows = q.shape[0]
    start = pl.program_id(0) * rows
    prefix = prefix_ref[0]

    def step(j, carry):
        top, total, out = carry
        s = scores_of(scale, prefix, k_ref[j], q, j * KEYS, start)
        new_top = jnp.maximum(top, jnp.max(s, axis=0, keepdims=True))
        p = jnp.exp(s - new_top)
        shrink = jnp.exp(top - new_top)
        total = total * shrink + jnp.sum(p, axis=0, keepdims=True)
        return new_top, total, out * shrink + dot(v_ref[j], p.astype(BF16))

    top, total, out = lax.fori_loop(
        0,
        key_blocks(prefix, start + rows),
        step,
        (
            jnp.full((1, rows), MASKED, F32),
            jnp.zeros((1, rows), F32),
            jnp.zeros((v_ref.shape[1], rows), F32),
        ),
    )
    lse_ref[...] = top + jnp.log(total)
    exact = (out / total).T
    exact_ref[...] = exact
    attended_ref[...] = exact.astype(BF16)


def attend(prefix, q, k, v):
    length, depth = q.shape
    values = v.shape[1]
    rows = 256
    v = v.reshape(length // KEYS, KEYS, values).transpose(0, 2, 1)
    k = k.reshape(length // KEYS, KEYS, depth)
    return pl.pallas_call(
        functools.partial(attend_kernel, 1.0 / math.sqrt(NOPE + ROPE)),
        grid=(length // rows,),
        in_specs=[
            pl.BlockSpec(memory_space=pltpu.SMEM),
            pl.BlockSpec((rows, depth), lambda i: (i, 0)),
            pl.BlockSpec(k.shape, lambda i: (0, 0, 0)),
            pl.BlockSpec(v.shape, lambda i: (0, 0, 0)),
        ],
        out_specs=[
            pl.BlockSpec((rows, values), lambda i: (i, 0)),
            pl.BlockSpec((rows, values), lambda i: (i, 0)),
            pl.BlockSpec((1, rows), lambda i: (0, i)),
        ],
        out_shape=[
            jax.ShapeDtypeStruct((length, values), BF16),
            jax.ShapeDtypeStruct((length, values), F32),
            jax.ShapeDtypeStruct((1, length), F32),
        ],
        compiler_params=pltpu.CompilerParams(vmem_limit_bytes=32 << 20),
        name="attend",
    )(prefix, q, k, v)


def attend_back_kernel(
    scale, prefix_ref, q_ref, g_ref, lse_ref, delta_ref, k_ref, v_ref, dq_ref, dk_ref, dv_ref
):
    q, g = q_ref[...], g_ref[...]
    rows = q.shape[0]
    start = pl.program_id(0) * rows
    prefix = prefix_ref[0]

    @pl.when(pl.program_id(0) == 0)
    def _():
        dk_ref[...] = jnp.zeros_like(dk_ref)
        dv_ref[...] = jnp.zeros_like(dv_ref)

    def step(j, dq):
        k = k_ref[j]
        p = jnp.exp(scores_of(scale, prefix, k, q, j * KEYS, start) - lse_ref[...])
        ds = (p * (dot_nt(v_ref[j], g) - delta_ref[...]) * scale).astype(BF16)
        dv_ref[j] += dot(p.astype(BF16), g)
        dk_ref[j] += dot(ds, q)
        return dq + lax.dot_general(
            ds, k, (((0,), (0,)), ((), ())), preferred_element_type=F32
        )

    dq_ref[...] = lax.fori_loop(
        0, key_blocks(prefix, start + rows), step, jnp.zeros(dq_ref.shape, F32)
    )


def attend_back(prefix, q, g, lse, delta, k, v):
    length, depth = q.shape
    values = v.shape[1]
    rows = 256
    k = k.reshape(length // KEYS, KEYS, depth)
    v = v.reshape(length // KEYS, KEYS, values)
    dq, dk, dv = pl.pallas_call(
        functools.partial(attend_back_kernel, 1.0 / math.sqrt(NOPE + ROPE)),
        grid=(length // rows,),
        in_specs=[
            pl.BlockSpec(memory_space=pltpu.SMEM),
            pl.BlockSpec((rows, depth), lambda i: (i, 0)),
            pl.BlockSpec((rows, values), lambda i: (i, 0)),
            pl.BlockSpec((1, rows), lambda i: (0, i)),
            pl.BlockSpec((1, rows), lambda i: (0, i)),
            pl.BlockSpec(k.shape, lambda i: (0, 0, 0)),
            pl.BlockSpec(v.shape, lambda i: (0, 0, 0)),
        ],
        out_specs=[
            pl.BlockSpec((rows, depth), lambda i: (i, 0)),
            pl.BlockSpec(k.shape, lambda i: (0, 0, 0)),
            pl.BlockSpec(v.shape, lambda i: (0, 0, 0)),
        ],
        out_shape=[
            jax.ShapeDtypeStruct((length, depth), F32),
            jax.ShapeDtypeStruct(k.shape, F32),
            jax.ShapeDtypeStruct(v.shape, F32),
        ],
        compiler_params=pltpu.CompilerParams(vmem_limit_bytes=40 << 20),
        name="attend_back",
    )(prefix, q, g, lse, delta, k, v)
    return dq, dk.reshape(length, depth), dv.reshape(length, values)


def ffn_kernel(
    n,
    x_ref,
    y_ref,
    slots_ref,
    tokens_ref,
    own_ref,
    router_ref,
    sg_ref,
    su_ref,
    sd_ref,
    eg_ref,
    eu_ref,
    ed_ref,
    out_ref,
    ffn_ref,
    dot_ref,
    probs_ref,
    rows_ref,
    hidden_ref,
    slot_grad_ref,
    grad_gu_ref,
    shared_h_ref,
    shared_gu_ref,
    expert_out,
    row_grad,
):
    blocks, tokens = x_ref.shape[:2]
    capacity = slots_ref.shape[1]
    own = own_ref[...]
    lanes = lax.broadcasted_iota(jnp.int32, (tokens, own.shape[1]), 1)
    gates = []
    for b in range(blocks):
        x, y = x_ref[b], y_ref[b]
        logits = jnp.where(lanes < n, dot(x, router_ref[...]), MASKED)
        raised = jnp.exp(logits - jnp.max(logits, axis=-1, keepdims=True))
        probs = raised / jnp.sum(raised, axis=-1, keepdims=True)
        probs_ref[b] = probs
        gate = jnp.sum(probs * own, axis=-1, keepdims=True)
        gates.append(gate)
        part = pl.ds(b * capacity, capacity)
        rows_ref[part] = dot(slots_ref[b], x).astype(BF16)
        weighted = (gate * y.astype(F32)).astype(BF16)
        slot_grad_ref[part] = dot(slots_ref[b], weighted).astype(BF16)
    rows = rows_ref[...]
    slot_grad = slot_grad_ref[...]
    g = dot(rows, eg_ref[...])
    u = dot(rows, eu_ref[...])
    sigmoid = 1.0 / (1.0 + jnp.exp(-g))
    silu = g * sigmoid
    hidden = (silu * u).astype(BF16)
    hidden_ref[...] = hidden
    expert_out[...] = dot(hidden, ed_ref[...]).astype(BF16)
    grad_hidden = dot_nt(slot_grad, ed_ref[...])
    grad_g = (grad_hidden * u * sigmoid * (1.0 + g * (1.0 - sigmoid))).astype(BF16)
    grad_u = (grad_hidden * silu).astype(BF16)
    grad_gu_ref[:, : grad_g.shape[1]] = grad_g
    grad_gu_ref[:, grad_g.shape[1] :] = grad_u
    row_grad[...] = (dot_nt(grad_g, eg_ref[...]) + dot_nt(grad_u, eu_ref[...])).astype(BF16)
    x = x_ref[...].reshape(blocks * tokens, -1)
    y = y_ref[...].reshape(blocks * tokens, -1)
    g = dot_nt(x, sg_ref[...])
    u = dot_nt(x, su_ref[...])
    grad_hidden = dot_nt(y, sd_ref[...])
    sigmoid = 1.0 / (1.0 + jnp.exp(-g))
    silu = g * sigmoid
    hidden = (silu * u).astype(BF16)
    grad_g = (grad_hidden * u * sigmoid * (1.0 + g * (1.0 - sigmoid))).astype(BF16)
    grad_u = (grad_hidden * silu).astype(BF16)
    shared = hidden.shape[1]
    shared_h_ref[...] = hidden.reshape(blocks, tokens, shared)
    shared_gu_ref[:, :, :shared] = grad_g.reshape(blocks, tokens, shared)
    shared_gu_ref[:, :, shared:] = grad_u.reshape(blocks, tokens, shared)
    width = x.shape[1]
    chunk = width // 4
    met = [0.0] * blocks
    for c in range(width // chunk):
        cols = pl.ds(c * chunk, chunk)
        shared_out = dot(hidden, sd_ref[:, cols])
        shared_ffn = dot(grad_g, sg_ref[:, cols]) + dot(grad_u, su_ref[:, cols])
        for b in range(blocks):
            part = pl.ds(b * capacity, capacity)
            here = slice(b * tokens, (b + 1) * tokens)
            picked = dot(tokens_ref[b], expert_out[part, cols])
            met[b] += jnp.sum(picked * y_ref[b, :, cols].astype(F32), axis=-1, keepdims=True)
            out_ref[b, :, cols] = (shared_out[here] + picked * gates[b]).astype(BF16)
            back = dot(tokens_ref[b], row_grad[part, cols])
            ffn_ref[b, :, cols] = (shared_ffn[here] + back).astype(BF16)
    for b in range(blocks):
        dot_ref[b] = (met[b] * own).astype(BF16)


def ffn(x, y, slots, own_lane, router_w, gate_t, up_t, down, gate_m, up_m, down_m):
    n, tokens, width = x.shape
    capacity = slots.shape[1]
    hidden = gate_m.shape[1]
    shared = gate_t.shape[0]
    group = 4

    def whole(a):
        return pl.BlockSpec(a.shape, lambda i: (0,) * a.ndim, pipeline_mode=pl.Buffered(1))

    def block(*shape):
        return pl.BlockSpec((group,) + shape, lambda i: (i, 0, 0))

    def slot_rows(cols):
        return pl.BlockSpec((group * capacity, cols), lambda i: (i, 0))

    def tokens_of(cols, kind=BF16):
        return jax.ShapeDtypeStruct((n, tokens, cols), kind)

    def slots_of(cols):
        return jax.ShapeDtypeStruct((n * capacity, cols), BF16)

    weights = (own_lane, router_w, gate_t, up_t, down, gate_m, up_m, down_m)
    return pl.pallas_call(
        functools.partial(ffn_kernel, n),
        grid=(n // group,),
        in_specs=[
            block(tokens, width),
            block(tokens, width),
            block(capacity, tokens),
            block(tokens, capacity),
        ]
        + [whole(a) for a in weights],
        out_specs=[
            block(tokens, width),
            block(tokens, width),
            block(tokens, 128),
            block(tokens, 128),
            slot_rows(width),
            slot_rows(hidden),
            slot_rows(width),
            slot_rows(2 * hidden),
            block(tokens, shared),
            block(tokens, 2 * shared),
        ],
        out_shape=[
            tokens_of(width),
            tokens_of(width),
            tokens_of(128),
            tokens_of(128, F32),
            slots_of(width),
            slots_of(hidden),
            slots_of(width),
            slots_of(2 * hidden),
            tokens_of(shared),
            tokens_of(2 * shared),
        ],
        scratch_shapes=[
            pltpu.VMEM((group * capacity, width), BF16),
            pltpu.VMEM((group * capacity, width), BF16),
        ],
        compiler_params=pltpu.CompilerParams(vmem_limit_bytes=60 << 20),
        name="ffn",
    )(x, y, slots, slots.transpose(0, 2, 1), *weights)


def product(form, left, right):
    return jnp.einsum(form, left, right, preferred_element_type=F32)


def rms_scale(values):
    return lax.rsqrt(jnp.mean(values * values, axis=-1, keepdims=True) + EPSILON)


def rotary_tables(tokens, n):
    halfway = ROPE // 2
    inverse = 10000.0 ** (-(jnp.arange(halfway, dtype=F32) * 2.0 / ROPE))
    inverse = jnp.concatenate([inverse] * 4)
    lane = jnp.arange(2 * ROPE)
    sign = jnp.where((lane < halfway) | (lane >= 3 * halfway), -1.0, 1.0)
    base = (jnp.arange(n, dtype=F32) * tokens)[:, None] * inverse
    step = jnp.arange(tokens, dtype=F32)[:, None] * inverse
    base_cos, base_sin = jnp.cos(base)[:, None], jnp.sin(base)[:, None]
    step_cos, step_sin = jnp.cos(step)[None], jnp.sin(step)[None]
    cos_table = base_cos * step_cos - base_sin * step_sin
    sin_table = (base_sin * step_cos + base_cos * step_sin) * sign
    return cos_table.reshape(n * tokens, -1), sin_table.reshape(n * tokens, -1)


def unrotate(grads, cos_table, sin_table):
    halfway = grads.shape[-1] // 2
    first = grads[..., :halfway]
    second = grads[..., halfway:]
    return jnp.concatenate(
        [first * cos_table + second * sin_table, second * cos_table - first * sin_table], axis=-1
    )


def norm_back(grad_unit, unit_values, scale_values):
    return scale_values * (
        grad_unit - unit_values * jnp.mean(grad_unit * unit_values, axis=-1, keepdims=True)
    )


def column_halves(weight, n, half):
    rows, width = weight.shape[0], weight.shape[1] // n
    parts = weight.T.reshape(n, 2, width // 2, rows)
    return lax.dynamic_index_in_dim(parts, half, 1, keepdims=False)


def columns_in(blocks):
    n, width, rows = blocks.shape
    return blocks.transpose(1, 0, 2).reshape(width, n * rows)


def both_halves(mine, other, even, axis=0):
    return jnp.concatenate([jnp.where(even, mine, other), jnp.where(even, other, mine)], axis=axis)


def per_device(
    layer_input,
    attention_gain,
    query_weight,
    latent_weight,
    latent_gain,
    expand_weight,
    output_weight,
    feedforward_gain,
    router_weight,
    shared_gate,
    shared_up,
    shared_down,
    expert_gate,
    expert_up,
    expert_down,
    expert_routes,
    prefix_length,
    output_grad,
):
    n = lax.axis_size("ep")
    groups = lax.axis_size("grp")
    e = lax.axis_index("ep")
    half = lax.axis_index("grp") % 2
    even = half == 0
    tokens = layer_input.shape[0]
    length = tokens * n
    capacity = tokens * TOPK * 4 // (3 * n)
    rows_dev = attention_gain.shape[0]
    latent_rows = latent_gain.shape[0]
    rows_out = D // (groups * n)
    expand_rows = LATENT // (groups * n)

    pad = jnp.zeros((rows_dev - latent_rows,), BF16)
    first_block = jnp.concatenate(
        [
            layer_input,
            latent_weight,
            router_weight,
            attention_gain[:, None],
            feedforward_gain[:, None],
            jnp.concatenate([latent_gain, pad])[:, None],
            expert_routes.astype(BF16),
        ],
        axis=1,
    )
    width = first_block.shape[1]
    out_w_half = lax.dynamic_slice_in_dim(output_weight, half * (D // 2), D // 2, 1)
    first_block = jnp.concatenate(
        [first_block, jnp.zeros((tokens, -width % 128), BF16), out_w_half], axis=1
    )
    shared_half = jnp.where(even, shared_gate, shared_up)
    expand_half = lax.dynamic_index_in_dim(
        expand_weight.reshape(latent_rows, n, 2, -1), half, 2, keepdims=False
    ).transpose(1, 0, 2)
    first_all, q_blocks, x_blocks, shared_blocks = gather(
        first_block,
        0,
        swaps=(
            column_halves(query_weight, n, half),
            expand_half,
            shared_half.T.reshape(n, shared_half.shape[1] // n, rows_dev),
        ),
    )
    c0 = D
    c1 = c0 + LATENT + ROPE
    c2 = c1 + n
    latent_w = first_all[:, :, c0:c1].reshape(D, LATENT + ROPE)
    router_w = first_all[:, :, c1:c2].reshape(D, n)
    attn_gain = first_all[:, :, c2].reshape(D).astype(F32)
    ffn_gain = first_all[:, :, c2 + 1].reshape(D).astype(F32)
    lat_gain = first_all[:, :latent_rows, c2 + 2].reshape(LATENT).astype(F32)
    routes = first_all[:, :, c2 + 3 : c2 + 3 + TOPK].astype(jnp.int32)

    out_w_mine = first_all[:, :, -(D // 2) :].reshape(D, D // 2)
    out_w_other = from_partner(out_w_mine)
    all_out_grad = lax.all_gather(output_grad, "ep", axis=0, tiled=True)

    q_mine, x_mine = columns_in(q_blocks), x_blocks.reshape(LATENT, -1)
    query_t = both_halves(q_mine, from_partner(q_mine), even)
    expand_w = both_halves(x_mine, from_partner(x_mine), even, 1)
    shared_mine = columns_in(shared_blocks)
    shared_other = from_partner(shared_mine)
    gate_t = jnp.where(even, shared_mine, shared_other)
    up_t = jnp.where(even, shared_other, shared_mine)

    def own(values):
        return lax.dynamic_slice_in_dim(values, e * tokens, tokens, 0)

    cos_table, sin_table = rotary_tables(tokens, n)
    turned = jnp.concatenate(
        [query_t, query_t[NOPE + ROPE // 2 :], query_t[NOPE : NOPE + ROPE // 2]], axis=0
    )
    latent_turned = jnp.concatenate(
        [latent_w, latent_w[:, LATENT + ROPE // 2 :], latent_w[:, LATENT : LATENT + ROPE // 2]],
        axis=1,
    )
    normed, query, keys, values, latent = front(
        first_all, cos_table, sin_table, attn_gain[None], lat_gain[None], turned, latent_turned, expand_w
    )
    attended_head, attended_exact, lse = attend(prefix_length, query, keys, values)
    (attended_blocks,) = exchange(2, swaps=(attended_head.reshape(n, tokens, VH),))
    attended = attended_blocks.transpose(1, 0, 2).reshape(tokens, HEADS * VH)

    residual_in = layer_input.astype(F32)
    input_scale = rms_scale(residual_in)
    input_unit = residual_in * input_scale
    out_mine = product("ta,ad->td", attended, out_w_mine)
    out_other = product("ta,ad->td", attended, out_w_other)
    residual_mid = residual_in + jnp.concatenate(
        [jnp.where(even, out_mine, out_other), jnp.where(even, out_other, out_mine)], axis=1
    )
    mid_scale = rms_scale(residual_mid)
    mid_unit = residual_mid * mid_scale
    own_ffn_in = (mid_unit * ffn_gain).astype(BF16)
    (ffn_blocks,) = gather(own_ffn_in, 3)
    query_cols = query_weight.shape[1] // 2
    query_w_half = lax.dynamic_slice_in_dim(query_weight, half * query_cols, query_cols, 1)
    query_w_half, ffn_blocks = lax.optimization_barrier((query_w_half, ffn_blocks))
    query_w_mine = lax.all_gather(query_w_half, "ep", axis=0, tiled=True)
    query_w_other = from_partner(query_w_mine)
    ffn_in = ffn_blocks.reshape(length, D)

    own_lane = (jnp.arange(128, dtype=jnp.int32) == e).astype(F32)[None]
    chosen = jnp.any(routes == e, axis=-1)
    chosen_int = chosen.astype(jnp.int32)
    place = jnp.cumsum(chosen_int, axis=1) - chosen_int
    kept = chosen & (place < capacity)
    dispatch = (
        (place[:, None, :] == jnp.arange(capacity, dtype=jnp.int32)[None, :, None])
        & kept[:, None, :]
    ).astype(BF16)
    shared_width = gate_t.shape[0]
    fill = ((0, -shared_width % 128), (0, 0))
    (
        out_partial,
        ffn_partial,
        dot_partial,
        router_all,
        incoming,
        expert_hidden,
        slot_grad,
        grad_expert_gu,
        shared_hidden,
        grad_shared_gu,
    ) = ffn(
        ffn_blocks,
        all_out_grad.reshape(n, tokens, D),
        dispatch,
        own_lane,
        jnp.pad(router_w, ((0, 0), (0, 128 - n))),
        jnp.pad(gate_t, fill),
        jnp.pad(up_t, fill),
        jnp.pad(shared_down, fill),
        expert_gate[0],
        expert_up[0],
        expert_down[0],
    )
    ffn_sum, dot_sum, out_sum, *products = exchange(
        4,
        sums=(ffn_partial, dot_partial, out_partial),
        jobs=((expert_hidden, slot_grad, 1, groups), (incoming, grad_expert_gu, 2, groups)),
    )
    layer_output = (residual_mid + out_sum).astype(BF16)

    def by_group(values):
        return over_groups(values.reshape(groups, values.shape[0] // groups, -1))

    def blocks_over_groups(blocks):
        total = blocks[0].astype(F32)
        for k in range(1, groups):
            shift = [(g, (g + k) % groups) for g in range(groups)]
            total = total + lax.ppermute(blocks[k], "grp", shift).astype(F32)
        return total

    expert_down_grad, expert_gate_grad, expert_up_grad = (
        blocks_over_groups(products[k * groups : (k + 1) * groups])[None] for k in range(3)
    )

    router_own = lax.dynamic_index_in_dim(router_all, e, 0, keepdims=False)[:, :n]
    grad_probs = dot_sum[:, :n]
    grad_logits = (
        router_own * (grad_probs - jnp.sum(router_own * grad_probs, axis=-1, keepdims=True))
    ).astype(BF16)
    grad_ffn_in = ffn_sum + product("te,de->td", grad_logits, router_w)
    grad_ffn_gain = jnp.sum(grad_ffn_in * mid_unit, axis=0)
    grad_mid = output_grad.astype(F32) + norm_back(grad_ffn_in * ffn_gain, mid_unit, mid_scale)
    grad_mid_b = grad_mid.astype(BF16)
    mid_left, mid_right = grad_mid_b[:, : D // 2], grad_mid_b[:, D // 2 :]
    grad_attended = (
        product("td,ad->ta", jnp.where(even, mid_left, mid_right), out_w_mine)
        + product("td,ad->ta", jnp.where(even, mid_right, mid_left), out_w_other)
    ).astype(BF16)
    output_w_partial = product_over_groups(attended, grad_mid_b).astype(BF16)
    output_w_partial, grad_attended = lax.optimization_barrier((output_w_partial, grad_attended))
    (grad_att_blocks,) = exchange(
        5, swaps=(grad_attended.reshape(tokens, HEADS, VH).transpose(1, 0, 2),)
    )
    grad_att = grad_att_blocks.reshape(length, VH)
    output_weight_grad = lax.psum_scatter(
        output_w_partial.reshape(n, rows_out, D), "ep", scatter_dimension=0
    ).astype(F32)
    grad_router = product("te,td->ed", grad_logits, own_ffn_in)

    delta = jnp.sum(grad_att.astype(F32) * attended_exact, axis=-1)[None]
    grad_query_raw, grad_keys, grad_values = attend_back(
        prefix_length, query, grad_att, lse, delta, keys, values
    )
    grad_query, grad_expanded, latent_partial, rope_partial = back(
        cos_table, sin_table, grad_query_raw, grad_keys, grad_values, expand_w
    )
    (
        latent_sum,
        rope_sum,
        query_blocks,
        side_down,
        *products,
    ) = exchange(
        6,
        sums=(
            latent_partial.reshape(n, tokens, LATENT),
            rope_partial.reshape(n, tokens, 2 * ROPE),
        ),
        swaps=(grad_query.reshape(n, tokens, -1),),
        jobs=(
            (shared_hidden.reshape(length, -1), all_out_grad, 1, 1),
            (ffn_in, grad_shared_gu.reshape(length, -1), 2, groups),
            (normed, grad_query, 1, groups),
            (latent, grad_expanded, 1, groups),
        ),
    )
    shared_down_grad = to_row_owner(by_group(side_down[:shared_width]))
    side_gate, side_up, side_query, grad_expand = (
        blocks_over_groups(products[k * groups : (k + 1) * groups]).astype(BF16) for k in range(4)
    )
    side_gate, side_up = side_gate[:, :shared_width], side_up[:, :shared_width]
    side_query = side_query[:, : query_t.shape[0]]

    own_normed = (input_unit * attn_gain).astype(BF16)
    own_raw = product("td,dc->tc", own_normed, latent_w[:, :LATENT])
    latent_scale = rms_scale(own_raw)
    latent_unit = own_raw * latent_scale
    grad_latent_gain = jnp.sum(latent_sum * latent_unit, axis=0)
    grad_compressed = jnp.concatenate(
        [
            norm_back(latent_sum * lat_gain, latent_unit, latent_scale),
            unrotate(
                rope_sum[:, :ROPE],
                own(cos_table)[:, : ROPE // 2],
                own(sin_table)[:, ROPE // 2 : ROPE],
            ),
        ],
        axis=-1,
    ).astype(BF16)
    latent_w_partial = product_over_groups(
        own_normed, jnp.pad(grad_compressed, ((0, 0), (0, 640 - LATENT - ROPE)))
    ).astype(BF16)
    own_part = product("tc,dc->td", grad_compressed, latent_w)

    def of_heads(part):
        heads = lax.dynamic_slice_in_dim(query_blocks, part * (n // 2), n // 2, 0)
        return heads[:, :, : NOPE + ROPE].transpose(1, 0, 2).reshape(tokens, -1)

    grad_normed = (
        product("tc,dc->td", of_heads(half), query_w_mine)
        + product("tc,dc->td", of_heads(1 - half), query_w_other)
        + own_part
    )
    grad_attn_gain = jnp.sum(grad_normed * input_unit, axis=0)

    def by_owner(values, rows):
        blocks = values.reshape(-1, groups, n, rows).transpose(2, 1, 0, 3)
        return blocks.reshape(n, groups, -1)

    small = jnp.concatenate(
        [
            by_owner(grad_attn_gain, rows_out),
            by_owner(grad_ffn_gain, rows_out),
            by_owner(grad_router, rows_out),
            by_owner(grad_latent_gain, expand_rows),
        ],
        axis=2,
    )
    small = small.transpose(1, 0, 2)
    if groups == 2:
        g = lax.axis_index("grp")
        mine = lax.dynamic_index_in_dim(small, g, 0, keepdims=False)
        theirs = lax.dynamic_index_in_dim(small, 1 - g, 0, keepdims=False)
        small = mine + lax.ppermute(theirs, "grp", [(0, 1), (1, 0)])
    else:
        small = lax.psum_scatter(small, "grp", scatter_dimension=0)
    (
        latent_weight_sum,
        small_all,
        query_weight_grad,
        shared_gate_grad,
        shared_up_grad,
        expand_weight_grad,
    ) = exchange(
        7,
        sums=(latent_w_partial.reshape(n, rows_out, -1),),
        swaps=(
            small[:, None],
            side_query.reshape(n, rows_out, -1),
            side_gate.reshape(n, rows_out, -1),
            side_up.reshape(n, rows_out, -1),
            grad_expand.reshape(n, expand_rows, -1),
        ),
        laid=4,
    )
    input_grad = (
        grad_mid + norm_back(grad_normed * attn_gain, input_unit, input_scale)
    ).astype(BF16)
    latent_weight_grad = latent_weight_sum[:, : LATENT + ROPE]
    small_sum = jnp.sum(small_all[:, 0], axis=0)
    attention_gain_grad = small_sum[:rows_out]
    feedforward_gain_grad = small_sum[rows_out : 2 * rows_out]
    router_weight_grad = small_sum[2 * rows_out : (2 + n) * rows_out].reshape(n, rows_out).T
    latent_gain_grad = small_sum[(2 + n) * rows_out :]
    return (
        layer_output,
        input_grad,
        attention_gain_grad,
        query_weight_grad,
        latent_weight_grad,
        latent_gain_grad,
        expand_weight_grad,
        output_weight_grad,
        feedforward_gain_grad,
        router_weight_grad,
        shared_gate_grad,
        shared_up_grad,
        shared_down_grad,
        expert_gate_grad,
        expert_up_grad,
        expert_down_grad,
    )


def solution(mesh):
    return jax.shard_map(
        per_device,
        mesh=mesh,
        in_specs=(
            P(("grp", "ep"), None),
            P("ep"),
            P("ep", None),
            P("ep", None),
            P("ep"),
            P("ep", None),
            P("ep", None),
            P("ep"),
            P("ep", None),
            P("ep", None),
            P("ep", None),
            P("ep", None),
            P("ep", None, None),
            P("ep", None, None),
            P("ep", None, None),
            P(("grp", "ep"), None),
            P("grp"),
            P(("grp", "ep"), None),
        ),
        out_specs=(
            P(("grp", "ep"), None),
            P(("grp", "ep"), None),
            P(("grp", "ep")),
            P(("grp", "ep"), None),
            P(("grp", "ep"), None),
            P(("grp", "ep")),
            P(("grp", "ep"), None),
            P(("grp", "ep"), None),
            P(("grp", "ep")),
            P(("grp", "ep"), None),
            P(("grp", "ep"), None),
            P(("grp", "ep"), None),
            P(("grp", "ep"), None),
            P("ep", "grp", None),
            P("ep", "grp", None),
            P("ep", "grp", None),
        ),
        check_vma=False,
    )
```

```python
import functools
import math

import jax
import jax.numpy as jnp
from jax import lax
from jax.experimental import pallas as pl
from jax.experimental.pallas import tpu as pltpu
from jax.sharding import PartitionSpec as P

D = 2048
HEADS = 16
NOPE = 128
ROPE = 64
VH = 128
LATENT = 512
TOPK = 6

EPSILON = 1e-06
MASKED = -1e30

MESH = pl.DeviceIdType.MESH
ANY = pl.BlockSpec(memory_space=pl.ANY)
DMA = pltpu.SemaphoreType.DMA
F32 = jnp.float32
BF16 = jnp.bfloat16


def remote(src, dst, send, recv, peer):
    return pltpu.make_async_remote_copy(
        src_ref=src,
        dst_ref=dst,
        send_sem=send,
        recv_sem=recv,
        device_id={"ep": peer},
        device_id_type=MESH,
    )


def greet(peers):
    barrier = pltpu.get_barrier_semaphore()
    for peer in peers:
        pl.semaphore_signal(barrier, inc=1, device_id={"ep": peer}, device_id_type=MESH)
    pl.semaphore_wait(barrier, len(peers))


def around(n):
    me = lax.axis_index("ep")
    x, y = me % 2, (me // 2) % 2
    return me, me // 4, y, x, me + 1 - 2 * x, me + 2 - 4 * y


def near(z, nz, below, above):
    for s in range(nz - 1):
        pl.when(z - 1 - s >= 0)(functools.partial(below, s, z - 1 - s))
        pl.when(z + 1 + s < nz)(functools.partial(above, s, z + 1 + s))


def greet_near(px, py, up, down, z, nz):
    barrier = pltpu.get_barrier_semaphore()
    for peer, there in ((px, None), (py, None), (up, z + 1 < nz), (down, z > 0)):

        def hello(peer=peer):
            pl.semaphore_signal(barrier, inc=1, device_id={"ep": peer}, device_id_type=MESH)

        hello() if there is None else pl.when(there)(hello)
    on_line = (z + 1 < nz).astype(jnp.int32) + (z > 0).astype(jnp.int32)
    pl.semaphore_wait(barrier, 2 + on_line)


def start_swaps(n, ins, outs, sems):
    own, ss, rs = sems
    me = lax.axis_index("ep")
    sends, copies = [], []
    for j in range(len(ins)):
        local = pltpu.make_async_copy(ins[j].at[me], outs[j].at[me], own.at[j])
        local.start()
        copies.append(local)
    for k in range(1, n):
        to = (me + k) % n
        for j in range(len(ins)):
            c = remote(ins[j].at[to], outs[j].at[me], ss.at[j, k], rs.at[j, k], to)
            c.start()
            sends.append(c)
    return sends, copies


def end_swaps(n, ins, outs, sems, started):
    own, ss, rs = sems
    me = lax.axis_index("ep")
    sends, copies = started
    for k in range(1, n):
        to, back = (me + k) % n, (me + n - k) % n
        for j in range(len(ins)):
            remote(ins[j].at[back], outs[j].at[back], ss.at[j, k], rs.at[j, k], to).wait_recv()
    for copy in sends:
        copy.wait_send()
    for copy in copies:
        copy.wait()


def gather_kernel(n, w, x_ref, *refs):
    swaps_in, o_ref, swaps_out = refs[:w], refs[w], refs[w + 1 : 2 * w + 1]
    own, us, ur, ds, dr, xs, xr, ys, yr, *swap_sems = refs[2 * w + 1 :]
    me, z, y, x, px, py = around(n)
    nz = n // 4
    low = me % 4
    half = x_ref.shape[0] // 2
    top, bottom = pl.ds(0, half), pl.ds(half, half)
    up, down = (me + 4) % n, (me + n - 4) % n
    everyone = [(me + k) % n for k in range(n)]
    if w:
        greet(everyone[1:])
    else:
        greet_near(px, py, up, down, z, nz)
    local = pltpu.make_async_copy(x_ref, o_ref.at[me], own)
    local.start()

    def over_x(src, b, part, i):
        return remote(src.at[part], o_ref.at[b, part], xs.at[i], xr.at[i], px)

    def over_y(src, b, part, i):
        return remote(src.at[part], o_ref.at[b, part], ys.at[i], yr.at[i], py)

    def upward(src, b, s):
        return remote(src, o_ref.at[b], us.at[s], ur.at[s], up)

    def downward(src, b, s):
        return remote(src, o_ref.at[b], ds.at[s], dr.at[s], down)

    def spread(src, t):
        b = t * 4 + low
        over_x(src, b, top, t).start()
        over_y(src, b, bottom, t).start()
        over_y(src, b, top, nz + t).start()
        over_x(src, b, bottom, nz + t).start()

    pl.when(z + 1 < nz)(lambda: upward(x_ref, me, 0).start())
    pl.when(z > 0)(lambda: downward(x_ref, me, 0).start())
    spread(x_ref, z)
    swapping = start_swaps(n, swaps_in, swaps_out, swap_sems) if w else None

    def from_below(s, t):
        b = t * 4 + low
        upward(o_ref.at[b], b, s).wait_recv()
        pl.when(z + 1 < nz)(lambda: upward(o_ref.at[b], b, s + 1).start())
        spread(o_ref.at[b], t)

    def from_above(s, t):
        b = t * 4 + low
        downward(o_ref.at[b], b, s).wait_recv()
        pl.when(z > 0)(lambda: downward(o_ref.at[b], b, s + 1).start())
        spread(o_ref.at[b], t)

    def turn(s, t):
        bx = t * 4 + low + px - me
        by = t * 4 + low + py - me
        over_x(o_ref.at[bx], bx, top, t).wait_recv()
        over_y(o_ref.at[bx], bx, top, 2 * nz + t).start()
        over_y(o_ref.at[by], by, bottom, t).wait_recv()
        over_x(o_ref.at[by], by, bottom, 2 * nz + t).start()

    for s in range(nz - 1):
        pl.when(z - 1 - s >= 0)(functools.partial(from_below, s, z - 1 - s))
        pl.when(z + 1 + s < nz)(functools.partial(from_above, s, z + 1 + s))
        if s == 0:
            turn(0, z)
        else:
            pl.when(z - s >= 0)(functools.partial(turn, s, z - s))
            pl.when(z + s < nz)(functools.partial(turn, s, z + s))
    pl.when(z - (nz - 1) >= 0)(functools.partial(turn, 0, z - (nz - 1)))
    pl.when(z + (nz - 1) < nz)(functools.partial(turn, 0, z + (nz - 1)))

    def finish(s, t):
        bx = t * 4 + low + px - me
        by = t * 4 + low + py - me
        bxy = bx + py - me
        over_y(o_ref.at[by], by, top, nz + t).wait_recv()
        over_x(o_ref.at[bx], bx, bottom, nz + t).wait_recv()
        over_y(o_ref.at[bxy], bxy, top, 2 * nz + t).wait_recv()
        over_x(o_ref.at[bxy], bxy, bottom, 2 * nz + t).wait_recv()
        for i in range(3):
            over_x(x_ref, me, top, i * nz + t).wait_send()
            over_y(x_ref, me, top, i * nz + t).wait_send()

    finish(0, z)
    near(z, nz, finish, finish)

    def sent_up(s, t):
        upward(x_ref, me, s).wait_send()

    def sent_down(s, t):
        downward(x_ref, me, s).wait_send()

    for s in range(nz - 1):
        pl.when((z + 1 < nz) & (z - s >= 0))(functools.partial(sent_up, s, z))
        pl.when((z > 0) & (z + s < nz))(functools.partial(sent_down, s, z))
    local.wait()
    if w:
        end_swaps(n, swaps_in, swaps_out, swap_sems, swapping)


def gather(x, cid, swaps=()):
    n = lax.axis_size("ep")
    w = len(swaps)
    nz = n // 4
    return pl.pallas_call(
        functools.partial(gather_kernel, n, w),
        out_shape=[jax.ShapeDtypeStruct((n,) + x.shape, x.dtype)]
        + [jax.ShapeDtypeStruct(a.shape, a.dtype) for a in swaps],
        in_specs=[ANY] * (1 + w),
        out_specs=[ANY] * (1 + w),
        scratch_shapes=[DMA]
        + [DMA((nz,))] * 4
        + [DMA((3 * nz,))] * 4
        + ([DMA((w,)), DMA((w, n)), DMA((w, n))] if w else []),
        compiler_params=pltpu.CompilerParams(collective_id=cid, has_side_effects=True),
        name="gather",
    )(x, *swaps)


def add_rows(dst, left, right, rows):
    step = 16

    def body(i, carry):
        r = pl.ds(pl.multiple_of(i * step, step), step)
        dst[r] = (left[r].astype(F32) + right[r].astype(F32)).astype(dst.dtype)
        return carry

    lax.fori_loop(0, rows // step, body, 0)


TILE = 128


def exchange_kernel(n, m, w, laid, groups, jobs, *refs):
    refs = list(refs)

    def take(count):
        out = refs[:count]
        del refs[:count]
        return out

    sums_in, swaps_in = take(m), take(w)
    jobs_in = [take(2) for _ in jobs]
    sums_out, swaps_out, jobs_out = take(m), take(w), [take(parts * blocks) for parts, blocks in jobs]
    room = [take(7) for _ in range(m)]
    sems = [take(8) for _ in range(m)]
    swap_sems = take(3) if w else None
    side_by_side = swaps_out[w - laid :]
    swaps_out = swaps_out[: w - laid] + take(laid)
    desks = [take(5) for _ in jobs]
    me, z, y, x, px, py = around(n)
    nz = n // 4
    low = me % 4
    to = [(z + k) % nz for k in range(nz)]
    at = [t * 4 + low for t in to]
    if w:
        greet([(me + k) % n for k in range(1, n)])
    else:
        greet([px, py] + at[1:])
    order = [2, 1, 3, 0] if nz == 4 else list(range(1, nz)) + [0]
    sends = []

    def halves(j):
        half = sums_in[j].shape[3] // 2
        return half, pl.ds(0, half), pl.ds(half, half)

    first, second, third = {}, {}, {}

    def stage_one(j, k):
        p = sums_in[j]
        half, top, bottom = halves(j)
        la, lb, a1, b1, a2, b2, zb = room[j]
        lsa, lsb, xs, xr, ys, yr, zs, zr = sems[j]
        t = to[k]
        c = remote(p.at[t, 1 - y, :, top], a1.at[k], ys.at[k], yr.at[k], py)
        d = remote(p.at[t, :, 1 - x, bottom], b1.at[k], xs.at[k], xr.at[k], px)
        c.start()
        d.start()
        e = pltpu.make_async_copy(p.at[t, y, :, top], la.at[k], lsa.at[k])
        f = pltpu.make_async_copy(p.at[t, :, x, bottom], lb.at[k], lsb.at[k])
        e.start()
        f.start()
        first[j, k] = (c, d, e, f)
        sends.extend([c, d])

    def stage_two(j, k):
        half, top, bottom = halves(j)
        la, lb, a1, b1, a2, b2, zb = room[j]
        lsa, lsb, xs, xr, ys, yr, zs, zr = sems[j]
        c, d, e, f = first[j, k]
        e.wait()
        c.wait_recv()
        for i in range(2):
            add_rows(la.at[k, i], la.at[k, i], a1.at[k, i], half)
        g = remote(la.at[k, 1 - x], a2.at[k], xs.at[nz + k], xr.at[nz + k], px)
        g.start()
        f.wait()
        d.wait_recv()
        for i in range(2):
            add_rows(lb.at[k, i], lb.at[k, i], b1.at[k, i], half)
        h = remote(lb.at[k, 1 - y], b2.at[k], ys.at[nz + k], yr.at[nz + k], py)
        h.start()
        second[j, k] = (g, h)
        sends.extend([g, h])

    def stage_three(j, k):
        half, top, bottom = halves(j)
        la, lb, a1, b1, a2, b2, zb = room[j]
        lsa, lsb, xs, xr, ys, yr, zs, zr = sems[j]
        g, h = second[j, k]
        g.wait_recv()
        add_rows(a2.at[k], la.at[k, x], a2.at[k], half)
        if k:
            c = remote(a2.at[k], zb.at[k, top], zs.at[k], zr.at[k], at[k])
            c.start()
        h.wait_recv()
        add_rows(b2.at[k], lb.at[k, y], b2.at[k], half)
        if k:
            d = remote(b2.at[k], zb.at[k, bottom], zs.at[nz + k], zr.at[nz + k], at[k])
            d.start()
            third[j, k] = (c, d)
            sends.extend([c, d])

    loads = []
    for (left, right), (left_v, right_v, page, in_sem, out_sem) in zip(jobs_in, desks):
        for i, (src, dst) in enumerate(((left, left_v), (right, right_v))):
            loads.append(pltpu.make_async_copy(src, dst, in_sem.at[i]))

    def pieces(j):
        parts, blocks = jobs[j]
        rows = jobs_out[j][0].shape[0]
        piece = math.gcd(TILE, rows)
        return [(q * piece, piece) for q in range(TILE // piece)]

    def start_write(j, i, part):
        left_v, right_v, page, in_sem, out_sem = desks[j]
        parts, blocks = jobs[j]
        outs = jobs_out[j][part * blocks : (part + 1) * blocks]
        rows = outs[0].shape[0]
        for q, (offset, piece) in enumerate(pieces(j)):
            row = i * TILE + offset
            src = page.at[i % 2, part, pl.ds(offset, piece)]
            owner = (row // rows + blocks - (lax.axis_index("grp") if blocks > 1 else 0)) % blocks
            inside = pl.ds(pl.multiple_of(row % rows, piece), piece)
            for k, out in enumerate(outs):
                copy = pltpu.make_async_copy(src, out.at[inside], out_sem.at[i % 2, part, q])
                if blocks > 1:
                    pl.when(owner == k)(copy.start)
                else:
                    copy.start()

    def wait_write(j, i, part):
        left_v, right_v, page, in_sem, out_sem = desks[j]
        for q, (offset, piece) in enumerate(pieces(j)):
            src = page.at[i % 2, part, pl.ds(offset, piece)]
            out = jobs_out[j][part * jobs[j][1]].at[pl.ds(0, piece)]
            pltpu.make_async_copy(src, out, out_sem.at[i % 2, part, q]).wait()

    def tile(j, i):
        left_v, right_v, page, in_sem, out_sem = desks[j]
        value = lax.dot_general(
            left_v[:, pl.ds(pl.multiple_of(i * TILE, TILE), TILE)],
            right_v[...],
            (((0,), (0,)), ((), ())),
            preferred_element_type=F32,
        ).astype(page.dtype)
        width = page.shape[3]
        for part in range(jobs[j][0]):
            pl.when(i >= 2)(functools.partial(wait_write, j, i, part))
            page[i % 2, part] = value[:, part * width : (part + 1) * width]
            start_write(j, i, part)

    tiles = [desk[0].shape[1] // TILE for desk in desks]
    loaded = []

    def work(step, of):
        first, last = sum(tiles) * step // of, sum(tiles) * (step + 1) // of
        for j in range(len(jobs)):
            start = sum(tiles[:j])
            low, high = max(first - start, 0), min(last - start, tiles[j])
            if low >= high:
                continue
            if j not in loaded:
                loaded.append(j)
                loads[2 * j].wait()
                loads[2 * j + 1].wait()
            lax.fori_loop(low, high, lambda i, c, j=j: (tile(j, i), c)[1], 0)

    steps = [(j, k) for j in range(m) for k in order]
    ahead = 3 if jobs else 2
    for i in range(min(ahead, len(steps))):
        stage_one(*steps[i])
    for copy in loads:
        copy.start()
    if w:
        swapping = start_swaps(n, swaps_in, swaps_out, swap_sems)
    for i, step in enumerate(steps):
        stage_two(*step)
        if i + ahead < len(steps):
            stage_one(*steps[i + ahead])
        if i:
            stage_three(*steps[i - 1])
        work(i, len(steps))
    if steps:
        stage_three(*steps[-1])
    if w:
        end_swaps(n, swaps_in, swaps_out, swap_sems, swapping)
        for wide, got in zip(side_by_side, swaps_out[w - laid :]):
            width = got.shape[2]
            for k in range(n):
                wide[:, k * width : (k + 1) * width] = got[k].astype(F32)
    for j in range(m):
        half, top, bottom = halves(j)
        la, lb, a1, b1, a2, b2, zb = room[j]
        o_ref = sums_out[j]
        for k in range(1, nz):
            c, d = third[j, k]
            c.wait_recv()
            d.wait_recv()
        for part, offset in ((a2, 0), (b2, half)):

            def body(i, carry, part=part, offset=offset, zb=zb, o_ref=o_ref):
                r = pl.ds(pl.multiple_of(i * 16, 16), 16)
                q = pl.ds(pl.multiple_of(i * 16 + offset, 16), 16)
                total = part[0, r].astype(F32)
                for k in range(1, nz):
                    total = total + zb[k, q].astype(F32)
                o_ref[q] = total.astype(o_ref.dtype)
                return carry

            lax.fori_loop(0, half // 16, body, 0)
    for copy in sends:
        copy.wait_send()
    for j in range(len(jobs)):
        for i in range(min(2, tiles[j])):
            for part in range(jobs[j][0]):
                wait_write(j, i, part)


def exchange(cid, sums=(), swaps=(), laid=0, jobs=()):
    n = lax.axis_size("ep")
    nz = n // 4
    groups = lax.axis_size("grp")
    m, w = len(sums), len(swaps)
    kept_rows = [p.shape[1] for p in sums]
    sums = [jnp.pad(p, ((0, 0), (0, -p.shape[1] % 32), (0, 0))) for p in sums]
    views = [p.reshape((nz, 2, 2) + p.shape[1:]) for p in sums]
    scratch = []
    for p in sums:
        rows, cols = p.shape[1:]
        half = rows // 2
        scratch += [pltpu.VMEM((nz, 2, half, cols), p.dtype)] * 4
        scratch += [pltpu.VMEM((nz, half, cols), p.dtype)] * 2
        scratch += [pltpu.VMEM((nz, rows, cols), p.dtype)]
    for p in sums:
        scratch += [DMA((nz,))] * 2 + [DMA((2 * nz,))] * 6
    if w:
        scratch += [DMA((w,)), DMA((w, n)), DMA((w, n))]
    plain, wide = swaps[: w - laid], swaps[w - laid :]
    scratch += [pltpu.VMEM(a.shape, a.dtype) for a in wide]
    jobs_out = []
    for left, right, parts, blocks in jobs:
        rows, cols = left.shape[1] // blocks, right.shape[1] // parts
        jobs_out += [jax.ShapeDtypeStruct((rows, cols), BF16)] * (parts * blocks)
        scratch += [pltpu.VMEM(left.shape, left.dtype), pltpu.VMEM(right.shape, right.dtype)]
        scratch += [pltpu.VMEM((2, parts, TILE, cols), BF16), DMA((2,))]
        scratch += [DMA((2, parts, TILE // math.gcd(TILE, rows)))]
    out = pl.pallas_call(
        functools.partial(exchange_kernel, n, m, w, laid, groups, [job[2:] for job in jobs]),
        out_shape=[jax.ShapeDtypeStruct(p.shape[1:], F32) for p in sums]
        + [jax.ShapeDtypeStruct(a.shape, a.dtype) for a in plain]
        + [jax.ShapeDtypeStruct((a.shape[1], n * a.shape[2]), F32) for a in wide]
        + jobs_out,
        in_specs=[ANY] * (m + w + 2 * len(jobs)),
        out_specs=[pl.BlockSpec(memory_space=pltpu.VMEM)] * m
        + [ANY] * (w - laid)
        + [pl.BlockSpec(memory_space=pltpu.VMEM)] * laid
        + [ANY] * len(jobs_out),
        scratch_shapes=scratch,
        compiler_params=pltpu.CompilerParams(
            collective_id=cid, has_side_effects=True, vmem_limit_bytes=(60 if jobs else 40) << 20 if m else None
        ),
        name="exchange",
    )(*views, *swaps, *(a for job in jobs for a in job[:2]))
    return [a[:rows] for a, rows in zip(out, kept_rows)] + list(out[m:])


def both(p):
    g = lax.axis_index("grp")
    mine = lax.dynamic_index_in_dim(p, g, 0, keepdims=False)
    theirs = lax.dynamic_index_in_dim(p, 1 - g, 0, keepdims=False)
    return mine, lax.ppermute(theirs.astype(BF16), "grp", [(0, 1), (1, 0)])


def over_groups(p):
    if lax.axis_size("grp") == 2:
        mine, other = both(p)
        return mine.astype(F32) + other.astype(F32)
    return lax.psum_scatter(p.astype(BF16), "grp", scatter_dimension=0, tiled=False).astype(F32)


def product_over_groups(left, right):
    groups = lax.axis_size("grp")
    rows = left.shape[1] // groups
    if groups != 2:
        whole = product("km,kn->mn", left, right)
        return over_groups(whole.reshape(groups, rows, -1))
    g = lax.axis_index("grp")
    mine = lax.dynamic_slice_in_dim(left, g * rows, rows, 1)
    theirs = lax.dynamic_slice_in_dim(left, (1 - g) * rows, rows, 1)
    sent = product("km,kn->mn", theirs, right).astype(BF16)
    other = lax.ppermute(sent, "grp", [(0, 1), (1, 0)])
    return product("km,kn->mn", mine, right) + other.astype(F32)


def from_partner(values):
    groups = lax.axis_size("grp")
    return lax.ppermute(values, "grp", [(g, g + 1 - 2 * (g % 2)) for g in range(groups)])


def to_row_owner(block):
    groups, n = lax.axis_size("grp"), lax.axis_size("ep")
    pairs = [(h * n + e, e * groups + h) for h in range(groups) for e in range(n)]
    return lax.ppermute(block.astype(BF16), ("grp", "ep"), pairs).astype(F32)


def dot(left, right):
    return jnp.dot(left, right, preferred_element_type=F32)


def dot_nt(left, right):
    return lax.dot_general(left, right, (((1,), (1,)), ((), ())), preferred_element_type=F32)


def front_kernel(
    x_ref, w_ref, cos_ref, sin_ref, gain_ref, lat_gain_ref, wq_ref, wl_ref, we_ref,
    normed_ref, query_ref, keys_ref, values_ref, latent_ref, out_w_ref,
):
    out_w_ref[...] = w_ref[...].reshape(out_w_ref.shape)
    blocks, tokens = x_ref.shape[:2]
    rows = blocks * tokens
    x = x_ref[...].reshape(rows, gain_ref.shape[1]).astype(F32)
    normed = (x * rms_scale(x) * gain_ref[...]).astype(BF16)
    normed_ref[...] = normed
    cos, sin = cos_ref[...], sin_ref[...]
    own_half = lax.broadcasted_iota(jnp.int32, cos.shape, 1) < ROPE

    def turn(pair):
        return pair * cos + pltpu.roll(pair, ROPE, 1) * sin

    query = dot_nt(normed, wq_ref[...])
    query_ref[:, :NOPE] = query[:, :NOPE].astype(BF16)
    query_ref[:, NOPE:] = jnp.where(own_half, turn(query[:, NOPE:]), 0.0).astype(BF16)
    compressed = dot(normed, wl_ref[...])
    raw = compressed[:, :LATENT]
    latent = (raw * rms_scale(raw) * lat_gain_ref[...]).astype(BF16)
    latent_ref[...] = latent
    expanded = dot(latent, we_ref[...])
    keys_ref[:, :NOPE] = expanded[:, :NOPE].astype(BF16)
    keys_ref[:, NOPE:] = turn(compressed[:, LATENT:]).astype(BF16)
    values_ref[...] = expanded[:, NOPE:].astype(BF16)


def front(x, cos, sin, gain, lat_gain, wq, wl, we):
    n, tokens = x.shape[:2]
    model = gain.shape[1]
    length = n * tokens
    blocks = 2
    rows = blocks * tokens

    def whole(a):
        return pl.BlockSpec(a.shape, lambda i: (0,) * a.ndim, pipeline_mode=pl.Buffered(1))

    def rows_of(cols):
        return pl.BlockSpec((rows, cols), lambda i: (i, 0))

    def out(cols):
        return jax.ShapeDtypeStruct((length, cols), BF16)

    cols = (model, wq.shape[0], NOPE + 2 * ROPE, VH, LATENT, model // 2)
    return pl.pallas_call(
        front_kernel,
        grid=(n // blocks,),
        in_specs=[
            pl.BlockSpec((blocks, tokens, model), lambda i: (i, 0, 0)),
            pl.BlockSpec((blocks, tokens, model // 2), lambda i: (i, 0, 2)),
            rows_of(2 * ROPE),
            rows_of(2 * ROPE),
        ]
        + [whole(a) for a in (gain, lat_gain, wq, wl, we)],
        out_specs=[rows_of(c) for c in cols],
        out_shape=[out(c) for c in cols],
        compiler_params=pltpu.CompilerParams(vmem_limit_bytes=48 << 20),
        name="front",
    )(x, x, cos, sin, gain, lat_gain, wq, wl, we)


def back_kernel(
    cos_ref, sin_ref, dq_ref, dk_ref, dv_ref, we_ref, query_ref, expanded_ref, latent_ref, rope_ref
):
    own_half = lax.broadcasted_iota(jnp.int32, cos_ref.shape, 1) < ROPE
    pair = dq_ref[:, NOPE:] * jnp.where(own_half, cos_ref[...], sin_ref[...])
    pair = jnp.where(own_half, pair + pltpu.roll(pair, ROPE, 1), 0.0)
    query_ref[:, :NOPE] = dq_ref[:, :NOPE].astype(BF16)
    query_ref[:, NOPE:] = pair.astype(BF16)
    expanded_ref[:, :NOPE] = dk_ref[:, :NOPE].astype(BF16)
    expanded_ref[:, NOPE:] = dv_ref[...].astype(BF16)
    latent_ref[...] = dot_nt(expanded_ref[...], we_ref[...]).astype(BF16)
    rope_ref[...] = dk_ref[:, NOPE:].astype(BF16)


def back(cos, sin, dq, dk, dv, we):
    length = dq.shape[0]
    rows = 512

    def rows_of(cols):
        return pl.BlockSpec((rows, cols), lambda i: (i, 0))

    def out(cols):
        return jax.ShapeDtypeStruct((length, cols), BF16)

    cols = (NOPE + 2 * ROPE, NOPE + VH, LATENT, 2 * ROPE)
    return pl.pallas_call(
        back_kernel,
        grid=(length // rows,),
        in_specs=[rows_of(a.shape[1]) for a in (cos, sin, dq, dk, dv)]
        + [pl.BlockSpec(we.shape, lambda i: (0, 0))],
        out_specs=[rows_of(c) for c in cols],
        out_shape=[out(c) for c in cols],
        compiler_params=pltpu.CompilerParams(vmem_limit_bytes=40 << 20),
        name="back",
    )(cos, sin, dq, dk, dv, we)


KEYS = 512


def scores_of(scale, prefix, k, q, first_key, first_query):
    scores = dot_nt(k, q) * scale
    key = first_key + lax.broadcasted_iota(jnp.int32, scores.shape, 0)
    query = first_query + lax.broadcasted_iota(jnp.int32, scores.shape, 1)
    return jnp.where((key <= query) | (key < prefix), scores, MASKED)


def key_blocks(prefix, last_query):
    return (jnp.maximum(last_query, prefix) + KEYS - 1) // KEYS


def attend_kernel(scale, prefix_ref, q_ref, k_ref, v_ref, attended_ref, exact_ref, lse_ref):
    q = q_ref[...]
    rows = q.shape[0]
    start = pl.program_id(0) * rows
    prefix = prefix_ref[0]

    def step(j, carry):
        top, total, out = carry
        s = scores_of(scale, prefix, k_ref[j], q, j * KEYS, start)
        new_top = jnp.maximum(top, jnp.max(s, axis=0, keepdims=True))
        p = jnp.exp(s - new_top)
        shrink = jnp.exp(top - new_top)
        total = total * shrink + jnp.sum(p, axis=0, keepdims=True)
        return new_top, total, out * shrink + dot(v_ref[j], p.astype(BF16))

    top, total, out = lax.fori_loop(
        0,
        key_blocks(prefix, start + rows),
        step,
        (
            jnp.full((1, rows), MASKED, F32),
            jnp.zeros((1, rows), F32),
            jnp.zeros((v_ref.shape[1], rows), F32),
        ),
    )
    lse_ref[...] = top + jnp.log(total)
    exact = (out / total).T
    exact_ref[...] = exact
    attended_ref[...] = exact.astype(BF16)


def attend(prefix, q, k, v):
    length, depth = q.shape
    values = v.shape[1]
    rows = 256
    v = v.reshape(length // KEYS, KEYS, values).transpose(0, 2, 1)
    k = k.reshape(length // KEYS, KEYS, depth)
    return pl.pallas_call(
        functools.partial(attend_kernel, 1.0 / math.sqrt(NOPE + ROPE)),
        grid=(length // rows,),
        in_specs=[
            pl.BlockSpec(memory_space=pltpu.SMEM),
            pl.BlockSpec((rows, depth), lambda i: (i, 0)),
            pl.BlockSpec(k.shape, lambda i: (0, 0, 0)),
            pl.BlockSpec(v.shape, lambda i: (0, 0, 0)),
        ],
        out_specs=[
            pl.BlockSpec((rows, values), lambda i: (i, 0)),
            pl.BlockSpec((rows, values), lambda i: (i, 0)),
            pl.BlockSpec((1, rows), lambda i: (0, i)),
        ],
        out_shape=[
            jax.ShapeDtypeStruct((length, values), BF16),
            jax.ShapeDtypeStruct((length, values), F32),
            jax.ShapeDtypeStruct((1, length), F32),
        ],
        compiler_params=pltpu.CompilerParams(vmem_limit_bytes=32 << 20),
        name="attend",
    )(prefix, q, k, v)


def attend_back_kernel(
    scale, prefix_ref, q_ref, g_ref, lse_ref, delta_ref, k_ref, v_ref, dq_ref, dk_ref, dv_ref
):
    q, g = q_ref[...], g_ref[...]
    rows = q.shape[0]
    start = pl.program_id(0) * rows
    prefix = prefix_ref[0]

    @pl.when(pl.program_id(0) == 0)
    def _():
        dk_ref[...] = jnp.zeros_like(dk_ref)
        dv_ref[...] = jnp.zeros_like(dv_ref)

    def step(j, dq):
        k = k_ref[j]
        p = jnp.exp(scores_of(scale, prefix, k, q, j * KEYS, start) - lse_ref[...])
        ds = (p * (dot_nt(v_ref[j], g) - delta_ref[...]) * scale).astype(BF16)
        dv_ref[j] += dot(p.astype(BF16), g)
        dk_ref[j] += dot(ds, q)
        return dq + lax.dot_general(
            ds, k, (((0,), (0,)), ((), ())), preferred_element_type=F32
        )

    dq_ref[...] = lax.fori_loop(
        0, key_blocks(prefix, start + rows), step, jnp.zeros(dq_ref.shape, F32)
    )


def attend_back(prefix, q, g, lse, delta, k, v):
    length, depth = q.shape
    values = v.shape[1]
    rows = 256
    k = k.reshape(length // KEYS, KEYS, depth)
    v = v.reshape(length // KEYS, KEYS, values)
    dq, dk, dv = pl.pallas_call(
        functools.partial(attend_back_kernel, 1.0 / math.sqrt(NOPE + ROPE)),
        grid=(length // rows,),
        in_specs=[
            pl.BlockSpec(memory_space=pltpu.SMEM),
            pl.BlockSpec((rows, depth), lambda i: (i, 0)),
            pl.BlockSpec((rows, values), lambda i: (i, 0)),
            pl.BlockSpec((1, rows), lambda i: (0, i)),
            pl.BlockSpec((1, rows), lambda i: (0, i)),
            pl.BlockSpec(k.shape, lambda i: (0, 0, 0)),
            pl.BlockSpec(v.shape, lambda i: (0, 0, 0)),
        ],
        out_specs=[
            pl.BlockSpec((rows, depth), lambda i: (i, 0)),
            pl.BlockSpec(k.shape, lambda i: (0, 0, 0)),
            pl.BlockSpec(v.shape, lambda i: (0, 0, 0)),
        ],
        out_shape=[
            jax.ShapeDtypeStruct((length, depth), F32),
            jax.ShapeDtypeStruct(k.shape, F32),
            jax.ShapeDtypeStruct(v.shape, F32),
        ],
        compiler_params=pltpu.CompilerParams(vmem_limit_bytes=40 << 20),
        name="attend_back",
    )(prefix, q, g, lse, delta, k, v)
    return dq, dk.reshape(length, depth), dv.reshape(length, values)


def ffn_kernel(
    n,
    x_ref,
    y_ref,
    slots_ref,
    tokens_ref,
    own_ref,
    router_ref,
    sg_ref,
    su_ref,
    sd_ref,
    eg_ref,
    eu_ref,
    ed_ref,
    out_ref,
    ffn_ref,
    dot_ref,
    probs_ref,
    rows_ref,
    hidden_ref,
    slot_grad_ref,
    grad_gu_ref,
    shared_h_ref,
    shared_gu_ref,
    expert_out,
    row_grad,
):
    blocks, tokens = x_ref.shape[:2]
    capacity = slots_ref.shape[1]
    own = own_ref[...]
    lanes = lax.broadcasted_iota(jnp.int32, (tokens, own.shape[1]), 1)
    gates = []
    for b in range(blocks):
        x, y = x_ref[b], y_ref[b]
        logits = jnp.where(lanes < n, dot(x, router_ref[...]), MASKED)
        raised = jnp.exp(logits - jnp.max(logits, axis=-1, keepdims=True))
        probs = raised / jnp.sum(raised, axis=-1, keepdims=True)
        probs_ref[b] = probs
        gate = jnp.sum(probs * own, axis=-1, keepdims=True)
        gates.append(gate)
        part = pl.ds(b * capacity, capacity)
        rows_ref[part] = dot(slots_ref[b], x).astype(BF16)
        weighted = (gate * y.astype(F32)).astype(BF16)
        slot_grad_ref[part] = dot(slots_ref[b], weighted).astype(BF16)
    rows = rows_ref[...]
    slot_grad = slot_grad_ref[...]
    g = dot(rows, eg_ref[...])
    u = dot(rows, eu_ref[...])
    sigmoid = 1.0 / (1.0 + jnp.exp(-g))
    silu = g * sigmoid
    hidden = (silu * u).astype(BF16)
    hidden_ref[...] = hidden
    expert_out[...] = dot(hidden, ed_ref[...]).astype(BF16)
    grad_hidden = dot_nt(slot_grad, ed_ref[...])
    grad_g = (grad_hidden * u * sigmoid * (1.0 + g * (1.0 - sigmoid))).astype(BF16)
    grad_u = (grad_hidden * silu).astype(BF16)
    grad_gu_ref[:, : grad_g.shape[1]] = grad_g
    grad_gu_ref[:, grad_g.shape[1] :] = grad_u
    row_grad[...] = (dot_nt(grad_g, eg_ref[...]) + dot_nt(grad_u, eu_ref[...])).astype(BF16)
    x = x_ref[...].reshape(blocks * tokens, -1)
    y = y_ref[...].reshape(blocks * tokens, -1)
    g = dot_nt(x, sg_ref[...])
    u = dot_nt(x, su_ref[...])
    grad_hidden = dot_nt(y, sd_ref[...])
    sigmoid = 1.0 / (1.0 + jnp.exp(-g))
    silu = g * sigmoid
    hidden = (silu * u).astype(BF16)
    grad_g = (grad_hidden * u * sigmoid * (1.0 + g * (1.0 - sigmoid))).astype(BF16)
    grad_u = (grad_hidden * silu).astype(BF16)
    shared = hidden.shape[1]
    shared_h_ref[...] = hidden.reshape(blocks, tokens, shared)
    shared_gu_ref[:, :, :shared] = grad_g.reshape(blocks, tokens, shared)
    shared_gu_ref[:, :, shared:] = grad_u.reshape(blocks, tokens, shared)
    width = x.shape[1]
    chunk = width // 4
    met = [0.0] * blocks
    for c in range(width // chunk):
        cols = pl.ds(c * chunk, chunk)
        shared_out = dot(hidden, sd_ref[:, cols])
        shared_ffn = dot(grad_g, sg_ref[:, cols]) + dot(grad_u, su_ref[:, cols])
        for b in range(blocks):
            part = pl.ds(b * capacity, capacity)
            here = slice(b * tokens, (b + 1) * tokens)
            picked = dot(tokens_ref[b], expert_out[part, cols])
            met[b] += jnp.sum(picked * y_ref[b, :, cols].astype(F32), axis=-1, keepdims=True)
            out_ref[b, :, cols] = (shared_out[here] + picked * gates[b]).astype(BF16)
            back = dot(tokens_ref[b], row_grad[part, cols])
            ffn_ref[b, :, cols] = (shared_ffn[here] + back).astype(BF16)
    for b in range(blocks):
        dot_ref[b] = (met[b] * own).astype(BF16)


def ffn(x, y, slots, own_lane, router_w, gate_t, up_t, down, gate_m, up_m, down_m):
    n, tokens, width = x.shape
    capacity = slots.shape[1]
    hidden = gate_m.shape[1]
    shared = gate_t.shape[0]
    group = 4

    def whole(a):
        return pl.BlockSpec(a.shape, lambda i: (0,) * a.ndim, pipeline_mode=pl.Buffered(1))

    def block(*shape):
        return pl.BlockSpec((group,) + shape, lambda i: (i, 0, 0))

    def slot_rows(cols):
        return pl.BlockSpec((group * capacity, cols), lambda i: (i, 0))

    def tokens_of(cols, kind=BF16):
        return jax.ShapeDtypeStruct((n, tokens, cols), kind)

    def slots_of(cols):
        return jax.ShapeDtypeStruct((n * capacity, cols), BF16)

    weights = (own_lane, router_w, gate_t, up_t, down, gate_m, up_m, down_m)
    return pl.pallas_call(
        functools.partial(ffn_kernel, n),
        grid=(n // group,),
        in_specs=[
            block(tokens, width),
            block(tokens, width),
            block(capacity, tokens),
            block(tokens, capacity),
        ]
        + [whole(a) for a in weights],
        out_specs=[
            block(tokens, width),
            block(tokens, width),
            block(tokens, 128),
            block(tokens, 128),
            slot_rows(width),
            slot_rows(hidden),
            slot_rows(width),
            slot_rows(2 * hidden),
            block(tokens, shared),
            block(tokens, 2 * shared),
        ],
        out_shape=[
            tokens_of(width),
            tokens_of(width),
            tokens_of(128),
            tokens_of(128, F32),
            slots_of(width),
            slots_of(hidden),
            slots_of(width),
            slots_of(2 * hidden),
            tokens_of(shared),
            tokens_of(2 * shared),
        ],
        scratch_shapes=[
            pltpu.VMEM((group * capacity, width), BF16),
            pltpu.VMEM((group * capacity, width), BF16),
        ],
        compiler_params=pltpu.CompilerParams(vmem_limit_bytes=60 << 20),
        name="ffn",
    )(x, y, slots, slots.transpose(0, 2, 1), *weights)


def product(form, left, right):
    return jnp.einsum(form, left, right, preferred_element_type=F32)


def rms_scale(values):
    return lax.rsqrt(jnp.mean(values * values, axis=-1, keepdims=True) + EPSILON)


def rotary_tables(tokens, n):
    halfway = ROPE // 2
    inverse = 10000.0 ** (-(jnp.arange(halfway, dtype=F32) * 2.0 / ROPE))
    inverse = jnp.concatenate([inverse] * 4)
    lane = jnp.arange(2 * ROPE)
    sign = jnp.where((lane < halfway) | (lane >= 3 * halfway), -1.0, 1.0)
    base = (jnp.arange(n, dtype=F32) * tokens)[:, None] * inverse
    step = jnp.arange(tokens, dtype=F32)[:, None] * inverse
    base_cos, base_sin = jnp.cos(base)[:, None], jnp.sin(base)[:, None]
    step_cos, step_sin = jnp.cos(step)[None], jnp.sin(step)[None]
    cos_table = base_cos * step_cos - base_sin * step_sin
    sin_table = (base_sin * step_cos + base_cos * step_sin) * sign
    return cos_table.reshape(n * tokens, -1), sin_table.reshape(n * tokens, -1)


def unrotate(grads, cos_table, sin_table):
    halfway = grads.shape[-1] // 2
    first = grads[..., :halfway]
    second = grads[..., halfway:]
    return jnp.concatenate(
        [first * cos_table + second * sin_table, second * cos_table - first * sin_table], axis=-1
    )


def norm_back(grad_unit, unit_values, scale_values):
    return scale_values * (
        grad_unit - unit_values * jnp.mean(grad_unit * unit_values, axis=-1, keepdims=True)
    )


def column_halves(weight, n, half):
    rows, width = weight.shape[0], weight.shape[1] // n
    parts = weight.T.reshape(n, 2, width // 2, rows)
    return lax.dynamic_index_in_dim(parts, half, 1, keepdims=False)


def columns_in(blocks):
    n, width, rows = blocks.shape
    return blocks.transpose(1, 0, 2).reshape(width, n * rows)


def both_halves(mine, other, even, axis=0):
    return jnp.concatenate([jnp.where(even, mine, other), jnp.where(even, other, mine)], axis=axis)


def per_device(
    layer_input,
    attention_gain,
    query_weight,
    latent_weight,
    latent_gain,
    expand_weight,
    output_weight,
    feedforward_gain,
    router_weight,
    shared_gate,
    shared_up,
    shared_down,
    expert_gate,
    expert_up,
    expert_down,
    expert_routes,
    prefix_length,
    output_grad,
):
    n = lax.axis_size("ep")
    groups = lax.axis_size("grp")
    e = lax.axis_index("ep")
    half = lax.axis_index("grp") % 2
    even = half == 0
    tokens = layer_input.shape[0]
    length = tokens * n
    capacity = tokens * TOPK * 4 // (3 * n)
    rows_dev = attention_gain.shape[0]
    latent_rows = latent_gain.shape[0]
    rows_out = D // (groups * n)
    expand_rows = LATENT // (groups * n)

    out_w_half = lax.dynamic_slice_in_dim(output_weight, half * (D // 2), D // 2, 1)
    first_block = jnp.concatenate(
        [layer_input, out_w_half, latent_weight, router_weight, expert_routes.astype(BF16)], axis=1
    )
    width = first_block.shape[1]
    first_block = jnp.pad(first_block, ((0, 0), (0, -width % 128)))
    gains = jnp.zeros((16, rows_dev), BF16)
    gains = gains.at[0].set(attention_gain).at[1].set(feedforward_gain)
    gains = gains.at[2, :latent_rows].set(latent_gain)
    shared_half = jnp.where(even, shared_gate, shared_up)
    expand_half = lax.dynamic_index_in_dim(
        expand_weight.reshape(latent_rows, n, 2, -1), half, 2, keepdims=False
    ).transpose(1, 0, 2)
    first_all, q_blocks, x_blocks, shared_blocks, gain_blocks = gather(
        first_block,
        0,
        swaps=(
            column_halves(query_weight, n, half),
            expand_half,
            shared_half.T.reshape(n, shared_half.shape[1] // n, rows_dev),
            jnp.broadcast_to(gains, (n,) + gains.shape),
        ),
    )
    c0 = D + D // 2
    c1 = c0 + LATENT + ROPE
    c2 = c1 + n
    latent_w = first_all[:, :, c0:c1].reshape(D, LATENT + ROPE)
    router_w = first_all[:, :, c1:c2].reshape(D, n)
    routes = first_all[:, :, c2 : c2 + TOPK].astype(jnp.int32)
    attn_gain = gain_blocks[:, 0].reshape(D).astype(F32)
    ffn_gain = gain_blocks[:, 1].reshape(D).astype(F32)
    lat_gain = gain_blocks[:, 2, :latent_rows].reshape(LATENT).astype(F32)

    later_grad, q_blocks = lax.optimization_barrier((output_grad, q_blocks))
    all_out_grad = lax.all_gather(later_grad, "ep", axis=0, tiled=True)

    q_mine, x_mine = columns_in(q_blocks), x_blocks.reshape(LATENT, -1)
    query_t = both_halves(q_mine, from_partner(q_mine), even)
    expand_w = both_halves(x_mine, from_partner(x_mine), even, 1)
    shared_mine = columns_in(shared_blocks)
    shared_other = from_partner(shared_mine)
    gate_t = jnp.where(even, shared_mine, shared_other)
    up_t = jnp.where(even, shared_other, shared_mine)

    def own(values):
        return lax.dynamic_slice_in_dim(values, e * tokens, tokens, 0)

    cos_table, sin_table = rotary_tables(tokens, n)
    turned = jnp.concatenate(
        [query_t, query_t[NOPE + ROPE // 2 :], query_t[NOPE : NOPE + ROPE // 2]], axis=0
    )
    latent_turned = jnp.concatenate(
        [latent_w, latent_w[:, LATENT + ROPE // 2 :], latent_w[:, LATENT : LATENT + ROPE // 2]],
        axis=1,
    )
    normed, query, keys, values, latent, out_w_mine = front(
        first_all, cos_table, sin_table, attn_gain[None], lat_gain[None], turned, latent_turned, expand_w
    )
    out_w_other = from_partner(out_w_mine)
    attended_head, attended_exact, lse = attend(prefix_length, query, keys, values)
    (attended_blocks,) = exchange(2, swaps=(attended_head.reshape(n, tokens, VH),))
    attended = attended_blocks.transpose(1, 0, 2).reshape(tokens, HEADS * VH)

    residual_in = layer_input.astype(F32)
    input_scale = rms_scale(residual_in)
    input_unit = residual_in * input_scale
    out_mine = product("ta,ad->td", attended, out_w_mine)
    out_other = product("ta,ad->td", attended, out_w_other)
    residual_mid = residual_in + jnp.concatenate(
        [jnp.where(even, out_mine, out_other), jnp.where(even, out_other, out_mine)], axis=1
    )
    mid_scale = rms_scale(residual_mid)
    mid_unit = residual_mid * mid_scale
    own_ffn_in = (mid_unit * ffn_gain).astype(BF16)
    (ffn_blocks,) = gather(own_ffn_in, 3)
    query_cols = query_weight.shape[1] // 2
    query_w_half = lax.dynamic_slice_in_dim(query_weight, half * query_cols, query_cols, 1)
    query_w_half, ffn_blocks = lax.optimization_barrier((query_w_half, ffn_blocks))
    query_w_mine = lax.all_gather(query_w_half, "ep", axis=0, tiled=True)
    query_w_other = from_partner(query_w_mine)
    ffn_in = ffn_blocks.reshape(length, D)

    own_lane = (jnp.arange(128, dtype=jnp.int32) == e).astype(F32)[None]
    chosen = jnp.any(routes == e, axis=-1)
    chosen_int = chosen.astype(jnp.int32)
    place = jnp.cumsum(chosen_int, axis=1) - chosen_int
    kept = chosen & (place < capacity)
    dispatch = (
        (place[:, None, :] == jnp.arange(capacity, dtype=jnp.int32)[None, :, None])
        & kept[:, None, :]
    ).astype(BF16)
    shared_width = gate_t.shape[0]
    fill = ((0, -shared_width % 128), (0, 0))
    (
        out_partial,
        ffn_partial,
        dot_partial,
        router_all,
        incoming,
        expert_hidden,
        slot_grad,
        grad_expert_gu,
        shared_hidden,
        grad_shared_gu,
    ) = ffn(
        ffn_blocks,
        all_out_grad.reshape(n, tokens, D),
        dispatch,
        own_lane,
        jnp.pad(router_w, ((0, 0), (0, 128 - n))),
        jnp.pad(gate_t, fill),
        jnp.pad(up_t, fill),
        jnp.pad(shared_down, fill),
        expert_gate[0],
        expert_up[0],
        expert_down[0],
    )
    ffn_sum, dot_sum, out_sum, *products = exchange(
        4,
        sums=(ffn_partial, dot_partial, out_partial),
        jobs=((expert_hidden, slot_grad, 1, groups), (incoming, grad_expert_gu, 2, groups)),
    )
    layer_output = (residual_mid + out_sum).astype(BF16)

    def by_group(values):
        return over_groups(values.reshape(groups, values.shape[0] // groups, -1))

    router_own = lax.dynamic_index_in_dim(router_all, e, 0, keepdims=False)[:, :n]
    grad_probs = dot_sum[:, :n]
    grad_logits = (
        router_own * (grad_probs - jnp.sum(router_own * grad_probs, axis=-1, keepdims=True))
    ).astype(BF16)
    grad_ffn_in = ffn_sum + product("te,de->td", grad_logits, router_w)
    grad_ffn_gain = jnp.sum(grad_ffn_in * mid_unit, axis=0)
    grad_mid = output_grad.astype(F32) + norm_back(grad_ffn_in * ffn_gain, mid_unit, mid_scale)
    grad_mid_b = grad_mid.astype(BF16)
    mid_left, mid_right = grad_mid_b[:, : D // 2], grad_mid_b[:, D // 2 :]
    grad_attended = (
        product("td,ad->ta", jnp.where(even, mid_left, mid_right), out_w_mine)
        + product("td,ad->ta", jnp.where(even, mid_right, mid_left), out_w_other)
    ).astype(BF16)
    output_w_partial = product_over_groups(attended, grad_mid_b).astype(BF16)
    output_w_partial, grad_attended = lax.optimization_barrier((output_w_partial, grad_attended))
    (grad_att_blocks,) = exchange(
        5, swaps=(grad_attended.reshape(tokens, HEADS, VH).transpose(1, 0, 2),)
    )
    *products, grad_att_blocks = lax.optimization_barrier((*products, grad_att_blocks))
    grad_att = grad_att_blocks.reshape(length, VH)

    def blocks_over_groups(blocks):
        total = blocks[0].astype(F32)
        for k in range(1, groups):
            shift = [(g, (g + k) % groups) for g in range(groups)]
            total = total + lax.ppermute(blocks[k], "grp", shift).astype(F32)
        return total

    expert_down_grad, expert_gate_grad, expert_up_grad = (
        blocks_over_groups(products[k * groups : (k + 1) * groups])[None] for k in range(3)
    )

    grad_router = product("te,td->ed", grad_logits, own_ffn_in)

    delta = jnp.sum(grad_att.astype(F32) * attended_exact, axis=-1)[None]
    grad_query_raw, grad_keys, grad_values = attend_back(
        prefix_length, query, grad_att, lse, delta, keys, values
    )
    grad_query, grad_expanded, latent_partial, rope_partial = back(
        cos_table, sin_table, grad_query_raw, grad_keys, grad_values, expand_w
    )
    (
        latent_sum,
        rope_sum,
        output_weight_grad,
        query_blocks,
        side_down,
        *products,
    ) = exchange(
        6,
        sums=(
            latent_partial.reshape(n, tokens, LATENT),
            rope_partial.reshape(n, tokens, 2 * ROPE),
            output_w_partial.reshape(n, rows_out, D),
        ),
        swaps=(grad_query.reshape(n, tokens, -1),),
        jobs=(
            (shared_hidden.reshape(length, -1), all_out_grad, 1, 1),
            (ffn_in, grad_shared_gu.reshape(length, -1), 2, groups),
            (normed, grad_query, 1, groups),
            (latent, grad_expanded, 1, groups),
        ),
    )
    shared_down_grad = to_row_owner(by_group(side_down[:shared_width]))
    side_gate, side_up, side_query, grad_expand = (
        blocks_over_groups(products[k * groups : (k + 1) * groups]).astype(BF16) for k in range(4)
    )
    side_gate, side_up = side_gate[:, :shared_width], side_up[:, :shared_width]
    side_query = side_query[:, : query_t.shape[0]]

    own_normed = (input_unit * attn_gain).astype(BF16)
    own_raw = product("td,dc->tc", own_normed, latent_w[:, :LATENT])
    latent_scale = rms_scale(own_raw)
    latent_unit = own_raw * latent_scale
    grad_latent_gain = jnp.sum(latent_sum * latent_unit, axis=0)
    grad_compressed = jnp.concatenate(
        [
            norm_back(latent_sum * lat_gain, latent_unit, latent_scale),
            unrotate(
                rope_sum[:, :ROPE],
                own(cos_table)[:, : ROPE // 2],
                own(sin_table)[:, ROPE // 2 : ROPE],
            ),
        ],
        axis=-1,
    ).astype(BF16)
    latent_w_partial = product_over_groups(
        own_normed, jnp.pad(grad_compressed, ((0, 0), (0, 640 - LATENT - ROPE)))
    ).astype(BF16)
    own_part = product("tc,dc->td", grad_compressed, latent_w)

    def of_heads(part):
        heads = lax.dynamic_slice_in_dim(query_blocks, part * (n // 2), n // 2, 0)
        return heads[:, :, : NOPE + ROPE].transpose(1, 0, 2).reshape(tokens, -1)

    grad_normed = (
        product("tc,dc->td", of_heads(half), query_w_mine)
        + product("tc,dc->td", of_heads(1 - half), query_w_other)
        + own_part
    )
    grad_attn_gain = jnp.sum(grad_normed * input_unit, axis=0)

    def by_owner(values, rows):
        blocks = values.reshape(-1, groups, n, rows).transpose(2, 1, 0, 3)
        return blocks.reshape(n, groups, -1)

    small = jnp.concatenate(
        [
            by_owner(grad_attn_gain, rows_out),
            by_owner(grad_ffn_gain, rows_out),
            by_owner(grad_router, rows_out),
            by_owner(grad_latent_gain, expand_rows),
        ],
        axis=2,
    )
    small = small.transpose(1, 0, 2)
    if groups == 2:
        g = lax.axis_index("grp")
        mine = lax.dynamic_index_in_dim(small, g, 0, keepdims=False)
        theirs = lax.dynamic_index_in_dim(small, 1 - g, 0, keepdims=False)
        small = mine + lax.ppermute(theirs, "grp", [(0, 1), (1, 0)])
    else:
        small = lax.psum_scatter(small, "grp", scatter_dimension=0)
    (
        latent_weight_sum,
        small_all,
        query_weight_grad,
        shared_gate_grad,
        shared_up_grad,
        expand_weight_grad,
    ) = exchange(
        7,
        sums=(latent_w_partial.reshape(n, rows_out, -1),),
        swaps=(
            small[:, None],
            side_query.reshape(n, rows_out, -1),
            side_gate.reshape(n, rows_out, -1),
            side_up.reshape(n, rows_out, -1),
            grad_expand.reshape(n, expand_rows, -1),
        ),
        laid=4,
    )
    input_grad = (
        grad_mid + norm_back(grad_normed * attn_gain, input_unit, input_scale)
    ).astype(BF16)
    latent_weight_grad = latent_weight_sum[:, : LATENT + ROPE]
    small_sum = jnp.sum(small_all[:, 0], axis=0)
    attention_gain_grad = small_sum[:rows_out]
    feedforward_gain_grad = small_sum[rows_out : 2 * rows_out]
    router_weight_grad = small_sum[2 * rows_out : (2 + n) * rows_out].reshape(n, rows_out).T
    latent_gain_grad = small_sum[(2 + n) * rows_out :]
    return (
        layer_output,
        input_grad,
        attention_gain_grad,
        query_weight_grad,
        latent_weight_grad,
        latent_gain_grad,
        expand_weight_grad,
        output_weight_grad,
        feedforward_gain_grad,
        router_weight_grad,
        shared_gate_grad,
        shared_up_grad,
        shared_down_grad,
        expert_gate_grad,
        expert_up_grad,
        expert_down_grad,
    )


def solution(mesh):
    return jax.shard_map(
        per_device,
        mesh=mesh,
        in_specs=(
            P(("grp", "ep"), None),
            P("ep"),
            P("ep", None),
            P("ep", None),
            P("ep"),
            P("ep", None),
            P("ep", None),
            P("ep"),
            P("ep", None),
            P("ep", None),
            P("ep", None),
            P("ep", None),
            P("ep", None, None),
            P("ep", None, None),
            P("ep", None, None),
            P(("grp", "ep"), None),
            P("grp"),
            P(("grp", "ep"), None),
        ),
        out_specs=(
            P(("grp", "ep"), None),
            P(("grp", "ep"), None),
            P(("grp", "ep")),
            P(("grp", "ep"), None),
            P(("grp", "ep"), None),
            P(("grp", "ep")),
            P(("grp", "ep"), None),
            P(("grp", "ep"), None),
            P(("grp", "ep")),
            P(("grp", "ep"), None),
            P(("grp", "ep"), None),
            P(("grp", "ep"), None),
            P(("grp", "ep"), None),
            P("ep", "grp", None),
            P("ep", "grp", None),
            P("ep", "grp", None),
        ),
        check_vma=False,
    )
```

```python
import functools
import math

import jax
import jax.numpy as jnp
from jax import lax
from jax.experimental import pallas as pl
from jax.experimental.pallas import tpu as pltpu
from jax.sharding import PartitionSpec as P

D = 2048
HEADS = 16
NOPE = 128
ROPE = 64
VH = 128
LATENT = 512
TOPK = 6

EPSILON = 1e-06
MASKED = -1e30

MESH = pl.DeviceIdType.MESH
ANY = pl.BlockSpec(memory_space=pl.ANY)
DMA = pltpu.SemaphoreType.DMA
F32 = jnp.float32
BF16 = jnp.bfloat16


def remote(src, dst, send, recv, peer):
    return pltpu.make_async_remote_copy(
        src_ref=src,
        dst_ref=dst,
        send_sem=send,
        recv_sem=recv,
        device_id={"ep": peer},
        device_id_type=MESH,
    )


def greet(peers):
    barrier = pltpu.get_barrier_semaphore()
    for peer in peers:
        pl.semaphore_signal(barrier, inc=1, device_id={"ep": peer}, device_id_type=MESH)
    pl.semaphore_wait(barrier, len(peers))


def around(n):
    me = lax.axis_index("ep")
    x, y = me % 2, (me // 2) % 2
    return me, me // 4, y, x, me + 1 - 2 * x, me + 2 - 4 * y


def near(z, nz, below, above):
    for s in range(nz - 1):
        pl.when(z - 1 - s >= 0)(functools.partial(below, s, z - 1 - s))
        pl.when(z + 1 + s < nz)(functools.partial(above, s, z + 1 + s))


def greet_near(px, py, up, down, z, nz):
    barrier = pltpu.get_barrier_semaphore()
    for peer, there in ((px, None), (py, None), (up, z + 1 < nz), (down, z > 0)):

        def hello(peer=peer):
            pl.semaphore_signal(barrier, inc=1, device_id={"ep": peer}, device_id_type=MESH)

        hello() if there is None else pl.when(there)(hello)
    on_line = (z + 1 < nz).astype(jnp.int32) + (z > 0).astype(jnp.int32)
    pl.semaphore_wait(barrier, 2 + on_line)


def start_swaps(n, ins, outs, sems):
    own, ss, rs = sems
    me = lax.axis_index("ep")
    sends, copies = [], []
    for j in range(len(ins)):
        local = pltpu.make_async_copy(ins[j].at[me], outs[j].at[me], own.at[j])
        local.start()
        copies.append(local)
    for k in range(1, n):
        to = (me + k) % n
        for j in range(len(ins)):
            c = remote(ins[j].at[to], outs[j].at[me], ss.at[j, k], rs.at[j, k], to)
            c.start()
            sends.append(c)
    return sends, copies


def end_swaps(n, ins, outs, sems, started):
    own, ss, rs = sems
    me = lax.axis_index("ep")
    sends, copies = started
    for k in range(1, n):
        to, back = (me + k) % n, (me + n - k) % n
        for j in range(len(ins)):
            remote(ins[j].at[back], outs[j].at[back], ss.at[j, k], rs.at[j, k], to).wait_recv()
    for copy in sends:
        copy.wait_send()
    for copy in copies:
        copy.wait()


def gather_kernel(n, w, x_ref, *refs):
    swaps_in, o_ref, swaps_out = refs[:w], refs[w], refs[w + 1 : 2 * w + 1]
    own, us, ur, ds, dr, xs, xr, ys, yr, *swap_sems = refs[2 * w + 1 :]
    me, z, y, x, px, py = around(n)
    nz = n // 4
    low = me % 4
    half = x_ref.shape[0] // 2
    top, bottom = pl.ds(0, half), pl.ds(half, half)
    up, down = (me + 4) % n, (me + n - 4) % n
    everyone = [(me + k) % n for k in range(n)]
    if w:
        greet(everyone[1:])
    else:
        greet_near(px, py, up, down, z, nz)
    local = pltpu.make_async_copy(x_ref, o_ref.at[me], own)
    local.start()

    def over_x(src, b, part, i):
        return remote(src.at[part], o_ref.at[b, part], xs.at[i], xr.at[i], px)

    def over_y(src, b, part, i):
        return remote(src.at[part], o_ref.at[b, part], ys.at[i], yr.at[i], py)

    def upward(src, b, s):
        return remote(src, o_ref.at[b], us.at[s], ur.at[s], up)

    def downward(src, b, s):
        return remote(src, o_ref.at[b], ds.at[s], dr.at[s], down)

    def spread(src, t):
        b = t * 4 + low
        over_x(src, b, top, t).start()
        over_y(src, b, bottom, t).start()
        over_y(src, b, top, nz + t).start()
        over_x(src, b, bottom, nz + t).start()

    pl.when(z + 1 < nz)(lambda: upward(x_ref, me, 0).start())
    pl.when(z > 0)(lambda: downward(x_ref, me, 0).start())
    spread(x_ref, z)
    swapping = start_swaps(n, swaps_in, swaps_out, swap_sems) if w else None

    def from_below(s, t):
        b = t * 4 + low
        upward(o_ref.at[b], b, s).wait_recv()
        pl.when(z + 1 < nz)(lambda: upward(o_ref.at[b], b, s + 1).start())
        spread(o_ref.at[b], t)

    def from_above(s, t):
        b = t * 4 + low
        downward(o_ref.at[b], b, s).wait_recv()
        pl.when(z > 0)(lambda: downward(o_ref.at[b], b, s + 1).start())
        spread(o_ref.at[b], t)

    def turn(s, t):
        bx = t * 4 + low + px - me
        by = t * 4 + low + py - me
        over_x(o_ref.at[bx], bx, top, t).wait_recv()
        over_y(o_ref.at[bx], bx, top, 2 * nz + t).start()
        over_y(o_ref.at[by], by, bottom, t).wait_recv()
        over_x(o_ref.at[by], by, bottom, 2 * nz + t).start()

    for s in range(nz - 1):
        pl.when(z - 1 - s >= 0)(functools.partial(from_below, s, z - 1 - s))
        pl.when(z + 1 + s < nz)(functools.partial(from_above, s, z + 1 + s))
        if s == 0:
            turn(0, z)
        else:
            pl.when(z - s >= 0)(functools.partial(turn, s, z - s))
            pl.when(z + s < nz)(functools.partial(turn, s, z + s))
    pl.when(z - (nz - 1) >= 0)(functools.partial(turn, 0, z - (nz - 1)))
    pl.when(z + (nz - 1) < nz)(functools.partial(turn, 0, z + (nz - 1)))

    def finish(s, t):
        bx = t * 4 + low + px - me
        by = t * 4 + low + py - me
        bxy = bx + py - me
        over_y(o_ref.at[by], by, top, nz + t).wait_recv()
        over_x(o_ref.at[bx], bx, bottom, nz + t).wait_recv()
        over_y(o_ref.at[bxy], bxy, top, 2 * nz + t).wait_recv()
        over_x(o_ref.at[bxy], bxy, bottom, 2 * nz + t).wait_recv()
        for i in range(3):
            over_x(x_ref, me, top, i * nz + t).wait_send()
            over_y(x_ref, me, top, i * nz + t).wait_send()

    finish(0, z)
    near(z, nz, finish, finish)

    def sent_up(s, t):
        upward(x_ref, me, s).wait_send()

    def sent_down(s, t):
        downward(x_ref, me, s).wait_send()

    for s in range(nz - 1):
        pl.when((z + 1 < nz) & (z - s >= 0))(functools.partial(sent_up, s, z))
        pl.when((z > 0) & (z + s < nz))(functools.partial(sent_down, s, z))
    local.wait()
    if w:
        end_swaps(n, swaps_in, swaps_out, swap_sems, swapping)


def gather(x, cid, swaps=()):
    n = lax.axis_size("ep")
    w = len(swaps)
    nz = n // 4
    return pl.pallas_call(
        functools.partial(gather_kernel, n, w),
        out_shape=[jax.ShapeDtypeStruct((n,) + x.shape, x.dtype)]
        + [jax.ShapeDtypeStruct(a.shape, a.dtype) for a in swaps],
        in_specs=[ANY] * (1 + w),
        out_specs=[ANY] * (1 + w),
        scratch_shapes=[DMA]
        + [DMA((nz,))] * 4
        + [DMA((3 * nz,))] * 4
        + ([DMA((w,)), DMA((w, n)), DMA((w, n))] if w else []),
        compiler_params=pltpu.CompilerParams(collective_id=cid, has_side_effects=True),
        name="gather",
    )(x, *swaps)


def add_rows(dst, left, right, rows):
    step = 16

    def body(i, carry):
        r = pl.ds(pl.multiple_of(i * step, step), step)
        dst[r] = (left[r].astype(F32) + right[r].astype(F32)).astype(dst.dtype)
        return carry

    lax.fori_loop(0, rows // step, body, 0)


TILE = 128


def exchange_kernel(n, m, w, laid, groups, jobs, *refs):
    refs = list(refs)

    def take(count):
        out = refs[:count]
        del refs[:count]
        return out

    sums_in, swaps_in = take(m), take(w)
    jobs_in = [take(2) for _ in jobs]
    sums_out, swaps_out, jobs_out = take(m), take(w), [take(parts * blocks) for parts, blocks in jobs]
    room = [take(7) for _ in range(m)]
    sems = [take(8) for _ in range(m)]
    swap_sems = take(3) if w else None
    side_by_side = swaps_out[w - laid :]
    swaps_out = swaps_out[: w - laid] + take(laid)
    desks = [take(5) for _ in jobs]
    me, z, y, x, px, py = around(n)
    nz = n // 4
    low = me % 4
    to = [(z + k) % nz for k in range(nz)]
    at = [t * 4 + low for t in to]
    if w:
        greet([(me + k) % n for k in range(1, n)])
    else:
        greet([px, py] + at[1:])
    order = [2, 1, 3, 0] if nz == 4 else list(range(1, nz)) + [0]
    sends = []

    def halves(j):
        half = sums_in[j].shape[3] // 2
        return half, pl.ds(0, half), pl.ds(half, half)

    first, second, third = {}, {}, {}

    def stage_one(j, k):
        p = sums_in[j]
        half, top, bottom = halves(j)
        la, lb, a1, b1, a2, b2, zb = room[j]
        lsa, lsb, xs, xr, ys, yr, zs, zr = sems[j]
        t = to[k]
        c = remote(p.at[t, 1 - y, :, top], a1.at[k], ys.at[k], yr.at[k], py)
        d = remote(p.at[t, :, 1 - x, bottom], b1.at[k], xs.at[k], xr.at[k], px)
        c.start()
        d.start()
        e = pltpu.make_async_copy(p.at[t, y, :, top], la.at[k], lsa.at[k])
        f = pltpu.make_async_copy(p.at[t, :, x, bottom], lb.at[k], lsb.at[k])
        e.start()
        f.start()
        first[j, k] = (c, d, e, f)
        sends.extend([c, d])

    def stage_two(j, k):
        half, top, bottom = halves(j)
        la, lb, a1, b1, a2, b2, zb = room[j]
        lsa, lsb, xs, xr, ys, yr, zs, zr = sems[j]
        c, d, e, f = first[j, k]
        e.wait()
        c.wait_recv()
        for i in range(2):
            add_rows(la.at[k, i], la.at[k, i], a1.at[k, i], half)
        g = remote(la.at[k, 1 - x], a2.at[k], xs.at[nz + k], xr.at[nz + k], px)
        g.start()
        f.wait()
        d.wait_recv()
        for i in range(2):
            add_rows(lb.at[k, i], lb.at[k, i], b1.at[k, i], half)
        h = remote(lb.at[k, 1 - y], b2.at[k], ys.at[nz + k], yr.at[nz + k], py)
        h.start()
        second[j, k] = (g, h)
        sends.extend([g, h])

    def stage_three(j, k):
        half, top, bottom = halves(j)
        la, lb, a1, b1, a2, b2, zb = room[j]
        lsa, lsb, xs, xr, ys, yr, zs, zr = sems[j]
        g, h = second[j, k]
        g.wait_recv()
        add_rows(a2.at[k], la.at[k, x], a2.at[k], half)
        if k:
            c = remote(a2.at[k], zb.at[k, top], zs.at[k], zr.at[k], at[k])
            c.start()
        h.wait_recv()
        add_rows(b2.at[k], lb.at[k, y], b2.at[k], half)
        if k:
            d = remote(b2.at[k], zb.at[k, bottom], zs.at[nz + k], zr.at[nz + k], at[k])
            d.start()
            third[j, k] = (c, d)
            sends.extend([c, d])

    loads = []
    for (left, right), (left_v, right_v, page, in_sem, out_sem) in zip(jobs_in, desks):
        for i, (src, dst) in enumerate(((left, left_v), (right, right_v))):
            loads.append(pltpu.make_async_copy(src, dst, in_sem.at[i]))

    def pieces(j):
        parts, blocks = jobs[j]
        rows = jobs_out[j][0].shape[0]
        piece = math.gcd(TILE, rows)
        return [(q * piece, piece) for q in range(TILE // piece)]

    def start_write(j, i, part):
        left_v, right_v, page, in_sem, out_sem = desks[j]
        parts, blocks = jobs[j]
        outs = jobs_out[j][part * blocks : (part + 1) * blocks]
        rows = outs[0].shape[0]
        for q, (offset, piece) in enumerate(pieces(j)):
            row = i * TILE + offset
            src = page.at[i % 2, part, pl.ds(offset, piece)]
            owner = (row // rows + blocks - (lax.axis_index("grp") if blocks > 1 else 0)) % blocks
            inside = pl.ds(pl.multiple_of(row % rows, piece), piece)
            for k, out in enumerate(outs):
                copy = pltpu.make_async_copy(src, out.at[inside], out_sem.at[i % 2, part, q])
                if blocks > 1:
                    pl.when(owner == k)(copy.start)
                else:
                    copy.start()

    def wait_write(j, i, part):
        left_v, right_v, page, in_sem, out_sem = desks[j]
        for q, (offset, piece) in enumerate(pieces(j)):
            src = page.at[i % 2, part, pl.ds(offset, piece)]
            out = jobs_out[j][part * jobs[j][1]].at[pl.ds(0, piece)]
            pltpu.make_async_copy(src, out, out_sem.at[i % 2, part, q]).wait()

    def tile(j, i):
        left_v, right_v, page, in_sem, out_sem = desks[j]
        value = lax.dot_general(
            left_v[:, pl.ds(pl.multiple_of(i * TILE, TILE), TILE)],
            right_v[...],
            (((0,), (0,)), ((), ())),
            preferred_element_type=F32,
        ).astype(page.dtype)
        width = page.shape[3]
        for part in range(jobs[j][0]):
            pl.when(i >= 2)(functools.partial(wait_write, j, i, part))
            page[i % 2, part] = value[:, part * width : (part + 1) * width]
            start_write(j, i, part)

    tiles = [desk[0].shape[1] // TILE for desk in desks]
    loaded = []

    def work(step, of):
        first, last = sum(tiles) * step // of, sum(tiles) * (step + 1) // of
        for j in range(len(jobs)):
            start = sum(tiles[:j])
            low, high = max(first - start, 0), min(last - start, tiles[j])
            if low >= high:
                continue
            if j not in loaded:
                loaded.append(j)
                loads[2 * j].wait()
                loads[2 * j + 1].wait()
            lax.fori_loop(low, high, lambda i, c, j=j: (tile(j, i), c)[1], 0)

    steps = [(j, k) for k in order for j in range(m)]
    ahead = 3 if jobs else 2
    for i in range(min(ahead, len(steps))):
        stage_one(*steps[i])
    for copy in loads:
        copy.start()
    if w:
        swapping = start_swaps(n, swaps_in, swaps_out, swap_sems)
    for i, step in enumerate(steps):
        stage_two(*step)
        if i + ahead < len(steps):
            stage_one(*steps[i + ahead])
        if i:
            stage_three(*steps[i - 1])
        work(i, len(steps))
    if steps:
        stage_three(*steps[-1])
    if w:
        end_swaps(n, swaps_in, swaps_out, swap_sems, swapping)
        for wide, got in zip(side_by_side, swaps_out[w - laid :]):
            width = got.shape[2]
            for k in range(n):
                wide[:, k * width : (k + 1) * width] = got[k].astype(F32)
    for j in range(m):
        half, top, bottom = halves(j)
        la, lb, a1, b1, a2, b2, zb = room[j]
        o_ref = sums_out[j]
        for k in range(1, nz):
            c, d = third[j, k]
            c.wait_recv()
            d.wait_recv()
        for part, offset in ((a2, 0), (b2, half)):

            def body(i, carry, part=part, offset=offset, zb=zb, o_ref=o_ref):
                r = pl.ds(pl.multiple_of(i * 16, 16), 16)
                q = pl.ds(pl.multiple_of(i * 16 + offset, 16), 16)
                total = part[0, r].astype(F32)
                for k in range(1, nz):
                    total = total + zb[k, q].astype(F32)
                o_ref[q] = total.astype(o_ref.dtype)
                return carry

            lax.fori_loop(0, half // 16, body, 0)
    for copy in sends:
        copy.wait_send()
    for j in range(len(jobs)):
        for i in range(min(2, tiles[j])):
            for part in range(jobs[j][0]):
                wait_write(j, i, part)


def exchange(cid, sums=(), swaps=(), laid=0, jobs=()):
    n = lax.axis_size("ep")
    nz = n // 4
    groups = lax.axis_size("grp")
    m, w = len(sums), len(swaps)
    kept_rows = [p.shape[1] for p in sums]
    sums = [jnp.pad(p, ((0, 0), (0, -p.shape[1] % 32), (0, 0))) for p in sums]
    views = [p.reshape((nz, 2, 2) + p.shape[1:]) for p in sums]
    scratch = []
    for p in sums:
        rows, cols = p.shape[1:]
        half = rows // 2
        scratch += [pltpu.VMEM((nz, 2, half, cols), p.dtype)] * 4
        scratch += [pltpu.VMEM((nz, half, cols), p.dtype)] * 2
        scratch += [pltpu.VMEM((nz, rows, cols), p.dtype)]
    for p in sums:
        scratch += [DMA((nz,))] * 2 + [DMA((2 * nz,))] * 6
    if w:
        scratch += [DMA((w,)), DMA((w, n)), DMA((w, n))]
    plain, wide = swaps[: w - laid], swaps[w - laid :]
    scratch += [pltpu.VMEM(a.shape, a.dtype) for a in wide]
    jobs_out = []
    for left, right, parts, blocks in jobs:
        rows, cols = left.shape[1] // blocks, right.shape[1] // parts
        jobs_out += [jax.ShapeDtypeStruct((rows, cols), BF16)] * (parts * blocks)
        scratch += [pltpu.VMEM(left.shape, left.dtype), pltpu.VMEM(right.shape, right.dtype)]
        scratch += [pltpu.VMEM((2, parts, TILE, cols), BF16), DMA((2,))]
        scratch += [DMA((2, parts, TILE // math.gcd(TILE, rows)))]
    out = pl.pallas_call(
        functools.partial(exchange_kernel, n, m, w, laid, groups, [job[2:] for job in jobs]),
        out_shape=[jax.ShapeDtypeStruct(p.shape[1:], F32) for p in sums]
        + [jax.ShapeDtypeStruct(a.shape, a.dtype) for a in plain]
        + [jax.ShapeDtypeStruct((a.shape[1], n * a.shape[2]), F32) for a in wide]
        + jobs_out,
        in_specs=[ANY] * (m + w + 2 * len(jobs)),
        out_specs=[pl.BlockSpec(memory_space=pltpu.VMEM)] * m
        + [ANY] * (w - laid)
        + [pl.BlockSpec(memory_space=pltpu.VMEM)] * laid
        + [ANY] * len(jobs_out),
        scratch_shapes=scratch,
        compiler_params=pltpu.CompilerParams(
            collective_id=cid, has_side_effects=True, vmem_limit_bytes=(60 if jobs else 40) << 20 if m else None
        ),
        name="exchange",
    )(*views, *swaps, *(a for job in jobs for a in job[:2]))
    return [a[:rows] for a, rows in zip(out, kept_rows)] + list(out[m:])


def both(p):
    g = lax.axis_index("grp")
    mine = lax.dynamic_index_in_dim(p, g, 0, keepdims=False)
    theirs = lax.dynamic_index_in_dim(p, 1 - g, 0, keepdims=False)
    return mine, lax.ppermute(theirs.astype(BF16), "grp", [(0, 1), (1, 0)])


def over_groups(p):
    if lax.axis_size("grp") == 2:
        mine, other = both(p)
        return mine.astype(F32) + other.astype(F32)
    return lax.psum_scatter(p.astype(BF16), "grp", scatter_dimension=0, tiled=False).astype(F32)


def product_over_groups(left, right):
    groups = lax.axis_size("grp")
    rows = left.shape[1] // groups
    if groups != 2:
        whole = product("km,kn->mn", left, right)
        return over_groups(whole.reshape(groups, rows, -1))
    g = lax.axis_index("grp")
    mine = lax.dynamic_slice_in_dim(left, g * rows, rows, 1)
    theirs = lax.dynamic_slice_in_dim(left, (1 - g) * rows, rows, 1)
    sent = product("km,kn->mn", theirs, right).astype(BF16)
    other = lax.ppermute(sent, "grp", [(0, 1), (1, 0)])
    return product("km,kn->mn", mine, right) + other.astype(F32)


def from_partner(values):
    groups = lax.axis_size("grp")
    return lax.ppermute(values, "grp", [(g, g + 1 - 2 * (g % 2)) for g in range(groups)])


def to_row_owner(block):
    groups, n = lax.axis_size("grp"), lax.axis_size("ep")
    pairs = [(h * n + e, e * groups + h) for h in range(groups) for e in range(n)]
    return lax.ppermute(block.astype(BF16), ("grp", "ep"), pairs).astype(F32)


def dot(left, right):
    return jnp.dot(left, right, preferred_element_type=F32)


def dot_nt(left, right):
    return lax.dot_general(left, right, (((1,), (1,)), ((), ())), preferred_element_type=F32)


def front_kernel(
    x_ref, w_ref, cos_ref, sin_ref, gain_ref, lat_gain_ref, wq_ref, wl_ref, we_ref,
    normed_ref, query_ref, keys_ref, values_ref, latent_ref, out_w_ref,
):
    out_w_ref[...] = w_ref[...].reshape(out_w_ref.shape)
    blocks, tokens = x_ref.shape[:2]
    rows = blocks * tokens
    x = x_ref[...].reshape(rows, gain_ref.shape[1]).astype(F32)
    normed = (x * rms_scale(x) * gain_ref[...]).astype(BF16)
    normed_ref[...] = normed
    cos, sin = cos_ref[...], sin_ref[...]
    own_half = lax.broadcasted_iota(jnp.int32, cos.shape, 1) < ROPE

    def turn(pair):
        return pair * cos + pltpu.roll(pair, ROPE, 1) * sin

    query = dot_nt(normed, wq_ref[...])
    query_ref[:, :NOPE] = query[:, :NOPE].astype(BF16)
    query_ref[:, NOPE:] = jnp.where(own_half, turn(query[:, NOPE:]), 0.0).astype(BF16)
    compressed = dot(normed, wl_ref[...])
    raw = compressed[:, :LATENT]
    latent = (raw * rms_scale(raw) * lat_gain_ref[...]).astype(BF16)
    latent_ref[...] = latent
    expanded = dot(latent, we_ref[...])
    keys_ref[:, :NOPE] = expanded[:, :NOPE].astype(BF16)
    keys_ref[:, NOPE:] = turn(compressed[:, LATENT:]).astype(BF16)
    values_ref[...] = expanded[:, NOPE:].astype(BF16)


def front(x, cos, sin, gain, lat_gain, wq, wl, we):
    n, tokens = x.shape[:2]
    model = gain.shape[1]
    length = n * tokens
    blocks = 2
    rows = blocks * tokens

    def whole(a):
        return pl.BlockSpec(a.shape, lambda i: (0,) * a.ndim, pipeline_mode=pl.Buffered(1))

    def rows_of(cols):
        return pl.BlockSpec((rows, cols), lambda i: (i, 0))

    def out(cols):
        return jax.ShapeDtypeStruct((length, cols), BF16)

    cols = (model, wq.shape[0], NOPE + 2 * ROPE, VH, LATENT, model // 2)
    return pl.pallas_call(
        front_kernel,
        grid=(n // blocks,),
        in_specs=[
            pl.BlockSpec((blocks, tokens, model), lambda i: (i, 0, 0)),
            pl.BlockSpec((blocks, tokens, model // 2), lambda i: (i, 0, 2)),
            rows_of(2 * ROPE),
            rows_of(2 * ROPE),
        ]
        + [whole(a) for a in (gain, lat_gain, wq, wl, we)],
        out_specs=[rows_of(c) for c in cols],
        out_shape=[out(c) for c in cols],
        compiler_params=pltpu.CompilerParams(vmem_limit_bytes=48 << 20),
        name="front",
    )(x, x, cos, sin, gain, lat_gain, wq, wl, we)


def back_kernel(
    cos_ref, sin_ref, dq_ref, dk_ref, dv_ref, we_ref, query_ref, expanded_ref, latent_ref, rope_ref
):
    own_half = lax.broadcasted_iota(jnp.int32, cos_ref.shape, 1) < ROPE
    pair = dq_ref[:, NOPE:] * jnp.where(own_half, cos_ref[...], sin_ref[...])
    pair = jnp.where(own_half, pair + pltpu.roll(pair, ROPE, 1), 0.0)
    query_ref[:, :NOPE] = dq_ref[:, :NOPE].astype(BF16)
    query_ref[:, NOPE:] = pair.astype(BF16)
    expanded_ref[:, :NOPE] = dk_ref[:, :NOPE].astype(BF16)
    expanded_ref[:, NOPE:] = dv_ref[...].astype(BF16)
    latent_ref[...] = dot_nt(expanded_ref[...], we_ref[...]).astype(BF16)
    rope_ref[...] = dk_ref[:, NOPE:].astype(BF16)


def back(cos, sin, dq, dk, dv, we):
    length = dq.shape[0]
    rows = 512

    def rows_of(cols):
        return pl.BlockSpec((rows, cols), lambda i: (i, 0))

    def out(cols):
        return jax.ShapeDtypeStruct((length, cols), BF16)

    cols = (NOPE + 2 * ROPE, NOPE + VH, LATENT, 2 * ROPE)
    return pl.pallas_call(
        back_kernel,
        grid=(length // rows,),
        in_specs=[rows_of(a.shape[1]) for a in (cos, sin, dq, dk, dv)]
        + [pl.BlockSpec(we.shape, lambda i: (0, 0))],
        out_specs=[rows_of(c) for c in cols],
        out_shape=[out(c) for c in cols],
        compiler_params=pltpu.CompilerParams(vmem_limit_bytes=40 << 20),
        name="back",
    )(cos, sin, dq, dk, dv, we)


KEYS = 512


def scores_of(scale, prefix, k, q, first_key, first_query):
    scores = dot_nt(k, q) * scale
    key = first_key + lax.broadcasted_iota(jnp.int32, scores.shape, 0)
    query = first_query + lax.broadcasted_iota(jnp.int32, scores.shape, 1)
    return jnp.where((key <= query) | (key < prefix), scores, MASKED)


def key_blocks(prefix, last_query):
    return (jnp.maximum(last_query, prefix) + KEYS - 1) // KEYS


def attend_kernel(scale, prefix_ref, q_ref, k_ref, v_ref, attended_ref, exact_ref, lse_ref):
    q = q_ref[...]
    rows = q.shape[0]
    start = pl.program_id(0) * rows
    prefix = prefix_ref[0]

    def step(j, carry):
        top, total, out = carry
        s = scores_of(scale, prefix, k_ref[j], q, j * KEYS, start)
        new_top = jnp.maximum(top, jnp.max(s, axis=0, keepdims=True))
        p = jnp.exp(s - new_top)
        shrink = jnp.exp(top - new_top)
        total = total * shrink + jnp.sum(p, axis=0, keepdims=True)
        return new_top, total, out * shrink + dot(v_ref[j], p.astype(BF16))

    top, total, out = lax.fori_loop(
        0,
        key_blocks(prefix, start + rows),
        step,
        (
            jnp.full((1, rows), MASKED, F32),
            jnp.zeros((1, rows), F32),
            jnp.zeros((v_ref.shape[1], rows), F32),
        ),
    )
    lse_ref[...] = top + jnp.log(total)
    exact = (out / total).T
    exact_ref[...] = exact
    attended_ref[...] = exact.astype(BF16)


def attend(prefix, q, k, v):
    length, depth = q.shape
    values = v.shape[1]
    rows = 256
    v = v.reshape(length // KEYS, KEYS, values).transpose(0, 2, 1)
    k = k.reshape(length // KEYS, KEYS, depth)
    return pl.pallas_call(
        functools.partial(attend_kernel, 1.0 / math.sqrt(NOPE + ROPE)),
        grid=(length // rows,),
        in_specs=[
            pl.BlockSpec(memory_space=pltpu.SMEM),
            pl.BlockSpec((rows, depth), lambda i: (i, 0)),
            pl.BlockSpec(k.shape, lambda i: (0, 0, 0)),
            pl.BlockSpec(v.shape, lambda i: (0, 0, 0)),
        ],
        out_specs=[
            pl.BlockSpec((rows, values), lambda i: (i, 0)),
            pl.BlockSpec((rows, values), lambda i: (i, 0)),
            pl.BlockSpec((1, rows), lambda i: (0, i)),
        ],
        out_shape=[
            jax.ShapeDtypeStruct((length, values), BF16),
            jax.ShapeDtypeStruct((length, values), F32),
            jax.ShapeDtypeStruct((1, length), F32),
        ],
        compiler_params=pltpu.CompilerParams(vmem_limit_bytes=32 << 20),
        name="attend",
    )(prefix, q, k, v)


def attend_back_kernel(
    scale, prefix_ref, q_ref, g_ref, lse_ref, delta_ref, k_ref, v_ref, dq_ref, dk_ref, dv_ref
):
    q, g = q_ref[...], g_ref[...]
    rows = q.shape[0]
    start = pl.program_id(0) * rows
    prefix = prefix_ref[0]

    @pl.when(pl.program_id(0) == 0)
    def _():
        dk_ref[...] = jnp.zeros_like(dk_ref)
        dv_ref[...] = jnp.zeros_like(dv_ref)

    def step(j, dq):
        k = k_ref[j]
        p = jnp.exp(scores_of(scale, prefix, k, q, j * KEYS, start) - lse_ref[...])
        ds = (p * (dot_nt(v_ref[j], g) - delta_ref[...]) * scale).astype(BF16)
        dv_ref[j] += dot(p.astype(BF16), g)
        dk_ref[j] += dot(ds, q)
        return dq + lax.dot_general(
            ds, k, (((0,), (0,)), ((), ())), preferred_element_type=F32
        )

    dq_ref[...] = lax.fori_loop(
        0, key_blocks(prefix, start + rows), step, jnp.zeros(dq_ref.shape, F32)
    )


def attend_back(prefix, q, g, lse, delta, k, v):
    length, depth = q.shape
    values = v.shape[1]
    rows = 256
    k = k.reshape(length // KEYS, KEYS, depth)
    v = v.reshape(length // KEYS, KEYS, values)
    dq, dk, dv = pl.pallas_call(
        functools.partial(attend_back_kernel, 1.0 / math.sqrt(NOPE + ROPE)),
        grid=(length // rows,),
        in_specs=[
            pl.BlockSpec(memory_space=pltpu.SMEM),
            pl.BlockSpec((rows, depth), lambda i: (i, 0)),
            pl.BlockSpec((rows, values), lambda i: (i, 0)),
            pl.BlockSpec((1, rows), lambda i: (0, i)),
            pl.BlockSpec((1, rows), lambda i: (0, i)),
            pl.BlockSpec(k.shape, lambda i: (0, 0, 0)),
            pl.BlockSpec(v.shape, lambda i: (0, 0, 0)),
        ],
        out_specs=[
            pl.BlockSpec((rows, depth), lambda i: (i, 0)),
            pl.BlockSpec(k.shape, lambda i: (0, 0, 0)),
            pl.BlockSpec(v.shape, lambda i: (0, 0, 0)),
        ],
        out_shape=[
            jax.ShapeDtypeStruct((length, depth), F32),
            jax.ShapeDtypeStruct(k.shape, F32),
            jax.ShapeDtypeStruct(v.shape, F32),
        ],
        compiler_params=pltpu.CompilerParams(vmem_limit_bytes=40 << 20),
        name="attend_back",
    )(prefix, q, g, lse, delta, k, v)
    return dq, dk.reshape(length, depth), dv.reshape(length, values)


def ffn_kernel(
    n,
    x_ref,
    y_ref,
    slots_ref,
    tokens_ref,
    own_ref,
    router_ref,
    sg_ref,
    su_ref,
    sd_ref,
    eg_ref,
    eu_ref,
    ed_ref,
    out_ref,
    ffn_ref,
    dot_ref,
    probs_ref,
    rows_ref,
    hidden_ref,
    slot_grad_ref,
    grad_gu_ref,
    shared_h_ref,
    shared_gu_ref,
    expert_out,
    row_grad,
):
    blocks, tokens = x_ref.shape[:2]
    capacity = slots_ref.shape[1]
    own = own_ref[...]
    lanes = lax.broadcasted_iota(jnp.int32, (tokens, own.shape[1]), 1)
    gates = []
    for b in range(blocks):
        x, y = x_ref[b], y_ref[b]
        logits = jnp.where(lanes < n, dot(x, router_ref[...]), MASKED)
        raised = jnp.exp(logits - jnp.max(logits, axis=-1, keepdims=True))
        probs = raised / jnp.sum(raised, axis=-1, keepdims=True)
        probs_ref[b] = probs
        gate = jnp.sum(probs * own, axis=-1, keepdims=True)
        gates.append(gate)
        part = pl.ds(b * capacity, capacity)
        rows_ref[part] = dot(slots_ref[b], x).astype(BF16)
        weighted = (gate * y.astype(F32)).astype(BF16)
        slot_grad_ref[part] = dot(slots_ref[b], weighted).astype(BF16)
    rows = rows_ref[...]
    slot_grad = slot_grad_ref[...]
    g = dot(rows, eg_ref[...])
    u = dot(rows, eu_ref[...])
    sigmoid = 1.0 / (1.0 + jnp.exp(-g))
    silu = g * sigmoid
    hidden = (silu * u).astype(BF16)
    hidden_ref[...] = hidden
    expert_out[...] = dot(hidden, ed_ref[...]).astype(BF16)
    grad_hidden = dot_nt(slot_grad, ed_ref[...])
    grad_g = (grad_hidden * u * sigmoid * (1.0 + g * (1.0 - sigmoid))).astype(BF16)
    grad_u = (grad_hidden * silu).astype(BF16)
    grad_gu_ref[:, : grad_g.shape[1]] = grad_g
    grad_gu_ref[:, grad_g.shape[1] :] = grad_u
    row_grad[...] = (dot_nt(grad_g, eg_ref[...]) + dot_nt(grad_u, eu_ref[...])).astype(BF16)
    x = x_ref[...].reshape(blocks * tokens, -1)
    y = y_ref[...].reshape(blocks * tokens, -1)
    g = dot_nt(x, sg_ref[...])
    u = dot_nt(x, su_ref[...])
    grad_hidden = dot_nt(y, sd_ref[...])
    sigmoid = 1.0 / (1.0 + jnp.exp(-g))
    silu = g * sigmoid
    hidden = (silu * u).astype(BF16)
    grad_g = (grad_hidden * u * sigmoid * (1.0 + g * (1.0 - sigmoid))).astype(BF16)
    grad_u = (grad_hidden * silu).astype(BF16)
    shared = hidden.shape[1]
    shared_h_ref[...] = hidden.reshape(blocks, tokens, shared)
    shared_gu_ref[:, :, :shared] = grad_g.reshape(blocks, tokens, shared)
    shared_gu_ref[:, :, shared:] = grad_u.reshape(blocks, tokens, shared)
    width = x.shape[1]
    chunk = width // 4
    met = [0.0] * blocks
    for c in range(width // chunk):
        cols = pl.ds(c * chunk, chunk)
        shared_out = dot(hidden, sd_ref[:, cols])
        shared_ffn = dot(grad_g, sg_ref[:, cols]) + dot(grad_u, su_ref[:, cols])
        for b in range(blocks):
            part = pl.ds(b * capacity, capacity)
            here = slice(b * tokens, (b + 1) * tokens)
            picked = dot(tokens_ref[b], expert_out[part, cols])
            met[b] += jnp.sum(picked * y_ref[b, :, cols].astype(F32), axis=-1, keepdims=True)
            out_ref[b, :, cols] = (shared_out[here] + picked * gates[b]).astype(BF16)
            back = dot(tokens_ref[b], row_grad[part, cols])
            ffn_ref[b, :, cols] = (shared_ffn[here] + back).astype(BF16)
    for b in range(blocks):
        dot_ref[b] = (met[b] * own).astype(BF16)


def ffn(x, y, slots, own_lane, router_w, gate_t, up_t, down, gate_m, up_m, down_m):
    n, tokens, width = x.shape
    capacity = slots.shape[1]
    hidden = gate_m.shape[1]
    shared = gate_t.shape[0]
    group = 4

    def whole(a):
        return pl.BlockSpec(a.shape, lambda i: (0,) * a.ndim, pipeline_mode=pl.Buffered(1))

    def block(*shape):
        return pl.BlockSpec((group,) + shape, lambda i: (i, 0, 0))

    def slot_rows(cols):
        return pl.BlockSpec((group * capacity, cols), lambda i: (i, 0))

    def tokens_of(cols, kind=BF16):
        return jax.ShapeDtypeStruct((n, tokens, cols), kind)

    def slots_of(cols):
        return jax.ShapeDtypeStruct((n * capacity, cols), BF16)

    weights = (own_lane, router_w, gate_t, up_t, down, gate_m, up_m, down_m)
    return pl.pallas_call(
        functools.partial(ffn_kernel, n),
        grid=(n // group,),
        in_specs=[
            block(tokens, width),
            block(tokens, width),
            block(capacity, tokens),
            block(tokens, capacity),
        ]
        + [whole(a) for a in weights],
        out_specs=[
            block(tokens, width),
            block(tokens, width),
            block(tokens, 128),
            block(tokens, 128),
            slot_rows(width),
            slot_rows(hidden),
            slot_rows(width),
            slot_rows(2 * hidden),
            block(tokens, shared),
            block(tokens, 2 * shared),
        ],
        out_shape=[
            tokens_of(width),
            tokens_of(width),
            tokens_of(128),
            tokens_of(128, F32),
            slots_of(width),
            slots_of(hidden),
            slots_of(width),
            slots_of(2 * hidden),
            tokens_of(shared),
            tokens_of(2 * shared),
        ],
        scratch_shapes=[
            pltpu.VMEM((group * capacity, width), BF16),
            pltpu.VMEM((group * capacity, width), BF16),
        ],
        compiler_params=pltpu.CompilerParams(vmem_limit_bytes=60 << 20),
        name="ffn",
    )(x, y, slots, slots.transpose(0, 2, 1), *weights)


def product(form, left, right):
    return jnp.einsum(form, left, right, preferred_element_type=F32)


def rms_scale(values):
    return lax.rsqrt(jnp.mean(values * values, axis=-1, keepdims=True) + EPSILON)


def rotary_tables(tokens, n):
    halfway = ROPE // 2
    inverse = 10000.0 ** (-(jnp.arange(halfway, dtype=F32) * 2.0 / ROPE))
    inverse = jnp.concatenate([inverse] * 4)
    lane = jnp.arange(2 * ROPE)
    sign = jnp.where((lane < halfway) | (lane >= 3 * halfway), -1.0, 1.0)
    base = (jnp.arange(n, dtype=F32) * tokens)[:, None] * inverse
    step = jnp.arange(tokens, dtype=F32)[:, None] * inverse
    base_cos, base_sin = jnp.cos(base)[:, None], jnp.sin(base)[:, None]
    step_cos, step_sin = jnp.cos(step)[None], jnp.sin(step)[None]
    cos_table = base_cos * step_cos - base_sin * step_sin
    sin_table = (base_sin * step_cos + base_cos * step_sin) * sign
    return cos_table.reshape(n * tokens, -1), sin_table.reshape(n * tokens, -1)


def unrotate(grads, cos_table, sin_table):
    halfway = grads.shape[-1] // 2
    first = grads[..., :halfway]
    second = grads[..., halfway:]
    return jnp.concatenate(
        [first * cos_table + second * sin_table, second * cos_table - first * sin_table], axis=-1
    )


def norm_back(grad_unit, unit_values, scale_values):
    return scale_values * (
        grad_unit - unit_values * jnp.mean(grad_unit * unit_values, axis=-1, keepdims=True)
    )


def column_halves(weight, n, half):
    rows, width = weight.shape[0], weight.shape[1] // n
    parts = weight.T.reshape(n, 2, width // 2, rows)
    return lax.dynamic_index_in_dim(parts, half, 1, keepdims=False)


def columns_in(blocks):
    n, width, rows = blocks.shape
    return blocks.transpose(1, 0, 2).reshape(width, n * rows)


def both_halves(mine, other, even, axis=0):
    return jnp.concatenate([jnp.where(even, mine, other), jnp.where(even, other, mine)], axis=axis)


def per_device(
    layer_input,
    attention_gain,
    query_weight,
    latent_weight,
    latent_gain,
    expand_weight,
    output_weight,
    feedforward_gain,
    router_weight,
    shared_gate,
    shared_up,
    shared_down,
    expert_gate,
    expert_up,
    expert_down,
    expert_routes,
    prefix_length,
    output_grad,
):
    n = lax.axis_size("ep")
    groups = lax.axis_size("grp")
    e = lax.axis_index("ep")
    half = lax.axis_index("grp") % 2
    even = half == 0
    tokens = layer_input.shape[0]
    length = tokens * n
    capacity = tokens * TOPK * 4 // (3 * n)
    rows_dev = attention_gain.shape[0]
    latent_rows = latent_gain.shape[0]
    rows_out = D // (groups * n)
    expand_rows = LATENT // (groups * n)

    out_w_half = lax.dynamic_slice_in_dim(output_weight, half * (D // 2), D // 2, 1)
    first_block = jnp.concatenate(
        [layer_input, out_w_half, latent_weight, router_weight, expert_routes.astype(BF16)], axis=1
    )
    width = first_block.shape[1]
    first_block = jnp.pad(first_block, ((0, 0), (0, -width % 128)))
    gains = jnp.zeros((16, rows_dev), BF16)
    gains = gains.at[0].set(attention_gain).at[1].set(feedforward_gain)
    gains = gains.at[2, :latent_rows].set(latent_gain)
    shared_half = jnp.where(even, shared_gate, shared_up)
    expand_half = lax.dynamic_index_in_dim(
        expand_weight.reshape(latent_rows, n, 2, -1), half, 2, keepdims=False
    ).transpose(1, 0, 2)
    first_all, q_blocks, x_blocks, shared_blocks, gain_blocks = gather(
        first_block,
        0,
        swaps=(
            column_halves(query_weight, n, half),
            expand_half,
            shared_half.T.reshape(n, shared_half.shape[1] // n, rows_dev),
            jnp.broadcast_to(gains, (n,) + gains.shape),
        ),
    )
    c0 = D + D // 2
    c1 = c0 + LATENT + ROPE
    c2 = c1 + n
    latent_w = first_all[:, :, c0:c1].reshape(D, LATENT + ROPE)
    router_w = first_all[:, :, c1:c2].reshape(D, n)
    routes = first_all[:, :, c2 : c2 + TOPK].astype(jnp.int32)
    attn_gain = gain_blocks[:, 0].reshape(D).astype(F32)
    ffn_gain = gain_blocks[:, 1].reshape(D).astype(F32)
    lat_gain = gain_blocks[:, 2, :latent_rows].reshape(LATENT).astype(F32)

    later_grad, q_blocks = lax.optimization_barrier((output_grad, q_blocks))
    all_out_grad = lax.all_gather(later_grad, "ep", axis=0, tiled=True)

    q_mine, x_mine = columns_in(q_blocks), x_blocks.reshape(LATENT, -1)
    query_t = both_halves(q_mine, from_partner(q_mine), even)
    expand_w = both_halves(x_mine, from_partner(x_mine), even, 1)
    shared_mine = columns_in(shared_blocks)
    shared_other = from_partner(shared_mine)
    gate_t = jnp.where(even, shared_mine, shared_other)
    up_t = jnp.where(even, shared_other, shared_mine)

    def own(values):
        return lax.dynamic_slice_in_dim(values, e * tokens, tokens, 0)

    cos_table, sin_table = rotary_tables(tokens, n)
    turned = jnp.concatenate(
        [query_t, query_t[NOPE + ROPE // 2 :], query_t[NOPE : NOPE + ROPE // 2]], axis=0
    )
    latent_turned = jnp.concatenate(
        [latent_w, latent_w[:, LATENT + ROPE // 2 :], latent_w[:, LATENT : LATENT + ROPE // 2]],
        axis=1,
    )
    normed, query, keys, values, latent, out_w_mine = front(
        first_all, cos_table, sin_table, attn_gain[None], lat_gain[None], turned, latent_turned, expand_w
    )
    out_w_other = from_partner(out_w_mine)
    attended_head, attended_exact, lse = attend(prefix_length, query, keys, values)
    (attended_blocks,) = exchange(2, swaps=(attended_head.reshape(n, tokens, VH),))
    attended = attended_blocks.transpose(1, 0, 2).reshape(tokens, HEADS * VH)

    residual_in = layer_input.astype(F32)
    input_scale = rms_scale(residual_in)
    input_unit = residual_in * input_scale
    out_mine = product("ta,ad->td", attended, out_w_mine)
    out_other = product("ta,ad->td", attended, out_w_other)
    residual_mid = residual_in + jnp.concatenate(
        [jnp.where(even, out_mine, out_other), jnp.where(even, out_other, out_mine)], axis=1
    )
    mid_scale = rms_scale(residual_mid)
    mid_unit = residual_mid * mid_scale
    own_ffn_in = (mid_unit * ffn_gain).astype(BF16)
    (ffn_blocks,) = gather(own_ffn_in, 3)
    query_cols = query_weight.shape[1] // 2
    query_w_half = lax.dynamic_slice_in_dim(query_weight, half * query_cols, query_cols, 1)
    query_w_half, ffn_blocks = lax.optimization_barrier((query_w_half, ffn_blocks))
    query_w_mine = lax.all_gather(query_w_half, "ep", axis=0, tiled=True)
    query_w_other = from_partner(query_w_mine)
    ffn_in = ffn_blocks.reshape(length, D)

    own_lane = (jnp.arange(128, dtype=jnp.int32) == e).astype(F32)[None]
    chosen = jnp.any(routes == e, axis=-1)
    chosen_int = chosen.astype(jnp.int32)
    place = jnp.cumsum(chosen_int, axis=1) - chosen_int
    kept = chosen & (place < capacity)
    dispatch = (
        (place[:, None, :] == jnp.arange(capacity, dtype=jnp.int32)[None, :, None])
        & kept[:, None, :]
    ).astype(BF16)
    shared_width = gate_t.shape[0]
    fill = ((0, -shared_width % 128), (0, 0))
    (
        out_partial,
        ffn_partial,
        dot_partial,
        router_all,
        incoming,
        expert_hidden,
        slot_grad,
        grad_expert_gu,
        shared_hidden,
        grad_shared_gu,
    ) = ffn(
        ffn_blocks,
        all_out_grad.reshape(n, tokens, D),
        dispatch,
        own_lane,
        jnp.pad(router_w, ((0, 0), (0, 128 - n))),
        jnp.pad(gate_t, fill),
        jnp.pad(up_t, fill),
        jnp.pad(shared_down, fill),
        expert_gate[0],
        expert_up[0],
        expert_down[0],
    )
    ffn_sum, dot_sum, out_sum, *products = exchange(
        4,
        sums=(ffn_partial, dot_partial, out_partial),
        jobs=((expert_hidden, slot_grad, 1, groups), (incoming, grad_expert_gu, 2, groups)),
    )
    layer_output = (residual_mid + out_sum).astype(BF16)

    def by_group(values):
        return over_groups(values.reshape(groups, values.shape[0] // groups, -1))

    router_own = lax.dynamic_index_in_dim(router_all, e, 0, keepdims=False)[:, :n]
    grad_probs = dot_sum[:, :n]
    grad_logits = (
        router_own * (grad_probs - jnp.sum(router_own * grad_probs, axis=-1, keepdims=True))
    ).astype(BF16)
    grad_ffn_in = ffn_sum + product("te,de->td", grad_logits, router_w)
    grad_ffn_gain = jnp.sum(grad_ffn_in * mid_unit, axis=0)
    grad_mid = output_grad.astype(F32) + norm_back(grad_ffn_in * ffn_gain, mid_unit, mid_scale)
    grad_mid_b = grad_mid.astype(BF16)
    mid_left, mid_right = grad_mid_b[:, : D // 2], grad_mid_b[:, D // 2 :]
    grad_attended = (
        product("td,ad->ta", jnp.where(even, mid_left, mid_right), out_w_mine)
        + product("td,ad->ta", jnp.where(even, mid_right, mid_left), out_w_other)
    ).astype(BF16)
    output_w_partial = product_over_groups(attended, grad_mid_b).astype(BF16)
    (grad_att_blocks,) = exchange(
        5, swaps=(grad_attended.reshape(tokens, HEADS, VH).transpose(1, 0, 2),)
    )
    grad_att = grad_att_blocks.reshape(length, VH)

    def blocks_over_groups(blocks):
        total = blocks[0].astype(F32)
        for k in range(1, groups):
            shift = [(g, (g + k) % groups) for g in range(groups)]
            total = total + lax.ppermute(blocks[k], "grp", shift).astype(F32)
        return total

    expert_down_grad, expert_gate_grad, expert_up_grad = (
        blocks_over_groups(products[k * groups : (k + 1) * groups])[None] for k in range(3)
    )

    grad_router = product("te,td->ed", grad_logits, own_ffn_in)

    delta = jnp.sum(grad_att.astype(F32) * attended_exact, axis=-1)[None]
    grad_query_raw, grad_keys, grad_values = attend_back(
        prefix_length, query, grad_att, lse, delta, keys, values
    )
    grad_query, grad_expanded, latent_partial, rope_partial = back(
        cos_table, sin_table, grad_query_raw, grad_keys, grad_values, expand_w
    )
    (
        latent_sum,
        rope_sum,
        output_weight_grad,
        query_blocks,
        side_down,
        *products,
    ) = exchange(
        6,
        sums=(
            latent_partial.reshape(n, tokens, LATENT),
            rope_partial.reshape(n, tokens, 2 * ROPE),
            output_w_partial.reshape(n, rows_out, D),
        ),
        swaps=(grad_query.reshape(n, tokens, -1),),
        jobs=(
            (shared_hidden.reshape(length, -1), all_out_grad, 1, 1),
            (ffn_in, grad_shared_gu.reshape(length, -1), 2, groups),
            (normed, grad_query, 1, groups),
            (latent, grad_expanded, 1, groups),
        ),
    )
    shared_down_grad = to_row_owner(by_group(side_down[:shared_width]))
    side_gate, side_up, side_query, grad_expand = (
        blocks_over_groups(products[k * groups : (k + 1) * groups]).astype(BF16) for k in range(4)
    )
    side_gate, side_up = side_gate[:, :shared_width], side_up[:, :shared_width]
    side_query = side_query[:, : query_t.shape[0]]

    own_normed = (input_unit * attn_gain).astype(BF16)
    own_raw = product("td,dc->tc", own_normed, latent_w[:, :LATENT])
    latent_scale = rms_scale(own_raw)
    latent_unit = own_raw * latent_scale
    grad_latent_gain = jnp.sum(latent_sum * latent_unit, axis=0)
    grad_compressed = jnp.concatenate(
        [
            norm_back(latent_sum * lat_gain, latent_unit, latent_scale),
            unrotate(
                rope_sum[:, :ROPE],
                own(cos_table)[:, : ROPE // 2],
                own(sin_table)[:, ROPE // 2 : ROPE],
            ),
        ],
        axis=-1,
    ).astype(BF16)
    latent_w_partial = product_over_groups(
        own_normed, jnp.pad(grad_compressed, ((0, 0), (0, 640 - LATENT - ROPE)))
    ).astype(BF16)
    own_part = product("tc,dc->td", grad_compressed, latent_w)

    def of_heads(part):
        heads = lax.dynamic_slice_in_dim(query_blocks, part * (n // 2), n // 2, 0)
        return heads[:, :, : NOPE + ROPE].transpose(1, 0, 2).reshape(tokens, -1)

    grad_normed = (
        product("tc,dc->td", of_heads(half), query_w_mine)
        + product("tc,dc->td", of_heads(1 - half), query_w_other)
        + own_part
    )
    grad_attn_gain = jnp.sum(grad_normed * input_unit, axis=0)

    def by_owner(values, rows):
        blocks = values.reshape(-1, groups, n, rows).transpose(2, 1, 0, 3)
        return blocks.reshape(n, groups, -1)

    small = jnp.concatenate(
        [
            by_owner(grad_attn_gain, rows_out),
            by_owner(grad_ffn_gain, rows_out),
            by_owner(grad_router, rows_out),
            by_owner(grad_latent_gain, expand_rows),
        ],
        axis=2,
    )
    small = small.transpose(1, 0, 2)
    if groups == 2:
        g = lax.axis_index("grp")
        mine = lax.dynamic_index_in_dim(small, g, 0, keepdims=False)
        theirs = lax.dynamic_index_in_dim(small, 1 - g, 0, keepdims=False)
        small = mine + lax.ppermute(theirs, "grp", [(0, 1), (1, 0)])
    else:
        small = lax.psum_scatter(small, "grp", scatter_dimension=0)
    (
        latent_weight_sum,
        small_all,
        query_weight_grad,
        shared_gate_grad,
        shared_up_grad,
        expand_weight_grad,
    ) = exchange(
        7,
        sums=(latent_w_partial.reshape(n, rows_out, -1),),
        swaps=(
            small[:, None],
            side_query.reshape(n, rows_out, -1),
            side_gate.reshape(n, rows_out, -1),
            side_up.reshape(n, rows_out, -1),
            grad_expand.reshape(n, expand_rows, -1),
        ),
        laid=4,
    )
    input_grad = (
        grad_mid + norm_back(grad_normed * attn_gain, input_unit, input_scale)
    ).astype(BF16)
    latent_weight_grad = latent_weight_sum[:, : LATENT + ROPE]
    small_sum = jnp.sum(small_all[:, 0], axis=0)
    attention_gain_grad = small_sum[:rows_out]
    feedforward_gain_grad = small_sum[rows_out : 2 * rows_out]
    router_weight_grad = small_sum[2 * rows_out : (2 + n) * rows_out].reshape(n, rows_out).T
    latent_gain_grad = small_sum[(2 + n) * rows_out :]
    return (
        layer_output,
        input_grad,
        attention_gain_grad,
        query_weight_grad,
        latent_weight_grad,
        latent_gain_grad,
        expand_weight_grad,
        output_weight_grad,
        feedforward_gain_grad,
        router_weight_grad,
        shared_gate_grad,
        shared_up_grad,
        shared_down_grad,
        expert_gate_grad,
        expert_up_grad,
        expert_down_grad,
    )


def solution(mesh):
    return jax.shard_map(
        per_device,
        mesh=mesh,
        in_specs=(
            P(("grp", "ep"), None),
            P("ep"),
            P("ep", None),
            P("ep", None),
            P("ep"),
            P("ep", None),
            P("ep", None),
            P("ep"),
            P("ep", None),
            P("ep", None),
            P("ep", None),
            P("ep", None),
            P("ep", None, None),
            P("ep", None, None),
            P("ep", None, None),
            P(("grp", "ep"), None),
            P("grp"),
            P(("grp", "ep"), None),
        ),
        out_specs=(
            P(("grp", "ep"), None),
            P(("grp", "ep"), None),
            P(("grp", "ep")),
            P(("grp", "ep"), None),
            P(("grp", "ep"), None),
            P(("grp", "ep")),
            P(("grp", "ep"), None),
            P(("grp", "ep"), None),
            P(("grp", "ep")),
            P(("grp", "ep"), None),
            P(("grp", "ep"), None),
            P(("grp", "ep"), None),
            P(("grp", "ep"), None),
            P("ep", "grp", None),
            P("ep", "grp", None),
            P("ep", "grp", None),
        ),
        check_vma=False,
    )
```

```python
import functools
import math

import jax
import jax.numpy as jnp
from jax import lax
from jax.experimental import pallas as pl
from jax.experimental.pallas import tpu as pltpu
from jax.sharding import PartitionSpec as P

D = 2048
HEADS = 16
NOPE = 128
ROPE = 64
VH = 128
LATENT = 512
TOPK = 6

EPSILON = 1e-06
MASKED = -1e30

MESH = pl.DeviceIdType.MESH
ANY = pl.BlockSpec(memory_space=pl.ANY)
DMA = pltpu.SemaphoreType.DMA
F32 = jnp.float32
BF16 = jnp.bfloat16


def remote(src, dst, send, recv, peer):
    return pltpu.make_async_remote_copy(
        src_ref=src,
        dst_ref=dst,
        send_sem=send,
        recv_sem=recv,
        device_id={"ep": peer},
        device_id_type=MESH,
    )


def greet(peers):
    barrier = pltpu.get_barrier_semaphore()
    for peer in peers:
        pl.semaphore_signal(barrier, inc=1, device_id={"ep": peer}, device_id_type=MESH)
    pl.semaphore_wait(barrier, len(peers))


def around(n):
    me = lax.axis_index("ep")
    x, y = me % 2, (me // 2) % 2
    return me, me // 4, y, x, me + 1 - 2 * x, me + 2 - 4 * y


def near(z, nz, below, above):
    for s in range(nz - 1):
        pl.when(z - 1 - s >= 0)(functools.partial(below, s, z - 1 - s))
        pl.when(z + 1 + s < nz)(functools.partial(above, s, z + 1 + s))


def greet_near(px, py, up, down, z, nz):
    barrier = pltpu.get_barrier_semaphore()
    for peer, there in ((px, None), (py, None), (up, z + 1 < nz), (down, z > 0)):

        def hello(peer=peer):
            pl.semaphore_signal(barrier, inc=1, device_id={"ep": peer}, device_id_type=MESH)

        hello() if there is None else pl.when(there)(hello)
    on_line = (z + 1 < nz).astype(jnp.int32) + (z > 0).astype(jnp.int32)
    pl.semaphore_wait(barrier, 2 + on_line)


def start_swaps(n, ins, outs, sems):
    own, ss, rs = sems
    me = lax.axis_index("ep")
    sends, copies = [], []
    for j in range(len(ins)):
        local = pltpu.make_async_copy(ins[j].at[me], outs[j].at[me], own.at[j])
        local.start()
        copies.append(local)
    for k in range(1, n):
        to = (me + k) % n
        for j in range(len(ins)):
            c = remote(ins[j].at[to], outs[j].at[me], ss.at[j, k], rs.at[j, k], to)
            c.start()
            sends.append(c)
    return sends, copies


def end_swaps(n, ins, outs, sems, started):
    own, ss, rs = sems
    me = lax.axis_index("ep")
    sends, copies = started
    for k in range(1, n):
        to, back = (me + k) % n, (me + n - k) % n
        for j in range(len(ins)):
            remote(ins[j].at[back], outs[j].at[back], ss.at[j, k], rs.at[j, k], to).wait_recv()
    for copy in sends:
        copy.wait_send()
    for copy in copies:
        copy.wait()


def gather_kernel(n, w, x_ref, *refs):
    swaps_in, o_ref, swaps_out = refs[:w], refs[w], refs[w + 1 : 2 * w + 1]
    own, us, ur, ds, dr, xs, xr, ys, yr, *swap_sems = refs[2 * w + 1 :]
    me, z, y, x, px, py = around(n)
    nz = n // 4
    low = me % 4
    half = x_ref.shape[0] // 2
    top, bottom = pl.ds(0, half), pl.ds(half, half)
    up, down = (me + 4) % n, (me + n - 4) % n
    everyone = [(me + k) % n for k in range(n)]
    if w:
        greet(everyone[1:])
    else:
        greet_near(px, py, up, down, z, nz)
    local = pltpu.make_async_copy(x_ref, o_ref.at[me], own)
    local.start()

    def over_x(src, b, part, i):
        return remote(src.at[part], o_ref.at[b, part], xs.at[i], xr.at[i], px)

    def over_y(src, b, part, i):
        return remote(src.at[part], o_ref.at[b, part], ys.at[i], yr.at[i], py)

    def upward(src, b, s):
        return remote(src, o_ref.at[b], us.at[s], ur.at[s], up)

    def downward(src, b, s):
        return remote(src, o_ref.at[b], ds.at[s], dr.at[s], down)

    def spread(src, t):
        b = t * 4 + low
        over_x(src, b, top, t).start()
        over_y(src, b, bottom, t).start()
        over_y(src, b, top, nz + t).start()
        over_x(src, b, bottom, nz + t).start()

    pl.when(z + 1 < nz)(lambda: upward(x_ref, me, 0).start())
    pl.when(z > 0)(lambda: downward(x_ref, me, 0).start())
    spread(x_ref, z)
    swapping = start_swaps(n, swaps_in, swaps_out, swap_sems) if w else None

    def from_below(s, t):
        b = t * 4 + low
        upward(o_ref.at[b], b, s).wait_recv()
        pl.when(z + 1 < nz)(lambda: upward(o_ref.at[b], b, s + 1).start())
        spread(o_ref.at[b], t)

    def from_above(s, t):
        b = t * 4 + low
        downward(o_ref.at[b], b, s).wait_recv()
        pl.when(z > 0)(lambda: downward(o_ref.at[b], b, s + 1).start())
        spread(o_ref.at[b], t)

    def turn(s, t):
        bx = t * 4 + low + px - me
        by = t * 4 + low + py - me
        over_x(o_ref.at[bx], bx, top, t).wait_recv()
        over_y(o_ref.at[bx], bx, top, 2 * nz + t).start()
        over_y(o_ref.at[by], by, bottom, t).wait_recv()
        over_x(o_ref.at[by], by, bottom, 2 * nz + t).start()

    for s in range(nz - 1):
        pl.when(z - 1 - s >= 0)(functools.partial(from_below, s, z - 1 - s))
        pl.when(z + 1 + s < nz)(functools.partial(from_above, s, z + 1 + s))
        if s == 0:
            turn(0, z)
        else:
            pl.when(z - s >= 0)(functools.partial(turn, s, z - s))
            pl.when(z + s < nz)(functools.partial(turn, s, z + s))
    pl.when(z - (nz - 1) >= 0)(functools.partial(turn, 0, z - (nz - 1)))
    pl.when(z + (nz - 1) < nz)(functools.partial(turn, 0, z + (nz - 1)))

    def finish(s, t):
        bx = t * 4 + low + px - me
        by = t * 4 + low + py - me
        bxy = bx + py - me
        over_y(o_ref.at[by], by, top, nz + t).wait_recv()
        over_x(o_ref.at[bx], bx, bottom, nz + t).wait_recv()
        over_y(o_ref.at[bxy], bxy, top, 2 * nz + t).wait_recv()
        over_x(o_ref.at[bxy], bxy, bottom, 2 * nz + t).wait_recv()
        for i in range(3):
            over_x(x_ref, me, top, i * nz + t).wait_send()
            over_y(x_ref, me, top, i * nz + t).wait_send()

    finish(0, z)
    near(z, nz, finish, finish)

    def sent_up(s, t):
        upward(x_ref, me, s).wait_send()

    def sent_down(s, t):
        downward(x_ref, me, s).wait_send()

    for s in range(nz - 1):
        pl.when((z + 1 < nz) & (z - s >= 0))(functools.partial(sent_up, s, z))
        pl.when((z > 0) & (z + s < nz))(functools.partial(sent_down, s, z))
    local.wait()
    if w:
        end_swaps(n, swaps_in, swaps_out, swap_sems, swapping)


def gather(x, cid, swaps=()):
    n = lax.axis_size("ep")
    w = len(swaps)
    nz = n // 4
    return pl.pallas_call(
        functools.partial(gather_kernel, n, w),
        out_shape=[jax.ShapeDtypeStruct((n,) + x.shape, x.dtype)]
        + [jax.ShapeDtypeStruct(a.shape, a.dtype) for a in swaps],
        in_specs=[ANY] * (1 + w),
        out_specs=[ANY] * (1 + w),
        scratch_shapes=[DMA]
        + [DMA((nz,))] * 4
        + [DMA((3 * nz,))] * 4
        + ([DMA((w,)), DMA((w, n)), DMA((w, n))] if w else []),
        compiler_params=pltpu.CompilerParams(collective_id=cid, has_side_effects=True),
        name="gather",
    )(x, *swaps)


def add_rows(dst, left, right, rows):
    step = 16

    def body(i, carry):
        r = pl.ds(pl.multiple_of(i * step, step), step)
        dst[r] = (left[r].astype(F32) + right[r].astype(F32)).astype(dst.dtype)
        return carry

    lax.fori_loop(0, rows // step, body, 0)


TILE = 128


def exchange_kernel(n, m, w, laid, groups, jobs, *refs):
    refs = list(refs)

    def take(count):
        out = refs[:count]
        del refs[:count]
        return out

    sums_in, swaps_in = take(m), take(w)
    jobs_in = [take(2) for _ in jobs]
    sums_out, swaps_out, jobs_out = take(m), take(w), [take(parts * blocks) for parts, blocks in jobs]
    room = [take(7) for _ in range(m)]
    sems = [take(8) for _ in range(m)]
    swap_sems = take(3) if w else None
    side_by_side = swaps_out[w - laid :]
    swaps_out = swaps_out[: w - laid] + take(laid)
    desks = [take(5) for _ in jobs]
    me, z, y, x, px, py = around(n)
    nz = n // 4
    low = me % 4
    to = [(z + k) % nz for k in range(nz)]
    at = [t * 4 + low for t in to]
    if w:
        greet([(me + k) % n for k in range(1, n)])
    else:
        greet([px, py] + at[1:])
    order = [2, 1, 3, 0] if nz == 4 else list(range(1, nz)) + [0]
    sends = []

    def halves(j):
        half = sums_in[j].shape[3] // 2
        return half, pl.ds(0, half), pl.ds(half, half)

    first, second, third = {}, {}, {}

    def stage_one(j, k):
        p = sums_in[j]
        half, top, bottom = halves(j)
        la, lb, a1, b1, a2, b2, zb = room[j]
        lsa, lsb, xs, xr, ys, yr, zs, zr = sems[j]
        t = to[k]
        c = remote(p.at[t, 1 - y, :, top], a1.at[k], ys.at[k], yr.at[k], py)
        d = remote(p.at[t, :, 1 - x, bottom], b1.at[k], xs.at[k], xr.at[k], px)
        c.start()
        d.start()
        e = pltpu.make_async_copy(p.at[t, y, :, top], la.at[k], lsa.at[k])
        f = pltpu.make_async_copy(p.at[t, :, x, bottom], lb.at[k], lsb.at[k])
        e.start()
        f.start()
        first[j, k] = (c, d, e, f)
        sends.extend([c, d])

    def stage_two(j, k):
        half, top, bottom = halves(j)
        la, lb, a1, b1, a2, b2, zb = room[j]
        lsa, lsb, xs, xr, ys, yr, zs, zr = sems[j]
        c, d, e, f = first[j, k]
        e.wait()
        c.wait_recv()
        for i in range(2):
            add_rows(la.at[k, i], la.at[k, i], a1.at[k, i], half)
        g = remote(la.at[k, 1 - x], a2.at[k], xs.at[nz + k], xr.at[nz + k], px)
        g.start()
        f.wait()
        d.wait_recv()
        for i in range(2):
            add_rows(lb.at[k, i], lb.at[k, i], b1.at[k, i], half)
        h = remote(lb.at[k, 1 - y], b2.at[k], ys.at[nz + k], yr.at[nz + k], py)
        h.start()
        second[j, k] = (g, h)
        sends.extend([g, h])

    def stage_three(j, k):
        half, top, bottom = halves(j)
        la, lb, a1, b1, a2, b2, zb = room[j]
        lsa, lsb, xs, xr, ys, yr, zs, zr = sems[j]
        g, h = second[j, k]
        g.wait_recv()
        add_rows(a2.at[k], la.at[k, x], a2.at[k], half)
        if k:
            c = remote(a2.at[k], zb.at[k, top], zs.at[k], zr.at[k], at[k])
            c.start()
        h.wait_recv()
        add_rows(b2.at[k], lb.at[k, y], b2.at[k], half)
        if k:
            d = remote(b2.at[k], zb.at[k, bottom], zs.at[nz + k], zr.at[nz + k], at[k])
            d.start()
            third[j, k] = (c, d)
            sends.extend([c, d])

    loads = []
    for (left, right), (left_v, right_v, page, in_sem, out_sem) in zip(jobs_in, desks):
        for i, (src, dst) in enumerate(((left, left_v), (right, right_v))):
            loads.append(pltpu.make_async_copy(src, dst, in_sem.at[i]))

    def pieces(j):
        parts, blocks = jobs[j]
        rows = jobs_out[j][0].shape[0]
        piece = math.gcd(TILE, rows)
        return [(q * piece, piece) for q in range(TILE // piece)]

    def start_write(j, i, part):
        left_v, right_v, page, in_sem, out_sem = desks[j]
        parts, blocks = jobs[j]
        outs = jobs_out[j][part * blocks : (part + 1) * blocks]
        rows = outs[0].shape[0]
        for q, (offset, piece) in enumerate(pieces(j)):
            row = i * TILE + offset
            src = page.at[i % 2, part, pl.ds(offset, piece)]
            owner = (row // rows + blocks - (lax.axis_index("grp") if blocks > 1 else 0)) % blocks
            inside = pl.ds(pl.multiple_of(row % rows, piece), piece)
            for k, out in enumerate(outs):
                copy = pltpu.make_async_copy(src, out.at[inside], out_sem.at[i % 2, part, q])
                if blocks > 1:
                    pl.when(owner == k)(copy.start)
                else:
                    copy.start()

    def wait_write(j, i, part):
        left_v, right_v, page, in_sem, out_sem = desks[j]
        for q, (offset, piece) in enumerate(pieces(j)):
            src = page.at[i % 2, part, pl.ds(offset, piece)]
            out = jobs_out[j][part * jobs[j][1]].at[pl.ds(0, piece)]
            pltpu.make_async_copy(src, out, out_sem.at[i % 2, part, q]).wait()

    def tile(j, i):
        left_v, right_v, page, in_sem, out_sem = desks[j]
        value = lax.dot_general(
            left_v[:, pl.ds(pl.multiple_of(i * TILE, TILE), TILE)],
            right_v[...],
            (((0,), (0,)), ((), ())),
            preferred_element_type=F32,
        ).astype(page.dtype)
        width = page.shape[3]
        for part in range(jobs[j][0]):
            pl.when(i >= 2)(functools.partial(wait_write, j, i, part))
            page[i % 2, part] = value[:, part * width : (part + 1) * width]
            start_write(j, i, part)

    tiles = [desk[0].shape[1] // TILE for desk in desks]
    loaded = []

    def work(step, of):
        first, last = sum(tiles) * step // of, sum(tiles) * (step + 1) // of
        for j in range(len(jobs)):
            start = sum(tiles[:j])
            low, high = max(first - start, 0), min(last - start, tiles[j])
            if low >= high:
                continue
            if j not in loaded:
                loaded.append(j)
                loads[2 * j].wait()
                loads[2 * j + 1].wait()
            lax.fori_loop(low, high, lambda i, c, j=j: (tile(j, i), c)[1], 0)

    steps = [(j, k) for k in order for j in range(m)]
    ahead = 3 if jobs else 2
    for i in range(min(ahead, len(steps))):
        stage_one(*steps[i])
    for copy in loads:
        copy.start()
    if w:
        swapping = start_swaps(n, swaps_in, swaps_out, swap_sems)
    for i, step in enumerate(steps):
        stage_two(*step)
        if i + ahead < len(steps):
            stage_one(*steps[i + ahead])
        if i:
            stage_three(*steps[i - 1])
        work(i, len(steps))
    if steps:
        stage_three(*steps[-1])
    if w:
        end_swaps(n, swaps_in, swaps_out, swap_sems, swapping)
        for wide, got in zip(side_by_side, swaps_out[w - laid :]):
            width = got.shape[2]
            for k in range(n):
                wide[:, k * width : (k + 1) * width] = got[k].astype(F32)
    for j in range(m):
        half, top, bottom = halves(j)
        la, lb, a1, b1, a2, b2, zb = room[j]
        o_ref = sums_out[j]
        for k in range(1, nz):
            c, d = third[j, k]
            c.wait_recv()
            d.wait_recv()
        for part, offset in ((a2, 0), (b2, half)):

            def body(i, carry, part=part, offset=offset, zb=zb, o_ref=o_ref):
                r = pl.ds(pl.multiple_of(i * 16, 16), 16)
                q = pl.ds(pl.multiple_of(i * 16 + offset, 16), 16)
                total = part[0, r].astype(F32)
                for k in range(1, nz):
                    total = total + zb[k, q].astype(F32)
                o_ref[q] = total.astype(o_ref.dtype)
                return carry

            lax.fori_loop(0, half // 16, body, 0)
    for copy in sends:
        copy.wait_send()
    for j in range(len(jobs)):
        for i in range(min(2, tiles[j])):
            for part in range(jobs[j][0]):
                wait_write(j, i, part)


def exchange(cid, sums=(), swaps=(), laid=0, jobs=()):
    n = lax.axis_size("ep")
    nz = n // 4
    groups = lax.axis_size("grp")
    m, w = len(sums), len(swaps)
    kept_rows = [p.shape[1] for p in sums]
    sums = [jnp.pad(p, ((0, 0), (0, -p.shape[1] % 32), (0, 0))) for p in sums]
    views = [p.reshape((nz, 2, 2) + p.shape[1:]) for p in sums]
    scratch = []
    for p in sums:
        rows, cols = p.shape[1:]
        half = rows // 2
        scratch += [pltpu.VMEM((nz, 2, half, cols), p.dtype)] * 4
        scratch += [pltpu.VMEM((nz, half, cols), p.dtype)] * 2
        scratch += [pltpu.VMEM((nz, rows, cols), p.dtype)]
    for p in sums:
        scratch += [DMA((nz,))] * 2 + [DMA((2 * nz,))] * 6
    if w:
        scratch += [DMA((w,)), DMA((w, n)), DMA((w, n))]
    plain, wide = swaps[: w - laid], swaps[w - laid :]
    scratch += [pltpu.VMEM(a.shape, a.dtype) for a in wide]
    jobs_out = []
    for left, right, parts, blocks in jobs:
        rows, cols = left.shape[1] // blocks, right.shape[1] // parts
        jobs_out += [jax.ShapeDtypeStruct((rows, cols), BF16)] * (parts * blocks)
        scratch += [pltpu.VMEM(left.shape, left.dtype), pltpu.VMEM(right.shape, right.dtype)]
        scratch += [pltpu.VMEM((2, parts, TILE, cols), BF16), DMA((2,))]
        scratch += [DMA((2, parts, TILE // math.gcd(TILE, rows)))]
    out = pl.pallas_call(
        functools.partial(exchange_kernel, n, m, w, laid, groups, [job[2:] for job in jobs]),
        out_shape=[jax.ShapeDtypeStruct(p.shape[1:], F32) for p in sums]
        + [jax.ShapeDtypeStruct(a.shape, a.dtype) for a in plain]
        + [jax.ShapeDtypeStruct((a.shape[1], n * a.shape[2]), F32) for a in wide]
        + jobs_out,
        in_specs=[ANY] * (m + w + 2 * len(jobs)),
        out_specs=[pl.BlockSpec(memory_space=pltpu.VMEM)] * m
        + [ANY] * (w - laid)
        + [pl.BlockSpec(memory_space=pltpu.VMEM)] * laid
        + [ANY] * len(jobs_out),
        scratch_shapes=scratch,
        compiler_params=pltpu.CompilerParams(
            collective_id=cid, has_side_effects=True, vmem_limit_bytes=(60 if jobs else 40) << 20 if m else None
        ),
        name="exchange",
    )(*views, *swaps, *(a for job in jobs for a in job[:2]))
    return [a[:rows] for a, rows in zip(out, kept_rows)] + list(out[m:])


def both(p):
    g = lax.axis_index("grp")
    mine = lax.dynamic_index_in_dim(p, g, 0, keepdims=False)
    theirs = lax.dynamic_index_in_dim(p, 1 - g, 0, keepdims=False)
    return mine, lax.ppermute(theirs.astype(BF16), "grp", [(0, 1), (1, 0)])


def over_groups(p):
    if lax.axis_size("grp") == 2:
        mine, other = both(p)
        return mine.astype(F32) + other.astype(F32)
    return lax.psum_scatter(p.astype(BF16), "grp", scatter_dimension=0, tiled=False).astype(F32)


def product_over_groups(left, right):
    groups = lax.axis_size("grp")
    rows = left.shape[1] // groups
    if groups != 2:
        whole = product("km,kn->mn", left, right)
        return over_groups(whole.reshape(groups, rows, -1))
    g = lax.axis_index("grp")
    mine = lax.dynamic_slice_in_dim(left, g * rows, rows, 1)
    theirs = lax.dynamic_slice_in_dim(left, (1 - g) * rows, rows, 1)
    sent = product("km,kn->mn", theirs, right).astype(BF16)
    other = lax.ppermute(sent, "grp", [(0, 1), (1, 0)])
    return product("km,kn->mn", mine, right) + other.astype(F32)


def from_partner(values):
    groups = lax.axis_size("grp")
    return lax.ppermute(values, "grp", [(g, g + 1 - 2 * (g % 2)) for g in range(groups)])


def to_row_owner(block):
    groups, n = lax.axis_size("grp"), lax.axis_size("ep")
    pairs = [(h * n + e, e * groups + h) for h in range(groups) for e in range(n)]
    return lax.ppermute(block.astype(BF16), ("grp", "ep"), pairs).astype(F32)


def dot(left, right):
    return jnp.dot(left, right, preferred_element_type=F32)


def dot_nt(left, right):
    return lax.dot_general(left, right, (((1,), (1,)), ((), ())), preferred_element_type=F32)


def front_kernel(
    x_ref, w_ref, cos_ref, sin_ref, gain_ref, lat_gain_ref, wq_ref, wl_ref, we_ref,
    normed_ref, query_ref, keys_ref, values_ref, latent_ref, out_w_ref,
):
    out_w_ref[...] = w_ref[...].reshape(out_w_ref.shape)
    blocks, tokens = x_ref.shape[:2]
    rows = blocks * tokens
    x = x_ref[...].reshape(rows, gain_ref.shape[1]).astype(F32)
    normed = (x * rms_scale(x) * gain_ref[...]).astype(BF16)
    normed_ref[...] = normed
    cos, sin = cos_ref[...], sin_ref[...]
    own_half = lax.broadcasted_iota(jnp.int32, cos.shape, 1) < ROPE

    def turn(pair):
        return pair * cos + pltpu.roll(pair, ROPE, 1) * sin

    query = dot_nt(normed, wq_ref[...])
    query_ref[:, :NOPE] = query[:, :NOPE].astype(BF16)
    query_ref[:, NOPE:] = jnp.where(own_half, turn(query[:, NOPE:]), 0.0).astype(BF16)
    compressed = dot(normed, wl_ref[...])
    raw = compressed[:, :LATENT]
    latent = (raw * rms_scale(raw) * lat_gain_ref[...]).astype(BF16)
    latent_ref[...] = latent
    expanded = dot(latent, we_ref[...])
    keys_ref[:, :NOPE] = expanded[:, :NOPE].astype(BF16)
    keys_ref[:, NOPE:] = turn(compressed[:, LATENT:]).astype(BF16)
    values_ref[...] = expanded[:, NOPE:].astype(BF16)


def front(x, cos, sin, gain, lat_gain, wq, wl, we):
    n, tokens = x.shape[:2]
    model = gain.shape[1]
    length = n * tokens
    blocks = 2
    rows = blocks * tokens

    def whole(a):
        return pl.BlockSpec(a.shape, lambda i: (0,) * a.ndim, pipeline_mode=pl.Buffered(1))

    def rows_of(cols):
        return pl.BlockSpec((rows, cols), lambda i: (i, 0))

    def out(cols):
        return jax.ShapeDtypeStruct((length, cols), BF16)

    cols = (model, wq.shape[0], NOPE + 2 * ROPE, VH, LATENT, model // 2)
    return pl.pallas_call(
        front_kernel,
        grid=(n // blocks,),
        in_specs=[
            pl.BlockSpec((blocks, tokens, model), lambda i: (i, 0, 0)),
            pl.BlockSpec((blocks, tokens, model // 2), lambda i: (i, 0, 2)),
            rows_of(2 * ROPE),
            rows_of(2 * ROPE),
        ]
        + [whole(a) for a in (gain, lat_gain, wq, wl, we)],
        out_specs=[rows_of(c) for c in cols],
        out_shape=[out(c) for c in cols],
        compiler_params=pltpu.CompilerParams(vmem_limit_bytes=48 << 20),
        name="front",
    )(x, x, cos, sin, gain, lat_gain, wq, wl, we)


def back_kernel(
    cos_ref, sin_ref, dq_ref, dk_ref, dv_ref, we_ref, query_ref, expanded_ref, latent_ref, rope_ref
):
    own_half = lax.broadcasted_iota(jnp.int32, cos_ref.shape, 1) < ROPE
    pair = dq_ref[:, NOPE:] * jnp.where(own_half, cos_ref[...], sin_ref[...])
    pair = jnp.where(own_half, pair + pltpu.roll(pair, ROPE, 1), 0.0)
    query_ref[:, :NOPE] = dq_ref[:, :NOPE].astype(BF16)
    query_ref[:, NOPE:] = pair.astype(BF16)
    expanded_ref[:, :NOPE] = dk_ref[:, :NOPE].astype(BF16)
    expanded_ref[:, NOPE:] = dv_ref[...].astype(BF16)
    latent_ref[...] = dot_nt(expanded_ref[...], we_ref[...]).astype(BF16)
    rope_ref[...] = dk_ref[:, NOPE:].astype(BF16)


def back(cos, sin, dq, dk, dv, we):
    length = dq.shape[0]
    rows = 512

    def rows_of(cols):
        return pl.BlockSpec((rows, cols), lambda i: (i, 0))

    def out(cols):
        return jax.ShapeDtypeStruct((length, cols), BF16)

    cols = (NOPE + 2 * ROPE, NOPE + VH, LATENT, 2 * ROPE)
    return pl.pallas_call(
        back_kernel,
        grid=(length // rows,),
        in_specs=[rows_of(a.shape[1]) for a in (cos, sin, dq, dk, dv)]
        + [pl.BlockSpec(we.shape, lambda i: (0, 0))],
        out_specs=[rows_of(c) for c in cols],
        out_shape=[out(c) for c in cols],
        compiler_params=pltpu.CompilerParams(vmem_limit_bytes=40 << 20),
        name="back",
    )(cos, sin, dq, dk, dv, we)


KEYS = 512


def scores_of(scale, prefix, k, q, first_key, first_query):
    scores = dot_nt(k, q) * scale
    key = first_key + lax.broadcasted_iota(jnp.int32, scores.shape, 0)
    query = first_query + lax.broadcasted_iota(jnp.int32, scores.shape, 1)
    return jnp.where((key <= query) | (key < prefix), scores, MASKED)


def key_blocks(prefix, last_query):
    return (jnp.maximum(last_query, prefix) + KEYS - 1) // KEYS


def attend_kernel(scale, prefix_ref, q_ref, k_ref, v_ref, attended_ref, exact_ref, lse_ref):
    q = q_ref[...]
    rows = q.shape[0]
    start = pl.program_id(0) * rows
    prefix = prefix_ref[0]

    def step(j, carry):
        top, total, out = carry
        s = scores_of(scale, prefix, k_ref[j], q, j * KEYS, start)
        new_top = jnp.maximum(top, jnp.max(s, axis=0, keepdims=True))
        p = jnp.exp(s - new_top)
        shrink = jnp.exp(top - new_top)
        total = total * shrink + jnp.sum(p, axis=0, keepdims=True)
        return new_top, total, out * shrink + dot(v_ref[j], p.astype(BF16))

    top, total, out = lax.fori_loop(
        0,
        key_blocks(prefix, start + rows),
        step,
        (
            jnp.full((1, rows), MASKED, F32),
            jnp.zeros((1, rows), F32),
            jnp.zeros((v_ref.shape[1], rows), F32),
        ),
    )
    lse_ref[...] = top + jnp.log(total)
    exact = (out / total).T
    exact_ref[...] = exact
    attended_ref[...] = exact.astype(BF16)


def attend(prefix, q, k, v):
    length, depth = q.shape
    values = v.shape[1]
    rows = 256
    v = v.reshape(length // KEYS, KEYS, values).transpose(0, 2, 1)
    k = k.reshape(length // KEYS, KEYS, depth)
    return pl.pallas_call(
        functools.partial(attend_kernel, 1.0 / math.sqrt(NOPE + ROPE)),
        grid=(length // rows,),
        in_specs=[
            pl.BlockSpec(memory_space=pltpu.SMEM),
            pl.BlockSpec((rows, depth), lambda i: (i, 0)),
            pl.BlockSpec(k.shape, lambda i: (0, 0, 0)),
            pl.BlockSpec(v.shape, lambda i: (0, 0, 0)),
        ],
        out_specs=[
            pl.BlockSpec((rows, values), lambda i: (i, 0)),
            pl.BlockSpec((rows, values), lambda i: (i, 0)),
            pl.BlockSpec((1, rows), lambda i: (0, i)),
        ],
        out_shape=[
            jax.ShapeDtypeStruct((length, values), BF16),
            jax.ShapeDtypeStruct((length, values), F32),
            jax.ShapeDtypeStruct((1, length), F32),
        ],
        compiler_params=pltpu.CompilerParams(vmem_limit_bytes=32 << 20),
        name="attend",
    )(prefix, q, k, v)


def attend_back_kernel(
    scale, prefix_ref, q_ref, g_ref, lse_ref, delta_ref, k_ref, v_ref, dq_ref, dk_ref, dv_ref
):
    q, g = q_ref[...], g_ref[...]
    rows = q.shape[0]
    start = pl.program_id(0) * rows
    prefix = prefix_ref[0]

    @pl.when(pl.program_id(0) == 0)
    def _():
        dk_ref[...] = jnp.zeros_like(dk_ref)
        dv_ref[...] = jnp.zeros_like(dv_ref)

    def step(j, dq):
        k = k_ref[j]
        p = jnp.exp(scores_of(scale, prefix, k, q, j * KEYS, start) - lse_ref[...])
        ds = (p * (dot_nt(v_ref[j], g) - delta_ref[...]) * scale).astype(BF16)
        dv_ref[j] += dot(p.astype(BF16), g)
        dk_ref[j] += dot(ds, q)
        return dq + lax.dot_general(
            ds, k, (((0,), (0,)), ((), ())), preferred_element_type=F32
        )

    dq_ref[...] = lax.fori_loop(
        0, key_blocks(prefix, start + rows), step, jnp.zeros(dq_ref.shape, F32)
    )


def attend_back(prefix, q, g, lse, delta, k, v):
    length, depth = q.shape
    values = v.shape[1]
    rows = 256
    k = k.reshape(length // KEYS, KEYS, depth)
    v = v.reshape(length // KEYS, KEYS, values)
    dq, dk, dv = pl.pallas_call(
        functools.partial(attend_back_kernel, 1.0 / math.sqrt(NOPE + ROPE)),
        grid=(length // rows,),
        in_specs=[
            pl.BlockSpec(memory_space=pltpu.SMEM),
            pl.BlockSpec((rows, depth), lambda i: (i, 0)),
            pl.BlockSpec((rows, values), lambda i: (i, 0)),
            pl.BlockSpec((1, rows), lambda i: (0, i)),
            pl.BlockSpec((1, rows), lambda i: (0, i)),
            pl.BlockSpec(k.shape, lambda i: (0, 0, 0)),
            pl.BlockSpec(v.shape, lambda i: (0, 0, 0)),
        ],
        out_specs=[
            pl.BlockSpec((rows, depth), lambda i: (i, 0)),
            pl.BlockSpec(k.shape, lambda i: (0, 0, 0)),
            pl.BlockSpec(v.shape, lambda i: (0, 0, 0)),
        ],
        out_shape=[
            jax.ShapeDtypeStruct((length, depth), F32),
            jax.ShapeDtypeStruct(k.shape, F32),
            jax.ShapeDtypeStruct(v.shape, F32),
        ],
        compiler_params=pltpu.CompilerParams(vmem_limit_bytes=40 << 20),
        name="attend_back",
    )(prefix, q, g, lse, delta, k, v)
    return dq, dk.reshape(length, depth), dv.reshape(length, values)


def ffn_kernel(
    n,
    x_ref,
    y_ref,
    slots_ref,
    tokens_ref,
    own_ref,
    router_ref,
    sg_ref,
    su_ref,
    sd_ref,
    eg_ref,
    eu_ref,
    ed_ref,
    out_ref,
    ffn_ref,
    dot_ref,
    probs_ref,
    rows_ref,
    hidden_ref,
    slot_grad_ref,
    grad_gu_ref,
    shared_h_ref,
    shared_gu_ref,
    expert_out,
    row_grad,
):
    blocks, tokens = x_ref.shape[:2]
    capacity = slots_ref.shape[1]
    own = own_ref[...]
    lanes = lax.broadcasted_iota(jnp.int32, (tokens, own.shape[1]), 1)
    gates = []
    for b in range(blocks):
        x, y = x_ref[b], y_ref[b]
        logits = jnp.where(lanes < n, dot(x, router_ref[...]), MASKED)
        raised = jnp.exp(logits - jnp.max(logits, axis=-1, keepdims=True))
        probs = raised / jnp.sum(raised, axis=-1, keepdims=True)
        probs_ref[b] = probs
        gate = jnp.sum(probs * own, axis=-1, keepdims=True)
        gates.append(gate)
        part = pl.ds(b * capacity, capacity)
        rows_ref[part] = dot(slots_ref[b], x).astype(BF16)
        weighted = (gate * y.astype(F32)).astype(BF16)
        slot_grad_ref[part] = dot(slots_ref[b], weighted).astype(BF16)
    rows = rows_ref[...]
    slot_grad = slot_grad_ref[...]
    g = dot(rows, eg_ref[...])
    u = dot(rows, eu_ref[...])
    sigmoid = 1.0 / (1.0 + jnp.exp(-g))
    silu = g * sigmoid
    hidden = (silu * u).astype(BF16)
    hidden_ref[...] = hidden
    expert_out[...] = dot(hidden, ed_ref[...]).astype(BF16)
    grad_hidden = dot_nt(slot_grad, ed_ref[...])
    grad_g = (grad_hidden * u * sigmoid * (1.0 + g * (1.0 - sigmoid))).astype(BF16)
    grad_u = (grad_hidden * silu).astype(BF16)
    grad_gu_ref[:, : grad_g.shape[1]] = grad_g
    grad_gu_ref[:, grad_g.shape[1] :] = grad_u
    row_grad[...] = (dot_nt(grad_g, eg_ref[...]) + dot_nt(grad_u, eu_ref[...])).astype(BF16)
    x = x_ref[...].reshape(blocks * tokens, -1)
    y = y_ref[...].reshape(blocks * tokens, -1)
    g = dot_nt(x, sg_ref[...])
    u = dot_nt(x, su_ref[...])
    grad_hidden = dot_nt(y, sd_ref[...])
    sigmoid = 1.0 / (1.0 + jnp.exp(-g))
    silu = g * sigmoid
    hidden = (silu * u).astype(BF16)
    grad_g = (grad_hidden * u * sigmoid * (1.0 + g * (1.0 - sigmoid))).astype(BF16)
    grad_u = (grad_hidden * silu).astype(BF16)
    shared = hidden.shape[1]
    shared_h_ref[...] = hidden.reshape(blocks, tokens, shared)
    shared_gu_ref[:, :, :shared] = grad_g.reshape(blocks, tokens, shared)
    shared_gu_ref[:, :, shared:] = grad_u.reshape(blocks, tokens, shared)
    width = x.shape[1]
    chunk = width // 4
    met = [0.0] * blocks
    for c in range(width // chunk):
        cols = pl.ds(c * chunk, chunk)
        shared_out = dot(hidden, sd_ref[:, cols])
        shared_ffn = dot(grad_g, sg_ref[:, cols]) + dot(grad_u, su_ref[:, cols])
        for b in range(blocks):
            part = pl.ds(b * capacity, capacity)
            here = slice(b * tokens, (b + 1) * tokens)
            picked = dot(tokens_ref[b], expert_out[part, cols])
            met[b] += jnp.sum(picked * y_ref[b, :, cols].astype(F32), axis=-1, keepdims=True)
            out_ref[b, :, cols] = (shared_out[here] + picked * gates[b]).astype(BF16)
            back = dot(tokens_ref[b], row_grad[part, cols])
            ffn_ref[b, :, cols] = (shared_ffn[here] + back).astype(BF16)
    for b in range(blocks):
        dot_ref[b] = (met[b] * own).astype(BF16)


def ffn(x, y, slots, own_lane, router_w, gate_t, up_t, down, gate_m, up_m, down_m):
    n, tokens, width = x.shape
    capacity = slots.shape[1]
    hidden = gate_m.shape[1]
    shared = gate_t.shape[0]
    group = 4

    def whole(a):
        return pl.BlockSpec(a.shape, lambda i: (0,) * a.ndim, pipeline_mode=pl.Buffered(1))

    def block(*shape):
        return pl.BlockSpec((group,) + shape, lambda i: (i, 0, 0))

    def slot_rows(cols):
        return pl.BlockSpec((group * capacity, cols), lambda i: (i, 0))

    def tokens_of(cols, kind=BF16):
        return jax.ShapeDtypeStruct((n, tokens, cols), kind)

    def slots_of(cols):
        return jax.ShapeDtypeStruct((n * capacity, cols), BF16)

    weights = (own_lane, router_w, gate_t, up_t, down, gate_m, up_m, down_m)
    return pl.pallas_call(
        functools.partial(ffn_kernel, n),
        grid=(n // group,),
        in_specs=[
            block(tokens, width),
            block(tokens, width),
            block(capacity, tokens),
            block(tokens, capacity),
        ]
        + [whole(a) for a in weights],
        out_specs=[
            block(tokens, width),
            block(tokens, width),
            block(tokens, 128),
            block(tokens, 128),
            slot_rows(width),
            slot_rows(hidden),
            slot_rows(width),
            slot_rows(2 * hidden),
            block(tokens, shared),
            block(tokens, 2 * shared),
        ],
        out_shape=[
            tokens_of(width),
            tokens_of(width),
            tokens_of(128),
            tokens_of(128, F32),
            slots_of(width),
            slots_of(hidden),
            slots_of(width),
            slots_of(2 * hidden),
            tokens_of(shared),
            tokens_of(2 * shared),
        ],
        scratch_shapes=[
            pltpu.VMEM((group * capacity, width), BF16),
            pltpu.VMEM((group * capacity, width), BF16),
        ],
        compiler_params=pltpu.CompilerParams(vmem_limit_bytes=60 << 20),
        name="ffn",
    )(x, y, slots, slots.transpose(0, 2, 1), *weights)


def product(form, left, right):
    return jnp.einsum(form, left, right, preferred_element_type=F32)


def rms_scale(values):
    return lax.rsqrt(jnp.mean(values * values, axis=-1, keepdims=True) + EPSILON)


def rotary_tables(tokens, n):
    halfway = ROPE // 2
    inverse = 10000.0 ** (-(jnp.arange(halfway, dtype=F32) * 2.0 / ROPE))
    inverse = jnp.concatenate([inverse] * 4)
    lane = jnp.arange(2 * ROPE)
    sign = jnp.where((lane < halfway) | (lane >= 3 * halfway), -1.0, 1.0)
    base = (jnp.arange(n, dtype=F32) * tokens)[:, None] * inverse
    step = jnp.arange(tokens, dtype=F32)[:, None] * inverse
    base_cos, base_sin = jnp.cos(base)[:, None], jnp.sin(base)[:, None]
    step_cos, step_sin = jnp.cos(step)[None], jnp.sin(step)[None]
    cos_table = base_cos * step_cos - base_sin * step_sin
    sin_table = (base_sin * step_cos + base_cos * step_sin) * sign
    return cos_table.reshape(n * tokens, -1), sin_table.reshape(n * tokens, -1)


def unrotate(grads, cos_table, sin_table):
    halfway = grads.shape[-1] // 2
    first = grads[..., :halfway]
    second = grads[..., halfway:]
    return jnp.concatenate(
        [first * cos_table + second * sin_table, second * cos_table - first * sin_table], axis=-1
    )


def norm_back(grad_unit, unit_values, scale_values):
    return scale_values * (
        grad_unit - unit_values * jnp.mean(grad_unit * unit_values, axis=-1, keepdims=True)
    )


def column_halves(weight, n, half):
    rows, width = weight.shape[0], weight.shape[1] // n
    parts = weight.T.reshape(n, 2, width // 2, rows)
    return lax.dynamic_index_in_dim(parts, half, 1, keepdims=False)


def columns_in(blocks):
    n, width, rows = blocks.shape
    return blocks.transpose(1, 0, 2).reshape(width, n * rows)


def both_halves(mine, other, even, axis=0):
    return jnp.concatenate([jnp.where(even, mine, other), jnp.where(even, other, mine)], axis=axis)


def per_device(
    layer_input,
    attention_gain,
    query_weight,
    latent_weight,
    latent_gain,
    expand_weight,
    output_weight,
    feedforward_gain,
    router_weight,
    shared_gate,
    shared_up,
    shared_down,
    expert_gate,
    expert_up,
    expert_down,
    expert_routes,
    prefix_length,
    output_grad,
):
    n = lax.axis_size("ep")
    groups = lax.axis_size("grp")
    e = lax.axis_index("ep")
    half = lax.axis_index("grp") % 2
    even = half == 0
    tokens = layer_input.shape[0]
    length = tokens * n
    capacity = tokens * TOPK * 4 // (3 * n)
    rows_dev = attention_gain.shape[0]
    latent_rows = latent_gain.shape[0]
    rows_out = D // (groups * n)
    expand_rows = LATENT // (groups * n)

    out_w_half = lax.dynamic_slice_in_dim(output_weight, half * (D // 2), D // 2, 1)
    first_block = jnp.concatenate(
        [layer_input, out_w_half, latent_weight, router_weight, expert_routes.astype(BF16)], axis=1
    )
    width = first_block.shape[1]
    first_block = jnp.pad(first_block, ((0, 0), (0, -width % 128)))
    gains = jnp.zeros((16, rows_dev), BF16)
    gains = gains.at[0].set(attention_gain).at[1].set(feedforward_gain)
    gains = gains.at[2, :latent_rows].set(latent_gain)
    shared_half = jnp.where(even, shared_gate, shared_up)
    expand_half = lax.dynamic_index_in_dim(
        expand_weight.reshape(latent_rows, n, 2, -1), half, 2, keepdims=False
    ).transpose(1, 0, 2)
    first_all, q_blocks, x_blocks, shared_blocks, gain_blocks = gather(
        first_block,
        0,
        swaps=(
            column_halves(query_weight, n, half),
            expand_half,
            shared_half.T.reshape(n, shared_half.shape[1] // n, rows_dev),
            jnp.broadcast_to(gains, (n,) + gains.shape),
        ),
    )
    c0 = D + D // 2
    c1 = c0 + LATENT + ROPE
    c2 = c1 + n
    latent_w = first_all[:, :, c0:c1].reshape(D, LATENT + ROPE)
    router_w = first_all[:, :, c1:c2].reshape(D, n)
    routes = first_all[:, :, c2 : c2 + TOPK].astype(jnp.int32)
    attn_gain = gain_blocks[:, 0].reshape(D).astype(F32)
    ffn_gain = gain_blocks[:, 1].reshape(D).astype(F32)
    lat_gain = gain_blocks[:, 2, :latent_rows].reshape(LATENT).astype(F32)

    later_grad, q_blocks = lax.optimization_barrier((output_grad, q_blocks))
    all_out_grad = lax.all_gather(later_grad, "ep", axis=0, tiled=True)

    q_mine, x_mine = columns_in(q_blocks), x_blocks.reshape(LATENT, -1)
    query_t = both_halves(q_mine, from_partner(q_mine), even)
    expand_w = both_halves(x_mine, from_partner(x_mine), even, 1)
    shared_mine = columns_in(shared_blocks)
    shared_other = from_partner(shared_mine)
    gate_t = jnp.where(even, shared_mine, shared_other)
    up_t = jnp.where(even, shared_other, shared_mine)

    def own(values):
        return lax.dynamic_slice_in_dim(values, e * tokens, tokens, 0)

    cos_table, sin_table = rotary_tables(tokens, n)
    turned = jnp.concatenate(
        [query_t, query_t[NOPE + ROPE // 2 :], query_t[NOPE : NOPE + ROPE // 2]], axis=0
    )
    latent_turned = jnp.concatenate(
        [latent_w, latent_w[:, LATENT + ROPE // 2 :], latent_w[:, LATENT : LATENT + ROPE // 2]],
        axis=1,
    )
    normed, query, keys, values, latent, out_w_mine = front(
        first_all, cos_table, sin_table, attn_gain[None], lat_gain[None], turned, latent_turned, expand_w
    )
    out_w_other = from_partner(out_w_mine)
    attended_head, attended_exact, lse = attend(prefix_length, query, keys, values)
    (attended_blocks,) = exchange(2, swaps=(attended_head.reshape(n, tokens, VH),))
    attended = attended_blocks.transpose(1, 0, 2).reshape(tokens, HEADS * VH)

    residual_in = layer_input.astype(F32)
    input_scale = rms_scale(residual_in)
    input_unit = residual_in * input_scale
    out_mine = product("ta,ad->td", attended, out_w_mine)
    out_other = product("ta,ad->td", attended, out_w_other)
    residual_mid = residual_in + jnp.concatenate(
        [jnp.where(even, out_mine, out_other), jnp.where(even, out_other, out_mine)], axis=1
    )
    mid_scale = rms_scale(residual_mid)
    mid_unit = residual_mid * mid_scale
    own_ffn_in = (mid_unit * ffn_gain).astype(BF16)
    (ffn_blocks,) = gather(own_ffn_in, 3)
    query_cols = query_weight.shape[1] // 2
    query_w_half = lax.dynamic_slice_in_dim(query_weight, half * query_cols, query_cols, 1)
    query_w_half, ffn_blocks = lax.optimization_barrier((query_w_half, ffn_blocks))
    query_w_mine = lax.all_gather(query_w_half, "ep", axis=0, tiled=True)
    query_w_other = from_partner(query_w_mine)
    ffn_in = ffn_blocks.reshape(length, D)

    own_lane = (jnp.arange(128, dtype=jnp.int32) == e).astype(F32)[None]
    chosen = jnp.any(routes == e, axis=-1)
    chosen_int = chosen.astype(jnp.int32)
    place = jnp.cumsum(chosen_int, axis=1) - chosen_int
    kept = chosen & (place < capacity)
    dispatch = (
        (place[:, None, :] == jnp.arange(capacity, dtype=jnp.int32)[None, :, None])
        & kept[:, None, :]
    ).astype(BF16)
    shared_width = gate_t.shape[0]
    fill = ((0, -shared_width % 128), (0, 0))
    (
        out_partial,
        ffn_partial,
        dot_partial,
        router_all,
        incoming,
        expert_hidden,
        slot_grad,
        grad_expert_gu,
        shared_hidden,
        grad_shared_gu,
    ) = ffn(
        ffn_blocks,
        all_out_grad.reshape(n, tokens, D),
        dispatch,
        own_lane,
        jnp.pad(router_w, ((0, 0), (0, 128 - n))),
        jnp.pad(gate_t, fill),
        jnp.pad(up_t, fill),
        jnp.pad(shared_down, fill),
        expert_gate[0],
        expert_up[0],
        expert_down[0],
    )
    ffn_sum, dot_sum, out_sum, *products = exchange(
        4,
        sums=(ffn_partial, dot_partial, out_partial),
        jobs=((expert_hidden, slot_grad, 1, groups), (incoming, grad_expert_gu, 2, groups)),
    )
    layer_output = (residual_mid + out_sum).astype(BF16)

    def by_group(values):
        return over_groups(values.reshape(groups, values.shape[0] // groups, -1))

    router_own = lax.dynamic_index_in_dim(router_all, e, 0, keepdims=False)[:, :n]
    grad_probs = dot_sum[:, :n]
    grad_logits = (
        router_own * (grad_probs - jnp.sum(router_own * grad_probs, axis=-1, keepdims=True))
    ).astype(BF16)
    grad_ffn_in = ffn_sum + product("te,de->td", grad_logits, router_w)
    grad_ffn_gain = jnp.sum(grad_ffn_in * mid_unit, axis=0)
    grad_mid = output_grad.astype(F32) + norm_back(grad_ffn_in * ffn_gain, mid_unit, mid_scale)
    grad_mid_b = grad_mid.astype(BF16)
    mid_left, mid_right = grad_mid_b[:, : D // 2], grad_mid_b[:, D // 2 :]
    grad_attended = (
        product("td,ad->ta", jnp.where(even, mid_left, mid_right), out_w_mine)
        + product("td,ad->ta", jnp.where(even, mid_right, mid_left), out_w_other)
    ).astype(BF16)
    output_w_partial = product_over_groups(attended, grad_mid_b).astype(BF16)
    (grad_att_blocks,) = exchange(
        5, swaps=(grad_attended.reshape(tokens, HEADS, VH).transpose(1, 0, 2),)
    )
    grad_att = grad_att_blocks.reshape(length, VH)

    def blocks_over_groups(blocks):
        total = blocks[0].astype(F32)
        for k in range(1, groups):
            shift = [(g, (g + k) % groups) for g in range(groups)]
            total = total + lax.ppermute(blocks[k], "grp", shift).astype(F32)
        return total

    expert_down_grad, expert_gate_grad, expert_up_grad = (
        blocks_over_groups(products[k * groups : (k + 1) * groups])[None] for k in range(3)
    )

    grad_router = product("te,td->ed", grad_logits, own_ffn_in)

    delta = jnp.sum(grad_att.astype(F32) * attended_exact, axis=-1)[None]
    grad_query_raw, grad_keys, grad_values = attend_back(
        prefix_length, query, grad_att, lse, delta, keys, values
    )
    grad_query, grad_expanded, latent_partial, rope_partial = back(
        cos_table, sin_table, grad_query_raw, grad_keys, grad_values, expand_w
    )
    (
        latent_sum,
        rope_sum,
        output_weight_grad,
        query_blocks,
        side_down,
        *products,
    ) = exchange(
        6,
        sums=(
            latent_partial.reshape(n, tokens, LATENT),
            rope_partial.reshape(n, tokens, 2 * ROPE),
            output_w_partial.reshape(n, rows_out, D),
        ),
        swaps=(grad_query.reshape(n, tokens, -1),),
        jobs=(
            (shared_hidden.reshape(length, -1), all_out_grad, 1, 1),
            (ffn_in, grad_shared_gu.reshape(length, -1), 2, groups),
            (normed, grad_query, 1, groups),
            (latent, grad_expanded, 1, groups),
        ),
    )
    shared_down_grad = to_row_owner(by_group(side_down[:shared_width]))
    side_gate, side_up, side_query, grad_expand = (
        blocks_over_groups(products[k * groups : (k + 1) * groups]).astype(BF16) for k in range(4)
    )
    side_gate, side_up = side_gate[:, :shared_width], side_up[:, :shared_width]
    side_query = side_query[:, : query_t.shape[0]]

    own_normed = (input_unit * attn_gain).astype(BF16)
    own_raw = product("td,dc->tc", own_normed, latent_w[:, :LATENT])
    latent_scale = rms_scale(own_raw)
    latent_unit = own_raw * latent_scale
    grad_latent_gain = jnp.sum(latent_sum * latent_unit, axis=0)
    grad_compressed = jnp.concatenate(
        [
            norm_back(latent_sum * lat_gain, latent_unit, latent_scale),
            unrotate(
                rope_sum[:, :ROPE],
                own(cos_table)[:, : ROPE // 2],
                own(sin_table)[:, ROPE // 2 : ROPE],
            ),
        ],
        axis=-1,
    ).astype(BF16)
    latent_w_partial = product_over_groups(
        own_normed, jnp.pad(grad_compressed, ((0, 0), (0, 640 - LATENT - ROPE)))
    ).astype(BF16)
    own_part = product("tc,dc->td", grad_compressed, latent_w)

    def of_heads(part):
        heads = lax.dynamic_slice_in_dim(query_blocks, part * (n // 2), n // 2, 0)
        return heads[:, :, : NOPE + ROPE].transpose(1, 0, 2).reshape(tokens, -1)

    grad_normed = (
        product("tc,dc->td", of_heads(half), query_w_mine)
        + product("tc,dc->td", of_heads(1 - half), query_w_other)
        + own_part
    )
    grad_attn_gain = jnp.sum(grad_normed * input_unit, axis=0)

    def by_owner(values, rows):
        blocks = values.reshape(-1, groups, n, rows).transpose(2, 1, 0, 3)
        return blocks.reshape(n, groups, -1)

    small = jnp.concatenate(
        [
            by_owner(grad_attn_gain, rows_out),
            by_owner(grad_ffn_gain, rows_out),
            by_owner(grad_router, rows_out),
            by_owner(grad_latent_gain, expand_rows),
        ],
        axis=2,
    )
    (
        latent_weight_sum,
        small_all,
        query_weight_grad,
        shared_gate_grad,
        shared_up_grad,
        expand_weight_grad,
    ) = exchange(
        7,
        sums=(latent_w_partial.reshape(n, rows_out, -1),),
        swaps=(
            small,
            side_query.reshape(n, rows_out, -1),
            side_gate.reshape(n, rows_out, -1),
            side_up.reshape(n, rows_out, -1),
            grad_expand.reshape(n, expand_rows, -1),
        ),
        laid=4,
    )
    input_grad = (
        grad_mid + norm_back(grad_normed * attn_gain, input_unit, input_scale)
    ).astype(BF16)
    latent_weight_grad = latent_weight_sum[:, : LATENT + ROPE]
    small_sum = jnp.sum(small_all, axis=0)
    if groups == 2:
        g = lax.axis_index("grp")
        mine = lax.dynamic_index_in_dim(small_sum, g, 0, keepdims=False)
        theirs = lax.dynamic_index_in_dim(small_sum, 1 - g, 0, keepdims=False)
        small_sum = mine + lax.ppermute(theirs, "grp", [(0, 1), (1, 0)])
    else:
        small_sum = lax.psum_scatter(small_sum, "grp", scatter_dimension=0)
    attention_gain_grad = small_sum[:rows_out]
    feedforward_gain_grad = small_sum[rows_out : 2 * rows_out]
    router_weight_grad = small_sum[2 * rows_out : (2 + n) * rows_out].reshape(n, rows_out).T
    latent_gain_grad = small_sum[(2 + n) * rows_out :]
    return (
        layer_output,
        input_grad,
        attention_gain_grad,
        query_weight_grad,
        latent_weight_grad,
        latent_gain_grad,
        expand_weight_grad,
        output_weight_grad,
        feedforward_gain_grad,
        router_weight_grad,
        shared_gate_grad,
        shared_up_grad,
        shared_down_grad,
        expert_gate_grad,
        expert_up_grad,
        expert_down_grad,
    )


def solution(mesh):
    return jax.shard_map(
        per_device,
        mesh=mesh,
        in_specs=(
            P(("grp", "ep"), None),
            P("ep"),
            P("ep", None),
            P("ep", None),
            P("ep"),
            P("ep", None),
            P("ep", None),
            P("ep"),
            P("ep", None),
            P("ep", None),
            P("ep", None),
            P("ep", None),
            P("ep", None, None),
            P("ep", None, None),
            P("ep", None, None),
            P(("grp", "ep"), None),
            P("grp"),
            P(("grp", "ep"), None),
        ),
        out_specs=(
            P(("grp", "ep"), None),
            P(("grp", "ep"), None),
            P(("grp", "ep")),
            P(("grp", "ep"), None),
            P(("grp", "ep"), None),
            P(("grp", "ep")),
            P(("grp", "ep"), None),
            P(("grp", "ep"), None),
            P(("grp", "ep")),
            P(("grp", "ep"), None),
            P(("grp", "ep"), None),
            P(("grp", "ep"), None),
            P(("grp", "ep"), None),
            P("ep", "grp", None),
            P("ep", "grp", None),
            P("ep", "grp", None),
        ),
        check_vma=False,
    )
```
